128 devices in a mesh: dp: 64 (over z, x_hi, y, core), tensor: 2 (over x_lo).
Axes of the slice: x: 4 (x_hi: 2, x_lo: 2; x = x_hi * 2 + x_lo), y: 4, z: 4, core: 2. Of those that a mesh axis runs over, the one named last changes fastest.
Arguments:
- resid: bfloat16 [32768, 1536], P(('dp', 'tensor')), may hold values from -6 to 6
- cotangent: bfloat16 [32768, 1536], P(('dp', 'tensor')), may hold values from -6 to 6
- segments: int32 [32768], P('dp'), may hold values from 0 to 127, as said below
- pre_gain: bfloat16 [1536], P(('dp', 'tensor')), may hold values from 0.25 to 1.75
- w_z: bfloat16 [1536, 3072], P('dp', 'tensor'), may hold values from -0.15625 to 0.15625
- w_x: bfloat16 [1536, 3072], P('dp', 'tensor'), may hold values from -0.5 to 0.5
- w_bc: bfloat16 [1536, 256], P(('dp', 'tensor')), may hold values from -0.15625 to 0.15625
- w_dt: bfloat16 [1536, 48], P('dp', 'tensor'), may hold values from -0.15625 to 0.15625
- conv_x: float32 [4, 3072], P(None, 'tensor'), may hold values from -3 to 3
- conv_x_bias: float32 [3072], P('tensor'), may hold values from -3 to 3
- conv_bc: float32 [4, 256], replicated, may hold values from -3 to 3
- conv_bc_bias: float32 [256], replicated, may hold values from -3 to 3
- dt_bias: float32 [48], P('tensor'), may hold values from -1 to 0.5
- a_log: float32 [48], P('tensor'), may hold values from -6.9 to -3
- d_skip: float32 [48], P('tensor'), may hold values from 0.5 to 1.5
- gate_gain: float32 [3072], P('tensor'), may hold values from 0.25 to 1.75
- w_out: bfloat16 [3072, 1536], P('tensor', 'dp'), may hold values from -0.109375 to 0.109375
Outputs:
- out: bfloat16 [32768, 1536], P(('dp', 'tensor'))
- grad_resid: float32 [32768, 1536], P(('dp', 'tensor'))
- grad_pre_gain: float32 [1536], P(('dp', 'tensor'))
- grad_w_z: float32 [1536, 3072], P('dp', 'tensor')
- grad_w_x: float32 [1536, 3072], P('dp', 'tensor')
- grad_w_bc: float32 [1536, 256], P(('dp', 'tensor'))
- grad_w_dt: float32 [1536, 48], P('dp', 'tensor')
- grad_conv_x: float32 [4, 3072], P(None, 'tensor')
- grad_conv_x_bias: float32 [3072], P('tensor')
- grad_conv_bc: float32 [4, 256], replicated
- grad_conv_bc_bias: float32 [256], replicated
- grad_dt_bias: float32 [48], P('tensor')
- grad_a_log: float32 [48], P('tensor')
- grad_d_skip: float32 [48], P('tensor')
- grad_gate_gain: float32 [3072], P('tensor')
- grad_w_out: float32 [3072, 1536], P('tensor', 'dp')
The draws below stay inside these ranges and needn't reach their ends.
Inputs may be any that keep to these rules, and one draw needn't show every extreme that they name: `segments`: numbers never fall along the tokens; each sequence of 512 tokens holds exactly two documents, the first of sequence s numbered 2 s and the second 2 s + 1, each of one token or more.
All inputs are finite; a program needn't handle non-finite values.
Results may differ from the reference program's by a relative error of at most 0.011.
Values may be sent and summed in bfloat16 or wider, within the bound.
No kernel may reach another device: no remote copies, remote signals or barrier semaphores. Data moves between devices by JAX's collectives and lax.ppermute only.
A program may use at most 192 MiB of HBM per device.

```python
import math
import jax
import jax.numpy as jnp
from jax import lax

D = 1536
HEADS = 48
NSTATE = 128
KCONV = 4
GROUP = 256
DI = 3072
SEQ = 512
TOKENS = 32768


def draw_segments(key, part):
    key = jax.random.fold_in(key, 7)
    first_key, second_key = jax.random.split(key)
    seq_count = TOKENS // SEQ
    cut_point = jax.random.randint(first_key, (seq_count,), 1, SEQ // 4 + 1)
    side_pick = jax.random.randint(second_key, (seq_count,), 0, 2)
    boundary = jnp.where(side_pick == 1, SEQ - cut_point, cut_point)
    position = jnp.arange(SEQ, dtype=jnp.int32)
    second_doc = (position[None, :] >= boundary[:, None]).astype(jnp.int32)
    numbers = jnp.arange(seq_count, dtype=jnp.int32)[:, None] * 2 + second_doc
    return numbers.reshape(-1).astype(jnp.int32)


def draw_w_x(key, part):
    key = jax.random.fold_in(key, 11)
    column = jnp.arange(DI, dtype=jnp.float32) / (DI - 1)
    base = jax.random.normal(key, (D, DI), jnp.float32)
    scale = jnp.exp(column * math.log(3.0) * 0.5) * 0.7
    return (base * scale / math.sqrt(D)).astype(jnp.bfloat16)


def block_scale(own_key, shape, cuts, least, high):
    factor_of = 1.0
    for dim, shards_of in cuts:
        draws = jax.random.uniform(jax.random.fold_in(jax.random.fold_in(own_key, 6), dim), (shards_of,), jnp.float32, least / len(cuts), high / len(cuts))
        factor_of = factor_of * jnp.repeat(jnp.exp(draws), shape[dim] // shards_of).reshape((-1,) + (1,) * (len(shape) - 1 - dim))
    return factor_of


def scatter_about(stream_key, extent, width, reach, cuts=(), kind=jnp.bfloat16):
    level = block_scale(stream_key, extent, cuts, -0.22, 0.18) if cuts else 1.0
    values = jax.random.normal(stream_key, extent, jnp.float32) * width * level
    return jnp.minimum(jnp.maximum(values, -reach), reach).astype(kind)


def setup_inputs(seed: int = 0) -> dict:
    arg_keys = jax.random.split(jax.random.key(seed), 18)
    return {
        "resid": scatter_about(arg_keys[0], (TOKENS, D), 1.0, 6.0, ((0, 128),)),
        "cotangent": scatter_about(arg_keys[1], (TOKENS, D), 1.0, 6.0, ((0, 128),)),
        "segments": draw_segments(jax.random.fold_in(arg_keys[17], 71), 0),
        "pre_gain": jnp.clip(1.0 + 0.15 * jax.random.normal(arg_keys[3], (D,), jnp.float32), 0.25, 1.75).astype(jnp.bfloat16),
        "w_z": scatter_about(arg_keys[4], (D, DI), D ** -0.5, 0.15625, ((0, 64), (1, 2))),
        "w_x": draw_w_x(jax.random.fold_in(arg_keys[17], 71), 0),
        "w_bc": scatter_about(arg_keys[6], (D, 2 * NSTATE), D ** -0.5, 0.15625, ((0, 128),)),
        "w_dt": scatter_about(arg_keys[7], (D, HEADS), D ** -0.5, 0.15625, ((0, 64), (1, 2))),
        "conv_x": scatter_about(arg_keys[8], (KCONV, DI), 0.5, 3.0, ((1, 2),), jnp.float32),
        "conv_x_bias": scatter_about(arg_keys[9], (DI,), 0.3, 3.0, ((0, 2),), jnp.float32),
        "conv_bc": scatter_about(arg_keys[10], (KCONV, 2 * NSTATE), 0.5, 3.0, (), jnp.float32),
        "conv_bc_bias": scatter_about(arg_keys[11], (2 * NSTATE,), 0.3, 3.0, (), jnp.float32),
        "dt_bias": jnp.clip(-1.0 + 1.5 * jax.random.uniform(arg_keys[12], (HEADS,), jnp.float32) ** block_scale(arg_keys[12], (HEADS,), ((0, 2),), -0.2, 0.2), -1.0, 0.5),
        "a_log": jnp.clip(-6.9 + 3.9 * jax.random.uniform(arg_keys[13], (HEADS,), jnp.float32) ** block_scale(arg_keys[13], (HEADS,), ((0, 2),), -0.2, 0.2), -6.9, -3.0),
        "d_skip": jnp.clip(0.5 + 1.0 * jax.random.uniform(arg_keys[14], (HEADS,), jnp.float32) ** block_scale(arg_keys[14], (HEADS,), ((0, 2),), -0.2, 0.2), 0.5, 1.5),
        "gate_gain": jnp.clip(1.0 + 0.15 * jax.random.normal(arg_keys[15], (DI,), jnp.float32), 0.25, 1.75),
        "w_out": scatter_about(arg_keys[16], (DI, D), DI ** -0.5, 0.109375, ((0, 2), (1, 64))),
    }


EPS = 1e-05
HIGH = lax.Precision.HIGHEST

@jax.custom_vjp
def low(v):
    return lax.optimization_barrier(v.astype(jnp.bfloat16)).astype(jnp.float32)

@jax.custom_vjp
def low_back(v):
    return v

def low_keep(v):
    return (low(v), None)

def low_pass(kept, grad):
    return (grad,)

def back_keep(v):
    return (v, None)

def back_low(kept, grad):
    return (low(grad),)
low.defvjp(low_keep, low_pass)
low_back.defvjp(back_keep, back_low)

def silu_act(values):
    return values * jax.nn.sigmoid(values)

def conv_mix(values, kernel, conv_bias, segment):
    kernel_size = kernel.shape[0]
    row_count = values.shape[0]
    padded = jnp.concatenate([jnp.zeros((kernel_size - 1, values.shape[1]), values.dtype), values], axis=0)
    seg_pad = jnp.concatenate([jnp.full((kernel_size - 1,), -1, jnp.int32), segment.astype(jnp.int32)], axis=0)
    summed = jnp.broadcast_to(conv_bias[None, :], values.shape)
    for offset in range(kernel_size):
        window = padded[offset:offset + row_count]
        keep_mask = (seg_pad[offset:offset + row_count] == segment).astype(values.dtype)
        summed = summed + window * kernel[offset][None, :] * keep_mask[:, None]
    return summed

def ssd_scan(x_heads, dt_full, decay_rate, b_state, c_state, segment):
    length = x_heads.shape[0]
    head_count = x_heads.shape[1]
    head_size = x_heads.shape[2]
    nstate = b_state.shape[1]
    blocks = length // GROUP
    row_ids = lax.broadcasted_iota(jnp.int32, (GROUP, GROUP), 0)
    col_ids = lax.broadcasted_iota(jnp.int32, (GROUP, GROUP), 1)
    causal = row_ids >= col_ids

    def regroup(values):
        return values.reshape((blocks, GROUP) + values.shape[1:])

    def advance(carried, pieces):
        states, last_seg = carried
        x_blk, dt_blk, b_blk, c_blk, seg_blk = pieces
        log_decay = jnp.cumsum(dt_blk * decay_rate[None, :], axis=0).T
        log_gaps = log_decay[:, :, None] - log_decay[:, None, :]
        inside = causal & (seg_blk[:, None] == seg_blk[None, :])
        decays = jnp.where(inside[None], jnp.exp(jnp.minimum(log_gaps, 0.0)), 0.0)
        scores = jnp.einsum('in,jn->ij', c_blk, b_blk, precision=HIGH)
        mixing = decays * scores[None] * dt_blk.T[:, None, :]
        within = jnp.einsum('hij,jhp->ihp', mixing, x_blk, precision=HIGH)
        alive_mask = (seg_blk == last_seg).astype(x_blk.dtype)
        carry_in = jnp.einsum('in,hpn->ihp', c_blk, states, precision=HIGH)
        output = within + carry_in * (jnp.exp(log_decay).T * alive_mask[:, None])[:, :, None]
        ending = (seg_blk == seg_blk[-1]).astype(x_blk.dtype)
        tail_weight = jnp.exp(log_decay[:, -1:] - log_decay).T * ending[:, None] * dt_blk
        fresh_state = jnp.einsum('jhp,jn->hpn', x_blk * tail_weight[:, :, None], b_blk, precision=HIGH)
        new_states = states * (jnp.exp(log_decay[:, -1]) * alive_mask[-1])[:, None, None] + fresh_state
        return ((new_states, seg_blk[-1]), output)
    start_carry = (jnp.zeros((head_count, head_size, nstate), x_heads.dtype), jnp.array(-1, jnp.int32))
    final_carry, block_outs = lax.scan(jax.checkpoint(advance), start_carry, (regroup(x_heads), regroup(dt_full), regroup(b_state), regroup(c_state), regroup(segment)))
    return block_outs.reshape(length, head_count, head_size)

def mixer_core(inputs, segment):
    x_raw, bc_raw, dt_raw, gate_raw, conv_x, conv_x_bias, conv_bc, conv_bc_bias, dt_bias, a_log, d_skip = inputs
    length = x_raw.shape[0]
    full_width = x_raw.shape[1]
    head_count = dt_bias.shape[0]
    head_size = full_width // head_count
    x_act = silu_act(conv_mix(x_raw, conv_x, conv_x_bias, segment))
    bc_act = silu_act(conv_mix(bc_raw, conv_bc, conv_bc_bias, segment))
    nstate = bc_act.shape[1] // 2
    dt_full = jax.nn.softplus(dt_raw + dt_bias[None, :])
    decay_rate = -jnp.exp(a_log)
    x_heads = x_act.reshape(length, head_count, head_size)
    mixed_heads = ssd_scan(x_heads, dt_full, decay_rate, bc_act[:, :nstate], bc_act[:, nstate:], segment)
    mixed_heads = mixed_heads + d_skip[None, :, None] * x_heads
    return mixed_heads.reshape(length, full_width) * silu_act(gate_raw)

def layer_block(resid, weights, segment):
    pre_gain, w_z, w_x, w_bc, w_dt, conv_x, conv_x_bias, conv_bc, conv_bc_bias, dt_bias, a_log, d_skip, gate_gain, w_out = weights
    mean_sq = lax.optimization_barrier(jnp.mean(resid * resid, axis=-1, keepdims=True))
    normed = low(resid * lax.rsqrt(mean_sq + EPS) * pre_gain[None, :])
    gate_raw = low_back(jnp.dot(normed, w_z, precision=HIGH))
    x_raw = low_back(jnp.dot(normed, w_x, precision=HIGH))
    bc_raw = low_back(jnp.dot(normed, w_bc, precision=HIGH))
    dt_raw = low_back(jnp.dot(normed, w_dt, precision=HIGH))
    mixed = mixer_core((x_raw, bc_raw, dt_raw, gate_raw, conv_x, conv_x_bias, conv_bc, conv_bc_bias, dt_bias, a_log, d_skip), segment)
    square_sum = lax.optimization_barrier(jnp.sum(mixed * mixed, axis=-1, keepdims=True))
    scaled = low(mixed * lax.rsqrt(square_sum / mixed.shape[1] + EPS) * gate_gain[None, :])
    return resid + jnp.dot(scaled, w_out, precision=HIGH)

def reference(resid, cotangent, segments, pre_gain, w_z, w_x, w_bc, w_dt, conv_x, conv_x_bias, conv_bc, conv_bc_bias, dt_bias, a_log, d_skip, gate_gain, w_out):
    weights = tuple((entry.astype(jnp.float32) for entry in (pre_gain, w_z, w_x, w_bc, w_dt, conv_x, conv_x_bias, conv_bc, conv_bc_bias, dt_bias, a_log, d_skip, gate_gain, w_out)))
    per_block = math.gcd(TOKENS // SEQ, max(1, 4096 // SEQ))
    block_rows = per_block * SEQ
    blocks = TOKENS // block_rows
    stacked = (resid.astype(jnp.float32).reshape(blocks, block_rows, D), cotangent.astype(jnp.float32).reshape(blocks, block_rows, D), segments.astype(jnp.int32).reshape(blocks, block_rows))

    def visit_block(totals, pieces):
        resid_blk, cot_blk, seg_blk = pieces
        result, pullback = jax.vjp(lambda inputs, params: layer_block(inputs, params, seg_blk), resid_blk, weights)
        grad_inputs, grad_params = pullback(cot_blk)
        summed = tuple((left + right for left, right in zip(totals, grad_params)))
        return (summed, (result.astype(jnp.bfloat16), grad_inputs))
    totals, (block_outs, block_grads) = lax.scan(visit_block, tuple((jnp.zeros_like(entry) for entry in weights)), stacked)
    grad_pre_gain, grad_w_z, grad_w_x, grad_w_bc, grad_w_dt, grad_conv_x, grad_conv_x_bias, grad_conv_bc, grad_conv_bc_bias, grad_dt_bias, grad_a_log, grad_d_skip, grad_gate_gain, grad_w_out = totals
    return (block_outs.reshape(TOKENS, D), block_grads.reshape(TOKENS, D), grad_pre_gain, grad_w_z, grad_w_x, grad_w_bc, grad_w_dt, grad_conv_x, grad_conv_x_bias, grad_conv_bc, grad_conv_bc_bias, grad_dt_bias, grad_a_log, grad_d_skip, grad_gate_gain, grad_w_out)
```

```python
import jax
import jax.numpy as jnp
from jax import lax
from jax.sharding import Mesh, PartitionSpec as P

GROUP = 256
EPS = 1e-05
HIGH = lax.Precision.HIGHEST
BF = jnp.bfloat16
F32 = jnp.float32


def silu_act(values):
    return values * jax.nn.sigmoid(values)


def conv_mix(values, kernel, conv_bias, segment):
    kernel_size = kernel.shape[0]
    row_count = values.shape[0]
    padded = jnp.concatenate(
        [jnp.zeros((kernel_size - 1, values.shape[1]), values.dtype), values], axis=0
    )
    seg_pad = jnp.concatenate([jnp.full((kernel_size - 1,), -1, jnp.int32), segment], axis=0)
    summed = jnp.broadcast_to(conv_bias[None, :], values.shape)
    for offset in range(kernel_size):
        window = padded[offset : offset + row_count]
        keep_mask = (seg_pad[offset : offset + row_count] == segment).astype(values.dtype)
        summed = summed + window * kernel[offset][None, :] * keep_mask[:, None]
    return summed


def ssd_scan(x_heads, dt_full, decay_rate, b_state, c_state, segment):
    length = x_heads.shape[0]
    head_count = x_heads.shape[1]
    head_size = x_heads.shape[2]
    nstate = b_state.shape[1]
    blocks = length // GROUP
    row_ids = lax.broadcasted_iota(jnp.int32, (GROUP, GROUP), 0)
    col_ids = lax.broadcasted_iota(jnp.int32, (GROUP, GROUP), 1)
    causal = row_ids >= col_ids

    def regroup(values):
        return values.reshape((blocks, GROUP) + values.shape[1:])

    def advance(carried, pieces):
        states, last_seg = carried
        x_blk, dt_blk, b_blk, c_blk, seg_blk = pieces
        log_decay = jnp.cumsum(dt_blk * decay_rate[None, :], axis=0).T
        log_gaps = log_decay[:, :, None] - log_decay[:, None, :]
        inside = causal & (seg_blk[:, None] == seg_blk[None, :])
        decays = jnp.where(inside[None], jnp.exp(jnp.minimum(log_gaps, 0.0)), 0.0)
        scores = jnp.einsum("in,jn->ij", c_blk, b_blk, precision=HIGH)
        mixing = decays * scores[None] * dt_blk.T[:, None, :]
        within = jnp.einsum("hij,jhp->ihp", mixing, x_blk, precision=HIGH)
        alive_mask = (seg_blk == last_seg).astype(x_blk.dtype)
        carry_in = jnp.einsum("in,hpn->ihp", c_blk, states, precision=HIGH)
        output = within + carry_in * (jnp.exp(log_decay).T * alive_mask[:, None])[:, :, None]
        ending = (seg_blk == seg_blk[-1]).astype(x_blk.dtype)
        tail_weight = jnp.exp(log_decay[:, -1:] - log_decay).T * ending[:, None] * dt_blk
        fresh_state = jnp.einsum(
            "jhp,jn->hpn", x_blk * tail_weight[:, :, None], b_blk, precision=HIGH
        )
        new_states = (
            states * (jnp.exp(log_decay[:, -1]) * alive_mask[-1])[:, None, None] + fresh_state
        )
        return ((new_states, seg_blk[-1]), output)

    start_carry = (
        jnp.zeros((head_count, head_size, nstate), x_heads.dtype),
        jnp.array(-1, jnp.int32),
    )
    final_carry, block_outs = lax.scan(
        jax.checkpoint(advance),
        start_carry,
        (regroup(x_heads), regroup(dt_full), regroup(b_state), regroup(c_state), regroup(segment)),
    )
    return block_outs.reshape(length, head_count, head_size)


def mixer_core(inputs, segment):
    (x_raw, bc_raw, dt_raw, gate_raw, conv_x, conv_x_bias, conv_bc, conv_bc_bias, dt_bias, a_log, d_skip) = inputs
    length, full_width = x_raw.shape
    head_count = dt_bias.shape[0]
    x_act = silu_act(conv_mix(x_raw, conv_x, conv_x_bias, segment))
    bc_act = silu_act(conv_mix(bc_raw, conv_bc, conv_bc_bias, segment))
    nstate = bc_act.shape[1] // 2
    dt_full = jax.nn.softplus(dt_raw + dt_bias[None, :])
    decay_rate = -jnp.exp(a_log)
    x_heads = x_act.reshape(length, head_count, full_width // head_count)
    mixed_heads = ssd_scan(x_heads, dt_full, decay_rate, bc_act[:, :nstate], bc_act[:, nstate:], segment)
    mixed_heads = mixed_heads + d_skip[None, :, None] * x_heads
    return mixed_heads.reshape(length, full_width) * silu_act(gate_raw)


def swap(a, axis):
    return lax.ppermute(a, axis, [(0, 1), (1, 0)])


def turn(a, axis, k):
    return lax.ppermute(a, axis, [(i, (i + k) % 4) for i in range(4)])


def pair(own, other, axis):
    first = lax.axis_index(axis) == 0
    return jnp.stack([jnp.where(first, own, other), jnp.where(first, other, own)])


def mine(a, axis, dim, size):
    i = lax.axis_index(axis)
    return (
        lax.dynamic_slice_in_dim(a, i * size, size, dim),
        lax.dynamic_slice_in_dim(a, (1 - i) * size, size, dim),
    )


def gather4(blk, axis, dim):
    i = lax.axis_index(axis)
    got = [blk, turn(blk, axis, 1), turn(blk, axis, 2), turn(blk, axis, 3)]
    shape = blk.shape[:dim] + (4,) + blk.shape[dim:]
    out = jnp.zeros(shape, blk.dtype)
    for k, piece in enumerate(got):
        out = lax.dynamic_update_slice_in_dim(out, jnp.expand_dims(piece, dim), (i - k) % 4, dim)
    return out


def gather_chips(blk, order):
    b = pair(blk, swap(blk, "xh"), "xh")
    if order == "yz":
        b = gather4(gather4(b, "y", 1), "z", 0)
    else:
        b = gather4(gather4(b, "z", 0), "y", 2)
    return b.reshape(1536, blk.shape[1])


def reduce4(a, axis, dim):
    i = lax.axis_index(axis)

    def entry(k):
        return lax.squeeze(lax.dynamic_slice_in_dim(a, (i + k) % 4, 1, dim), (dim,))

    total = entry(0).astype(F32)
    for k in (1, 2, 3):
        total = total + turn(entry(k), axis, k).astype(F32)
    return total


def reduce_chips(g, order):
    b = g.reshape(4, 2, 4, 48, g.shape[1])
    if order == "yz":
        b = reduce4(b, "y", 2).astype(BF)
        b = reduce4(b, "z", 0).astype(BF)
    else:
        b = reduce4(b, "z", 0).astype(BF)
        b = reduce4(b, "y", 1).astype(BF)
    own, other = mine(b, "xh", 0, 1)
    return own[0].astype(F32) + swap(other[0], "xh").astype(F32)


def sum_chips(a):
    a = a + swap(a, "xh")
    a = a + turn(a, "y", 1) + turn(a, "y", 2) + turn(a, "y", 3)
    return a + turn(a, "z", 1) + turn(a, "z", 2) + turn(a, "z", 3)


def shards(resid, cotangent, segments, pre_gain, w_z, w_x, w_bc, w_dt, conv_x, conv_x_bias, conv_bc, conv_bc_bias, dt_bias, a_log, d_skip, gate_gain, w_out):
    core = lax.axis_index("c")
    def group_tokens(a):
        half = pair(a, swap(a, "xl"), "xl").reshape(512, a.shape[1])
        return pair(half, swap(half, "c"), "c")

    def quarter(a, size):
        own, other = mine(a, "c", 1, size)
        return pair(own, swap(other, "c"), "c").reshape(48, size)

    bc_rows = pair(w_bc, swap(w_bc, "xl"), "xl").reshape(24, 256)
    gain_rows = pair(pre_gain[:, None], swap(pre_gain[:, None], "xl"), "xl").reshape(24, 1)
    bc_rows = pair(bc_rows, swap(bc_rows, "c"), "c").reshape(48, 256)
    gain_rows = pair(gain_rows, swap(gain_rows, "c"), "c").reshape(48, 1)
    wx_q, wz_q, wo_q, wdt_q = quarter(w_x, 768), quarter(w_z, 768), quarter(w_out.T, 768), quarter(w_dt, 12)
    side = jnp.concatenate([wdt_q, gain_rows, jnp.zeros((48, 115), BF)], axis=1)
    first = jnp.concatenate([wx_q, bc_rows, side], axis=1)
    full_a = gather_chips(first[:, :512], "yz")
    full_b = gather_chips(first[:, 512:], "zy")
    full_z = gather_chips(wz_q, "yz")
    full_o = gather_chips(wo_q, "zy")
    full_1 = jnp.concatenate([full_a, full_b], axis=1)
    full_x, full_bc, full_dt, full_gain = full_1[:, :768], full_1[:, 768:1024], full_1[:, 1024:1036], full_1[:, 1036]

    tokens = group_tokens(resid).reshape(1024, 1536)
    cot = group_tokens(cotangent).reshape(1024, 1536)
    seg = pair(segments, swap(segments, "c"), "c")

    gain_wide = full_gain.astype(F32)
    wide = tokens.astype(F32)
    inv_all = lax.rsqrt(jnp.mean(wide * wide, axis=-1, keepdims=True) + EPS)
    normed = (wide * inv_all * gain_wide[None, :]).astype(BF)

    def dot(a, b):
        return jnp.dot(a, b, preferred_element_type=F32)

    gate_raw, x_raw, bc_raw, dt_raw = dot(normed, full_z), dot(normed, full_x), dot(normed, full_bc), dot(normed, full_dt)

    def own(a, size):
        return mine(a, "c", a.ndim - 1, size)[0]

    cx, cxb, gg = own(conv_x, 768), own(conv_x_bias, 768), own(gate_gain, 768)
    dtb, al, dsk = own(dt_bias, 12), own(a_log, 12), own(d_skip, 12)

    def core_fn(inputs):
        x, bc, dt, gate, *params = inputs
        r = lambda a: a.reshape(2, 512, a.shape[-1])
        f = lambda x, bc, dt, gate, s: mixer_core((x, bc, dt, gate, *params), s)
        return jax.vmap(f)(r(x), r(bc), r(dt), r(gate), seg).reshape(1024, 768)

    mixed, pullback = jax.vjp(core_fn, (x_raw, bc_raw, dt_raw, gate_raw, cx, cxb, conv_bc, conv_bc_bias, dtb, al, dsk))
    grad_scaled = lax.dot_general(cot, full_o, (((1,), (0,)), ((), ())), preferred_element_type=F32)
    weighted = grad_scaled * gg[None, :]
    sums = jnp.stack([jnp.sum(mixed * mixed, axis=-1), jnp.sum(weighted * mixed, axis=-1)])
    sums = sums + swap(sums, "c")
    sums = sums + swap(sums, "xl")
    inv_gate = lax.rsqrt(sums[0] / 3072 + EPS)[:, None]
    scaled = (mixed * inv_gate * gg[None, :]).astype(BF)
    out_part = lax.dot_general(scaled, full_o, (((1,), (1,)), ((), ())), preferred_element_type=F32).astype(BF)

    def scatter_tokens(a):
        a = a.reshape(2, 512, a.shape[1])
        keep, send = mine(a, "c", 0, 1)
        half = (keep[0].astype(F32) + swap(send[0], "c").astype(F32)).astype(BF)
        keep, send = mine(half, "xl", 0, 256)
        return keep.astype(F32) + swap(send, "xl").astype(F32)

    layer_out = (resid.astype(F32) + scatter_tokens(out_part)).astype(BF)

    def over_tokens(a, b):
        return lax.dot_general(a, b, (((0,), (0,)), ((), ())), preferred_element_type=F32)

    g_out = reduce_chips(over_tokens(cot, scaled).astype(BF), "yz")
    g_gain = jnp.sum(grad_scaled * mixed * inv_gate, axis=0)
    grad_mixed = weighted * inv_gate - mixed * (inv_gate * inv_gate * inv_gate) * (sums[1] / 3072)[:, None]
    (gx, gbc, gdt, gz, g_cx, g_cxb, g_cbc, g_cbcb, g_dtb, g_al, g_dsk) = pullback(grad_mixed)[0]
    gate_low, x_low, dt_low = gz.astype(BF), gx.astype(BF), gdt.astype(BF)
    g_z = reduce_chips(over_tokens(normed, gate_low).astype(BF), "zy")

    keep, send = mine(gbc.astype(BF), "c", 1, 128)
    half = (keep.astype(F32) + swap(send, "c").astype(F32)).astype(BF)
    keep, send = mine(half, "xl", 1, 64)
    bc_low = (keep.astype(F32) + swap(send, "xl").astype(F32)).astype(BF)
    q = core * 2 + lax.axis_index("xl")
    bc_q = lax.dynamic_slice_in_dim(full_bc, q * 64, 64, 1)
    side_w = jnp.concatenate([full_x, bc_q, full_dt, jnp.zeros((1536, 52), BF)], axis=1)
    side_g = jnp.concatenate([x_low, bc_low, dt_low, jnp.zeros((1024, 52), BF)], axis=1)
    nt = lambda a, b: lax.dot_general(a, b, (((1,), (1,)), ((), ())), preferred_element_type=F32)
    token_term = nt(gate_low, full_z) + nt(side_g, side_w)
    grad_normed = scatter_tokens(token_term.astype(BF))
    g_side_full = over_tokens(normed, side_g).astype(BF)
    g_side = jnp.concatenate([reduce_chips(g_side_full[:, :512], "yz"), reduce_chips(g_side_full[:, 512:], "zy")], axis=1)

    rw = resid.astype(F32)
    inv = lax.rsqrt(jnp.mean(rw * rw, axis=-1, keepdims=True) + EPS)
    inner = jnp.sum(gain_wide[None, :] * grad_normed * rw, axis=-1, keepdims=True)
    grad_resid = cotangent.astype(F32) + gain_wide[None, :] * grad_normed * inv - rw * (inv * inv * inv) * inner / 1536

    def spread(a):
        keep, send = mine(a, "c", 0, 24)
        got = pair(keep, swap(send, "c"), "c")
        return jnp.concatenate([got[0], got[1]], axis=1)

    grad_w_z, grad_w_x, grad_w_dt = spread(g_z), spread(g_side[:, :768]), spread(g_side[:, 832:844])
    grad_w_out_t = spread(g_out)
    bc24 = spread(g_side[:, 768:832]).reshape(24, 2, 64)
    keep, send = mine(bc24, "xl", 0, 12)
    got = pair(keep, swap(send, "xl"), "xl")
    grad_w_bc = got.transpose(1, 2, 0, 3).reshape(12, 256)

    tall = lambda a, b: jnp.sum(a.astype(F32) * b, axis=1)
    pg = tall(w_z, grad_w_z) + tall(w_x, grad_w_x) + tall(w_dt, grad_w_dt)
    pg_keep, pg_send = mine(pg, "xl", 0, 12)
    pg = pg_keep + swap(pg_send, "xl") + tall(w_bc, grad_w_bc)
    grad_pre_gain = pg / pre_gain.astype(F32)

    small = jnp.concatenate([g_cx.reshape(-1), g_cxb, g_gain, g_dtb, g_al, g_dsk, g_cbc.reshape(-1), g_cbcb])
    small = sum_chips(small)
    nx = 6 * 768 + 36
    cbc = small[nx:]
    cbc = cbc + swap(cbc, "c")
    cbc = cbc + swap(cbc, "xl")
    both = pair(small[:nx], swap(small[:nx], "c"), "c")
    grad_conv_x = both[:, :3072].reshape(2, 4, 768).transpose(1, 0, 2).reshape(4, 1536)
    pick = lambda a, n: both[:, a : a + n].reshape(-1)
    return (
        layer_out,
        grad_resid,
        grad_pre_gain,
        grad_w_z,
        grad_w_x,
        grad_w_bc,
        grad_w_dt,
        grad_conv_x,
        pick(3072, 768),
        cbc[:1024].reshape(4, 256),
        cbc[1024:],
        pick(4608, 12),
        pick(4620, 12),
        pick(4632, 12),
        pick(3840, 768),
        grad_w_out_t.T,
    )


def solution(mesh):
    fine = Mesh(mesh.devices.reshape(4, 2, 4, 2, 2), ("z", "xh", "y", "c", "xl"))
    dp, tp, every = ("z", "xh", "y", "c"), "xl", ("z", "xh", "y", "c", "xl")
    return jax.shard_map(
        shards,
        mesh=fine,
        in_specs=(P(every, None), P(every, None), P(dp), P(every), P(dp, tp), P(dp, tp), P(every, None), P(dp, tp), P(None, tp), P(tp), P(), P(), P(tp), P(tp), P(tp), P(tp), P(tp, dp)),
        out_specs=(P(every, None), P(every, None), P(every), P(dp, tp), P(dp, tp), P(every, None), P(dp, tp), P(None, tp), P(tp), P(), P(), P(tp), P(tp), P(tp), P(tp), P(tp, dp)),
        check_vma=False,
    )
```

```python
import jax
import jax.numpy as jnp
from jax import lax
from jax.experimental import pallas as pl
from jax.experimental.pallas import tpu as pltpu
from jax.sharding import Mesh, PartitionSpec as P

EPS = 1e-05
BF = jnp.bfloat16
F32 = jnp.float32
SEQ = 512
HALF = 256
SUB = 128


def mm(a, b):
    return jnp.dot(a, b, preferred_element_type=F32)


def mm_nt(a, b):
    return lax.dot_general(a, b, (((1,), (1,)), ((), ())), preferred_element_type=F32)


def mm_tn(a, b):
    return lax.dot_general(a, b, (((0,), (0,)), ((), ())), preferred_element_type=F32)


def parts(v, count):
    out = []
    for _ in range(count):
        low = v.astype(BF)
        out.append(low)
        v = v - low.astype(F32)
    return out


def split_left(v, m, count=2):
    return sum(mm(p, m) for p in parts(v, count))


def split_right(m, v, count=3):
    return sum(mm(m, p) for p in parts(v, count))


def rows(shape):
    return lax.broadcasted_iota(jnp.int32, shape, 0)


def cols(shape):
    return lax.broadcasted_iota(jnp.int32, shape, 1)


def softplus(v):
    e = jnp.exp(-jnp.abs(v))
    tail = jnp.where(e < 1e-3, e * (1.0 - 0.5 * e), jnp.log(1.0 + e))
    return jnp.maximum(v, 0.0) + tail


def sigmoid(v):
    return 1.0 / (1.0 + jnp.exp(-v))


def same_doc(t, s, cut):
    return (t < cut) == (s < cut)


def conv_masks(cut):
    t = rows((SEQ, SUB))
    return [jnp.where((t >= j) & ((t < cut) | (t - j >= cut)), 1.0, 0.0) for j in (1, 2, 3)]


def conv(v, taps, masks):
    u = taps[4:5] + taps[3:4] * v
    for j in (1, 2, 3):
        u = u + taps[3 - j : 4 - j] * (pltpu.roll(v, j, 0) * masks[j - 1])
    return u


def time_steps(dt_raw, heads, cut):
    dt = softplus(dt_raw + heads[0:1])
    a = dt * heads[1:2]
    tri = jnp.where(rows((HALF, HALF)) >= cols((HALF, HALF)), 1.0, 0.0).astype(BF)
    c = [split_right(tri, a[:HALF]), split_right(tri, a[HALF:])]
    t = rows((HALF, SUB))
    ending = same_doc(t, HALF - 1, cut)
    alive = same_doc(t + HALF, HALF - 1, cut)
    ew = jnp.where(ending, jnp.exp(c[0][HALF - 1 : HALF] - c[0]), 0.0)
    e1 = jnp.where(alive, jnp.exp(c[1]), 0.0)
    return dt, c, ew, e1


def masked_scores(cb, bb, block, cut, lower=True):
    out = {}
    for i, j in ((0, 0), (1, 0), (1, 1)):
        ti, sj = slice(i * SUB, i * SUB + SUB), slice(j * SUB, j * SUB + SUB)
        if lower:
            s = mm_nt(cb[ti], bb[sj])
            t = rows((SUB, SUB)) + (block * HALF + i * SUB)
            r = cols((SUB, SUB)) + (block * HALF + j * SUB)
        else:
            s = mm_nt(bb[sj], cb[ti])
            r = rows((SUB, SUB)) + (block * HALF + j * SUB)
            t = cols((SUB, SUB)) + (block * HALF + i * SUB)
        out[i, j] = jnp.where((t >= r) & same_doc(t, r, cut), s, 0.0)
    return out


def head_lanes(k):
    lane = cols((HALF, SUB))
    return (lane < 64) if k == 0 else (lane >= 64)


def fwd_kernel(cut_ref, xr_ref, bcr_ref, dtr_ref, tx_ref, tbc_ref, hd_ref, e_ref, y_ref, st_ref):
    cut = cut_ref[pl.program_id(0)]
    masks = conv_masks(cut)
    act = []
    for i in range(2):
        sl = slice(i * SUB, i * SUB + SUB)
        u = conv(bcr_ref[:, sl], tbc_ref[:, sl], masks)
        act.append((u * sigmoid(u)).astype(BF))
    bb, cb = act
    dt, c, ew, e1 = time_steps(dtr_ref[...], hd_ref[...], cut)
    ct = [c[0].T, c[1].T]
    tw = ew * dt[:HALF]
    scores = [masked_scores(cb[k * HALF : k * HALF + HALF], bb[k * HALF : k * HALF + HALF], k, cut) for k in (0, 1)]
    b0t = bb[:HALF].T
    for p in range(6):
        sl = slice(p * SUB, p * SUB + SUB)
        e = e_ref[:, sl]
        u = conv(xr_ref[:, sl], tx_ref[:, sl], masks)
        x = u * sigmoid(u)
        xt = (x * split_left(dt, e)).astype(BF)
        skip = tx_ref[5:6, sl] * x
        st = mm(b0t, (x[:HALF] * split_left(tw, e)).astype(BF))
        st_ref[0, :, sl] = st
        carry = mm(cb[HALF:], st.astype(BF)) * split_left(e1, e)
        for k in (0, 1):
            ys = [0.0, 0.0]
            for h in (0, 1):
                head = 2 * p + h
                xm = jnp.where(head_lanes(h), xt[k * HALF : k * HALF + HALF], jnp.zeros((), BF))
                col = c[k][:, head : head + 1]
                row = ct[k][head : head + 1, :]
                m = {}
                for i, j in ((0, 0), (1, 0), (1, 1)):
                    gap = col[i * SUB : i * SUB + SUB] - row[:, j * SUB : j * SUB + SUB]
                    m[i, j] = (jnp.exp(jnp.minimum(gap, 0.0)) * scores[k][i, j]).astype(BF)
                ys[0] = ys[0] + mm(m[0, 0], xm[:SUB])
                ys[1] = ys[1] + mm(jnp.concatenate([m[1, 0], m[1, 1]], axis=1), xm)
            for i in (0, 1):
                at = k * HALF + i * SUB
                y = ys[i] + skip[at : at + SUB]
                if k == 1:
                    y = y + carry[i * SUB : i * SUB + SUB]
                y_ref[at : at + SUB, sl] = y


def seq_spec(width):
    return pl.BlockSpec((SEQ, width), lambda i: (i, 0))


def whole(shape):
    return pl.BlockSpec(shape, lambda i: (0,) * len(shape))


SMEM = pl.BlockSpec(memory_space=pltpu.SMEM)


def ssd_forward(cut, x_raw, bc_raw, dt_raw, taps_x, taps_bc, heads, spread):
    return pl.pallas_call(
        fwd_kernel,
        grid=(2,),
        in_specs=[SMEM, seq_spec(768), seq_spec(256), seq_spec(128), whole((8, 768)), whole((8, 256)), whole((8, 128)), whole((128, 768))],
        out_specs=[seq_spec(768), pl.BlockSpec((1, 128, 768), lambda i: (i, 0, 0))],
        out_shape=[jax.ShapeDtypeStruct((1024, 768), F32), jax.ShapeDtypeStruct((2, 128, 768), F32)],
        compiler_params=pltpu.CompilerParams(vmem_limit_bytes=48 * 1024 * 1024),
        cost_estimate=pl.CostEstimate(flops=4_000_000_000, bytes_accessed=9_000_000, transcendentals=4_000_000),
    )(cut, x_raw, bc_raw, dt_raw, taps_x, taps_bc, heads, spread)


def bwd_kernel(cut_ref, xr_ref, bcr_ref, dtr_ref, dy_ref, y_ref, st_ref, tx_ref, tbc_ref, hd_ref, e_ref, et_ref,
               gx_ref, gbc_ref, gdt_ref, gtx_ref, gtbc_ref, ghd_ref, ds_ref):
    seq = pl.program_id(0)
    cut = cut_ref[seq]
    masks = conv_masks(cut)

    def conv_back(du, v, taps):
        g = taps[3:4] * du
        sums = [jnp.sum(du * v, axis=0, keepdims=True)]
        for j in (1, 2, 3):
            dm = du * masks[j - 1]
            g = g + taps[3 - j : 4 - j] * pltpu.roll(dm, SEQ - j, 0)
            sums.append(jnp.sum(dm * pltpu.roll(v, j, 0), axis=0, keepdims=True))
        return g, [sums[3], sums[2], sums[1], sums[0], jnp.sum(du, axis=0, keepdims=True)]

    @pl.when(seq == 0)
    def _():
        gtx_ref[...] = jnp.zeros_like(gtx_ref)
        gtbc_ref[...] = jnp.zeros_like(gtbc_ref)
        ghd_ref[...] = jnp.zeros_like(ghd_ref)

    act = []
    for i in range(2):
        sl = slice(i * SUB, i * SUB + SUB)
        u = conv(bcr_ref[:, sl], tbc_ref[:, sl], masks)
        act.append((u * sigmoid(u)).astype(BF))
    bb, cb = act
    dt, c, ew, e1 = time_steps(dtr_ref[...], hd_ref[...], cut)
    ct = [c[0].T, c[1].T]
    tw = ew * dt[:HALF]
    blk = lambda a, k: a[k * HALF : k * HALF + HALF]
    low = [masked_scores(blk(cb, k), blk(bb, k), k, cut) for k in (0, 1)]
    up = [masked_scores(blk(cb, k), blk(bb, k), k, cut, lower=False) for k in (0, 1)]
    c1t = cb[HALF:].T
    ds_ref[...] = jnp.zeros_like(ds_ref)
    d_c1 = jnp.zeros((HALF, SUB), F32)
    d_b0 = jnp.zeros((HALF, SUB), F32)
    sum_y = jnp.zeros((SEQ, SUB), F32)
    sum_x = jnp.zeros((SEQ, SUB), F32)
    sum_d = jnp.zeros((SEQ, SUB), F32)
    for p in range(6):
        sl = slice(p * SUB, p * SUB + SUB)
        e, et = e_ref[:, sl], et_ref[sl, :]
        xr = xr_ref[:, sl]
        u = conv(xr, tx_ref[:, sl], masks)
        sg = sigmoid(u)
        x = u * sg
        dtx = split_left(dt, e)
        xt = (x * dtx).astype(BF)
        dyb = dy_ref[:, sl]
        dy = dyb.astype(F32)
        sum_y = sum_y + split_left(dy * y_ref[:, sl], et)
        sum_x = sum_x + split_left(dy * x, et)
        dxs = []
        for k in (0, 1):
            halves = [0.0, 0.0]
            for h in (0, 1):
                head = 2 * p + h
                dm = jnp.where(head_lanes(h), blk(dyb, k), jnp.zeros((), BF))
                col = c[k][:, head : head + 1]
                row = ct[k][head : head + 1, :]
                mt = {}
                for i, j in ((0, 0), (1, 0), (1, 1)):
                    ti, sj = slice(i * SUB, i * SUB + SUB), slice(j * SUB, j * SUB + SUB)
                    decay = jnp.exp(-jnp.abs(col[ti] - row[:, sj]))
                    if i == j:
                        decay_t = decay
                    else:
                        decay_t = jnp.exp(-jnp.abs(col[sj] - row[:, ti]))
                    g = mm_nt(dm[ti], blk(xt, k)[sj])
                    ds_ref[k, i + j] += g * decay
                    mt[i, j] = (decay_t * up[k][i, j]).astype(BF)
                halves[0] = halves[0] + mm(jnp.concatenate([mt[0, 0], mt[1, 0]], axis=1), dm)
                halves[1] = halves[1] + mm(mt[1, 1], dm[SUB:])
            dxs.append(jnp.concatenate(halves, axis=0))
        st = st_ref[0, :, sl].astype(BF)
        dcs = (dy[HALF:] * split_left(e1, e)).astype(BF)
        d_c1 = d_c1 + mm_nt(dcs, st)
        dst = mm(c1t, dcs).astype(BF)
        dxw = mm(bb[:HALF], dst)
        d_b0 = d_b0 + mm_nt((x[:HALF] * split_left(tw, e)).astype(BF), dst)
        dx0 = dxs[0] + dxw * split_left(ew, e)
        dxt = jnp.concatenate([dx0, dxs[1]], axis=0)
        sum_d = sum_d + split_left(x * dxt, et)
        dx = dtx * dxt + tx_ref[5:6, sl] * dy
        du = dx * (sg * (1.0 + u * (1.0 - sg)))
        g, sums = conv_back(du, xr, tx_ref[:, sl])
        gx_ref[:, sl] = g.astype(BF)
        for r, s in enumerate(sums):
            gtx_ref[r : r + 1, sl] += s
    d_b, d_c = [], []
    for k in (0, 1):
        bk, ck = blk(bb, k), blk(cb, k)
        m = {}
        for i, j in ((0, 0), (1, 0), (1, 1)):
            t = rows((SUB, SUB)) + (k * HALF + i * SUB)
            r = cols((SUB, SUB)) + (k * HALF + j * SUB)
            m[i, j] = jnp.where((t >= r) & same_doc(t, r, cut), ds_ref[k, i + j], 0.0).astype(BF)
        lowr = jnp.concatenate([m[1, 0], m[1, 1]], axis=1)
        d_c += [mm(m[0, 0], bk[:SUB]), mm(lowr, bk)]
        d_b += [mm_tn(m[0, 0], ck[:SUB]) + mm_tn(m[1, 0], ck[SUB:]), mm_tn(m[1, 1], ck[SUB:])]
    d_b = jnp.concatenate([jnp.concatenate(d_b[:2], axis=0) + d_b0] + d_b[2:], axis=0)
    d_c = jnp.concatenate(d_c[:2] + [jnp.concatenate(d_c[2:], axis=0) + d_c1], axis=0)
    for i, d in ((0, d_b), (1, d_c)):
        sl = slice(i * SUB, i * SUB + SUB)
        v = bcr_ref[:, sl]
        u = conv(v, tbc_ref[:, sl], masks)
        sg = sigmoid(u)
        g, sums = conv_back(d * (sg * (1.0 + u * (1.0 - sg))), v, tbc_ref[:, sl])
        gbc_ref[:, sl] = g.astype(BF)
        for r, s in enumerate(sums):
            gtbc_ref[r : r + 1, sl] += s
    hd = hd_ref[...]
    w = (sum_y - hd[2:3] * sum_x) - dt * sum_d
    tri = jnp.where((cols((SEQ, SEQ)) >= rows((SEQ, SEQ))) & same_doc(rows((SEQ, SEQ)), cols((SEQ, SEQ)), cut), 1.0, 0.0).astype(BF)
    run = split_right(tri, w)
    d_dt = sum_d + hd[1:2] * run
    gd = d_dt * sigmoid(dtr_ref[...] + hd[0:1])
    gdt_ref[...] = gd.astype(BF)
    ghd_ref[0:1] += jnp.sum(gd, axis=0, keepdims=True)
    ghd_ref[1:2] += jnp.sum(dt * run, axis=0, keepdims=True) * hd[1:2]
    ghd_ref[2:3] += jnp.sum(sum_x, axis=0, keepdims=True)


def ssd_backward(cut, x_raw, bc_raw, dt_raw, dy, y, st, taps_x, taps_bc, heads, spread, spread_t):
    return pl.pallas_call(
        bwd_kernel,
        grid=(2,),
        in_specs=[SMEM, seq_spec(768), seq_spec(256), seq_spec(128), seq_spec(768), seq_spec(768),
                  pl.BlockSpec((1, 128, 768), lambda i: (i, 0, 0)), whole((8, 768)), whole((8, 256)), whole((8, 128)), whole((128, 768)), whole((768, 128))],
        out_specs=[seq_spec(768), seq_spec(256), seq_spec(128), whole((8, 768)), whole((8, 256)), whole((8, 128))],
        out_shape=[jax.ShapeDtypeStruct((1024, 768), BF), jax.ShapeDtypeStruct((1024, 256), BF), jax.ShapeDtypeStruct((1024, 128), BF),
                   jax.ShapeDtypeStruct((8, 768), F32), jax.ShapeDtypeStruct((8, 256), F32), jax.ShapeDtypeStruct((8, 128), F32)],
        scratch_shapes=[pltpu.VMEM((2, 3, SUB, SUB), F32)],
        compiler_params=pltpu.CompilerParams(vmem_limit_bytes=56 * 1024 * 1024),
        cost_estimate=pl.CostEstimate(flops=12_000_000_000, bytes_accessed=14_000_000, transcendentals=4_000_000),
    )(cut, x_raw, bc_raw, dt_raw, dy, y, st, taps_x, taps_bc, heads, spread, spread_t)


def swap(a, axis):
    return lax.ppermute(a, axis, [(0, 1), (1, 0)])


def turn(a, axis, k):
    return lax.ppermute(a, axis, [(i, (i + k) % 4) for i in range(4)])


def pair(own, other, axis):
    first = lax.axis_index(axis) == 0
    return jnp.stack([jnp.where(first, own, other), jnp.where(first, other, own)])


def mine(a, axis, dim, size):
    i = lax.axis_index(axis)
    return (
        lax.dynamic_slice_in_dim(a, i * size, size, dim),
        lax.dynamic_slice_in_dim(a, (1 - i) * size, size, dim),
    )


def gather4(blk, axis, dim):
    i = lax.axis_index(axis)
    got = [blk, turn(blk, axis, 1), turn(blk, axis, 2), turn(blk, axis, 3)]
    shape = blk.shape[:dim] + (4,) + blk.shape[dim:]
    out = jnp.zeros(shape, blk.dtype)
    for k, piece in enumerate(got):
        out = lax.dynamic_update_slice_in_dim(out, jnp.expand_dims(piece, dim), (i - k) % 4, dim)
    return out


def gather_chips(blk, order):
    b = pair(blk, swap(blk, "xh"), "xh")
    if order == "yz":
        b = gather4(gather4(b, "y", 1), "z", 0)
    else:
        b = gather4(gather4(b, "z", 0), "y", 2)
    return b.reshape(1536, blk.shape[1])


def reduce4(a, axis, dim):
    i = lax.axis_index(axis)

    def entry(k):
        return lax.squeeze(lax.dynamic_slice_in_dim(a, (i + k) % 4, 1, dim), (dim,))

    total = entry(0).astype(F32)
    for k in (1, 2, 3):
        total = total + turn(entry(k), axis, k).astype(F32)
    return total


def reduce_chips(g, order):
    b = g.reshape(4, 2, 4, 48, g.shape[1])
    if order == "yz":
        b = reduce4(b, "y", 2).astype(BF)
        b = reduce4(b, "z", 0).astype(BF)
    else:
        b = reduce4(b, "z", 0).astype(BF)
        b = reduce4(b, "y", 1).astype(BF)
    own, other = mine(b, "xh", 0, 1)
    return own[0].astype(F32) + swap(other[0], "xh").astype(F32)


def sum_chips(a):
    a = a + swap(a, "xh")
    a = a + turn(a, "y", 1) + turn(a, "y", 2) + turn(a, "y", 3)
    return a + turn(a, "z", 1) + turn(a, "z", 2) + turn(a, "z", 3)


def shards(resid, cotangent, segments, pre_gain, w_z, w_x, w_bc, w_dt, conv_x, conv_x_bias, conv_bc, conv_bc_bias, dt_bias, a_log, d_skip, gate_gain, w_out):
    core = lax.axis_index("c")
    def group_tokens(a):
        half = pair(a, swap(a, "xl"), "xl").reshape(512, a.shape[1])
        return pair(half, swap(half, "c"), "c")

    def quarter(a, size):
        own, other = mine(a, "c", 1, size)
        return pair(own, swap(other, "c"), "c").reshape(48, size)

    bc_rows = pair(w_bc, swap(w_bc, "xl"), "xl").reshape(24, 256)
    gain_rows = pair(pre_gain[:, None], swap(pre_gain[:, None], "xl"), "xl").reshape(24, 1)
    bc_rows = pair(bc_rows, swap(bc_rows, "c"), "c").reshape(48, 256)
    gain_rows = pair(gain_rows, swap(gain_rows, "c"), "c").reshape(48, 1)
    wx_q, wz_q, wo_q, wdt_q = quarter(w_x, 768), quarter(w_z, 768), quarter(w_out.T, 768), quarter(w_dt, 12)
    side = jnp.concatenate([wdt_q, gain_rows, jnp.zeros((48, 115), BF)], axis=1)
    first = jnp.concatenate([wx_q, bc_rows, side], axis=1)
    full_a = gather_chips(first[:, :512], "yz")
    full_b = gather_chips(first[:, 512:], "zy")
    full_z = gather_chips(wz_q, "yz")
    full_o = gather_chips(wo_q, "zy")
    full_1 = jnp.concatenate([full_a, full_b], axis=1)
    full_x, full_bc, full_dt, full_gain = full_1[:, :768], full_1[:, 768:1024], full_1[:, 1024:1036], full_1[:, 1036]

    tokens = group_tokens(resid).reshape(1024, 1536)
    cot = group_tokens(cotangent).reshape(1024, 1536)
    seg = pair(segments, swap(segments, "c"), "c")

    gain_wide = full_gain.astype(F32)
    wide = tokens.astype(F32)
    inv_all = lax.rsqrt(jnp.mean(wide * wide, axis=-1, keepdims=True) + EPS)
    normed = (wide * inv_all * gain_wide[None, :]).astype(BF)

    def dot(a, b):
        return jnp.dot(a, b, preferred_element_type=F32)

    gate_raw, x_raw, bc_raw = dot(normed, full_z), dot(normed, full_x), dot(normed, full_bc)

    def own(a, size):
        return mine(a, "c", a.ndim - 1, size)[0]

    cx, cxb, gg = own(conv_x, 768), own(conv_x_bias, 768), own(gate_gain, 768)
    dtb, al, dsk = own(dt_bias, 12), own(a_log, 12), own(d_skip, 12)

    taps_x = jnp.concatenate([cx, cxb[None], jnp.repeat(dsk, 64)[None], jnp.zeros((2, 768), F32)], axis=0)
    taps_bc = jnp.concatenate([conv_bc, conv_bc_bias[None], jnp.zeros((3, 256), F32)], axis=0)
    wide_heads = lambda v: jnp.pad(v, (0, 116))[None]
    heads = jnp.concatenate([wide_heads(dtb), wide_heads(-jnp.exp(al)), wide_heads(dsk), jnp.zeros((5, 128), F32)], axis=0)
    spread = (jnp.arange(768)[None, :] // 64 == jnp.arange(128)[:, None]).astype(BF)
    cut = jnp.sum((seg == seg[:, :1]).astype(jnp.int32), axis=1)
    dt_wide = dot(normed, full_1[:, 1024:])
    dt_wide = jnp.where(jnp.arange(128)[None] < 12, dt_wide, 0.0)
    y, st = ssd_forward(cut, x_raw, bc_raw, dt_wide, taps_x, taps_bc, heads, spread)
    sg = jax.nn.sigmoid(gate_raw)
    silu_gate = gate_raw * sg
    mixed = y * silu_gate
    grad_scaled = lax.dot_general(cot, full_o, (((1,), (0,)), ((), ())), preferred_element_type=F32)
    weighted = grad_scaled * gg[None, :]
    sums = jnp.stack([jnp.sum(mixed * mixed, axis=-1), jnp.sum(weighted * mixed, axis=-1)])
    sums = sums + swap(sums, "c")
    sums = sums + swap(sums, "xl")
    inv_gate = lax.rsqrt(sums[0] / 3072 + EPS)[:, None]
    scaled = (mixed * inv_gate * gg[None, :]).astype(BF)
    out_part = lax.dot_general(scaled, full_o, (((1,), (1,)), ((), ())), preferred_element_type=F32).astype(BF)

    def scatter_tokens(a):
        a = a.reshape(2, 512, a.shape[1])
        keep, send = mine(a, "c", 0, 1)
        half = (keep[0].astype(F32) + swap(send[0], "c").astype(F32)).astype(BF)
        keep, send = mine(half, "xl", 0, 256)
        return keep.astype(F32) + swap(send, "xl").astype(F32)

    layer_out = (resid.astype(F32) + scatter_tokens(out_part)).astype(BF)

    def over_tokens(a, b):
        return lax.dot_general(a, b, (((0,), (0,)), ((), ())), preferred_element_type=F32)

    g_out = reduce_chips(over_tokens(cot, scaled).astype(BF), "yz")
    g_gain = jnp.sum(grad_scaled * mixed * inv_gate, axis=0)
    grad_mixed = weighted * inv_gate - mixed * (inv_gate * inv_gate * inv_gate) * (sums[1] / 3072)[:, None]
    gate_low = (grad_mixed * y * (sg * (1.0 + gate_raw * (1.0 - sg)))).astype(BF)
    dy = (grad_mixed * silu_gate).astype(BF)
    x_low, gbc, gdt, g_tx, g_tbc, g_hd = ssd_backward(cut, x_raw, bc_raw, dt_wide, dy, y, st, taps_x, taps_bc, heads, spread, spread.T)
    dt_low = gdt[:, :12]
    g_cx, g_cxb, g_cbc, g_cbcb = g_tx[:4], g_tx[4], g_tbc[:4], g_tbc[4]
    g_dtb, g_al, g_dsk = g_hd[0, :12], g_hd[1, :12], g_hd[2, :12]
    g_z = reduce_chips(over_tokens(normed, gate_low).astype(BF), "zy")

    keep, send = mine(gbc, "c", 1, 128)
    half = (keep.astype(F32) + swap(send, "c").astype(F32)).astype(BF)
    keep, send = mine(half, "xl", 1, 64)
    bc_low = (keep.astype(F32) + swap(send, "xl").astype(F32)).astype(BF)
    q = core * 2 + lax.axis_index("xl")
    bc_q = lax.dynamic_slice_in_dim(full_bc, q * 64, 64, 1)
    side_w = jnp.concatenate([full_x, bc_q, full_dt, jnp.zeros((1536, 52), BF)], axis=1)
    side_g = jnp.concatenate([x_low, bc_low, dt_low, jnp.zeros((1024, 52), BF)], axis=1)
    nt = lambda a, b: lax.dot_general(a, b, (((1,), (1,)), ((), ())), preferred_element_type=F32)
    token_term = nt(gate_low, full_z) + nt(side_g, side_w)
    grad_normed = scatter_tokens(token_term.astype(BF))
    g_side_full = over_tokens(normed, side_g).astype(BF)
    g_side = jnp.concatenate([reduce_chips(g_side_full[:, :512], "yz"), reduce_chips(g_side_full[:, 512:], "zy")], axis=1)

    rw = resid.astype(F32)
    inv = lax.rsqrt(jnp.mean(rw * rw, axis=-1, keepdims=True) + EPS)
    inner = jnp.sum(gain_wide[None, :] * grad_normed * rw, axis=-1, keepdims=True)
    grad_resid = cotangent.astype(F32) + gain_wide[None, :] * grad_normed * inv - rw * (inv * inv * inv) * inner / 1536

    def spread(a):
        keep, send = mine(a, "c", 0, 24)
        got = pair(keep, swap(send, "c"), "c")
        return jnp.concatenate([got[0], got[1]], axis=1)

    grad_w_z, grad_w_x, grad_w_dt = spread(g_z), spread(g_side[:, :768]), spread(g_side[:, 832:844])
    grad_w_out_t = spread(g_out)
    bc24 = spread(g_side[:, 768:832]).reshape(24, 2, 64)
    keep, send = mine(bc24, "xl", 0, 12)
    got = pair(keep, swap(send, "xl"), "xl")
    grad_w_bc = got.transpose(1, 2, 0, 3).reshape(12, 256)

    tall = lambda a, b: jnp.sum(a.astype(F32) * b, axis=1)
    pg = tall(w_z, grad_w_z) + tall(w_x, grad_w_x) + tall(w_dt, grad_w_dt)
    pg_keep, pg_send = mine(pg, "xl", 0, 12)
    pg = pg_keep + swap(pg_send, "xl") + tall(w_bc, grad_w_bc)
    grad_pre_gain = pg / pre_gain.astype(F32)

    small = jnp.concatenate([g_cx.reshape(-1), g_cxb, g_gain, g_dtb, g_al, g_dsk, g_cbc.reshape(-1), g_cbcb])
    small = sum_chips(small)
    nx = 6 * 768 + 36
    cbc = small[nx:]
    cbc = cbc + swap(cbc, "c")
    cbc = cbc + swap(cbc, "xl")
    both = pair(small[:nx], swap(small[:nx], "c"), "c")
    grad_conv_x = both[:, :3072].reshape(2, 4, 768).transpose(1, 0, 2).reshape(4, 1536)
    pick = lambda a, n: both[:, a : a + n].reshape(-1)
    return (
        layer_out,
        grad_resid,
        grad_pre_gain,
        grad_w_z,
        grad_w_x,
        grad_w_bc,
        grad_w_dt,
        grad_conv_x,
        pick(3072, 768),
        cbc[:1024].reshape(4, 256),
        cbc[1024:],
        pick(4608, 12),
        pick(4620, 12),
        pick(4632, 12),
        pick(3840, 768),
        grad_w_out_t.T,
    )


def solution(mesh):
    fine = Mesh(mesh.devices.reshape(4, 2, 4, 2, 2), ("z", "xh", "y", "c", "xl"))
    dp, tp, every = ("z", "xh", "y", "c"), "xl", ("z", "xh", "y", "c", "xl")
    return jax.shard_map(
        shards,
        mesh=fine,
        in_specs=(P(every, None), P(every, None), P(dp), P(every), P(dp, tp), P(dp, tp), P(every, None), P(dp, tp), P(None, tp), P(tp), P(), P(), P(tp), P(tp), P(tp), P(tp), P(tp, dp)),
        out_specs=(P(every, None), P(every, None), P(every), P(dp, tp), P(dp, tp), P(every, None), P(dp, tp), P(None, tp), P(tp), P(), P(), P(tp), P(tp), P(tp), P(tp), P(tp, dp)),
        check_vma=False,
    )
```

```python
import jax
import jax.numpy as jnp
import numpy as np
from jax import lax
from jax.experimental import pallas as pl
from jax.experimental.pallas import tpu as pltpu
from jax.sharding import Mesh, PartitionSpec as P

EPS = 1e-05
VMEM_LIMIT = 60 * 1024 * 1024
BF = jnp.bfloat16
F32 = jnp.float32
SEQ = 512
HALF = 256
SUB = 128


def mm(a, b):
    return jnp.dot(a, b, preferred_element_type=F32)


def mm_nt(a, b):
    return lax.dot_general(a, b, (((1,), (1,)), ((), ())), preferred_element_type=F32)


def mm_tn(a, b):
    return lax.dot_general(a, b, (((0,), (0,)), ((), ())), preferred_element_type=F32)


def parts(v, count):
    out = []
    for _ in range(count):
        low = v.astype(BF)
        out.append(low)
        v = v - low.astype(F32)
    return out


def split_left(v, m, count=2):
    return sum(mm(p, m) for p in parts(v, count))


def split_right(m, v, count=3):
    return sum(mm(m, p) for p in parts(v, count))


def rows(shape):
    return lax.broadcasted_iota(jnp.int32, shape, 0)


def cols(shape):
    return lax.broadcasted_iota(jnp.int32, shape, 1)


def softplus(v):
    e = jnp.exp(-jnp.abs(v))
    tail = jnp.where(e < 1e-3, e * (1.0 - 0.5 * e), jnp.log(1.0 + e))
    return jnp.maximum(v, 0.0) + tail


def sigmoid(v):
    return 1.0 / (1.0 + jnp.exp(-v))


def same_doc(t, s, cut):
    return (t < cut) == (s < cut)


def conv_masks(cut):
    t = rows((SEQ, SUB))
    return [jnp.where((t >= j) & ((t < cut) | (t - j >= cut)), 1.0, 0.0) for j in (1, 2, 3)]


def conv(v, taps, masks):
    u = taps[4:5] + taps[3:4] * v
    for j in (1, 2, 3):
        u = u + taps[3 - j : 4 - j] * (pltpu.roll(v, j, 0) * masks[j - 1])
    return u


def time_steps(dt_raw, heads, cut):
    dt = softplus(dt_raw + heads[0:1])
    a = dt * heads[1:2]
    tri = jnp.where(rows((HALF, HALF)) >= cols((HALF, HALF)), 1.0, 0.0).astype(BF)
    c = [split_right(tri, a[:HALF]), split_right(tri, a[HALF:])]
    t = rows((HALF, SUB))
    ending = same_doc(t, HALF - 1, cut)
    alive = same_doc(t + HALF, HALF - 1, cut)
    ew = jnp.where(ending, jnp.exp(c[0][HALF - 1 : HALF] - c[0]), 0.0)
    e1 = jnp.where(alive, jnp.exp(c[1]), 0.0)
    return dt, c, ew, e1


def masked_scores(cb, bb, block, cut, lower=True):
    out = {}
    for i, j in ((0, 0), (1, 0), (1, 1)):
        ti, sj = slice(i * SUB, i * SUB + SUB), slice(j * SUB, j * SUB + SUB)
        if lower:
            s = mm_nt(cb[ti], bb[sj])
            t = rows((SUB, SUB)) + (block * HALF + i * SUB)
            r = cols((SUB, SUB)) + (block * HALF + j * SUB)
        else:
            s = mm_nt(bb[sj], cb[ti])
            r = rows((SUB, SUB)) + (block * HALF + j * SUB)
            t = cols((SUB, SUB)) + (block * HALF + i * SUB)
        out[i, j] = jnp.where((t >= r) & same_doc(t, r, cut), s, 0.0)
    return out


def head_lanes(k):
    lane = cols((HALF, SUB))
    return (lane < 64) if k == 0 else (lane >= 64)


def fwd_kernel(cut_ref, xr_ref, bcr_ref, dtr_ref, tx_ref, tbc_ref, hd_ref, e_ref, y_ref, st_ref):
    cut = cut_ref[pl.program_id(0)]
    masks = conv_masks(cut)
    act = []
    for i in range(2):
        sl = slice(i * SUB, i * SUB + SUB)
        u = conv(bcr_ref[:, sl], tbc_ref[:, sl], masks)
        act.append((u * sigmoid(u)).astype(BF))
    bb, cb = act
    dt, c, ew, e1 = time_steps(dtr_ref[...], hd_ref[...], cut)
    ct = [c[0].T, c[1].T]
    tw = ew * dt[:HALF]
    scores = [masked_scores(cb[k * HALF : k * HALF + HALF], bb[k * HALF : k * HALF + HALF], k, cut) for k in (0, 1)]
    b0t = bb[:HALF].T
    for p in range(6):
        sl = slice(p * SUB, p * SUB + SUB)
        e = e_ref[:, sl]
        u = conv(xr_ref[:, sl], tx_ref[:, sl], masks)
        x = u * sigmoid(u)
        xt = (x * split_left(dt, e)).astype(BF)
        skip = tx_ref[5:6, sl] * x
        st = mm(b0t, (x[:HALF] * split_left(tw, e)).astype(BF))
        st_ref[0, :, sl] = st
        carry = mm(cb[HALF:], st.astype(BF)) * split_left(e1, e)
        for k in (0, 1):
            ys = [0.0, 0.0]
            for h in (0, 1):
                head = 2 * p + h
                xm = jnp.where(head_lanes(h), xt[k * HALF : k * HALF + HALF], jnp.zeros((), BF))
                col = c[k][:, head : head + 1]
                row = ct[k][head : head + 1, :]
                m = {}
                for i, j in ((0, 0), (1, 0), (1, 1)):
                    gap = col[i * SUB : i * SUB + SUB] - row[:, j * SUB : j * SUB + SUB]
                    m[i, j] = (jnp.exp(jnp.minimum(gap, 0.0)) * scores[k][i, j]).astype(BF)
                ys[0] = ys[0] + mm(m[0, 0], xm[:SUB])
                ys[1] = ys[1] + mm(jnp.concatenate([m[1, 0], m[1, 1]], axis=1), xm)
            for i in (0, 1):
                at = k * HALF + i * SUB
                y = ys[i] + skip[at : at + SUB]
                if k == 1:
                    y = y + carry[i * SUB : i * SUB + SUB]
                y_ref[at : at + SUB, sl] = y


def seq_spec(width):
    return pl.BlockSpec((SEQ, width), lambda i: (i, 0))


def whole(shape):
    return pl.BlockSpec(shape, lambda i: (0,) * len(shape))


SMEM = pl.BlockSpec(memory_space=pltpu.SMEM)


def ssd_forward(cut, x_raw, bc_raw, dt_raw, taps_x, taps_bc, heads, spread):
    return pl.pallas_call(
        fwd_kernel,
        grid=(2,),
        in_specs=[SMEM, seq_spec(768), seq_spec(256), seq_spec(128), whole((8, 768)), whole((8, 256)), whole((8, 128)), whole((128, 768))],
        out_specs=[seq_spec(768), pl.BlockSpec((1, 128, 768), lambda i: (i, 0, 0))],
        out_shape=[jax.ShapeDtypeStruct((1024, 768), F32), jax.ShapeDtypeStruct((2, 128, 768), F32)],
        compiler_params=pltpu.CompilerParams(vmem_limit_bytes=VMEM_LIMIT),
        cost_estimate=pl.CostEstimate(flops=4_000_000_000, bytes_accessed=9_000_000, transcendentals=4_000_000),
    )(cut, x_raw, bc_raw, dt_raw, taps_x, taps_bc, heads, spread)


def bwd_kernel(cut_ref, place_ref, xr_ref, bcr_ref, dtr_ref, dy_ref, y_ref, st_ref, tx_ref, tbc_ref, hd_ref, e_ref, et_ref,
               gx_ref, keep_ref, send_ref, gdt_ref, gtx_ref, keepc_ref, sendc_ref, ghd_ref, ds_ref):
    seq = pl.program_id(0)
    cut = cut_ref[seq]
    masks = conv_masks(cut)

    def conv_back(du, v, taps):
        g = taps[3:4] * du
        sums = [jnp.sum(du * v, axis=0, keepdims=True)]
        for j in (1, 2, 3):
            dm = du * masks[j - 1]
            g = g + taps[3 - j : 4 - j] * pltpu.roll(dm, SEQ - j, 0)
            sums.append(jnp.sum(dm * pltpu.roll(v, j, 0), axis=0, keepdims=True))
        return g, [sums[3], sums[2], sums[1], sums[0], jnp.sum(du, axis=0, keepdims=True)]

    @pl.when(seq == 0)
    def _():
        gtx_ref[...] = jnp.zeros_like(gtx_ref)
        keepc_ref[...] = jnp.zeros_like(keepc_ref)
        sendc_ref[...] = jnp.zeros_like(sendc_ref)
        ghd_ref[...] = jnp.zeros_like(ghd_ref)

    act = []
    for i in range(2):
        sl = slice(i * SUB, i * SUB + SUB)
        u = conv(bcr_ref[:, sl], tbc_ref[:, sl], masks)
        act.append((u * sigmoid(u)).astype(BF))
    bb, cb = act
    dt, c, ew, e1 = time_steps(dtr_ref[...], hd_ref[...], cut)
    ct = [c[0].T, c[1].T]
    tw = ew * dt[:HALF]
    blk = lambda a, k: a[k * HALF : k * HALF + HALF]
    low = [masked_scores(blk(cb, k), blk(bb, k), k, cut) for k in (0, 1)]
    up = [masked_scores(blk(cb, k), blk(bb, k), k, cut, lower=False) for k in (0, 1)]
    c1t = cb[HALF:].T
    ds_ref[...] = jnp.zeros_like(ds_ref)
    d_c1 = jnp.zeros((HALF, SUB), F32)
    d_b0 = jnp.zeros((HALF, SUB), F32)
    g_skip = jnp.zeros((8, SUB), F32)
    sum_y = jnp.zeros((SEQ, SUB), F32)
    sum_x = jnp.zeros((SEQ, SUB), F32)
    sum_d = jnp.zeros((SEQ, SUB), F32)
    for p in range(6):
        sl = slice(p * SUB, p * SUB + SUB)
        e, et = e_ref[:, sl], et_ref[sl, :]
        xr = xr_ref[:, sl]
        u = conv(xr, tx_ref[:, sl], masks)
        sg = sigmoid(u)
        x = u * sg
        dtx = split_left(dt, e)
        xtf = x * dtx
        xt = xtf.astype(BF)
        dy = dy_ref[:, sl]
        dyb = dy.astype(BF)
        dyh = dyb.astype(F32)
        xh = xt.astype(F32)
        xl = (xtf - xh).astype(BF)
        dl_turned = pltpu.roll(dy - dyh, 64, 1).astype(BF)
        xh_turned = pltpu.roll(xh, 64, 1).astype(BF)
        sum_y = sum_y + split_left(dyh * y_ref[:, sl], et)
        sum_x = sum_x + split_left(dyh * x, et)
        g_skip = g_skip + split_left(jnp.broadcast_to(jnp.sum(dy * x, axis=0, keepdims=True), (8, SUB)), et, 3)
        dxs = []
        for k in (0, 1):
            halves = [0.0, 0.0]
            for h in (0, 1):
                head = 2 * p + h
                lanes, none = head_lanes(h), jnp.zeros((), BF)
                dm = jnp.where(lanes, blk(dyb, k), none)
                dm2 = jnp.concatenate([jnp.where(lanes, blk(dyb, k), blk(dl_turned, k)), dm], axis=1)
                xm2 = jnp.concatenate([jnp.where(lanes, blk(xt, k), blk(xh_turned, k)), jnp.where(lanes, blk(xl, k), none)], axis=1)
                col = c[k][:, head : head + 1]
                row = ct[k][head : head + 1, :]
                mt = {}
                for i, j in ((0, 0), (1, 0), (1, 1)):
                    ti, sj = slice(i * SUB, i * SUB + SUB), slice(j * SUB, j * SUB + SUB)
                    decay = jnp.exp(-jnp.abs(col[ti] - row[:, sj]))
                    if i == j:
                        decay_t = decay
                    else:
                        decay_t = jnp.exp(-jnp.abs(col[sj] - row[:, ti]))
                    g = mm_nt(dm2[ti], xm2[sj])
                    ds_ref[k, i + j] += g * decay
                    mt[i, j] = (decay_t * up[k][i, j]).astype(BF)
                halves[0] = halves[0] + mm(jnp.concatenate([mt[0, 0], mt[1, 0]], axis=1), dm)
                halves[1] = halves[1] + mm(mt[1, 1], dm[SUB:])
            dxs.append(jnp.concatenate(halves, axis=0))
        st, st_low = parts(st_ref[0, :, sl], 2)
        dcs, dcs_low = parts(dy[HALF:] * split_left(e1, e), 2)
        d_c1 = d_c1 + (mm_nt(dcs, st) + (mm_nt(dcs_low, st) + mm_nt(dcs, st_low)))
        dst, dst_low = parts(mm(c1t, dcs) + mm(c1t, dcs_low), 2)
        dxw = mm(bb[:HALF], dst)
        xw, xw_low = parts(x[:HALF] * split_left(tw, e), 2)
        d_b0 = d_b0 + (mm_nt(xw, dst) + (mm_nt(xw_low, dst) + mm_nt(xw, dst_low)))
        dx0 = dxs[0] + dxw * split_left(ew, e)
        dxt = jnp.concatenate([dx0, dxs[1]], axis=0)
        sum_d = sum_d + split_left(x * dxt, et)
        dx = dtx * dxt + tx_ref[5:6, sl] * dy
        du = dx * (sg * (1.0 + u * (1.0 - sg)))
        g, sums = conv_back(du, xr, tx_ref[:, sl])
        gx_ref[:, sl] = g.astype(BF)
        for r, s in enumerate(sums):
            gtx_ref[r : r + 1, sl] += s
    d_b, d_c = [], []
    for k in (0, 1):
        bk, ck = blk(bb, k), blk(cb, k)
        m = {}
        for i, j in ((0, 0), (1, 0), (1, 1)):
            t = rows((SUB, SUB)) + (k * HALF + i * SUB)
            r = cols((SUB, SUB)) + (k * HALF + j * SUB)
            m[i, j] = jnp.where((t >= r) & same_doc(t, r, cut), ds_ref[k, i + j], 0.0).astype(BF)
        lowr = jnp.concatenate([m[1, 0], m[1, 1]], axis=1)
        d_c += [mm(m[0, 0], bk[:SUB]), mm(lowr, bk)]
        d_b += [mm_tn(m[0, 0], ck[:SUB]) + mm_tn(m[1, 0], ck[SUB:]), mm_tn(m[1, 1], ck[SUB:])]
    d_b = jnp.concatenate([jnp.concatenate(d_b[:2], axis=0) + d_b0] + d_b[2:], axis=0)
    d_c = jnp.concatenate(d_c[:2] + [jnp.concatenate(d_c[2:], axis=0) + d_c1], axis=0)
    for i, d in ((0, d_b), (1, d_c)):
        sl = slice(i * SUB, i * SUB + SUB)
        v = bcr_ref[:, sl]
        u = conv(v, tbc_ref[:, sl], masks)
        sg = sigmoid(u)
        g, sums = conv_back(d * (sg * (1.0 + u * (1.0 - sg))), v, tbc_ref[:, sl])

        @pl.when(place_ref[3] == i)
        def _():
            keep_ref[...] = g
            for r, s in enumerate(sums):
                keepc_ref[r : r + 1] += s

        @pl.when(place_ref[3] != i)
        def _():
            send_ref[...] = g
            for r, s in enumerate(sums):
                sendc_ref[r : r + 1] += s

    hd = hd_ref[...]
    w = (sum_y - hd[2:3] * sum_x) - dt * sum_d
    tri = jnp.where((cols((SEQ, SEQ)) >= rows((SEQ, SEQ))) & same_doc(rows((SEQ, SEQ)), cols((SEQ, SEQ)), cut), 1.0, 0.0).astype(BF)
    run = split_right(tri, w)
    d_dt = sum_d + hd[1:2] * run
    gd = d_dt * sigmoid(dtr_ref[...] + hd[0:1])
    gdt_ref[...] = gd.astype(BF)
    ghd_ref[0:1] += jnp.sum(gd, axis=0, keepdims=True)
    ghd_ref[2:3] += g_skip[0:1]
    ghd_ref[1:2] += jnp.sum(dt * run, axis=0, keepdims=True) * hd[1:2]


def ssd_backward(cut, place, x_raw, bc_raw, dt_raw, dy, y, st, taps_x, taps_bc, heads, spread, spread_t):
    return pl.pallas_call(
        bwd_kernel,
        grid=(2,),
        in_specs=[SMEM, SMEM, seq_spec(768), seq_spec(256), seq_spec(128), seq_spec(768), seq_spec(768),
                  pl.BlockSpec((1, 128, 768), lambda i: (i, 0, 0)), whole((8, 768)), whole((8, 256)), whole((8, 128)), whole((128, 768)), whole((768, 128))],
        out_specs=[seq_spec(768), seq_spec(128), seq_spec(128), seq_spec(128), whole((8, 768)), whole((8, 128)), whole((8, 128)), whole((8, 128))],
        out_shape=[jax.ShapeDtypeStruct((1024, 768), BF), jax.ShapeDtypeStruct((1024, 128), F32), jax.ShapeDtypeStruct((1024, 128), F32), jax.ShapeDtypeStruct((1024, 128), BF),
                   jax.ShapeDtypeStruct((8, 768), F32), jax.ShapeDtypeStruct((8, 128), F32), jax.ShapeDtypeStruct((8, 128), F32), jax.ShapeDtypeStruct((8, 128), F32)],
        scratch_shapes=[pltpu.VMEM((2, 3, SUB, SUB), F32)],
        compiler_params=pltpu.CompilerParams(vmem_limit_bytes=VMEM_LIMIT),
        cost_estimate=pl.CostEstimate(flops=12_000_000_000, bytes_accessed=14_000_000, transcendentals=4_000_000),
    )(cut, place, x_raw, bc_raw, dt_raw, dy, y, st, taps_x, taps_bc, heads, spread, spread_t)


def place_blocks(pieces, w_ref, sem, row_of):
    for ref, k, first in pieces:
        for r in range(ref.shape[0]):
            for h in range(2):
                row = pl.multiple_of(row_of(k, first + r, h) * 48, 48)
                pltpu.make_async_copy(ref.at[r, h], w_ref.at[pl.ds(row, 48)], sem).start()


def ring_pieces(refs):
    return list(zip(refs, (0, 1, 3, 2, 2), (0, 0, 0, 0, 2)))


def start_halves(refs, buf, sems):
    for k in range(4):
        at = (k % 2) * HALF
        pltpu.make_async_copy(refs[k // 2].at[at : at + HALF], buf.at[k], sems.at[k]).start()


def project_kernel(order_ref, place_ref, *refs):
    a_refs, t_refs = refs[0:5], refs[5:7]
    normed_ref, nt_ref, xr_ref, bc_ref, dt_ref, w_ref, wbc_ref, gain, tok, w_sem, t_sem = refs[7:]
    step = pl.program_id(0)

    @pl.when(step == 0)
    def _():
        z, xh, y = place_ref[0], place_ref[1], place_ref[2]
        start_halves(t_refs, tok, t_sem)

        def row_of(k, r, h):
            return (lax.rem(z - k + 4, 4) * 2 + lax.rem(xh + h, 2)) * 4 + lax.rem(y - r + 4, 4)

        place_blocks(ring_pieces(a_refs), w_ref, w_sem, row_of)
        pltpu.make_async_copy(w_ref, w_ref, w_sem).wait()
        gain[...] = w_ref[:, 1024:1152].astype(F32).T[8:16]
        wbc_ref[...] = w_ref[:, 768:1024]

    pltpu.make_async_copy(t_refs[0].at[0:HALF], tok.at[step], t_sem.at[step]).wait()
    wide = tok[step].astype(F32)
    inv = lax.rsqrt(jnp.mean(wide * wide, axis=-1, keepdims=True) + EPS)
    normed = (wide * inv * gain[4:5]).astype(BF)
    normed_ref[...] = normed
    nt_ref[...] = normed.T
    xr_ref[...] = mm(normed, w_ref[:, 0:768])
    bc_ref[...] = mm(normed, w_ref[:, 768:1024])
    dt_ref[...] = jnp.where(cols((HALF, SUB)) < 12, mm(normed, w_ref[:, 1024:1152]), 0.0)


ANY = pl.BlockSpec(memory_space=pl.ANY)


def by_order(width):
    return pl.BlockSpec((HALF, width), lambda i, order, place: (order[i], 0))


def turned():
    return pl.BlockSpec((1536, HALF), lambda i, order, place: (0, order[i]))


def fixed(shape):
    return pl.BlockSpec(shape, lambda i, *_: (0,) * len(shape))


def project(order, place, parts_in, tokens):
    sd = jax.ShapeDtypeStruct
    return pl.pallas_call(
        project_kernel,
        grid_spec=pltpu.PrefetchScalarGridSpec(
            num_scalar_prefetch=2,
            grid=(4,),
            in_specs=[ANY] * 7,
            out_specs=[by_order(1536), turned(), by_order(768), by_order(256), by_order(128), fixed((1536, 1152)), fixed((1536, 256)), fixed((8, 1536))],
            scratch_shapes=[pltpu.VMEM((4, HALF, 1536), BF), pltpu.SemaphoreType.DMA, pltpu.SemaphoreType.DMA((4,))],
        ),
        out_shape=[sd((1024, 1536), BF), sd((1536, 1024), BF), sd((1024, 768), F32), sd((1024, 256), F32), sd((1024, 128), F32), sd((1536, 1152), BF), sd((1536, 256), BF), sd((8, 1536), F32)],
        compiler_params=pltpu.CompilerParams(vmem_limit_bytes=VMEM_LIMIT),
        cost_estimate=pl.CostEstimate(flops=3_700_000_000, bytes_accessed=22_000_000, transcendentals=0),
    )(order, place, *parts_in, *tokens)


def gate_kernel(order_ref, place_ref, b0, b1, b2, b3, b4, c0, c1, normed_ref, y_ref, gg_ref, gate_ref, gs_ref, cot_ref, s_ref, w_ref, buf, w_sem, t_sem):
    step = pl.program_id(0)

    @pl.when(step == 0)
    def _():
        z, xh, y = place_ref[0], place_ref[1], place_ref[2]
        start_halves((c0, c1), buf, t_sem)

        def row_of(k, r, h):
            return (lax.rem(z - r + 4, 4) * 2 + lax.rem(xh + h, 2)) * 4 + lax.rem(y - k + 4, 4)

        place_blocks(ring_pieces((b0, b1, b2, b3, b4)), w_ref, w_sem, row_of)
        pltpu.make_async_copy(w_ref, w_ref, w_sem).wait()

    pltpu.make_async_copy(c0.at[0:HALF], buf.at[step], t_sem.at[step]).wait()
    cot = buf[step]
    cot_ref[...] = cot.T
    gate = mm(normed_ref[...], w_ref[:, 0:768])
    gs = mm(cot, w_ref[:, 768:1536])
    gate_ref[...] = gate
    gs_ref[...] = gs
    mixed = y_ref[...] * (gate * sigmoid(gate))
    sq = jnp.sum(mixed * mixed, axis=-1, keepdims=True)
    cr = jnp.sum((gs * gg_ref[0:1]) * mixed, axis=-1, keepdims=True)
    lane = cols((HALF, SUB))
    s_ref[...] = jnp.where(lane == 0, sq, jnp.where(lane == 1, cr, 0.0)).T[0:8]


def gate_side(order, place, parts_in, cots, normed, y, gg):
    sd = jax.ShapeDtypeStruct
    return pl.pallas_call(
        gate_kernel,
        grid_spec=pltpu.PrefetchScalarGridSpec(
            num_scalar_prefetch=2,
            grid=(4,),
            in_specs=[ANY] * 7 + [by_order(1536), by_order(768), fixed((8, 768))],
            out_specs=[by_order(768), by_order(768), turned(), pl.BlockSpec((8, HALF), lambda i, order, place: (0, order[i])), fixed((1536, 1536))],
            scratch_shapes=[pltpu.VMEM((4, HALF, 1536), BF), pltpu.SemaphoreType.DMA, pltpu.SemaphoreType.DMA((4,))],
        ),
        out_shape=[sd((1024, 768), F32), sd((1024, 768), F32), sd((1536, 1024), BF), sd((8, 1024), F32), sd((1536, 1536), BF)],
        compiler_params=pltpu.CompilerParams(vmem_limit_bytes=VMEM_LIMIT),
        cost_estimate=pl.CostEstimate(flops=4_900_000_000, bytes_accessed=30_000_000, transcendentals=800_000),
    )(order, place, *parts_in, *cots, normed, y, gg)


def mix_kernel(s0, s1, s2, s3, gate_ref, gs_ref, y_ref, gg_ref, scaled_ref, low_ref, dy_ref, gain_ref):
    sums = ((s0[...] + s1[...]) + (s2[...] + s3[...])).T
    inv = lax.rsqrt(sums[:, 0:1] / 3072 + EPS)
    corr = inv * inv * inv * (sums[:, 1:2] / 3072)
    gate, gs, y, gg = gate_ref[...], gs_ref[...], y_ref[...], gg_ref[0:1]
    sg = sigmoid(gate)
    act = gate * sg
    mixed = y * act
    normal = mixed * inv
    scaled_ref[...] = (normal * gg).astype(BF)
    gm = gs * gg * inv - mixed * corr
    low_ref[...] = (gm * y * (sg * (1.0 + gate * (1.0 - sg)))).astype(BF)
    dy_ref[...] = gm * act

    @pl.when(pl.program_id(0) == 0)
    def _():
        gain_ref[...] = jnp.zeros_like(gain_ref)

    gain_ref[0:1] += jnp.sum(gs * normal, axis=0, keepdims=True)


def mix(sums, gate, gs, y, gg):
    sd = jax.ShapeDtypeStruct
    block = pl.BlockSpec((HALF, 768), lambda i: (i, 0))
    return pl.pallas_call(
        mix_kernel,
        grid=(4,),
        in_specs=[pl.BlockSpec((8, HALF), lambda i: (0, i))] * 4 + [block] * 3 + [whole((8, 768))],
        out_specs=[block] * 3 + [whole((8, 768))],
        out_shape=[sd((1024, 768), BF), sd((1024, 768), BF), sd((1024, 768), F32), sd((8, 768), F32)],
        compiler_params=pltpu.CompilerParams(vmem_limit_bytes=VMEM_LIMIT),
        cost_estimate=pl.CostEstimate(flops=20_000_000, bytes_accessed=16_000_000, transcendentals=800_000),
    )(*sums, gate, gs, y, gg)


def outer_pair_kernel(n_ref, c_ref, g_ref, s_ref, o_ref):
    for at, a_ref, b_ref in ((0, n_ref, g_ref), (768, c_ref, s_ref)):
        r = mm(a_ref[...], b_ref[...]).astype(BF)
        for yi in range(4):
            for xi in range(2):
                row = (xi * 4 + yi) * 48
                o_ref[yi, xi * 48 : xi * 48 + 48, at : at + 768] = r[row : row + 48]


def outer_pair(normed_t, cot_t, gate_low, scaled):
    chunk = pl.BlockSpec((384, 1024), lambda i: (i, 0))
    return pl.pallas_call(
        outer_pair_kernel,
        grid=(4,),
        in_specs=[chunk, chunk, whole((1024, 768)), whole((1024, 768))],
        out_specs=pl.BlockSpec((4, 96, 1536), lambda i: (i, 0, 0)),
        out_shape=jax.ShapeDtypeStruct((16, 96, 1536), BF),
        compiler_params=pltpu.CompilerParams(vmem_limit_bytes=VMEM_LIMIT),
        cost_estimate=pl.CostEstimate(flops=4_900_000_000, bytes_accessed=14_000_000, transcendentals=0),
    )(normed_t, cot_t, gate_low, scaled)


def outer_kernel(n_ref, g_ref, small_ref, o_ref):
    r = mm(n_ref[...], g_ref[...]).astype(BF)
    small = small_ref[...].astype(BF)
    for yi in range(4):
        for xi in range(2):
            at = (xi * 4 + yi) * 48
            o_ref[yi, xi * 48 : xi * 48 + 48] = r[at : at + 48]
        o_ref[yi, 96:104] = small


def outer_messages(normed, grad, small):
    w = grad.shape[1]
    return pl.pallas_call(
        outer_kernel,
        grid=(4,),
        in_specs=[pl.BlockSpec((384, 1024), lambda i: (i, 0)), whole((1024, w)), whole((8, w))],
        out_specs=pl.BlockSpec((4, 104, w), lambda i: (i, 0, 0)),
        out_shape=jax.ShapeDtypeStruct((16, 104, w), BF),
        compiler_params=pltpu.CompilerParams(vmem_limit_bytes=VMEM_LIMIT),
        cost_estimate=pl.CostEstimate(flops=2 * 1024 * 1536 * w, bytes_accessed=3_200_000 + 5 * 1024 * w, transcendentals=0),
    )(normed, grad, small)


def outer_near_kernel(place_ref, n_ref, g_ref, d_ref, small_ref, dep_ref, *out):
    step = pl.program_id(0)
    y, xl = place_ref[2], place_ref[4]

    def columns(maps, steps):
        lane = cols(maps.shape)
        maps = jnp.where(xl == 0, maps, pltpu.roll(maps, 64, 1))
        return jnp.where(lane < 64, maps, pltpu.roll(steps, 64, 1)).astype(BF)

    r = columns(mm(n_ref[...], g_ref[...]), mm(n_ref[...], d_ref[...]))
    small = columns(small_ref[:, 0:128], small_ref[:, 128:256])
    for k in range(4):

        @pl.when(step == k)
        def _():
            for yi in range(4):
                to = lax.rem(yi - y + 4, 4)
                for xi in range(2):
                    at = (xi * 4 + yi) * 48
                    out[k][to, xi * 48 : xi * 48 + 48] = r[at : at + 48]
                out[k][to, 96:104] = small


def outer_near(place, normed, maps, steps, small, dep):
    w = 128
    return pl.pallas_call(
        outer_near_kernel,
        grid_spec=pltpu.PrefetchScalarGridSpec(
            num_scalar_prefetch=1,
            grid=(4,),
            in_specs=[pl.BlockSpec((384, 1024), lambda i, place: (lax.rem(place[0] + i, 4), 0)), fixed((1024, w)), fixed((1024, w)), fixed((8, 256)), ANY],
            out_specs=[fixed((4, 104, w))] * 4,
        ),
        out_shape=[jax.ShapeDtypeStruct((4, 104, w), BF)] * 4,
        compiler_params=pltpu.CompilerParams(vmem_limit_bytes=VMEM_LIMIT),
        cost_estimate=pl.CostEstimate(flops=1, bytes_accessed=1, transcendentals=0),
    )(place, normed, maps, steps, small, dep)


def rows_out(place_ref, total, send_ref, keep_ref):
    for core in range(2):

        @pl.when(place_ref[3] == core)
        def _():
            keep_ref[...] = total[core * SEQ : core * SEQ + SEQ]
            send_ref[...] = total[SEQ - core * SEQ : 2 * SEQ - core * SEQ].astype(BF)


def out_kernel(place_ref, s_ref, w_ref, send_ref, keep_ref):
    rows_out(place_ref, mm_nt(s_ref[...], w_ref[...]), send_ref, keep_ref)


def token_kernel(place_ref, g_ref, x_ref, d_ref, wz_ref, wx_ref, wd_ref, send_ref, keep_ref):
    total = mm_nt(g_ref[...], wz_ref[...]) + mm_nt(x_ref[...], wx_ref[...]) + mm_nt(d_ref[...], wd_ref[...])
    rows_out(place_ref, total, send_ref, keep_ref)


def by_rows(kernel, place, tokens, weights, places):
    columns = lambda at: lambda i, place: (i, at(place))
    return pl.pallas_call(
        kernel,
        grid_spec=pltpu.PrefetchScalarGridSpec(
            num_scalar_prefetch=1,
            grid=(6,),
            in_specs=[fixed(t.shape) for t in tokens] + [pl.BlockSpec((256, t.shape[1]), columns(at)) for t, at in zip(tokens, places)],
            out_specs=[pl.BlockSpec((SEQ, 256), lambda i, place: (0, i))] * 2,
        ),
        out_shape=[jax.ShapeDtypeStruct((SEQ, 1536), BF), jax.ShapeDtypeStruct((SEQ, 1536), F32)],
        compiler_params=pltpu.CompilerParams(vmem_limit_bytes=VMEM_LIMIT),
        cost_estimate=pl.CostEstimate(flops=1, bytes_accessed=1, transcendentals=0),
    )(place, *tokens, *weights)


def after_kernel(x_ref, *refs):
    pass


def after(x, *deps):
    return pl.pallas_call(
        after_kernel,
        in_specs=[ANY] * (1 + len(deps)),
        out_specs=ANY,
        out_shape=jax.ShapeDtypeStruct(x.shape, x.dtype),
        input_output_aliases={0: 0},
    )(x, *deps)


def swap(a, axis):
    return lax.ppermute(a, axis, [(0, 1), (1, 0)])


def turn(a, axis, k):
    return lax.ppermute(a, axis, [(i, (i + k) % 4) for i in range(4)])


def pair(own, other, axis):
    first = lax.axis_index(axis) == 0
    return jnp.stack([jnp.where(first, own, other), jnp.where(first, other, own)])


def mine(a, axis, dim, size):
    i = lax.axis_index(axis)
    return (
        lax.dynamic_slice_in_dim(a, i * size, size, dim),
        lax.dynamic_slice_in_dim(a, (1 - i) * size, size, dim),
    )


def turns(a, axis):
    return [a] + [turn(a, axis, k) for k in (1, 2, 3)]


def shards(resid, cotangent, segments, pre_gain, w_z, w_x, w_bc, w_dt, conv_x, conv_x_bias, conv_bc, conv_bc_bias, dt_bias, a_log, d_skip, gate_gain, w_out):
    core, xl = lax.axis_index("c"), lax.axis_index("xl")
    place = jnp.stack([lax.axis_index("z"), lax.axis_index("xh"), lax.axis_index("y"), core, xl])
    base = core * 2 + xl
    order = jnp.stack([core * 2, core * 2 + 1, 2 - core * 2, 3 - core * 2])

    own_bc = jnp.concatenate([w_bc, pre_gain[:, None], jnp.zeros((12, 127), BF)], axis=1)
    keep_x, send_x = mine(w_x, "c", 1, 768)
    keep_dt, send_dt = mine(w_dt, "c", 1, 12)
    bc_x, bc_c = swap(own_bc, "xl"), swap(own_bc, "c")
    bc_d = lax.ppermute(own_bc, ("c", "xl"), [(i, 3 - i) for i in range(4)])
    got = swap(jnp.concatenate([send_x, send_dt], axis=1), "c")
    bc48 = pair(pair(own_bc, bc_x, "xl"), pair(bc_c, bc_d, "xl"), "c").reshape(48, 384)
    xdt = pair(jnp.concatenate([keep_x, keep_dt], axis=1), got, "c").reshape(48, 780)
    first = jnp.concatenate([xdt[:, :768], bc48[:, :256], xdt[:, 768:], bc48[:, 256:372]], axis=1)
    first_far = swap(first, "xh")
    first = jnp.stack([first, first_far])

    keep_z, send_z = mine(w_z, "c", 1, 768)
    keep_o, send_o = mine(w_out.T, "c", 1, 768)
    got = swap(jnp.concatenate([send_z, send_o], axis=1), "c")
    second = pair(jnp.concatenate([keep_z, keep_o], axis=1), got, "c").reshape(48, 1536)
    second = jnp.stack([second, swap(second, "xh")])

    near_x, near = turns(first, "y"), turns(second, "z")
    b_own = jnp.stack(near)
    b_ahead, b_back = turn(b_own, "y", 1), turn(b_own, "y", 3)
    a_own = after(jnp.stack(near_x), *near[1:])
    a_ahead, a_back = turn(a_own, "z", 1), turn(a_own, "z", 3)
    b_low, b_high = b_ahead[:2], b_back[2:]
    a_parts = [a_own, a_ahead, a_back, turn(after(a_ahead[:2], b_low, b_high), "z", 1), turn(after(a_back[2:], b_low, b_high), "z", 3)]
    b_parts = [b_own, b_ahead, b_back, turn(b_low, "y", 1), turn(b_high, "y", 3)]

    def halves(a, *deps):
        half = after(lax.all_gather(a, "xl", axis=0, tiled=True), *deps)
        return [half, swap(half, "c")]

    tokens = halves(resid, a_parts[1], a_parts[2])
    cots = halves(cotangent, a_parts[3], a_parts[4])
    cut = jnp.sum((segments == segments[0]).astype(jnp.int32))[None]
    cuts = pair(cut, swap(cut, "c"), "c").reshape(2)

    normed, normed_t, x_raw, bc_raw, dt_raw, w_1, w_maps, gain_rows = project(order, place, a_parts, tokens)

    def own(a, size):
        return mine(a, "c", a.ndim - 1, size)[0]

    cx, cxb, gg = own(conv_x, 768), own(conv_x_bias, 768), own(gate_gain, 768)
    dtb, al, dsk = own(dt_bias, 12), own(a_log, 12), own(d_skip, 12)
    taps_x = jnp.concatenate([cx, cxb[None], jnp.repeat(dsk, 64)[None], jnp.zeros((2, 768), F32)], axis=0)
    taps_bc = jnp.concatenate([conv_bc, conv_bc_bias[None], jnp.zeros((3, 256), F32)], axis=0)
    wide_heads = lambda v: jnp.pad(v, (0, 116))[None]
    heads = jnp.concatenate([wide_heads(dtb), wide_heads(-jnp.exp(al)), wide_heads(dsk), jnp.zeros((5, 128), F32)], axis=0)
    gains = jnp.broadcast_to(gg[None], (8, 768))
    spread_np = np.arange(768)[None, :] // 64 == np.arange(128)[:, None]
    spread, spread_t = jnp.asarray(spread_np, BF), jnp.asarray(spread_np.T, BF)
    y, st = ssd_forward(cuts, x_raw, bc_raw, dt_raw, taps_x, taps_bc, heads, spread)

    gate, gs, cot_t, sums, w_2 = gate_side(order, place, b_parts, cots, normed, y, gains)
    sums_c, sums_x = swap(sums, "c"), swap(sums, "xl")
    sums_d = lax.ppermute(sums, ("c", "xl"), [(i, 3 - i) for i in range(4)])
    scaled, gate_low, dy, g_gain = mix([sums, sums_c, sums_x, sums_d], gate, gs, y, gains)

    def over_cores(send, keep):
        return (keep + swap(send, "c").astype(F32)).astype(BF)

    def cross_xl(half):
        keep, send = mine(half, "xl", 0, 256)
        return keep, swap(send, "xl")

    out_rows = by_rows(out_kernel, place, [scaled], [w_2], [lambda place: 1])
    g_zo = outer_pair(normed_t, after(cot_t, out_rows[0]), gate_low, scaled)
    g_zo_z = lax.psum_scatter(g_zo.reshape(1536, 1536), "z", scatter_dimension=0, tiled=True)
    g_zo_y = lax.psum_scatter(g_zo_z, "y", scatter_dimension=0, tiled=True)

    out_half = over_cores(*out_rows)
    out_own, out_far = cross_xl(out_half)
    layer_out = (resid.astype(F32) + (out_own.astype(F32) + out_far.astype(F32))).astype(BF)

    dy = after(dy, out_half, g_zo)
    x_low, keep, send, gdt, g_tx, keep_c, send_c, g_hd = ssd_backward(cuts, place, x_raw, bc_raw, dt_raw, dy, y, st, taps_x, taps_bc, heads, spread, spread_t)

    keep, keep_c = keep + swap(after(send, out_far), "c"), keep_c + swap(send_c, "c")
    keep_h = keep_c.astype(BF)
    keep = jnp.concatenate([keep.astype(BF), keep_h, (keep_c - keep_h.astype(F32)).astype(BF)], axis=0)
    small_x = jnp.concatenate([g_tx[:5], g_gain[:1], jnp.zeros((2, 768), F32)], axis=0)
    x_blocks = outer_messages(normed_t, x_low, small_x)
    x_message = lax.all_to_all(x_blocks, ("z", "y"), 0, 0, tiled=True)
    far = swap(keep, "xl")
    group = keep.astype(F32) + far.astype(F32)
    bc_low = group[:1024].astype(BF)
    small_s = jnp.concatenate([group[1024:1032] + group[1032:], g_hd], axis=1)
    token_rows = by_rows(token_kernel, place, [after(gate_low, keep, x_blocks, g_zo_z), x_low, gdt], [w_2, w_1, w_1], [lambda place: 0, lambda place: 0, lambda place: 8])
    token_half = over_cores(after(token_rows[0], far), token_rows[1])
    grad_own, grad_far = cross_xl(token_half)
    near_z = outer_near(place, normed_t, bc_low, gdt, small_s, x_blocks)
    near_z = [near_z[0]] + [turn(near_z[k], "z", k) for k in (1, 2, 3)]
    near_y = [((near_z[0][k].astype(F32) + near_z[2][k].astype(F32)) + (near_z[1][k].astype(F32) + near_z[3][k].astype(F32))).astype(BF) for k in range(4)]
    near_y[2] = after(near_y[2], x_message)
    near_y = [after(near_y[0], grad_far)] + [turn(near_y[k], "y", k) for k in (1, 2, 3)]

    rows_own, rows_send = mine(bc_low, "c", 0, SEQ)
    bc_own = pair(rows_own, swap(rows_send, "c"), "c")
    bc_own = jnp.concatenate([bc_own[0], bc_own[1]], axis=1)
    bc_own = lax.dynamic_slice_in_dim(bc_own, xl * 256, 256, 0)
    bc_part = lax.dot_general(bc_own, w_maps, (((1,), (1,)), ((), ())), preferred_element_type=F32)
    grad_normed = (grad_own.astype(F32) + grad_far.astype(F32)) + bc_part

    wide = lambda a: a.astype(F32)
    zo = jnp.concatenate([wide(g_zo_y), jnp.zeros((8, 1536), F32)], axis=0)
    total = jnp.concatenate([jnp.sum(wide(x_message), axis=0), zo, (wide(near_y[0]) + wide(near_y[2])) + (wide(near_y[1]) + wide(near_y[3]))], axis=1)
    keep, send = mine(total[:96], "xh", 0, 48)
    small = total[96:].astype(BF)
    far = swap(jnp.concatenate([send.astype(BF), small], axis=0), "xh")
    total = jnp.concatenate([keep, wide(small)], axis=0) + wide(far)

    gain_wide = gain_rows[4]
    rw = resid.astype(F32)
    inv = lax.rsqrt(jnp.mean(rw * rw, axis=-1, keepdims=True) + EPS)
    inner = jnp.sum(gain_wide[None, :] * grad_normed * rw, axis=-1, keepdims=True)
    grad_resid = cotangent.astype(F32) + gain_wide[None, :] * grad_normed * inv - rw * (inv * inv * inv) * inner / 1536

    keep, send = mine(total[:48], "c", 0, 24)
    far = swap(jnp.concatenate([send, total[48:]], axis=0), "c")
    got = pair(jnp.concatenate([keep, total[48:]], axis=0), far, "c")
    both = lambda rows, at, width: jnp.concatenate([got[0, rows, at : at + width], got[1, rows, at : at + width]], axis=1)
    main, rest = slice(0, 24), slice(24, 32)
    grad_w_x, grad_w_z, grad_w_out_t = both(main, 0, 768), both(main, 768, 768), both(main, 1536, 768)
    grad_w_dt = both(main, 2368, 12)
    bc24, conv24 = both(main, 2304, 64), both(rest, 2304, 64)
    small_wide = both(rest, 0, 768)
    small_heads = both(rest, 2368, 12)

    tall = lambda a, b: jnp.sum(a.astype(F32) * b, axis=1)
    pg = tall(w_z, grad_w_z) + tall(w_x, grad_w_x) + tall(w_dt, grad_w_dt)
    pg, pg_send = mine(pg, "xl", 0, 12)
    bc12, bc_send = mine(bc24, "xl", 0, 12)
    far = swap(jnp.concatenate([bc_send, conv24, jnp.pad(pg_send, (0, 116))[None]], axis=0), "xl")
    got = pair(jnp.concatenate([bc12, conv24], axis=0), far[:20], "xl")
    got = got.reshape(2, 20, 2, 64).transpose(1, 2, 0, 3).reshape(20, 256)
    grad_w_bc, grad_conv_bc = got[:12], got[12:]
    grad_pre_gain = (pg + far[20, :12] + tall(w_bc, grad_w_bc)) / pre_gain.astype(F32)
    return (
        layer_out,
        grad_resid,
        grad_pre_gain,
        grad_w_z,
        grad_w_x,
        grad_w_bc,
        grad_w_dt,
        small_wide[:4],
        small_wide[4],
        grad_conv_bc[:4],
        grad_conv_bc[4],
        small_heads[0],
        small_heads[1],
        small_heads[2],
        small_wide[5],
        grad_w_out_t.T,
    )


def solution(mesh):
    fine = Mesh(mesh.devices.reshape(4, 2, 4, 2, 2), ("z", "xh", "y", "c", "xl"))
    dp, tp, every = ("z", "xh", "y", "c"), "xl", ("z", "xh", "y", "c", "xl")
    return jax.shard_map(
        shards,
        mesh=fine,
        in_specs=(P(every, None), P(every, None), P(dp), P(every), P(dp, tp), P(dp, tp), P(every, None), P(dp, tp), P(None, tp), P(tp), P(), P(), P(tp), P(tp), P(tp), P(tp), P(tp, dp)),
        out_specs=(P(every, None), P(every, None), P(every), P(dp, tp), P(dp, tp), P(every, None), P(dp, tp), P(None, tp), P(tp), P(), P(), P(tp), P(tp), P(tp), P(tp), P(tp, dp)),
        check_vma=False,
    )
```

```python
import jax
import jax.numpy as jnp
import numpy as np
from jax import lax
from jax.experimental import pallas as pl
from jax.experimental.pallas import tpu as pltpu
from jax.sharding import Mesh, PartitionSpec as P

EPS = 1e-05
VMEM_LIMIT = 60 * 1024 * 1024
BF = jnp.bfloat16
F32 = jnp.float32
SEQ = 512
HALF = 256
SUB = 128
PAIRS = 2


def mm(a, b):
    return jnp.dot(a, b, preferred_element_type=F32)


def mm_nt(a, b):
    return lax.dot_general(a, b, (((1,), (1,)), ((), ())), preferred_element_type=F32)


def mm_tn(a, b):
    return lax.dot_general(a, b, (((0,), (0,)), ((), ())), preferred_element_type=F32)


def parts(v, count):
    out = []
    for _ in range(count):
        low = v.astype(BF)
        out.append(low)
        v = v - low.astype(F32)
    return out


def split_left(v, m, count=2):
    return sum(mm(p, m) for p in parts(v, count))


def split_right(m, v, count=3):
    return sum(mm(m, p) for p in parts(v, count))


def rows(shape):
    return lax.broadcasted_iota(jnp.int32, shape, 0)


def cols(shape):
    return lax.broadcasted_iota(jnp.int32, shape, 1)


def softplus(v):
    e = jnp.exp(-jnp.abs(v))
    tail = jnp.where(e < 1e-3, e * (1.0 - 0.5 * e), jnp.log(1.0 + e))
    return jnp.maximum(v, 0.0) + tail


def sigmoid(v):
    return 1.0 / (1.0 + jnp.exp(-v))


def same_doc(t, s, cut):
    return (t < cut) == (s < cut)


def conv_masks(cut):
    t = rows((SEQ, SUB))
    return [jnp.where((t >= j) & ((t < cut) | (t - j >= cut)), 1.0, 0.0) for j in (1, 2, 3)]


def conv(v, taps, masks):
    u = taps[4:5] + taps[3:4] * v
    for j in (1, 2, 3):
        u = u + taps[3 - j : 4 - j] * (pltpu.roll(v, j, 0) * masks[j - 1])
    return u


def time_steps(dt_raw, heads, cut):
    dt = softplus(dt_raw + heads[0:1])
    a = dt * heads[1:2]
    tri = jnp.where(rows((HALF, HALF)) >= cols((HALF, HALF)), 1.0, 0.0).astype(BF)
    c = [split_right(tri, a[:HALF]), split_right(tri, a[HALF:])]
    t = rows((HALF, SUB))
    ending = same_doc(t, HALF - 1, cut)
    alive = same_doc(t + HALF, HALF - 1, cut)
    ew = jnp.where(ending, jnp.exp(c[0][HALF - 1 : HALF] - c[0]), 0.0)
    e1 = jnp.where(alive, jnp.exp(c[1]), 0.0)
    return dt, c, ew, e1


def masked_scores(cb, bb, block, cut, lower=True):
    out = {}
    for i, j in ((0, 0), (1, 0), (1, 1)):
        ti, sj = slice(i * SUB, i * SUB + SUB), slice(j * SUB, j * SUB + SUB)
        if lower:
            s = mm_nt(cb[ti], bb[sj])
            t = rows((SUB, SUB)) + (block * HALF + i * SUB)
            r = cols((SUB, SUB)) + (block * HALF + j * SUB)
        else:
            s = mm_nt(bb[sj], cb[ti])
            r = rows((SUB, SUB)) + (block * HALF + j * SUB)
            t = cols((SUB, SUB)) + (block * HALF + i * SUB)
        out[i, j] = jnp.where((t >= r) & same_doc(t, r, cut), s, 0.0)
    return out


def head_lanes(k):
    lane = cols((HALF, SUB))
    return (lane < 64) if k == 0 else (lane >= 64)


def fill_columns(c, ccol_ref, ct_ref):
    for k in (0, 1):
        ct_ref[k] = c[k].T
        for head in range(12):
            ccol_ref[k, head] = jnp.broadcast_to(c[k][:, head : head + 1], (HALF, SUB))


def put_stack(ref, values):
    at = 0
    for v in values:
        for p in parts(v, 2):
            ref[at : at + v.shape[0]] = p
            at += v.shape[0]


def spread_stack(ref, e, heights):
    wide, out, at = mm(ref[...], e), [], 0
    for n in heights:
        out.append(wide[at : at + n] + wide[at + n : at + 2 * n])
        at += 2 * n
    return out


BLOCKS = ((0, 0), (1, 0), (1, 1))


def fwd_kernel(cut_ref, xr_ref, bcr_ref, dtr_ref, tx_ref, tbc_ref, hd_ref, e_ref, y_ref, st_ref):
    cut = cut_ref[pl.program_id(0)]
    masks = conv_masks(cut)
    act = []
    for i in range(2):
        sl = slice(i * SUB, i * SUB + SUB)
        u = conv(bcr_ref[:, sl], tbc_ref[:, sl], masks)
        act.append(parts(u * sigmoid(u), 2))
    (bb, bb_low), (cb, cb_low) = act
    cb3 = jnp.concatenate([cb, cb_low, cb], axis=1)
    bb3 = jnp.concatenate([bb, bb, bb_low], axis=1)
    dt, c, ew, e1 = time_steps(dtr_ref[...], hd_ref[...], cut)
    ct = [c[0].T, c[1].T]
    tw = ew * dt[:HALF]
    scores = [masked_scores(cb3[k * HALF : k * HALF + HALF], bb3[k * HALF : k * HALF + HALF], k, cut) for k in (0, 1)]
    b0t, b0t_low = bb[:HALF].T, bb_low[:HALF].T
    for p in range(6):
        sl = slice(p * SUB, p * SUB + SUB)
        e = e_ref[:, sl]
        u = conv(xr_ref[:, sl], tx_ref[:, sl], masks)
        x = u * sigmoid(u)
        xtf = x * split_left(dt, e)
        xh = xtf.astype(BF)
        xhf = xh.astype(F32)
        xl_turned = pltpu.roll(xtf - xhf, 64, 1).astype(BF)
        skip = tx_ref[5:6, sl] * x
        xw, xw_low = parts(x[:HALF] * split_left(tw, e), 2)
        st = mm(b0t, xw) + (mm(b0t, xw_low) + mm(b0t_low, xw))
        st_ref[0, :, sl] = st
        st, st_low = parts(st, 2)
        carry = (mm(cb[HALF:], st) + (mm(cb[HALF:], st_low) + mm(cb_low[HALF:], st))) * split_left(e1, e)
        for k in (0, 1):
            ys = [[], []]
            for h in (0, 1):
                head = 2 * p + h
                at = slice(k * HALF, k * HALF + HALF)
                xm = jnp.where(head_lanes(h), xh[at], xl_turned[at])
                col = c[k][:, head : head + 1]
                row = ct[k][head : head + 1, :]
                m = {}
                for i, j in ((0, 0), (1, 0), (1, 1)):
                    gap = col[i * SUB : i * SUB + SUB] - row[:, j * SUB : j * SUB + SUB]
                    full = jnp.exp(jnp.minimum(gap, 0.0)) * scores[k][i, j]
                    m[i, j] = parts(full, 2)
                ys[0].append(mm(jnp.concatenate(m[0, 0], axis=1), jnp.concatenate([xm[:SUB], xm[:SUB]], axis=0)))
                wide = [m[1, 0][0], m[1, 1][0], m[1, 0][1], m[1, 1][1]]
                ys[1].append(mm(jnp.concatenate(wide, axis=1), jnp.concatenate([xm, xm], axis=0)))
            for i in (0, 1):
                at = k * HALF + i * SUB
                first = cols((SUB, SUB)) < 64
                y0, y1 = ys[i]
                y = jnp.where(first, y0, y1) + pltpu.roll(jnp.where(first, y1, y0), 64, 1) + skip[at : at + SUB]
                if k == 1:
                    y = y + carry[i * SUB : i * SUB + SUB]
                y_ref[at : at + SUB, sl] = y


def seq_spec(width):
    return pl.BlockSpec((SEQ, width), lambda i: (i, 0))


def whole(shape):
    return pl.BlockSpec(shape, lambda i: (0,) * len(shape))


SMEM = pl.BlockSpec(memory_space=pltpu.SMEM)


def ssd_forward(cut, x_raw, bc_raw, dt_raw, taps_x, taps_bc, heads, spread):
    return pl.pallas_call(
        fwd_kernel,
        grid=(2,),
        in_specs=[SMEM, seq_spec(768), seq_spec(256), seq_spec(128), whole((8, 768)), whole((8, 256)), whole((8, 128)), whole((128, 768))],
        out_specs=[seq_spec(768), pl.BlockSpec((1, 128, 768), lambda i: (i, 0, 0))],
        out_shape=[jax.ShapeDtypeStruct((1024, 768), F32), jax.ShapeDtypeStruct((2, 128, 768), F32)],
        compiler_params=pltpu.CompilerParams(vmem_limit_bytes=VMEM_LIMIT),
        cost_estimate=pl.CostEstimate(flops=4_000_000_000, bytes_accessed=9_000_000, transcendentals=4_000_000),
    )(cut, x_raw, bc_raw, dt_raw, taps_x, taps_bc, heads, spread)


def bwd_kernel(cut_ref, place_ref, xr_ref, bcr_ref, dtr_ref, dy_ref, y_ref, st_ref, tx_ref, tbc_ref, hd_ref, e_ref, et_ref,
               gx_ref, keep_ref, send_ref, gdt_ref, gtx_ref, keepc_ref, sendc_ref, ghd_ref,
               ds_ref, masks_ref, steps_ref, up_ref, ccol_ref, ct_ref, c1t_ref, b0_ref, acc_ref, accb_ref, skip_ref):
    seq = pl.program_id(0)
    cut = cut_ref[seq]
    masks = conv_masks(cut)

    def conv_back(du, v, taps, masks):
        g = taps[3:4] * du
        sums = [jnp.sum(du * v, axis=0, keepdims=True)]
        for j in (1, 2, 3):
            dm = du * masks[j - 1]
            g = g + taps[3 - j : 4 - j] * pltpu.roll(dm, SEQ - j, 0)
            sums.append(jnp.sum(dm * pltpu.roll(v, j, 0), axis=0, keepdims=True))
        return g, [sums[3], sums[2], sums[1], sums[0], jnp.sum(du, axis=0, keepdims=True)]

    @pl.when(seq == 0)
    def _():
        gtx_ref[...] = jnp.zeros_like(gtx_ref)
        keepc_ref[...] = jnp.zeros_like(keepc_ref)
        sendc_ref[...] = jnp.zeros_like(sendc_ref)
        ghd_ref[...] = jnp.zeros_like(ghd_ref)

    act = []
    for i in range(2):
        sl = slice(i * SUB, i * SUB + SUB)
        u = conv(bcr_ref[:, sl], tbc_ref[:, sl], masks)
        act.append((u * sigmoid(u)).astype(BF))
    for j in range(3):
        masks_ref[j] = masks[j]
    bb, cb = act
    dt, c, ew, e1 = time_steps(dtr_ref[...], hd_ref[...], cut)
    fill_columns(c, ccol_ref, ct_ref)
    put_stack(steps_ref, [dt, ew * dt[:HALF], e1, ew])
    blk = lambda a, k: a[k * HALF : k * HALF + HALF]
    for k in (0, 1):
        up = masked_scores(blk(cb, k), blk(bb, k), k, cut, lower=False)
        for n, at in enumerate(BLOCKS):
            up_ref[k, n] = up[at]
    c1t_ref[...] = cb[HALF:].T
    b0_ref[...] = bb[:HALF]
    ds_ref[...] = jnp.zeros_like(ds_ref)
    acc_ref[...] = jnp.zeros_like(acc_ref)
    accb_ref[...] = jnp.zeros_like(accb_ref)
    skip_ref[...] = jnp.zeros_like(skip_ref)

    def one_pair(p, carried):
        sl = pl.ds(pl.multiple_of(p * SUB, SUB), SUB)
        e, et, taps = e_ref[:, sl], et_ref[sl, :], tx_ref[:, sl]
        xr = xr_ref[:, sl]
        pair_masks = [masks_ref[j] for j in range(3)]
        u = conv(xr, taps, pair_masks)
        sg = sigmoid(u)
        x = u * sg
        dtx, twx, e1x, ewx = spread_stack(steps_ref, e, (SEQ, HALF, HALF, HALF))
        xtf = x * dtx
        xt = xtf.astype(BF)
        dy = dy_ref[:, sl]
        dyb = dy.astype(BF)
        dyh = dyb.astype(F32)
        xh = xt.astype(F32)
        xl = (xtf - xh).astype(BF)
        dl_turned = pltpu.roll(dy - dyh, 64, 1).astype(BF)
        xh_turned = pltpu.roll(xh, 64, 1).astype(BF)
        skip = jnp.broadcast_to(jnp.sum(dy * x, axis=0, keepdims=True), (16, SUB))
        stack = parts(dyh * y_ref[:, sl], 2) + parts(dyh * x, 2) + parts(skip, 3)
        wide = mm(jnp.concatenate(stack, axis=0), et)
        acc_ref[0] += wide[0:SEQ] + wide[SEQ : 2 * SEQ]
        acc_ref[1] += wide[2 * SEQ : 3 * SEQ] + wide[3 * SEQ : 4 * SEQ]
        skip_ref[...] += wide[2048:2056] + wide[2064:2072] + wide[2080:2088]
        dxs = []
        for k in (0, 1):
            back = 0.0
            for h in (0, 1):
                head = 2 * p + h
                lanes, none = head_lanes(h), jnp.zeros((), BF)
                dm = jnp.where(lanes, blk(dyb, k), none)
                dm2 = jnp.concatenate([jnp.where(lanes, blk(dyb, k), blk(dl_turned, k)), dm], axis=1)
                xm2 = jnp.concatenate([jnp.where(lanes, blk(xt, k), blk(xh_turned, k)), jnp.where(lanes, blk(xl, k), none)], axis=1)
                row = ct_ref[k, pl.ds(head, 1), :]
                gfull = mm_nt(dm2, xm2)
                mt = {}
                for n, (i, j) in enumerate(BLOCKS):
                    ti, sj = slice(i * SUB, i * SUB + SUB), slice(j * SUB, j * SUB + SUB)
                    decay = jnp.exp(-jnp.abs(ccol_ref[k, head, ti, :] - row[:, sj]))
                    if i == j:
                        decay_t = decay
                    else:
                        decay_t = jnp.exp(-jnp.abs(ccol_ref[k, head, sj, :] - row[:, ti]))
                    ds_ref[k, i + j] += gfull[ti, sj] * decay
                    mt[i, j] = (decay_t * up_ref[k, n]).astype(BF)
                rows0 = jnp.concatenate([mt[0, 0], mt[1, 0]], axis=1)
                rows1 = jnp.concatenate([jnp.zeros((SUB, SUB), BF), mt[1, 1]], axis=1)
                back = back + mm(jnp.concatenate([rows0, rows1], axis=0), dm)
            dxs.append(back)
        st, st_low = parts(st_ref[0, :, sl], 2)
        dcs, dcs_low = parts(dy[HALF:] * e1x, 2)
        accb_ref[0] += mm_nt(dcs, st) + (mm_nt(dcs_low, st) + mm_nt(dcs, st_low))
        dst, dst_low = parts(mm(c1t_ref[...], dcs) + mm(c1t_ref[...], dcs_low), 2)
        dxw = mm(b0_ref[...], dst)
        xw, xw_low = parts(x[:HALF] * twx, 2)
        accb_ref[1] += mm_nt(xw, dst) + (mm_nt(xw_low, dst) + mm_nt(xw, dst_low))
        dx0 = dxs[0] + dxw * ewx
        dxt = jnp.concatenate([dx0, dxs[1]], axis=0)
        wide = mm(jnp.concatenate(parts(x * dxt, 2), axis=0), et)
        acc_ref[2] += wide[:SEQ] + wide[SEQ:]
        dx = dtx * dxt + taps[5:6] * dy
        du = dx * (sg * (1.0 + u * (1.0 - sg)))
        g, sums = conv_back(du, xr, taps, pair_masks)
        gx_ref[:, sl] = g.astype(BF)
        gtx_ref[0:5, sl] += jnp.concatenate(sums, axis=0)
        return carried

    lax.fori_loop(0, 6 // PAIRS, lambda i, x: [one_pair(i * PAIRS + j, x) for j in range(PAIRS)][0], 0)
    sum_y, sum_x, sum_d = acc_ref[0], acc_ref[1], acc_ref[2]
    d_c1, d_b0 = accb_ref[0], accb_ref[1]
    d_b, d_c = [], []
    for k in (0, 1):
        bk, ck = blk(bb, k), blk(cb, k)
        m = {}
        for i, j in ((0, 0), (1, 0), (1, 1)):
            t = rows((SUB, SUB)) + (k * HALF + i * SUB)
            r = cols((SUB, SUB)) + (k * HALF + j * SUB)
            m[i, j] = jnp.where((t >= r) & same_doc(t, r, cut), ds_ref[k, i + j], 0.0).astype(BF)
        lowr = jnp.concatenate([m[1, 0], m[1, 1]], axis=1)
        d_c += [mm(m[0, 0], bk[:SUB]), mm(lowr, bk)]
        d_b += [mm_tn(m[0, 0], ck[:SUB]) + mm_tn(m[1, 0], ck[SUB:]), mm_tn(m[1, 1], ck[SUB:])]
    d_b = jnp.concatenate([jnp.concatenate(d_b[:2], axis=0) + d_b0] + d_b[2:], axis=0)
    d_c = jnp.concatenate(d_c[:2] + [jnp.concatenate(d_c[2:], axis=0) + d_c1], axis=0)
    for i, d in ((0, d_b), (1, d_c)):
        sl = slice(i * SUB, i * SUB + SUB)
        v = bcr_ref[:, sl]
        u = conv(v, tbc_ref[:, sl], masks)
        sg = sigmoid(u)
        g, sums = conv_back(d * (sg * (1.0 + u * (1.0 - sg))), v, tbc_ref[:, sl], masks)

        @pl.when(place_ref[3] == i)
        def _():
            keep_ref[...] = g
            for r, s in enumerate(sums):
                keepc_ref[r : r + 1] += s

        @pl.when(place_ref[3] != i)
        def _():
            send_ref[...] = g
            for r, s in enumerate(sums):
                sendc_ref[r : r + 1] += s

    hd = hd_ref[...]
    w = (sum_y - hd[2:3] * sum_x) - dt * sum_d
    tri = jnp.where((cols((SEQ, SEQ)) >= rows((SEQ, SEQ))) & same_doc(rows((SEQ, SEQ)), cols((SEQ, SEQ)), cut), 1.0, 0.0).astype(BF)
    run = split_right(tri, w)
    d_dt = sum_d + hd[1:2] * run
    gd = d_dt * sigmoid(dtr_ref[...] + hd[0:1])
    gdt_ref[...] = gd.astype(BF)
    ghd_ref[0:1] += jnp.sum(gd, axis=0, keepdims=True)
    ghd_ref[2:3] += skip_ref[0:1]
    ghd_ref[1:2] += jnp.sum(dt * run, axis=0, keepdims=True) * hd[1:2]


def ssd_backward(cut, place, x_raw, bc_raw, dt_raw, dy, y, st, taps_x, taps_bc, heads, spread, spread_t):
    return pl.pallas_call(
        bwd_kernel,
        grid=(2,),
        in_specs=[SMEM, SMEM, seq_spec(768), seq_spec(256), seq_spec(128), seq_spec(768), seq_spec(768),
                  pl.BlockSpec((1, 128, 768), lambda i: (i, 0, 0)), whole((8, 768)), whole((8, 256)), whole((8, 128)), whole((128, 768)), whole((768, 128))],
        out_specs=[seq_spec(768), seq_spec(128), seq_spec(128), seq_spec(128), whole((8, 768)), whole((8, 128)), whole((8, 128)), whole((8, 128))],
        out_shape=[jax.ShapeDtypeStruct((1024, 768), BF), jax.ShapeDtypeStruct((1024, 128), F32), jax.ShapeDtypeStruct((1024, 128), F32), jax.ShapeDtypeStruct((1024, 128), BF),
                   jax.ShapeDtypeStruct((8, 768), F32), jax.ShapeDtypeStruct((8, 128), F32), jax.ShapeDtypeStruct((8, 128), F32), jax.ShapeDtypeStruct((8, 128), F32)],
        scratch_shapes=[
            pltpu.VMEM((2, 3, SUB, SUB), F32),
            pltpu.VMEM((3, SEQ, SUB), F32),
            pltpu.VMEM((5 * SEQ, SUB), BF),
            pltpu.VMEM((2, 3, SUB, SUB), F32),
            pltpu.VMEM((2, 12, HALF, SUB), F32),
            pltpu.VMEM((2, SUB, HALF), F32),
            pltpu.VMEM((SUB, HALF), BF),
            pltpu.VMEM((HALF, SUB), BF),
            pltpu.VMEM((3, SEQ, SUB), F32),
            pltpu.VMEM((2, HALF, SUB), F32),
            pltpu.VMEM((8, SUB), F32),
        ],
        compiler_params=pltpu.CompilerParams(vmem_limit_bytes=VMEM_LIMIT),
        cost_estimate=pl.CostEstimate(flops=12_000_000_000, bytes_accessed=14_000_000, transcendentals=4_000_000),
    )(cut, place, x_raw, bc_raw, dt_raw, dy, y, st, taps_x, taps_bc, heads, spread, spread_t)


def place_blocks(pieces, w_ref, sem, row_of):
    for ref, k, first in pieces:
        for r in range(ref.shape[0]):
            for h in range(2):
                row = pl.multiple_of(row_of(k, first + r, h) * 48, 48)
                pltpu.make_async_copy(ref.at[r, h], w_ref.at[pl.ds(row, 48)], sem).start()


def ring_pieces(refs):
    return list(zip(refs, (0, 1, 3, 2, 2), (0, 0, 0, 0, 2)))


def start_halves(refs, buf, sems):
    for k in range(4):
        at = (k % 2) * HALF
        pltpu.make_async_copy(refs[k // 2].at[at : at + HALF], buf.at[k], sems.at[k]).start()


def project_kernel(order_ref, place_ref, *refs):
    a_refs, t_refs = refs[0:5], refs[5:7]
    normed_ref, nt_ref, xr_ref, bc_ref, dt_ref, w_ref, wbc_ref, gain, tok, w_sem, t_sem = refs[7:]
    step = pl.program_id(0)

    @pl.when(step == 0)
    def _():
        z, xh, y = place_ref[0], place_ref[1], place_ref[2]
        start_halves(t_refs, tok, t_sem)

        def row_of(k, r, h):
            return (lax.rem(z - k + 4, 4) * 2 + lax.rem(xh + h, 2)) * 4 + lax.rem(y - r + 4, 4)

        place_blocks(ring_pieces(a_refs), w_ref, w_sem, row_of)
        pltpu.make_async_copy(w_ref, w_ref, w_sem).wait()
        gain[...] = w_ref[:, 1024:1152].astype(F32).T[8:16]
        wbc_ref[...] = w_ref[:, 768:1024]

    pltpu.make_async_copy(t_refs[0].at[0:HALF], tok.at[step], t_sem.at[step]).wait()
    wide = tok[step].astype(F32)
    inv = lax.rsqrt(jnp.mean(wide * wide, axis=-1, keepdims=True) + EPS)
    normed = (wide * inv * gain[4:5]).astype(BF)
    normed_ref[...] = normed
    nt_ref[...] = normed.T
    xr_ref[...] = mm(normed, w_ref[:, 0:768])
    bc_ref[...] = mm(normed, w_ref[:, 768:1024])
    dt_ref[...] = jnp.where(cols((HALF, SUB)) < 12, mm(normed, w_ref[:, 1024:1152]), 0.0)


ANY = pl.BlockSpec(memory_space=pl.ANY)


def by_order(width):
    return pl.BlockSpec((HALF, width), lambda i, order, place: (order[i], 0))


def turned():
    return pl.BlockSpec((1536, HALF), lambda i, order, place: (0, order[i]))


def fixed(shape):
    return pl.BlockSpec(shape, lambda i, *_: (0,) * len(shape))


def project(order, place, parts_in, tokens):
    sd = jax.ShapeDtypeStruct
    return pl.pallas_call(
        project_kernel,
        grid_spec=pltpu.PrefetchScalarGridSpec(
            num_scalar_prefetch=2,
            grid=(4,),
            in_specs=[ANY] * 7,
            out_specs=[by_order(1536), turned(), by_order(768), by_order(256), by_order(128), fixed((1536, 1152)), fixed((1536, 256)), fixed((8, 1536))],
            scratch_shapes=[pltpu.VMEM((4, HALF, 1536), BF), pltpu.SemaphoreType.DMA, pltpu.SemaphoreType.DMA((4,))],
        ),
        out_shape=[sd((1024, 1536), BF), sd((1536, 1024), BF), sd((1024, 768), F32), sd((1024, 256), F32), sd((1024, 128), F32), sd((1536, 1152), BF), sd((1536, 256), BF), sd((8, 1536), F32)],
        compiler_params=pltpu.CompilerParams(vmem_limit_bytes=VMEM_LIMIT),
        cost_estimate=pl.CostEstimate(flops=3_700_000_000, bytes_accessed=22_000_000, transcendentals=0),
    )(order, place, *parts_in, *tokens)


def gate_kernel(order_ref, place_ref, b0, b1, b2, b3, b4, c0, c1, normed_ref, y_ref, gg_ref, gate_ref, gs_ref, cot_ref, s_ref, w_ref, buf, w_sem, t_sem):
    step = pl.program_id(0)

    @pl.when(step == 0)
    def _():
        z, xh, y = place_ref[0], place_ref[1], place_ref[2]
        start_halves((c0, c1), buf, t_sem)

        def row_of(k, r, h):
            return (lax.rem(z - r + 4, 4) * 2 + lax.rem(xh + h, 2)) * 4 + lax.rem(y - k + 4, 4)

        place_blocks(ring_pieces((b0, b1, b2, b3, b4)), w_ref, w_sem, row_of)
        pltpu.make_async_copy(w_ref, w_ref, w_sem).wait()

    pltpu.make_async_copy(c0.at[0:HALF], buf.at[step], t_sem.at[step]).wait()
    cot = buf[step]
    cot_ref[...] = cot.T
    gate = mm(normed_ref[...], w_ref[:, 0:768])
    gs = mm(cot, w_ref[:, 768:1536])
    gate_ref[...] = gate
    gs_ref[...] = gs
    mixed = y_ref[...] * (gate * sigmoid(gate))
    sq = jnp.sum(mixed * mixed, axis=-1, keepdims=True)
    cr = jnp.sum((gs * gg_ref[0:1]) * mixed, axis=-1, keepdims=True)
    lane = cols((HALF, SUB))
    s_ref[...] = jnp.where(lane == 0, sq, jnp.where(lane == 1, cr, 0.0)).T[0:8]


def gate_side(order, place, parts_in, cots, normed, y, gg):
    sd = jax.ShapeDtypeStruct
    return pl.pallas_call(
        gate_kernel,
        grid_spec=pltpu.PrefetchScalarGridSpec(
            num_scalar_prefetch=2,
            grid=(4,),
            in_specs=[ANY] * 7 + [by_order(1536), by_order(768), fixed((8, 768))],
            out_specs=[by_order(768), by_order(768), turned(), pl.BlockSpec((8, HALF), lambda i, order, place: (0, order[i])), fixed((1536, 1536))],
            scratch_shapes=[pltpu.VMEM((4, HALF, 1536), BF), pltpu.SemaphoreType.DMA, pltpu.SemaphoreType.DMA((4,))],
        ),
        out_shape=[sd((1024, 768), F32), sd((1024, 768), F32), sd((1536, 1024), BF), sd((8, 1024), F32), sd((1536, 1536), BF)],
        compiler_params=pltpu.CompilerParams(vmem_limit_bytes=VMEM_LIMIT),
        cost_estimate=pl.CostEstimate(flops=4_900_000_000, bytes_accessed=30_000_000, transcendentals=800_000),
    )(order, place, *parts_in, *cots, normed, y, gg)


def mix_kernel(s0, s1, s2, s3, gate_ref, gs_ref, y_ref, gg_ref, scaled_ref, low_ref, dy_ref, gain_ref):
    sums = ((s0[...] + s1[...]) + (s2[...] + s3[...])).T
    inv = lax.rsqrt(sums[:, 0:1] / 3072 + EPS)
    corr = inv * inv * inv * (sums[:, 1:2] / 3072)
    gate, gs, y, gg = gate_ref[...], gs_ref[...], y_ref[...], gg_ref[0:1]
    sg = sigmoid(gate)
    act = gate * sg
    mixed = y * act
    normal = mixed * inv
    scaled_ref[...] = (normal * gg).astype(BF)
    gm = gs * gg * inv - mixed * corr
    low_ref[...] = (gm * y * (sg * (1.0 + gate * (1.0 - sg)))).astype(BF)
    dy_ref[...] = gm * act

    @pl.when(pl.program_id(0) == 0)
    def _():
        gain_ref[...] = jnp.zeros_like(gain_ref)

    gain_ref[0:1] += jnp.sum(gs * normal, axis=0, keepdims=True)


def mix(sums, gate, gs, y, gg):
    sd = jax.ShapeDtypeStruct
    block = pl.BlockSpec((HALF, 768), lambda i: (i, 0))
    return pl.pallas_call(
        mix_kernel,
        grid=(4,),
        in_specs=[pl.BlockSpec((8, HALF), lambda i: (0, i))] * 4 + [block] * 3 + [whole((8, 768))],
        out_specs=[block] * 3 + [whole((8, 768))],
        out_shape=[sd((1024, 768), BF), sd((1024, 768), BF), sd((1024, 768), F32), sd((8, 768), F32)],
        compiler_params=pltpu.CompilerParams(vmem_limit_bytes=VMEM_LIMIT),
        cost_estimate=pl.CostEstimate(flops=20_000_000, bytes_accessed=16_000_000, transcendentals=800_000),
    )(*sums, gate, gs, y, gg)


def outer_pair_kernel(n_ref, c_ref, g_ref, s_ref, o_ref):
    for at, a_ref, b_ref in ((0, n_ref, g_ref), (768, c_ref, s_ref)):
        r = mm(a_ref[...], b_ref[...]).astype(BF)
        for yi in range(4):
            for xi in range(2):
                row = (xi * 4 + yi) * 48
                o_ref[yi, xi * 48 : xi * 48 + 48, at : at + 768] = r[row : row + 48]


def outer_pair(normed_t, cot_t, gate_low, scaled):
    chunk = pl.BlockSpec((384, 1024), lambda i: (i, 0))
    return pl.pallas_call(
        outer_pair_kernel,
        grid=(4,),
        in_specs=[chunk, chunk, whole((1024, 768)), whole((1024, 768))],
        out_specs=pl.BlockSpec((4, 96, 1536), lambda i: (i, 0, 0)),
        out_shape=jax.ShapeDtypeStruct((16, 96, 1536), BF),
        compiler_params=pltpu.CompilerParams(vmem_limit_bytes=VMEM_LIMIT),
        cost_estimate=pl.CostEstimate(flops=4_900_000_000, bytes_accessed=14_000_000, transcendentals=0),
    )(normed_t, cot_t, gate_low, scaled)


def outer_z_kernel(place_ref, n_ref, g_ref, small_ref, *out):
    step = pl.program_id(0)
    y = place_ref[2]
    r = mm(n_ref[...], g_ref[...]).astype(BF)
    small = small_ref[...].astype(BF)
    for k in range(4):

        @pl.when(step == k)
        def _():
            for yi in range(4):
                to = lax.rem(yi - y + 4, 4)
                for xi in range(2):
                    at = (xi * 4 + yi) * 48
                    out[k][to, xi * 48 : xi * 48 + 48] = r[at : at + 48]
                out[k][to, 96:104] = small


def outer_side_kernel(place_ref, n_ref, g_ref, m_ref, d_ref, small_ref, maps_ref, *out):
    step = pl.program_id(0)
    y, xl = place_ref[2], place_ref[4]

    def columns(maps, steps):
        lane = cols(maps.shape)
        maps = jnp.where(xl == 0, maps, pltpu.roll(maps, 64, 1))
        return jnp.where(lane < 64, maps, pltpu.roll(steps, 64, 1)).astype(BF)

    n = n_ref[...]
    r = [mm(n, g_ref[...]).astype(BF), columns(mm(n, m_ref[...]), mm(n, d_ref[...]))]
    small = [small_ref[...].astype(BF), columns(maps_ref[:, 0:128], maps_ref[:, 128:256])]
    for k in range(4):

        @pl.when(step == k)
        def _():
            for part, lanes in ((0, slice(0, 256)), (1, slice(256, 384))):
                for yi in range(4):
                    to = lax.rem(yi - y + 4, 4)
                    for xi in range(2):
                        at = (xi * 4 + yi) * 48
                        out[k][to, xi * 48 : xi * 48 + 48, lanes] = r[part][at : at + 48]
                    out[k][to, 96:104, lanes] = small[part]


def outer_split(kernel, place, normed_t, grads, smalls, width):
    return pl.pallas_call(
        kernel,
        grid_spec=pltpu.PrefetchScalarGridSpec(
            num_scalar_prefetch=1,
            grid=(4,),
            in_specs=[pl.BlockSpec((384, 1024), lambda i, place: (lax.rem(place[0] + i, 4), 0))] + [spec for _, spec in grads] + [fixed(t.shape) for t in smalls],
            out_specs=[fixed((4, 104, width))] * 4,
        ),
        out_shape=[jax.ShapeDtypeStruct((4, 104, width), BF)] * 4,
        compiler_params=pltpu.CompilerParams(vmem_limit_bytes=VMEM_LIMIT),
        cost_estimate=pl.CostEstimate(flops=2 * 1024 * 1536 * width, bytes_accessed=5_000_000, transcendentals=0),
    )(place, normed_t, *[g for g, _ in grads], *smalls)


def fold_kernel(*refs):
    for parts4, lanes in ((refs[0:4], slice(0, 512)), (refs[4:8], slice(512, 896))):
        for k in range(4):
            near = parts4[1][k].astype(F32) + parts4[3][k].astype(F32)
            refs[8 + k][:, lanes] = ((parts4[0][k].astype(F32) + parts4[2][k].astype(F32)) + near).astype(BF)


def fold(a_parts, b_parts):
    vmem = pl.BlockSpec(memory_space=pltpu.VMEM)
    return pl.pallas_call(
        fold_kernel,
        in_specs=[vmem] * 8,
        out_specs=[vmem] * 4,
        out_shape=[jax.ShapeDtypeStruct((104, 896), BF)] * 4,
        compiler_params=pltpu.CompilerParams(vmem_limit_bytes=VMEM_LIMIT),
        cost_estimate=pl.CostEstimate(flops=1, bytes_accessed=1, transcendentals=0),
    )(*a_parts, *b_parts)


def rows_out(place_ref, total, out):
    for base in range(4):

        @pl.when(place_ref[3] * 2 + place_ref[4] == base)
        def _():
            for ref, at in zip(out, (base, base ^ 2, base ^ 1, base ^ 3)):
                ref[...] = total[at * HALF : at * HALF + HALF].astype(ref.dtype)


def out_kernel(place_ref, s_ref, w_ref, *out):
    rows_out(place_ref, mm_nt(s_ref[...], w_ref[...]), out)


def token_kernel(place_ref, g_ref, x_ref, d_ref, wz_ref, wx_ref, wd_ref, own_ref, mate_ref, send_ref):
    total = mm_nt(g_ref[...], wz_ref[...]) + mm_nt(x_ref[...], wx_ref[...]) + mm_nt(d_ref[...], wd_ref[...])
    rows_out(place_ref, total, [own_ref, send_ref.at[0:HALF], mate_ref, send_ref.at[HALF:SEQ]])


def by_rows(kernel, place, tokens, weights, places, outs):
    columns = lambda at: lambda i, place: (i, at(place))
    return pl.pallas_call(
        kernel,
        grid_spec=pltpu.PrefetchScalarGridSpec(
            num_scalar_prefetch=1,
            grid=(6,),
            in_specs=[fixed(t.shape) for t in tokens] + [pl.BlockSpec((256, t.shape[1]), columns(at)) for t, at in zip(tokens, places)],
            out_specs=[pl.BlockSpec((n, 256), lambda i, place: (0, i)) for n, _ in outs],
        ),
        out_shape=[jax.ShapeDtypeStruct((n, 1536), t) for n, t in outs],
        compiler_params=pltpu.CompilerParams(vmem_limit_bytes=VMEM_LIMIT),
        cost_estimate=pl.CostEstimate(flops=1, bytes_accessed=1, transcendentals=0),
    )(place, *tokens, *weights)


def sum_pieces_kernel(place_ref, p0, p1, p2, p3, zo_ref, keep_ref, send_ref):
    total = (p0[...].astype(F32) + p2[...].astype(F32)) + (p1[...].astype(F32) + p3[...].astype(F32))
    small = total[96:104].astype(BF)
    send_ref[48:56, 0:896] = small
    keep_ref[48:56, 0:896] = small.astype(F32)
    for xh in (0, 1):

        @pl.when(place_ref[1] == xh)
        def _():
            keep_ref[0:48, 0:896] = total[xh * 48 : xh * 48 + 48]
            send_ref[0:48, 0:896] = total[48 - xh * 48 : 96 - xh * 48].astype(BF)

    for xh in (0, 1):

        @pl.when(place_ref[1] == xh)
        def _():
            keep_ref[0:48, 896:2432] = zo_ref[xh * 48 : xh * 48 + 48].astype(F32)
            send_ref[0:48, 896:2432] = zo_ref[48 - xh * 48 : 96 - xh * 48]

    keep_ref[48:56, 896:2432] = jnp.zeros((8, 1536), F32)
    send_ref[48:56, 896:2432] = jnp.zeros((8, 1536), BF)


def sum_far_kernel(place_ref, own_ref, far_ref, keep_ref, send_ref):
    total = own_ref[...] + far_ref[...].astype(F32)
    keep_ref[24:32] = total[48:56]
    send_ref[24:32] = total[48:56]
    for core in (0, 1):

        @pl.when(place_ref[3] == core)
        def _():
            keep_ref[0:24] = total[core * 24 : core * 24 + 24]
            send_ref[0:24] = total[24 - core * 24 : 48 - core * 24]


def whole_call(kernel, place, arrays, shapes):
    vmem = pl.BlockSpec(memory_space=pltpu.VMEM)
    return pl.pallas_call(
        kernel,
        in_specs=[SMEM] + [vmem] * len(arrays),
        out_specs=[vmem] * len(shapes),
        out_shape=shapes,
        compiler_params=pltpu.CompilerParams(vmem_limit_bytes=VMEM_LIMIT),
        cost_estimate=pl.CostEstimate(flops=1, bytes_accessed=1, transcendentals=0),
    )(place, *arrays)


def sum_pieces(place, pieces, zo):
    shapes = [jax.ShapeDtypeStruct((56, 2432), F32), jax.ShapeDtypeStruct((56, 2432), BF)]
    return whole_call(sum_pieces_kernel, place, [*pieces, zo], shapes)


def sum_far(place, own, far):
    return whole_call(sum_far_kernel, place, [own, far], [jax.ShapeDtypeStruct((32, 2432), F32)] * 2)


def after_kernel(x_ref, *refs):
    pass


def after(x, *deps):
    return pl.pallas_call(
        after_kernel,
        in_specs=[ANY] * (1 + len(deps)),
        out_specs=ANY,
        out_shape=jax.ShapeDtypeStruct(x.shape, x.dtype),
        input_output_aliases={0: 0},
    )(x, *deps)


def swap(a, axis):
    return lax.ppermute(a, axis, [(0, 1), (1, 0)])


def turn(a, axis, k):
    return lax.ppermute(a, axis, [(i, (i + k) % 4) for i in range(4)])


def pair(own, other, axis):
    first = lax.axis_index(axis) == 0
    return jnp.stack([jnp.where(first, own, other), jnp.where(first, other, own)])


def mine(a, axis, dim, size):
    i = lax.axis_index(axis)
    return (
        lax.dynamic_slice_in_dim(a, i * size, size, dim),
        lax.dynamic_slice_in_dim(a, (1 - i) * size, size, dim),
    )


def turns(a, axis):
    return [a] + [turn(a, axis, k) for k in (1, 2, 3)]


def shards(resid, cotangent, segments, pre_gain, w_z, w_x, w_bc, w_dt, conv_x, conv_x_bias, conv_bc, conv_bc_bias, dt_bias, a_log, d_skip, gate_gain, w_out):
    core, xl = lax.axis_index("c"), lax.axis_index("xl")
    place = jnp.stack([lax.axis_index("z"), lax.axis_index("xh"), lax.axis_index("y"), core, xl])
    base = core * 2 + xl
    order = jnp.stack([core * 2, core * 2 + 1, 2 - core * 2, 3 - core * 2])

    own_bc = jnp.concatenate([w_bc, pre_gain[:, None], jnp.zeros((12, 127), BF)], axis=1)
    keep_x, send_x = mine(w_x, "c", 1, 768)
    keep_dt, send_dt = mine(w_dt, "c", 1, 12)
    bc_x, bc_c = swap(own_bc, "xl"), swap(own_bc, "c")
    bc_d = lax.ppermute(own_bc, ("c", "xl"), [(i, 3 - i) for i in range(4)])
    got = swap(jnp.concatenate([send_x, send_dt], axis=1), "c")
    bc48 = pair(pair(own_bc, bc_x, "xl"), pair(bc_c, bc_d, "xl"), "c").reshape(48, 384)
    xdt = pair(jnp.concatenate([keep_x, keep_dt], axis=1), got, "c").reshape(48, 780)
    first = jnp.concatenate([xdt[:, :768], bc48[:, :256], xdt[:, 768:], bc48[:, 256:372]], axis=1)
    first_far = swap(first, "xh")
    first = jnp.stack([first, first_far])

    keep_z, send_z = mine(w_z, "c", 1, 768)
    keep_o, send_o = mine(w_out.T, "c", 1, 768)
    got = swap(jnp.concatenate([send_z, send_o], axis=1), "c")
    second = pair(jnp.concatenate([keep_z, keep_o], axis=1), got, "c").reshape(48, 1536)
    second = jnp.stack([second, swap(second, "xh")])

    near_x, near = turns(first, "y"), turns(second, "z")
    b_own = jnp.stack(near)
    b_ahead, b_back = turn(b_own, "y", 1), turn(b_own, "y", 3)
    a_own = after(jnp.stack(near_x), *near[1:])
    a_ahead, a_back = turn(a_own, "z", 1), turn(a_own, "z", 3)
    b_low, b_high = b_ahead[:2], b_back[2:]
    a_parts = [a_own, a_ahead, a_back, turn(after(a_ahead[:2], b_low, b_high), "z", 1), turn(after(a_back[2:], b_low, b_high), "z", 3)]
    b_parts = [b_own, b_ahead, b_back, turn(b_low, "y", 1), turn(b_high, "y", 3)]

    def halves(a, *deps):
        half = after(lax.all_gather(a, "xl", axis=0, tiled=True), *deps)
        return [half, swap(half, "c")]

    tokens = halves(resid, a_parts[1], a_parts[2])
    cots = halves(cotangent, a_parts[3], a_parts[4])
    cut = jnp.sum((segments == segments[0]).astype(jnp.int32))[None]
    cuts = pair(cut, swap(cut, "c"), "c").reshape(2)

    normed, normed_t, x_raw, bc_raw, dt_raw, w_1, w_maps, gain_rows = project(order, place, a_parts, tokens)

    def own(a, size):
        return mine(a, "c", a.ndim - 1, size)[0]

    cx, cxb, gg = own(conv_x, 768), own(conv_x_bias, 768), own(gate_gain, 768)
    dtb, al, dsk = own(dt_bias, 12), own(a_log, 12), own(d_skip, 12)
    taps_x = jnp.concatenate([cx, cxb[None], jnp.repeat(dsk, 64)[None], jnp.zeros((2, 768), F32)], axis=0)
    taps_bc = jnp.concatenate([conv_bc, conv_bc_bias[None], jnp.zeros((3, 256), F32)], axis=0)
    wide_heads = lambda v: jnp.pad(v, (0, 116))[None]
    heads = jnp.concatenate([wide_heads(dtb), wide_heads(-jnp.exp(al)), wide_heads(dsk), jnp.zeros((5, 128), F32)], axis=0)
    gains = jnp.broadcast_to(gg[None], (8, 768))
    spread_np = np.arange(768)[None, :] // 64 == np.arange(128)[:, None]
    spread, spread_t = jnp.asarray(spread_np, BF), jnp.asarray(spread_np.T, BF)
    y, st = ssd_forward(cuts, x_raw, bc_raw, dt_raw, taps_x, taps_bc, heads, spread)

    gate, gs, cot_t, sums, w_2 = gate_side(order, place, b_parts, cots, normed, y, gains)
    sums_c, sums_x = swap(sums, "c"), swap(sums, "xl")
    sums_d = lax.ppermute(sums, ("c", "xl"), [(i, 3 - i) for i in range(4)])
    scaled, gate_low, dy, g_gain = mix([sums, sums_c, sums_x, sums_d], gate, gs, y, gains)

    def exchange(rows):
        diagonal = lax.ppermute(rows[3], ("c", "xl"), [(i, 3 - i) for i in range(4)])
        return rows[0], swap(rows[1], "c"), swap(rows[2], "xl"), diagonal

    out_rows = by_rows(out_kernel, place, [scaled], [w_2], [lambda place: 1], [(HALF, F32)] + [(HALF, BF)] * 3)
    g_zo = outer_pair(normed_t, after(cot_t, out_rows[1]), gate_low, scaled)
    g_zo_z = lax.psum_scatter(g_zo.reshape(1536, 1536), "z", scatter_dimension=0, tiled=True)
    g_zo_y = lax.psum_scatter(g_zo_z, "y", scatter_dimension=0, tiled=True)
    out_rows = exchange(out_rows)
    wide = lambda a: a.astype(F32)
    layer_out = (wide(resid) + ((out_rows[0] + wide(out_rows[1])) + (wide(out_rows[2]) + wide(out_rows[3])))).astype(BF)

    dy = after(dy, g_zo)
    x_low, keep, send, gdt, g_tx, keep_c, send_c, g_hd = ssd_backward(cuts, place, x_raw, bc_raw, dt_raw, dy, y, st, taps_x, taps_bc, heads, spread, spread_t)

    keep, keep_c = keep + swap(after(send, *out_rows[1:]), "c"), keep_c + swap(send_c, "c")
    keep_h = keep_c.astype(BF)
    keep = jnp.concatenate([keep.astype(BF), keep_h, (keep_c - keep_h.astype(F32)).astype(BF)], axis=0)
    small_x = jnp.concatenate([g_tx[:5], g_gain[:1], jnp.zeros((2, 768), F32)], axis=0)
    left = pl.BlockSpec((1024, 512), lambda i, place: (0, 0))
    right = pl.BlockSpec((1024, 256), lambda i, place: (0, 2))
    a_grad = outer_split(outer_z_kernel, place, normed_t, [(x_low, left)], [small_x[:, :512]], 512)
    a_grad = [a_grad[0]] + [turn(a_grad[k], "z", k) for k in (1, 2, 3)]
    far = swap(keep, "xl")
    group = keep.astype(F32) + far.astype(F32)
    bc_low = group[:1024].astype(BF)
    small_s = jnp.concatenate([group[1024:1032] + group[1032:], g_hd], axis=1)
    full = lambda t: (t, fixed(t.shape))
    b_grad = outer_split(outer_side_kernel, place, normed_t, [(x_low, right), full(bc_low), full(gdt)], [small_x[:, 512:], small_s], 384)
    b_first = b_grad[0]
    b_grad = [b_first] + [turn(b_grad[k], "z", k) for k in (1, 2, 3)]
    token_rows = by_rows(token_kernel, place, [after(gate_low, b_first, g_zo_z), x_low, gdt], [w_2, w_1, w_1], [lambda place: 0, lambda place: 0, lambda place: 8], [(HALF, F32), (HALF, F32), (SEQ, BF)])
    token_far = swap(after(token_rows[2], *a_grad[1:], *b_grad[1:]), "c")
    pieces = fold(a_grad, b_grad)
    token_far = after(token_far, pieces[1])
    grad_own = token_rows[0] + wide(token_far[:HALF])
    grad_far = swap((token_rows[1] + wide(token_far[HALF:])).astype(BF), "xl")
    pieces = [pieces[0]] + [turn(pieces[k], "y", k) for k in (1, 2, 3)]

    rows_own, rows_send = mine(bc_low, "c", 0, SEQ)
    bc_own = pair(rows_own, swap(rows_send, "c"), "c")
    bc_own = jnp.concatenate([bc_own[0], bc_own[1]], axis=1)
    bc_own = lax.dynamic_slice_in_dim(bc_own, xl * 256, 256, 0)
    bc_part = lax.dot_general(bc_own, w_maps, (((1,), (1,)), ((), ())), preferred_element_type=F32)
    grad_normed = (grad_own + wide(grad_far)) + bc_part

    keep, send = sum_pieces(place, pieces, g_zo_y)
    keep, send = sum_far(place, after(keep, grad_far), swap(send, "xh"))
    far = swap(send, "c")

    gain_wide = gain_rows[4]
    rw = resid.astype(F32)
    inv = lax.rsqrt(jnp.mean(rw * rw, axis=-1, keepdims=True) + EPS)
    inner = jnp.sum(gain_wide[None, :] * grad_normed * rw, axis=-1, keepdims=True)
    grad_resid = cotangent.astype(F32) + gain_wide[None, :] * grad_normed * inv - rw * (inv * inv * inv) * inner / 1536

    got = pair(keep, far, "c")
    both = lambda rows, at, width: jnp.concatenate([got[0, rows, at : at + width], got[1, rows, at : at + width]], axis=1)
    main, rest = slice(0, 24), slice(24, 32)
    grad_w_x, grad_w_z, grad_w_out_t = both(main, 0, 768), both(main, 896, 768), both(main, 1664, 768)
    grad_w_dt = both(main, 832, 12)
    bc24, conv24 = both(main, 768, 64), both(rest, 768, 64)
    small_wide = both(rest, 0, 768)
    small_heads = both(rest, 832, 12)

    tall = lambda a, b: jnp.sum(a.astype(F32) * b, axis=1)
    pg = tall(w_z, grad_w_z) + tall(w_x, grad_w_x) + tall(w_dt, grad_w_dt)
    pg, pg_send = mine(pg, "xl", 0, 12)
    bc12, bc_send = mine(bc24, "xl", 0, 12)
    far = swap(jnp.concatenate([bc_send, conv24, jnp.pad(pg_send, (0, 116))[None]], axis=0), "xl")
    got = pair(jnp.concatenate([bc12, conv24], axis=0), far[:20], "xl")
    got = got.reshape(2, 20, 2, 64).transpose(1, 2, 0, 3).reshape(20, 256)
    grad_w_bc, grad_conv_bc = got[:12], got[12:]
    grad_pre_gain = (pg + far[20, :12] + tall(w_bc, grad_w_bc)) / pre_gain.astype(F32)
    return (
        layer_out,
        grad_resid,
        grad_pre_gain,
        grad_w_z,
        grad_w_x,
        grad_w_bc,
        grad_w_dt,
        small_wide[:4],
        small_wide[4],
        grad_conv_bc[:4],
        grad_conv_bc[4],
        small_heads[0],
        small_heads[1],
        small_heads[2],
        small_wide[5],
        grad_w_out_t.T,
    )


def solution(mesh):
    fine = Mesh(mesh.devices.reshape(4, 2, 4, 2, 2), ("z", "xh", "y", "c", "xl"))
    dp, tp, every = ("z", "xh", "y", "c"), "xl", ("z", "xh", "y", "c", "xl")
    return jax.shard_map(
        shards,
        mesh=fine,
        in_specs=(P(every, None), P(every, None), P(dp), P(every), P(dp, tp), P(dp, tp), P(every, None), P(dp, tp), P(None, tp), P(tp), P(), P(), P(tp), P(tp), P(tp), P(tp), P(tp, dp)),
        out_specs=(P(every, None), P(every, None), P(every), P(dp, tp), P(dp, tp), P(every, None), P(dp, tp), P(None, tp), P(tp), P(), P(), P(tp), P(tp), P(tp), P(tp), P(tp, dp)),
        check_vma=False,
    )
```

```python
import jax
import jax.numpy as jnp
import numpy as np
from jax import lax
from jax.experimental import pallas as pl
from jax.experimental.pallas import tpu as pltpu
from jax.sharding import Mesh, PartitionSpec as P

EPS = 1e-05
VMEM_LIMIT = 60 * 1024 * 1024
BF = jnp.bfloat16
F32 = jnp.float32
SEQ = 512
HALF = 256
SUB = 128
PAIRS = 2


def mm(a, b):
    return jnp.dot(a, b, preferred_element_type=F32)


def mm_nt(a, b):
    return lax.dot_general(a, b, (((1,), (1,)), ((), ())), preferred_element_type=F32)


def mm_tn(a, b):
    return lax.dot_general(a, b, (((0,), (0,)), ((), ())), preferred_element_type=F32)


def parts(v, count):
    out = []
    for _ in range(count):
        low = v.astype(BF)
        out.append(low)
        v = v - low.astype(F32)
    return out


def split_left(v, m, count=2):
    return sum(mm(p, m) for p in parts(v, count))


def split_right(m, v, count=3):
    return sum(mm(m, p) for p in parts(v, count))


def rows(shape):
    return lax.broadcasted_iota(jnp.int32, shape, 0)


def cols(shape):
    return lax.broadcasted_iota(jnp.int32, shape, 1)


def softplus(v):
    e = jnp.exp(-jnp.abs(v))
    tail = jnp.where(e < 1e-3, e * (1.0 - 0.5 * e), jnp.log(1.0 + e))
    return jnp.maximum(v, 0.0) + tail


def sigmoid(v):
    return 1.0 / (1.0 + jnp.exp(-v))


def same_doc(t, s, cut):
    return (t < cut) == (s < cut)


def conv_masks(cut):
    t = rows((SEQ, SUB))
    return [jnp.where((t >= j) & ((t < cut) | (t - j >= cut)), 1.0, 0.0) for j in (1, 2, 3)]


def conv(v, taps, masks):
    u = taps[4:5] + taps[3:4] * v
    for j in (1, 2, 3):
        u = u + taps[3 - j : 4 - j] * (pltpu.roll(v, j, 0) * masks[j - 1])
    return u


def time_steps(dt_raw, heads, cut):
    dt = softplus(dt_raw + heads[0:1])
    a = dt * heads[1:2]
    tri = jnp.where(rows((HALF, HALF)) >= cols((HALF, HALF)), 1.0, 0.0).astype(BF)
    c = [split_right(tri, a[:HALF]), split_right(tri, a[HALF:])]
    t = rows((HALF, SUB))
    ending = same_doc(t, HALF - 1, cut)
    alive = same_doc(t + HALF, HALF - 1, cut)
    ew = jnp.where(ending, jnp.exp(c[0][HALF - 1 : HALF] - c[0]), 0.0)
    e1 = jnp.where(alive, jnp.exp(c[1]), 0.0)
    return dt, c, ew, e1


def masked_scores(cb, bb, block, cut, lower=True):
    out = {}
    for i, j in ((0, 0), (1, 0), (1, 1)):
        ti, sj = slice(i * SUB, i * SUB + SUB), slice(j * SUB, j * SUB + SUB)
        if lower:
            s = mm_nt(cb[ti], bb[sj])
            t = rows((SUB, SUB)) + (block * HALF + i * SUB)
            r = cols((SUB, SUB)) + (block * HALF + j * SUB)
        else:
            s = mm_nt(bb[sj], cb[ti])
            r = rows((SUB, SUB)) + (block * HALF + j * SUB)
            t = cols((SUB, SUB)) + (block * HALF + i * SUB)
        out[i, j] = jnp.where((t >= r) & same_doc(t, r, cut), s, 0.0)
    return out


def head_lanes(k):
    lane = cols((HALF, SUB))
    return (lane < 64) if k == 0 else (lane >= 64)


def fill_columns(c, ccol_ref, ct_ref):
    for k in (0, 1):
        ct_ref[k] = c[k].T
        for head in range(12):
            ccol_ref[k, head] = jnp.broadcast_to(c[k][:, head : head + 1], (HALF, SUB))


def put_stack(ref, values):
    at = 0
    for v in values:
        for p in parts(v, 2):
            ref[at : at + v.shape[0]] = p
            at += v.shape[0]


def spread_stack(ref, e, heights):
    wide, out, at = mm(ref[...], e), [], 0
    for n in heights:
        out.append(wide[at : at + n] + wide[at + n : at + 2 * n])
        at += 2 * n
    return out


BLOCKS = ((0, 0), (1, 0), (1, 1))


def fwd_kernel(cut_ref, xr_ref, bcr_ref, dtr_ref, tx_ref, tbc_ref, hd_ref, e_ref, y_ref, st_ref):
    cut = cut_ref[pl.program_id(0)]
    masks = conv_masks(cut)
    act = []
    for i in range(2):
        sl = slice(i * SUB, i * SUB + SUB)
        u = conv(bcr_ref[:, sl], tbc_ref[:, sl], masks)
        act.append(parts(u * sigmoid(u), 2))
    (bb, bb_low), (cb, cb_low) = act
    cb3 = jnp.concatenate([cb, cb_low, cb], axis=1)
    bb3 = jnp.concatenate([bb, bb, bb_low], axis=1)
    dt, c, ew, e1 = time_steps(dtr_ref[...], hd_ref[...], cut)
    ct = [c[0].T, c[1].T]
    tw = ew * dt[:HALF]
    scores = [masked_scores(cb3[k * HALF : k * HALF + HALF], bb3[k * HALF : k * HALF + HALF], k, cut) for k in (0, 1)]
    b0t, b0t_low = bb[:HALF].T, bb_low[:HALF].T
    for p in range(6):
        sl = slice(p * SUB, p * SUB + SUB)
        e = e_ref[:, sl]
        u = conv(xr_ref[:, sl], tx_ref[:, sl], masks)
        x = u * sigmoid(u)
        xtf = x * split_left(dt, e)
        xh = xtf.astype(BF)
        xhf = xh.astype(F32)
        xl_turned = pltpu.roll(xtf - xhf, 64, 1).astype(BF)
        skip = tx_ref[5:6, sl] * x
        xw, xw_low = parts(x[:HALF] * split_left(tw, e), 2)
        st = mm(b0t, xw) + (mm(b0t, xw_low) + mm(b0t_low, xw))
        st_ref[0, :, sl] = st
        st, st_low = parts(st, 2)
        carry = (mm(cb[HALF:], st) + (mm(cb[HALF:], st_low) + mm(cb_low[HALF:], st))) * split_left(e1, e)
        for k in (0, 1):
            ys = [[], []]
            for h in (0, 1):
                head = 2 * p + h
                at = slice(k * HALF, k * HALF + HALF)
                xm = jnp.where(head_lanes(h), xh[at], xl_turned[at])
                col = c[k][:, head : head + 1]
                row = ct[k][head : head + 1, :]
                m = {}
                for i, j in ((0, 0), (1, 0), (1, 1)):
                    gap = col[i * SUB : i * SUB + SUB] - row[:, j * SUB : j * SUB + SUB]
                    full = jnp.exp(jnp.minimum(gap, 0.0)) * scores[k][i, j]
                    m[i, j] = parts(full, 2)
                ys[0].append(mm(jnp.concatenate(m[0, 0], axis=1), jnp.concatenate([xm[:SUB], xm[:SUB]], axis=0)))
                wide = [m[1, 0][0], m[1, 1][0], m[1, 0][1], m[1, 1][1]]
                ys[1].append(mm(jnp.concatenate(wide, axis=1), jnp.concatenate([xm, xm], axis=0)))
            for i in (0, 1):
                at = k * HALF + i * SUB
                first = cols((SUB, SUB)) < 64
                y0, y1 = ys[i]
                y = jnp.where(first, y0, y1) + pltpu.roll(jnp.where(first, y1, y0), 64, 1) + skip[at : at + SUB]
                if k == 1:
                    y = y + carry[i * SUB : i * SUB + SUB]
                y_ref[at : at + SUB, sl] = y


def seq_spec(width):
    return pl.BlockSpec((SEQ, width), lambda i: (i, 0))


def whole(shape):
    return pl.BlockSpec(shape, lambda i: (0,) * len(shape))


SMEM = pl.BlockSpec(memory_space=pltpu.SMEM)


def ssd_forward(cut, x_raw, bc_raw, dt_raw, taps_x, taps_bc, heads, spread):
    return pl.pallas_call(
        fwd_kernel,
        grid=(2,),
        in_specs=[SMEM, seq_spec(768), seq_spec(256), seq_spec(128), whole((8, 768)), whole((8, 256)), whole((8, 128)), whole((128, 768))],
        out_specs=[seq_spec(768), pl.BlockSpec((1, 128, 768), lambda i: (i, 0, 0))],
        out_shape=[jax.ShapeDtypeStruct((1024, 768), F32), jax.ShapeDtypeStruct((2, 128, 768), F32)],
        compiler_params=pltpu.CompilerParams(vmem_limit_bytes=VMEM_LIMIT),
        cost_estimate=pl.CostEstimate(flops=4_000_000_000, bytes_accessed=9_000_000, transcendentals=4_000_000),
    )(cut, x_raw, bc_raw, dt_raw, taps_x, taps_bc, heads, spread)


def bwd_kernel(cut_ref, place_ref, xr_ref, bcr_ref, dtr_ref, dy_ref, y_ref, st_ref, tx_ref, tbc_ref, hd_ref, e_ref, et_ref,
               gx_ref, keep_ref, send_ref, gdt_ref, gtx_ref, keepc_ref, sendc_ref, ghd_ref,
               ds_ref, masks_ref, steps_ref, up_ref, ccol_ref, ct_ref, c1t_ref, b0_ref, acc_ref, accb_ref, skip_ref):
    seq = pl.program_id(0)
    cut = cut_ref[seq]
    masks = conv_masks(cut)

    def conv_back(du, v, taps, masks):
        g = taps[3:4] * du
        sums = [jnp.sum(du * v, axis=0, keepdims=True)]
        for j in (1, 2, 3):
            dm = du * masks[j - 1]
            g = g + taps[3 - j : 4 - j] * pltpu.roll(dm, SEQ - j, 0)
            sums.append(jnp.sum(dm * pltpu.roll(v, j, 0), axis=0, keepdims=True))
        return g, [sums[3], sums[2], sums[1], sums[0], jnp.sum(du, axis=0, keepdims=True)]

    @pl.when(seq == 0)
    def _():
        gtx_ref[...] = jnp.zeros_like(gtx_ref)
        keepc_ref[...] = jnp.zeros_like(keepc_ref)
        sendc_ref[...] = jnp.zeros_like(sendc_ref)
        ghd_ref[...] = jnp.zeros_like(ghd_ref)

    act = []
    for i in range(2):
        sl = slice(i * SUB, i * SUB + SUB)
        u = conv(bcr_ref[:, sl], tbc_ref[:, sl], masks)
        act.append((u * sigmoid(u)).astype(BF))
    for j in range(3):
        masks_ref[j] = masks[j]
    bb, cb = act
    dt, c, ew, e1 = time_steps(dtr_ref[...], hd_ref[...], cut)
    fill_columns(c, ccol_ref, ct_ref)
    put_stack(steps_ref, [dt, ew * dt[:HALF], e1, ew])
    blk = lambda a, k: a[k * HALF : k * HALF + HALF]
    for k in (0, 1):
        up = masked_scores(blk(cb, k), blk(bb, k), k, cut, lower=False)
        for n, at in enumerate(BLOCKS):
            up_ref[k, n] = up[at]
    c1t_ref[...] = cb[HALF:].T
    b0_ref[...] = bb[:HALF]
    ds_ref[...] = jnp.zeros_like(ds_ref)
    acc_ref[...] = jnp.zeros_like(acc_ref)
    accb_ref[...] = jnp.zeros_like(accb_ref)
    skip_ref[...] = jnp.zeros_like(skip_ref)

    def one_pair(p, carried):
        sl = pl.ds(pl.multiple_of(p * SUB, SUB), SUB)
        e, et, taps = e_ref[:, sl], et_ref[sl, :], tx_ref[:, sl]
        xr = xr_ref[:, sl]
        pair_masks = [masks_ref[j] for j in range(3)]
        u = conv(xr, taps, pair_masks)
        sg = sigmoid(u)
        x = u * sg
        dtx, twx, e1x, ewx = spread_stack(steps_ref, e, (SEQ, HALF, HALF, HALF))
        xtf = x * dtx
        xt = xtf.astype(BF)
        dy = dy_ref[:, sl]
        dyb = dy.astype(BF)
        dyh = dyb.astype(F32)
        xh = xt.astype(F32)
        xl = (xtf - xh).astype(BF)
        dl_turned = pltpu.roll(dy - dyh, 64, 1).astype(BF)
        xh_turned = pltpu.roll(xh, 64, 1).astype(BF)
        skip = jnp.broadcast_to(jnp.sum(dy * x, axis=0, keepdims=True), (16, SUB))
        stack = parts(dyh * y_ref[:, sl], 2) + parts(dyh * x, 2) + parts(skip, 3)
        wide = mm(jnp.concatenate(stack, axis=0), et)
        acc_ref[0] += wide[0:SEQ] + wide[SEQ : 2 * SEQ]
        acc_ref[1] += wide[2 * SEQ : 3 * SEQ] + wide[3 * SEQ : 4 * SEQ]
        skip_ref[...] += wide[2048:2056] + wide[2064:2072] + wide[2080:2088]
        dxs = []
        for k in (0, 1):
            back = 0.0
            for h in (0, 1):
                head = 2 * p + h
                lanes, none = head_lanes(h), jnp.zeros((), BF)
                dm = jnp.where(lanes, blk(dyb, k), none)
                dm2 = jnp.concatenate([jnp.where(lanes, blk(dyb, k), blk(dl_turned, k)), dm], axis=1)
                xm2 = jnp.concatenate([jnp.where(lanes, blk(xt, k), blk(xh_turned, k)), jnp.where(lanes, blk(xl, k), none)], axis=1)
                row = ct_ref[k, pl.ds(head, 1), :]
                gfull = mm_nt(dm2, xm2)
                mt = {}
                for n, (i, j) in enumerate(BLOCKS):
                    ti, sj = slice(i * SUB, i * SUB + SUB), slice(j * SUB, j * SUB + SUB)
                    decay = jnp.exp(-jnp.abs(ccol_ref[k, head, ti, :] - row[:, sj]))
                    if i == j:
                        decay_t = decay
                    else:
                        decay_t = jnp.exp(-jnp.abs(ccol_ref[k, head, sj, :] - row[:, ti]))
                    ds_ref[k, i + j] += gfull[ti, sj] * decay
                    mt[i, j] = (decay_t * up_ref[k, n]).astype(BF)
                rows0 = jnp.concatenate([mt[0, 0], mt[1, 0]], axis=1)
                rows1 = jnp.concatenate([jnp.zeros((SUB, SUB), BF), mt[1, 1]], axis=1)
                back = back + mm(jnp.concatenate([rows0, rows1], axis=0), dm)
            dxs.append(back)
        st, st_low = parts(st_ref[0, :, sl], 2)
        dcs, dcs_low = parts(dy[HALF:] * e1x, 2)
        accb_ref[0] += mm_nt(dcs, st) + (mm_nt(dcs_low, st) + mm_nt(dcs, st_low))
        dst, dst_low = parts(mm(c1t_ref[...], dcs) + mm(c1t_ref[...], dcs_low), 2)
        dxw = mm(b0_ref[...], dst)
        xw, xw_low = parts(x[:HALF] * twx, 2)
        accb_ref[1] += mm_nt(xw, dst) + (mm_nt(xw_low, dst) + mm_nt(xw, dst_low))
        dx0 = dxs[0] + dxw * ewx
        dxt = jnp.concatenate([dx0, dxs[1]], axis=0)
        wide = mm(jnp.concatenate(parts(x * dxt, 2), axis=0), et)
        acc_ref[2] += wide[:SEQ] + wide[SEQ:]
        dx = dtx * dxt + taps[5:6] * dy
        du = dx * (sg * (1.0 + u * (1.0 - sg)))
        g, sums = conv_back(du, xr, taps, pair_masks)
        gx_ref[:, sl] = g.astype(BF)
        gtx_ref[0:5, sl] += jnp.concatenate(sums, axis=0)
        return carried

    lax.fori_loop(0, 6 // PAIRS, lambda i, x: [one_pair(i * PAIRS + j, x) for j in range(PAIRS)][0], 0)
    sum_y, sum_x, sum_d = acc_ref[0], acc_ref[1], acc_ref[2]
    d_c1, d_b0 = accb_ref[0], accb_ref[1]
    d_b, d_c = [], []
    for k in (0, 1):
        bk, ck = blk(bb, k), blk(cb, k)
        m = {}
        for i, j in ((0, 0), (1, 0), (1, 1)):
            t = rows((SUB, SUB)) + (k * HALF + i * SUB)
            r = cols((SUB, SUB)) + (k * HALF + j * SUB)
            m[i, j] = jnp.where((t >= r) & same_doc(t, r, cut), ds_ref[k, i + j], 0.0).astype(BF)
        lowr = jnp.concatenate([m[1, 0], m[1, 1]], axis=1)
        d_c += [mm(m[0, 0], bk[:SUB]), mm(lowr, bk)]
        d_b += [mm_tn(m[0, 0], ck[:SUB]) + mm_tn(m[1, 0], ck[SUB:]), mm_tn(m[1, 1], ck[SUB:])]
    d_b = jnp.concatenate([jnp.concatenate(d_b[:2], axis=0) + d_b0] + d_b[2:], axis=0)
    d_c = jnp.concatenate(d_c[:2] + [jnp.concatenate(d_c[2:], axis=0) + d_c1], axis=0)
    for i, d in ((0, d_b), (1, d_c)):
        sl = slice(i * SUB, i * SUB + SUB)
        v = bcr_ref[:, sl]
        u = conv(v, tbc_ref[:, sl], masks)
        sg = sigmoid(u)
        g, sums = conv_back(d * (sg * (1.0 + u * (1.0 - sg))), v, tbc_ref[:, sl], masks)

        @pl.when(place_ref[3] == i)
        def _():
            keep_ref[...] = g
            for r, s in enumerate(sums):
                keepc_ref[r : r + 1] += s

        @pl.when(place_ref[3] != i)
        def _():
            send_ref[...] = g
            for r, s in enumerate(sums):
                sendc_ref[r : r + 1] += s

    hd = hd_ref[...]
    w = (sum_y - hd[2:3] * sum_x) - dt * sum_d
    tri = jnp.where((cols((SEQ, SEQ)) >= rows((SEQ, SEQ))) & same_doc(rows((SEQ, SEQ)), cols((SEQ, SEQ)), cut), 1.0, 0.0).astype(BF)
    run = split_right(tri, w)
    d_dt = sum_d + hd[1:2] * run
    gd = d_dt * sigmoid(dtr_ref[...] + hd[0:1])
    gdt_ref[...] = gd.astype(BF)
    ghd_ref[0:1] += jnp.sum(gd, axis=0, keepdims=True)
    ghd_ref[2:3] += skip_ref[0:1]
    ghd_ref[1:2] += jnp.sum(dt * run, axis=0, keepdims=True) * hd[1:2]


def ssd_backward(cut, place, x_raw, bc_raw, dt_raw, dy, y, st, taps_x, taps_bc, heads, spread, spread_t):
    return pl.pallas_call(
        bwd_kernel,
        grid=(2,),
        in_specs=[SMEM, SMEM, seq_spec(768), seq_spec(256), seq_spec(128), seq_spec(768), seq_spec(768),
                  pl.BlockSpec((1, 128, 768), lambda i: (i, 0, 0)), whole((8, 768)), whole((8, 256)), whole((8, 128)), whole((128, 768)), whole((768, 128))],
        out_specs=[seq_spec(768), seq_spec(128), seq_spec(128), seq_spec(128), whole((8, 768)), whole((8, 128)), whole((8, 128)), whole((8, 128))],
        out_shape=[jax.ShapeDtypeStruct((1024, 768), BF), jax.ShapeDtypeStruct((1024, 128), F32), jax.ShapeDtypeStruct((1024, 128), F32), jax.ShapeDtypeStruct((1024, 128), BF),
                   jax.ShapeDtypeStruct((8, 768), F32), jax.ShapeDtypeStruct((8, 128), F32), jax.ShapeDtypeStruct((8, 128), F32), jax.ShapeDtypeStruct((8, 128), F32)],
        scratch_shapes=[
            pltpu.VMEM((2, 3, SUB, SUB), F32),
            pltpu.VMEM((3, SEQ, SUB), F32),
            pltpu.VMEM((5 * SEQ, SUB), BF),
            pltpu.VMEM((2, 3, SUB, SUB), F32),
            pltpu.VMEM((2, 12, HALF, SUB), F32),
            pltpu.VMEM((2, SUB, HALF), F32),
            pltpu.VMEM((SUB, HALF), BF),
            pltpu.VMEM((HALF, SUB), BF),
            pltpu.VMEM((3, SEQ, SUB), F32),
            pltpu.VMEM((2, HALF, SUB), F32),
            pltpu.VMEM((8, SUB), F32),
        ],
        compiler_params=pltpu.CompilerParams(vmem_limit_bytes=VMEM_LIMIT),
        cost_estimate=pl.CostEstimate(flops=12_000_000_000, bytes_accessed=14_000_000, transcendentals=4_000_000),
    )(cut, place, x_raw, bc_raw, dt_raw, dy, y, st, taps_x, taps_bc, heads, spread, spread_t)


def place_blocks(pieces, w_ref, sem, row_of):
    for ref, k, first in pieces:
        for r in range(ref.shape[0]):
            for h in range(2):
                row = pl.multiple_of(row_of(k, first + r, h) * 48, 48)
                pltpu.make_async_copy(ref.at[r, h], w_ref.at[pl.ds(row, 48)], sem).start()


def ring_pieces(refs):
    return list(zip(refs, (0, 1, 3, 2, 2), (0, 0, 0, 0, 2)))


def start_halves(refs, which, buf, sems):
    for k in range(4):
        pltpu.make_async_copy(refs[k // 2].at[k % 2, which], buf.at[k], sems.at[k]).start()


def project_kernel(order_ref, place_ref, *refs):
    a_refs, t_refs = refs[0:5], refs[5:7]
    normed_ref, nt_ref, xr_ref, bc_ref, dt_ref, w_ref, wbc_ref, gain, tok, w_sem, t_sem = refs[7:]
    step = pl.program_id(0)

    @pl.when(step == 0)
    def _():
        z, xh, y = place_ref[0], place_ref[1], place_ref[2]
        start_halves(t_refs, 0, tok, t_sem)

        def row_of(k, r, h):
            return (lax.rem(z - k + 4, 4) * 2 + lax.rem(xh + h, 2)) * 4 + lax.rem(y - r + 4, 4)

        place_blocks(ring_pieces(a_refs), w_ref, w_sem, row_of)
        pltpu.make_async_copy(w_ref, w_ref, w_sem).wait()
        gain[...] = w_ref[:, 1024:1152].astype(F32).T[8:16]
        wbc_ref[...] = w_ref[:, 768:1024]

    pltpu.make_async_copy(t_refs[0].at[0, 0], tok.at[step], t_sem.at[step]).wait()
    wide = tok[step].astype(F32)
    inv = lax.rsqrt(jnp.mean(wide * wide, axis=-1, keepdims=True) + EPS)
    normed = (wide * inv * gain[4:5]).astype(BF)
    normed_ref[...] = normed
    nt_ref[...] = normed.T
    xr_ref[...] = mm(normed, w_ref[:, 0:768])
    bc_ref[...] = mm(normed, w_ref[:, 768:1024])
    dt_ref[...] = jnp.where(cols((HALF, SUB)) < 12, mm(normed, w_ref[:, 1024:1152]), 0.0)


ANY = pl.BlockSpec(memory_space=pl.ANY)


def by_order(width):
    return pl.BlockSpec((HALF, width), lambda i, order, place: (order[i], 0))


def turned():
    return pl.BlockSpec((1536, HALF), lambda i, order, place: (0, order[i]))


def fixed(shape):
    return pl.BlockSpec(shape, lambda i, *_: (0,) * len(shape))


def project(order, place, parts_in, tokens):
    sd = jax.ShapeDtypeStruct
    return pl.pallas_call(
        project_kernel,
        grid_spec=pltpu.PrefetchScalarGridSpec(
            num_scalar_prefetch=2,
            grid=(4,),
            in_specs=[ANY] * 7,
            out_specs=[by_order(1536), turned(), by_order(768), by_order(256), by_order(128), fixed((1536, 1152)), fixed((1536, 256)), fixed((8, 1536))],
            scratch_shapes=[pltpu.VMEM((4, HALF, 1536), BF), pltpu.SemaphoreType.DMA, pltpu.SemaphoreType.DMA((4,))],
        ),
        out_shape=[sd((1024, 1536), BF), sd((1536, 1024), BF), sd((1024, 768), F32), sd((1024, 256), F32), sd((1024, 128), F32), sd((1536, 1152), BF), sd((1536, 256), BF), sd((8, 1536), F32)],
        compiler_params=pltpu.CompilerParams(vmem_limit_bytes=VMEM_LIMIT),
        cost_estimate=pl.CostEstimate(flops=3_700_000_000, bytes_accessed=22_000_000, transcendentals=0),
    )(order, place, *parts_in, *tokens)


def gate_kernel(order_ref, place_ref, b0, b1, b2, b3, b4, c0, c1, normed_ref, y_ref, gg_ref, gate_ref, gs_ref, cot_ref, s_ref, w_ref, buf, w_sem, t_sem):
    step = pl.program_id(0)

    @pl.when(step == 0)
    def _():
        z, xh, y = place_ref[0], place_ref[1], place_ref[2]
        start_halves((c0, c1), 1, buf, t_sem)

        def row_of(k, r, h):
            return (lax.rem(z - r + 4, 4) * 2 + lax.rem(xh + h, 2)) * 4 + lax.rem(y - k + 4, 4)

        place_blocks(ring_pieces((b0, b1, b2, b3, b4)), w_ref, w_sem, row_of)
        pltpu.make_async_copy(w_ref, w_ref, w_sem).wait()

    pltpu.make_async_copy(c0.at[0, 1], buf.at[step], t_sem.at[step]).wait()
    cot = buf[step]
    cot_ref[...] = cot.T
    gate = mm(normed_ref[...], w_ref[:, 0:768])
    gs = mm(cot, w_ref[:, 768:1536])
    gate_ref[...] = gate
    gs_ref[...] = gs
    mixed = y_ref[...] * (gate * sigmoid(gate))
    sq = jnp.sum(mixed * mixed, axis=-1, keepdims=True)
    cr = jnp.sum((gs * gg_ref[0:1]) * mixed, axis=-1, keepdims=True)
    lane = cols((HALF, SUB))
    s_ref[...] = jnp.where(lane == 0, sq, jnp.where(lane == 1, cr, 0.0)).T[0:8]


def gate_side(order, place, parts_in, cots, normed, y, gg):
    sd = jax.ShapeDtypeStruct
    return pl.pallas_call(
        gate_kernel,
        grid_spec=pltpu.PrefetchScalarGridSpec(
            num_scalar_prefetch=2,
            grid=(4,),
            in_specs=[ANY] * 7 + [by_order(1536), by_order(768), fixed((8, 768))],
            out_specs=[by_order(768), by_order(768), turned(), pl.BlockSpec((8, HALF), lambda i, order, place: (0, order[i])), fixed((1536, 1536))],
            scratch_shapes=[pltpu.VMEM((4, HALF, 1536), BF), pltpu.SemaphoreType.DMA, pltpu.SemaphoreType.DMA((4,))],
        ),
        out_shape=[sd((1024, 768), F32), sd((1024, 768), F32), sd((1536, 1024), BF), sd((8, 1024), F32), sd((1536, 1536), BF)],
        compiler_params=pltpu.CompilerParams(vmem_limit_bytes=VMEM_LIMIT),
        cost_estimate=pl.CostEstimate(flops=4_900_000_000, bytes_accessed=30_000_000, transcendentals=800_000),
    )(order, place, *parts_in, *cots, normed, y, gg)


def mix_kernel(s0, s1, s2, s3, gate_ref, gs_ref, y_ref, gg_ref, scaled_ref, low_ref, dy_ref, gain_ref):
    sums = ((s0[...] + s1[...]) + (s2[...] + s3[...])).T
    inv = lax.rsqrt(sums[:, 0:1] / 3072 + EPS)
    corr = inv * inv * inv * (sums[:, 1:2] / 3072)
    gate, gs, y, gg = gate_ref[...], gs_ref[...], y_ref[...], gg_ref[0:1]
    sg = sigmoid(gate)
    act = gate * sg
    mixed = y * act
    normal = mixed * inv
    scaled_ref[...] = (normal * gg).astype(BF)
    gm = gs * gg * inv - mixed * corr
    low_ref[...] = (gm * y * (sg * (1.0 + gate * (1.0 - sg)))).astype(BF)
    dy_ref[...] = gm * act

    @pl.when(pl.program_id(0) == 0)
    def _():
        gain_ref[...] = jnp.zeros_like(gain_ref)

    gain_ref[0:1] += jnp.sum(gs * normal, axis=0, keepdims=True)


def mix(sums, gate, gs, y, gg):
    sd = jax.ShapeDtypeStruct
    block = pl.BlockSpec((HALF, 768), lambda i: (i, 0))
    return pl.pallas_call(
        mix_kernel,
        grid=(4,),
        in_specs=[pl.BlockSpec((8, HALF), lambda i: (0, i))] * 4 + [block] * 3 + [whole((8, 768))],
        out_specs=[block] * 3 + [whole((8, 768))],
        out_shape=[sd((1024, 768), BF), sd((1024, 768), BF), sd((1024, 768), F32), sd((8, 768), F32)],
        compiler_params=pltpu.CompilerParams(vmem_limit_bytes=VMEM_LIMIT),
        cost_estimate=pl.CostEstimate(flops=20_000_000, bytes_accessed=16_000_000, transcendentals=800_000),
    )(*sums, gate, gs, y, gg)


def outer_pair_kernel(n_ref, c_ref, g_ref, s_ref, o_ref):
    for at, a_ref, b_ref in ((0, n_ref, g_ref), (768, c_ref, s_ref)):
        r = mm(a_ref[...], b_ref[...]).astype(BF)
        for yi in range(4):
            for xi in range(2):
                row = (xi * 4 + yi) * 48
                o_ref[yi, xi * 48 : xi * 48 + 48, at : at + 768] = r[row : row + 48]


def outer_pair(normed_t, cot_t, gate_low, scaled):
    chunk = pl.BlockSpec((384, 1024), lambda i: (i, 0))
    return pl.pallas_call(
        outer_pair_kernel,
        grid=(4,),
        in_specs=[chunk, chunk, whole((1024, 768)), whole((1024, 768))],
        out_specs=pl.BlockSpec((4, 96, 1536), lambda i: (i, 0, 0)),
        out_shape=jax.ShapeDtypeStruct((16, 96, 1536), BF),
        compiler_params=pltpu.CompilerParams(vmem_limit_bytes=VMEM_LIMIT),
        cost_estimate=pl.CostEstimate(flops=4_900_000_000, bytes_accessed=14_000_000, transcendentals=0),
    )(normed_t, cot_t, gate_low, scaled)


def outer_z_kernel(place_ref, n_ref, g_ref, small_ref, *out):
    step = pl.program_id(0)
    y = place_ref[2]
    r = mm(n_ref[...], g_ref[...]).astype(BF)
    small = small_ref[...].astype(BF)
    for k in range(4):

        @pl.when(step == k)
        def _():
            for yi in range(4):
                to = lax.rem(yi - y + 4, 4)
                for xi in range(2):
                    at = (xi * 4 + yi) * 48
                    out[k][to, xi * 48 : xi * 48 + 48] = r[at : at + 48]
                out[k][to, 96:104] = small


def outer_side_kernel(place_ref, n_ref, g_ref, m_ref, d_ref, small_ref, maps_ref, *out):
    step = pl.program_id(0)
    y, xl = place_ref[2], place_ref[4]

    def columns(maps, steps):
        lane = cols(maps.shape)
        maps = jnp.where(xl == 0, maps, pltpu.roll(maps, 64, 1))
        return jnp.where(lane < 64, maps, pltpu.roll(steps, 64, 1)).astype(BF)

    n = n_ref[...]
    r = [mm(n, g_ref[...]).astype(BF), columns(mm(n, m_ref[...]), mm(n, d_ref[...]))]
    small = [small_ref[...].astype(BF), columns(maps_ref[:, 0:128], maps_ref[:, 128:256])]
    for k in range(4):

        @pl.when(step == k)
        def _():
            for part, lanes in ((0, slice(0, 256)), (1, slice(256, 384))):
                for yi in range(4):
                    to = lax.rem(yi - y + 4, 4)
                    for xi in range(2):
                        at = (xi * 4 + yi) * 48
                        out[k][to, xi * 48 : xi * 48 + 48, lanes] = r[part][at : at + 48]
                    out[k][to, 96:104, lanes] = small[part]


def outer_split(kernel, place, normed_t, grads, smalls, width):
    return pl.pallas_call(
        kernel,
        grid_spec=pltpu.PrefetchScalarGridSpec(
            num_scalar_prefetch=1,
            grid=(4,),
            in_specs=[pl.BlockSpec((384, 1024), lambda i, place: (lax.rem(place[0] + i, 4), 0))] + [spec for _, spec in grads] + [fixed(t.shape) for t in smalls],
            out_specs=[fixed((4, 104, width))] * 4,
        ),
        out_shape=[jax.ShapeDtypeStruct((4, 104, width), BF)] * 4,
        compiler_params=pltpu.CompilerParams(vmem_limit_bytes=VMEM_LIMIT),
        cost_estimate=pl.CostEstimate(flops=2 * 1024 * 1536 * width, bytes_accessed=5_000_000, transcendentals=0),
    )(place, normed_t, *[g for g, _ in grads], *smalls)


def fold_kernel(*refs):
    for parts4, lanes in ((refs[0:4], slice(0, 512)), (refs[4:8], slice(512, 896))):
        for k in range(4):
            near = parts4[1][k].astype(F32) + parts4[3][k].astype(F32)
            refs[8 + k][:, lanes] = ((parts4[0][k].astype(F32) + parts4[2][k].astype(F32)) + near).astype(BF)


def fold(a_parts, b_parts):
    vmem = pl.BlockSpec(memory_space=pltpu.VMEM)
    return pl.pallas_call(
        fold_kernel,
        in_specs=[vmem] * 8,
        out_specs=[vmem] * 4,
        out_shape=[jax.ShapeDtypeStruct((104, 896), BF)] * 4,
        compiler_params=pltpu.CompilerParams(vmem_limit_bytes=VMEM_LIMIT),
        cost_estimate=pl.CostEstimate(flops=1, bytes_accessed=1, transcendentals=0),
    )(*a_parts, *b_parts)


def rows_out(place_ref, total, out):
    for base in range(4):

        @pl.when(place_ref[3] * 2 + place_ref[4] == base)
        def _():
            for ref, at in zip(out, (base, base ^ 2, base ^ 1, base ^ 3)):
                ref[...] = total[at * HALF : at * HALF + HALF].astype(ref.dtype)


def out_kernel(place_ref, s_ref, w_ref, *out):
    rows_out(place_ref, mm_nt(s_ref[...], w_ref[...]), out)


def token_kernel(place_ref, g_ref, x_ref, d_ref, wz_ref, wx_ref, wd_ref, own_ref, mate_ref, send_ref):
    total = mm_nt(g_ref[...], wz_ref[...]) + mm_nt(x_ref[...], wx_ref[...]) + mm_nt(d_ref[...], wd_ref[...])
    rows_out(place_ref, total, [own_ref, send_ref.at[0:HALF], mate_ref, send_ref.at[HALF:SEQ]])


def by_rows(kernel, place, tokens, weights, places, outs):
    columns = lambda at: lambda i, place: (i, at(place))
    return pl.pallas_call(
        kernel,
        grid_spec=pltpu.PrefetchScalarGridSpec(
            num_scalar_prefetch=1,
            grid=(6,),
            in_specs=[fixed(t.shape) for t in tokens] + [pl.BlockSpec((256, t.shape[1]), columns(at)) for t, at in zip(tokens, places)],
            out_specs=[pl.BlockSpec((n, 256), lambda i, place: (0, i)) for n, _ in outs],
        ),
        out_shape=[jax.ShapeDtypeStruct((n, 1536), t) for n, t in outs],
        compiler_params=pltpu.CompilerParams(vmem_limit_bytes=VMEM_LIMIT),
        cost_estimate=pl.CostEstimate(flops=1, bytes_accessed=1, transcendentals=0),
    )(place, *tokens, *weights)


def sum_pieces_kernel(place_ref, p0, p1, p2, p3, zo_ref, keep_ref, send_ref):
    total = (p0[...].astype(F32) + p2[...].astype(F32)) + (p1[...].astype(F32) + p3[...].astype(F32))
    small = total[96:104].astype(BF)
    send_ref[48:56, 0:896] = small
    keep_ref[48:56, 0:896] = small.astype(F32)
    for xh in (0, 1):

        @pl.when(place_ref[1] == xh)
        def _():
            keep_ref[0:48, 0:896] = total[xh * 48 : xh * 48 + 48]
            send_ref[0:48, 0:896] = total[48 - xh * 48 : 96 - xh * 48].astype(BF)

    for xh in (0, 1):

        @pl.when(place_ref[1] == xh)
        def _():
            keep_ref[0:48, 896:2432] = zo_ref[xh * 48 : xh * 48 + 48].astype(F32)
            send_ref[0:48, 896:2432] = zo_ref[48 - xh * 48 : 96 - xh * 48]

    keep_ref[48:56, 896:2432] = jnp.zeros((8, 1536), F32)
    send_ref[48:56, 896:2432] = jnp.zeros((8, 1536), BF)


def sum_far_kernel(place_ref, own_ref, far_ref, keep_ref, send_ref):
    total = own_ref[...] + far_ref[...].astype(F32)
    keep_ref[24:32] = total[48:56]
    send_ref[24:32] = total[48:56]
    for core in (0, 1):

        @pl.when(place_ref[3] == core)
        def _():
            keep_ref[0:24] = total[core * 24 : core * 24 + 24]
            send_ref[0:24] = total[24 - core * 24 : 48 - core * 24]


def whole_call(kernel, place, arrays, shapes):
    vmem = pl.BlockSpec(memory_space=pltpu.VMEM)
    return pl.pallas_call(
        kernel,
        in_specs=[SMEM] + [vmem] * len(arrays),
        out_specs=[vmem] * len(shapes),
        out_shape=shapes,
        compiler_params=pltpu.CompilerParams(vmem_limit_bytes=VMEM_LIMIT),
        cost_estimate=pl.CostEstimate(flops=1, bytes_accessed=1, transcendentals=0),
    )(place, *arrays)


def sum_pieces(place, pieces, zo):
    shapes = [jax.ShapeDtypeStruct((56, 2432), F32), jax.ShapeDtypeStruct((56, 2432), BF)]
    return whole_call(sum_pieces_kernel, place, [*pieces, zo], shapes)


def sum_far(place, own, far):
    return whole_call(sum_far_kernel, place, [own, far], [jax.ShapeDtypeStruct((32, 2432), F32)] * 2)


def after_kernel(x_ref, *refs):
    pass


def after(x, *deps):
    return pl.pallas_call(
        after_kernel,
        in_specs=[ANY] * (1 + len(deps)),
        out_specs=ANY,
        out_shape=jax.ShapeDtypeStruct(x.shape, x.dtype),
        input_output_aliases={0: 0},
    )(x, *deps)


def swap(a, axis):
    return lax.ppermute(a, axis, [(0, 1), (1, 0)])


def turn(a, axis, k):
    return lax.ppermute(a, axis, [(i, (i + k) % 4) for i in range(4)])


def pair(own, other, axis):
    first = lax.axis_index(axis) == 0
    return jnp.stack([jnp.where(first, own, other), jnp.where(first, other, own)])


def mine(a, axis, dim, size):
    i = lax.axis_index(axis)
    return (
        lax.dynamic_slice_in_dim(a, i * size, size, dim),
        lax.dynamic_slice_in_dim(a, (1 - i) * size, size, dim),
    )


def turns(a, axis):
    return [a] + [turn(a, axis, k) for k in (1, 2, 3)]


def shards(resid, cotangent, segments, pre_gain, w_z, w_x, w_bc, w_dt, conv_x, conv_x_bias, conv_bc, conv_bc_bias, dt_bias, a_log, d_skip, gate_gain, w_out):
    core, xl = lax.axis_index("c"), lax.axis_index("xl")
    place = jnp.stack([lax.axis_index("z"), lax.axis_index("xh"), lax.axis_index("y"), core, xl])
    base = core * 2 + xl
    order = jnp.stack([core * 2, core * 2 + 1, 2 - core * 2, 3 - core * 2])

    own_bc = jnp.concatenate([w_bc, pre_gain[:, None], jnp.zeros((12, 127), BF)], axis=1)
    keep_x, send_x = mine(w_x, "c", 1, 768)
    keep_dt, send_dt = mine(w_dt, "c", 1, 12)
    bc_x, bc_c = swap(own_bc, "xl"), swap(own_bc, "c")
    bc_d = lax.ppermute(own_bc, ("c", "xl"), [(i, 3 - i) for i in range(4)])
    got = swap(jnp.concatenate([send_x, send_dt], axis=1), "c")
    bc48 = pair(pair(own_bc, bc_x, "xl"), pair(bc_c, bc_d, "xl"), "c").reshape(48, 384)
    xdt = pair(jnp.concatenate([keep_x, keep_dt], axis=1), got, "c").reshape(48, 780)
    first = jnp.concatenate([xdt[:, :768], bc48[:, :256], xdt[:, 768:], bc48[:, 256:372]], axis=1)
    first_far = swap(first, "xh")
    first = jnp.stack([first, first_far])

    keep_z, send_z = mine(w_z, "c", 1, 768)
    keep_o, send_o = mine(w_out.T, "c", 1, 768)
    got = swap(jnp.concatenate([send_z, send_o], axis=1), "c")
    second = pair(jnp.concatenate([keep_z, keep_o], axis=1), got, "c").reshape(48, 1536)
    second = jnp.stack([second, swap(second, "xh")])

    half = lax.all_gather(jnp.stack([resid, cotangent]), "xl", axis=0, tiled=False)
    near_x, near = turns(first, "y"), turns(second, "z")
    b_own = jnp.stack(near)
    b_ahead, b_back = turn(b_own, "y", 1), turn(b_own, "y", 3)
    a_own = after(jnp.stack(near_x), *near[1:])
    a_ahead, a_back = turn(a_own, "z", 1), turn(a_own, "z", 3)
    a_parts = [a_own, a_ahead, a_back, turn(after(a_ahead[:2], b_ahead, b_back), "z", 1), turn(after(a_back[2:], b_ahead, b_back), "z", 3)]

    def own(a, size):
        return mine(a, "c", a.ndim - 1, size)[0]

    cx, cxb, gg = own(conv_x, 768), own(conv_x_bias, 768), own(gate_gain, 768)
    dtb, al, dsk = own(dt_bias, 12), own(a_log, 12), own(d_skip, 12)
    taps_x = jnp.concatenate([cx, cxb[None], jnp.repeat(dsk, 64)[None], jnp.zeros((2, 768), F32)], axis=0)
    taps_bc = jnp.concatenate([conv_bc, conv_bc_bias[None], jnp.zeros((3, 256), F32)], axis=0)
    wide_heads = lambda v: jnp.pad(v, (0, 116))[None]
    heads = jnp.concatenate([wide_heads(dtb), wide_heads(-jnp.exp(al)), wide_heads(dsk), jnp.zeros((5, 128), F32)], axis=0)
    gains = jnp.broadcast_to(gg[None], (8, 768))
    spread_np = np.arange(768)[None, :] // 64 == np.arange(128)[:, None]
    spread, spread_t = jnp.asarray(spread_np, BF), jnp.asarray(spread_np.T, BF)
    half = after(half, a_parts[1], a_parts[2], b_ahead, b_back, taps_x, taps_bc, heads, gains)
    tokens = [half, swap(half, "c")]
    cut = jnp.sum((segments == segments[0]).astype(jnp.int32))[None]
    cuts = pair(cut, swap(cut, "c"), "c").reshape(2)

    normed, normed_t, x_raw, bc_raw, dt_raw, w_1, w_maps, gain_rows = project(order, place, a_parts, tokens)

    b_ahead, b_back = after(b_ahead, dt_raw), after(b_back, dt_raw)
    b_parts = [b_own, b_ahead, b_back, turn(b_ahead[:2], "y", 1), turn(b_back[2:], "y", 3)]
    y, st = ssd_forward(cuts, x_raw, bc_raw, dt_raw, taps_x, taps_bc, heads, spread)

    gate, gs, cot_t, sums, w_2 = gate_side(order, place, b_parts, tokens, normed, y, gains)
    sums_c, sums_x = swap(sums, "c"), swap(sums, "xl")
    sums_d = lax.ppermute(sums, ("c", "xl"), [(i, 3 - i) for i in range(4)])
    scaled, gate_low, dy, g_gain = mix([sums, sums_c, sums_x, sums_d], gate, gs, y, gains)

    def exchange(rows):
        diagonal = lax.ppermute(rows[3], ("c", "xl"), [(i, 3 - i) for i in range(4)])
        return rows[0], swap(rows[1], "c"), swap(rows[2], "xl"), diagonal

    out_rows = by_rows(out_kernel, place, [scaled], [w_2], [lambda place: 1], [(HALF, F32)] + [(HALF, BF)] * 3)
    g_zo = outer_pair(normed_t, after(cot_t, out_rows[1]), gate_low, scaled)
    g_zo_z = lax.psum_scatter(g_zo.reshape(1536, 1536), "z", scatter_dimension=0, tiled=True)
    g_zo_y = lax.psum_scatter(g_zo_z, "y", scatter_dimension=0, tiled=True)
    out_rows = exchange(out_rows)
    wide = lambda a: a.astype(F32)
    layer_out = (wide(resid) + ((out_rows[0] + wide(out_rows[1])) + (wide(out_rows[2]) + wide(out_rows[3])))).astype(BF)

    dy = after(dy, g_zo)
    x_low, keep, send, gdt, g_tx, keep_c, send_c, g_hd = ssd_backward(cuts, place, x_raw, bc_raw, dt_raw, dy, y, st, taps_x, taps_bc, heads, spread, spread_t)

    keep, keep_c = keep + swap(after(send, *out_rows[1:]), "c"), keep_c + swap(send_c, "c")
    keep_h = keep_c.astype(BF)
    keep = jnp.concatenate([keep.astype(BF), keep_h, (keep_c - keep_h.astype(F32)).astype(BF)], axis=0)
    small_x = jnp.concatenate([g_tx[:5], g_gain[:1], jnp.zeros((2, 768), F32)], axis=0)
    left = pl.BlockSpec((1024, 512), lambda i, place: (0, 0))
    right = pl.BlockSpec((1024, 256), lambda i, place: (0, 2))
    a_grad = outer_split(outer_z_kernel, place, normed_t, [(x_low, left)], [small_x[:, :512]], 512)
    a_grad = [a_grad[0]] + [turn(a_grad[k], "z", k) for k in (1, 2, 3)]
    far = swap(keep, "xl")
    group = keep.astype(F32) + far.astype(F32)
    bc_low = group[:1024].astype(BF)
    small_s = after(jnp.concatenate([group[1024:1032] + group[1032:], g_hd], axis=1), g_zo_z)
    full = lambda t: (t, fixed(t.shape))
    b_grad = outer_split(outer_side_kernel, place, normed_t, [(x_low, right), full(bc_low), full(gdt)], [small_x[:, 512:], small_s], 384)
    b_first = b_grad[0]
    b_grad = [b_first] + [turn(b_grad[k], "z", k) for k in (1, 2, 3)]
    token_rows = by_rows(token_kernel, place, [after(gate_low, b_first), x_low, gdt], [w_2, w_1, w_1], [lambda place: 0, lambda place: 0, lambda place: 8], [(HALF, F32), (HALF, F32), (SEQ, BF)])
    token_far = swap(after(token_rows[2], *a_grad[1:], *b_grad[1:], g_zo_y), "c")
    pieces = fold(a_grad, b_grad)
    token_far = after(token_far, pieces[1])
    grad_own = token_rows[0] + wide(token_far[:HALF])
    grad_far = swap((token_rows[1] + wide(token_far[HALF:])).astype(BF), "xl")
    pieces = [pieces[0]] + [turn(pieces[k], "y", k) for k in (1, 2, 3)]

    rows_own, rows_send = mine(bc_low, "c", 0, SEQ)
    bc_own = pair(rows_own, swap(rows_send, "c"), "c")
    bc_own = jnp.concatenate([bc_own[0], bc_own[1]], axis=1)
    bc_own = lax.dynamic_slice_in_dim(bc_own, xl * 256, 256, 0)
    bc_part = lax.dot_general(bc_own, w_maps, (((1,), (1,)), ((), ())), preferred_element_type=F32)
    grad_normed = (grad_own + wide(grad_far)) + bc_part

    keep, send = sum_pieces(place, pieces, g_zo_y)
    keep, send = sum_far(place, after(keep, grad_far), swap(send, "xh"))
    far = swap(send, "c")

    gain_wide = gain_rows[4]
    rw = resid.astype(F32)
    inv = lax.rsqrt(jnp.mean(rw * rw, axis=-1, keepdims=True) + EPS)
    inner = jnp.sum(gain_wide[None, :] * grad_normed * rw, axis=-1, keepdims=True)
    grad_resid = cotangent.astype(F32) + gain_wide[None, :] * grad_normed * inv - rw * (inv * inv * inv) * inner / 1536

    got = pair(keep, far, "c")
    both = lambda rows, at, width: jnp.concatenate([got[0, rows, at : at + width], got[1, rows, at : at + width]], axis=1)
    main, rest = slice(0, 24), slice(24, 32)
    grad_w_x, grad_w_z, grad_w_out_t = both(main, 0, 768), both(main, 896, 768), both(main, 1664, 768)
    grad_w_dt = both(main, 832, 12)
    bc24, conv24 = both(main, 768, 64), both(rest, 768, 64)
    small_wide = both(rest, 0, 768)
    small_heads = both(rest, 832, 12)

    tall = lambda a, b: jnp.sum(a.astype(F32) * b, axis=1)
    pg = tall(w_z, grad_w_z) + tall(w_x, grad_w_x) + tall(w_dt, grad_w_dt)
    pg, pg_send = mine(pg, "xl", 0, 12)
    bc12, bc_send = mine(bc24, "xl", 0, 12)
    far = swap(jnp.concatenate([bc_send, conv24, jnp.pad(pg_send, (0, 116))[None]], axis=0), "xl")
    got = pair(jnp.concatenate([bc12, conv24], axis=0), far[:20], "xl")
    got = got.reshape(2, 20, 2, 64).transpose(1, 2, 0, 3).reshape(20, 256)
    grad_w_bc, grad_conv_bc = got[:12], got[12:]
    grad_pre_gain = (pg + far[20, :12] + tall(w_bc, grad_w_bc)) / pre_gain.astype(F32)
    return (
        layer_out,
        grad_resid,
        grad_pre_gain,
        grad_w_z,
        grad_w_x,
        grad_w_bc,
        grad_w_dt,
        small_wide[:4],
        small_wide[4],
        grad_conv_bc[:4],
        grad_conv_bc[4],
        small_heads[0],
        small_heads[1],
        small_heads[2],
        small_wide[5],
        grad_w_out_t.T,
    )


def solution(mesh):
    fine = Mesh(mesh.devices.reshape(4, 2, 4, 2, 2), ("z", "xh", "y", "c", "xl"))
    dp, tp, every = ("z", "xh", "y", "c"), "xl", ("z", "xh", "y", "c", "xl")
    return jax.shard_map(
        shards,
        mesh=fine,
        in_specs=(P(every, None), P(every, None), P(dp), P(every), P(dp, tp), P(dp, tp), P(every, None), P(dp, tp), P(None, tp), P(tp), P(), P(), P(tp), P(tp), P(tp), P(tp), P(tp, dp)),
        out_specs=(P(every, None), P(every, None), P(every), P(dp, tp), P(dp, tp), P(every, None), P(dp, tp), P(None, tp), P(tp), P(), P(), P(tp), P(tp), P(tp), P(tp), P(tp, dp)),
        check_vma=False,
    )
```

```python
import jax
import jax.numpy as jnp
import numpy as np
from jax import lax
from jax.experimental import pallas as pl
from jax.experimental.pallas import tpu as pltpu
from jax.sharding import Mesh, PartitionSpec as P

EPS = 1e-05
VMEM_LIMIT = 60 * 1024 * 1024
BF = jnp.bfloat16
F32 = jnp.float32
SEQ = 512
HALF = 256
SUB = 128
PAIRS = 2


def mm(a, b):
    return jnp.dot(a, b, preferred_element_type=F32)


def mm_nt(a, b):
    return lax.dot_general(a, b, (((1,), (1,)), ((), ())), preferred_element_type=F32)


def mm_tn(a, b):
    return lax.dot_general(a, b, (((0,), (0,)), ((), ())), preferred_element_type=F32)


def parts(v, count):
    out = []
    for _ in range(count):
        low = v.astype(BF)
        out.append(low)
        v = v - low.astype(F32)
    return out


def split_left(v, m, count=2):
    return sum(mm(p, m) for p in parts(v, count))


def split_right(m, v, count=3):
    return sum(mm(m, p) for p in parts(v, count))


def rows(shape):
    return lax.broadcasted_iota(jnp.int32, shape, 0)


def cols(shape):
    return lax.broadcasted_iota(jnp.int32, shape, 1)


def softplus(v):
    e = jnp.exp(-jnp.abs(v))
    tail = jnp.where(e < 1e-3, e * (1.0 - 0.5 * e), jnp.log(1.0 + e))
    return jnp.maximum(v, 0.0) + tail


def sigmoid(v):
    return 1.0 / (1.0 + jnp.exp(-v))


def same_doc(t, s, cut):
    return (t < cut) == (s < cut)


def conv_masks(cut):
    t = rows((SEQ, SUB))
    return [jnp.where((t >= j) & ((t < cut) | (t - j >= cut)), 1.0, 0.0) for j in (1, 2, 3)]


def conv(v, taps, masks):
    u = taps[4:5] + taps[3:4] * v
    for j in (1, 2, 3):
        u = u + taps[3 - j : 4 - j] * (pltpu.roll(v, j, 0) * masks[j - 1])
    return u


def time_steps(dt_raw, heads, cut):
    dt = softplus(dt_raw + heads[0:1])
    a = dt * heads[1:2]
    tri = jnp.where(rows((HALF, HALF)) >= cols((HALF, HALF)), 1.0, 0.0).astype(BF)
    c = [split_right(tri, a[:HALF]), split_right(tri, a[HALF:])]
    t = rows((HALF, SUB))
    ending = same_doc(t, HALF - 1, cut)
    alive = same_doc(t + HALF, HALF - 1, cut)
    ew = jnp.where(ending, jnp.exp(c[0][HALF - 1 : HALF] - c[0]), 0.0)
    e1 = jnp.where(alive, jnp.exp(c[1]), 0.0)
    return dt, c, ew, e1


def masked_scores(cb, bb, block, cut, lower=True):
    out = {}
    for i, j in ((0, 0), (1, 0), (1, 1)):
        ti, sj = slice(i * SUB, i * SUB + SUB), slice(j * SUB, j * SUB + SUB)
        if lower:
            s = mm_nt(cb[ti], bb[sj])
            t = rows((SUB, SUB)) + (block * HALF + i * SUB)
            r = cols((SUB, SUB)) + (block * HALF + j * SUB)
        else:
            s = mm_nt(bb[sj], cb[ti])
            r = rows((SUB, SUB)) + (block * HALF + j * SUB)
            t = cols((SUB, SUB)) + (block * HALF + i * SUB)
        out[i, j] = jnp.where((t >= r) & same_doc(t, r, cut), s, 0.0)
    return out


def head_lanes(k):
    lane = cols((HALF, SUB))
    return (lane < 64) if k == 0 else (lane >= 64)


def fill_columns(c, ccol_ref, ct_ref):
    for k in (0, 1):
        ct_ref[k] = c[k].T
        for head in range(12):
            ccol_ref[k, head] = jnp.broadcast_to(c[k][:, head : head + 1], (HALF, SUB))


def put_stack(ref, values):
    at = 0
    for v in values:
        for p in parts(v, 2):
            ref[at : at + v.shape[0]] = p
            at += v.shape[0]


def spread_stack(ref, e, heights):
    wide, out, at = mm(ref[...], e), [], 0
    for n in heights:
        out.append(wide[at : at + n] + wide[at + n : at + 2 * n])
        at += 2 * n
    return out


BLOCKS = ((0, 0), (1, 0), (1, 1))


def fwd_kernel(cut_ref, xr_ref, bcr_ref, dtr_ref, tx_ref, tbc_ref, hd_ref, e_ref, y_ref, st_ref):
    cut = cut_ref[pl.program_id(0)]
    masks = conv_masks(cut)
    act = []
    for i in range(2):
        sl = slice(i * SUB, i * SUB + SUB)
        u = conv(bcr_ref[:, sl], tbc_ref[:, sl], masks)
        act.append(parts(u * sigmoid(u), 2))
    (bb, bb_low), (cb, cb_low) = act
    cb3 = jnp.concatenate([cb, cb_low, cb], axis=1)
    bb3 = jnp.concatenate([bb, bb, bb_low], axis=1)
    dt, c, ew, e1 = time_steps(dtr_ref[...], hd_ref[...], cut)
    ct = [c[0].T, c[1].T]
    tw = ew * dt[:HALF]
    scores = [masked_scores(cb3[k * HALF : k * HALF + HALF], bb3[k * HALF : k * HALF + HALF], k, cut) for k in (0, 1)]
    b0t, b0t_low = bb[:HALF].T, bb_low[:HALF].T
    for p in range(6):
        sl = slice(p * SUB, p * SUB + SUB)
        e = e_ref[:, sl]
        u = conv(xr_ref[:, sl], tx_ref[:, sl], masks)
        x = u * sigmoid(u)
        xtf = x * split_left(dt, e)
        xh = xtf.astype(BF)
        xhf = xh.astype(F32)
        xl_turned = pltpu.roll(xtf - xhf, 64, 1).astype(BF)
        skip = tx_ref[5:6, sl] * x
        xw, xw_low = parts(x[:HALF] * split_left(tw, e), 2)
        st = mm(b0t, xw) + (mm(b0t, xw_low) + mm(b0t_low, xw))
        st_ref[0, :, sl] = st
        st, st_low = parts(st, 2)
        carry = (mm(cb[HALF:], st) + (mm(cb[HALF:], st_low) + mm(cb_low[HALF:], st))) * split_left(e1, e)
        for k in (0, 1):
            ys = [[], []]
            for h in (0, 1):
                head = 2 * p + h
                at = slice(k * HALF, k * HALF + HALF)
                xm = jnp.where(head_lanes(h), xh[at], xl_turned[at])
                col = c[k][:, head : head + 1]
                row = ct[k][head : head + 1, :]
                m = {}
                for i, j in ((0, 0), (1, 0), (1, 1)):
                    gap = col[i * SUB : i * SUB + SUB] - row[:, j * SUB : j * SUB + SUB]
                    full = jnp.exp(jnp.minimum(gap, 0.0)) * scores[k][i, j]
                    m[i, j] = parts(full, 2)
                ys[0].append(mm(jnp.concatenate(m[0, 0], axis=1), jnp.concatenate([xm[:SUB], xm[:SUB]], axis=0)))
                wide = [m[1, 0][0], m[1, 1][0], m[1, 0][1], m[1, 1][1]]
                ys[1].append(mm(jnp.concatenate(wide, axis=1), jnp.concatenate([xm, xm], axis=0)))
            for i in (0, 1):
                at = k * HALF + i * SUB
                first = cols((SUB, SUB)) < 64
                y0, y1 = ys[i]
                y = jnp.where(first, y0, y1) + pltpu.roll(jnp.where(first, y1, y0), 64, 1) + skip[at : at + SUB]
                if k == 1:
                    y = y + carry[i * SUB : i * SUB + SUB]
                y_ref[at : at + SUB, sl] = y


def seq_spec(width):
    return pl.BlockSpec((SEQ, width), lambda i: (i, 0))


def whole(shape):
    return pl.BlockSpec(shape, lambda i: (0,) * len(shape))


SMEM = pl.BlockSpec(memory_space=pltpu.SMEM)


def ssd_forward(cut, x_raw, bc_raw, dt_raw, taps_x, taps_bc, heads, spread):
    return pl.pallas_call(
        fwd_kernel,
        grid=(2,),
        in_specs=[SMEM, seq_spec(768), seq_spec(256), seq_spec(128), whole((8, 768)), whole((8, 256)), whole((8, 128)), whole((128, 768))],
        out_specs=[seq_spec(768), pl.BlockSpec((1, 128, 768), lambda i: (i, 0, 0))],
        out_shape=[jax.ShapeDtypeStruct((1024, 768), F32), jax.ShapeDtypeStruct((2, 128, 768), F32)],
        compiler_params=pltpu.CompilerParams(vmem_limit_bytes=VMEM_LIMIT),
        cost_estimate=pl.CostEstimate(flops=4_000_000_000, bytes_accessed=9_000_000, transcendentals=4_000_000),
    )(cut, x_raw, bc_raw, dt_raw, taps_x, taps_bc, heads, spread)


def bwd_kernel(cut_ref, place_ref, xr_ref, bcr_ref, dtr_ref, dy_ref, y_ref, st_ref, tx_ref, tbc_ref, hd_ref, e_ref, et_ref,
               gx_ref, keep_ref, send_ref, gdt_ref, gtx_ref, keepc_ref, sendc_ref, ghd_ref,
               ds_ref, masks_ref, steps_ref, up_ref, ccol_ref, ct_ref, c1t_ref, b0_ref, acc_ref, accb_ref, skip_ref):
    seq = pl.program_id(0)
    cut = cut_ref[seq]
    masks = conv_masks(cut)

    def conv_back(du, v, taps, masks):
        g = taps[3:4] * du
        sums = [jnp.sum(du * v, axis=0, keepdims=True)]
        for j in (1, 2, 3):
            dm = du * masks[j - 1]
            g = g + taps[3 - j : 4 - j] * pltpu.roll(dm, SEQ - j, 0)
            sums.append(jnp.sum(dm * pltpu.roll(v, j, 0), axis=0, keepdims=True))
        return g, [sums[3], sums[2], sums[1], sums[0], jnp.sum(du, axis=0, keepdims=True)]

    @pl.when(seq == 0)
    def _():
        gtx_ref[...] = jnp.zeros_like(gtx_ref)
        keepc_ref[...] = jnp.zeros_like(keepc_ref)
        sendc_ref[...] = jnp.zeros_like(sendc_ref)
        ghd_ref[...] = jnp.zeros_like(ghd_ref)

    act = []
    for i in range(2):
        sl = slice(i * SUB, i * SUB + SUB)
        u = conv(bcr_ref[:, sl], tbc_ref[:, sl], masks)
        act.append((u * sigmoid(u)).astype(BF))
    for j in range(3):
        masks_ref[j] = masks[j]
    bb, cb = act
    dt, c, ew, e1 = time_steps(dtr_ref[...], hd_ref[...], cut)
    fill_columns(c, ccol_ref, ct_ref)
    put_stack(steps_ref, [dt, ew * dt[:HALF], e1, ew])
    blk = lambda a, k: a[k * HALF : k * HALF + HALF]
    for k in (0, 1):
        up = masked_scores(blk(cb, k), blk(bb, k), k, cut, lower=False)
        for n, at in enumerate(BLOCKS):
            up_ref[k, n] = up[at]
    c1t_ref[...] = cb[HALF:].T
    b0_ref[...] = bb[:HALF]
    ds_ref[...] = jnp.zeros_like(ds_ref)
    acc_ref[...] = jnp.zeros_like(acc_ref)
    accb_ref[...] = jnp.zeros_like(accb_ref)
    skip_ref[...] = jnp.zeros_like(skip_ref)

    def one_pair(p, carried):
        sl = pl.ds(pl.multiple_of(p * SUB, SUB), SUB)
        e, et, taps = e_ref[:, sl], et_ref[sl, :], tx_ref[:, sl]
        xr = xr_ref[:, sl]
        pair_masks = [masks_ref[j] for j in range(3)]
        u = conv(xr, taps, pair_masks)
        sg = sigmoid(u)
        x = u * sg
        dtx, twx, e1x, ewx = spread_stack(steps_ref, e, (SEQ, HALF, HALF, HALF))
        xtf = x * dtx
        xt = xtf.astype(BF)
        dy = dy_ref[:, sl]
        dyb = dy.astype(BF)
        dyh = dyb.astype(F32)
        xh = xt.astype(F32)
        xl = (xtf - xh).astype(BF)
        dl_turned = pltpu.roll(dy - dyh, 64, 1).astype(BF)
        xh_turned = pltpu.roll(xh, 64, 1).astype(BF)
        skip = jnp.broadcast_to(jnp.sum(dy * x, axis=0, keepdims=True), (16, SUB))
        stack = parts(dyh * y_ref[:, sl], 2) + parts(dyh * x, 2) + parts(skip, 3)
        wide = mm(jnp.concatenate(stack, axis=0), et)
        acc_ref[0] += wide[0:SEQ] + wide[SEQ : 2 * SEQ]
        acc_ref[1] += wide[2 * SEQ : 3 * SEQ] + wide[3 * SEQ : 4 * SEQ]
        skip_ref[...] += wide[2048:2056] + wide[2064:2072] + wide[2080:2088]
        dxs = []
        for k in (0, 1):
            back = 0.0
            for h in (0, 1):
                head = 2 * p + h
                lanes, none = head_lanes(h), jnp.zeros((), BF)
                dm = jnp.where(lanes, blk(dyb, k), none)
                dm2 = jnp.concatenate([jnp.where(lanes, blk(dyb, k), blk(dl_turned, k)), dm], axis=1)
                xm2 = jnp.concatenate([jnp.where(lanes, blk(xt, k), blk(xh_turned, k)), jnp.where(lanes, blk(xl, k), none)], axis=1)
                row = ct_ref[k, pl.ds(head, 1), :]
                gfull = mm_nt(dm2, xm2)
                mt = {}
                for n, (i, j) in enumerate(BLOCKS):
                    ti, sj = slice(i * SUB, i * SUB + SUB), slice(j * SUB, j * SUB + SUB)
                    decay = jnp.exp(-jnp.abs(ccol_ref[k, head, ti, :] - row[:, sj]))
                    if i == j:
                        decay_t = decay
                    else:
                        decay_t = jnp.exp(-jnp.abs(ccol_ref[k, head, sj, :] - row[:, ti]))
                    ds_ref[k, i + j] += gfull[ti, sj] * decay
                    mt[i, j] = (decay_t * up_ref[k, n]).astype(BF)
                rows0 = jnp.concatenate([mt[0, 0], mt[1, 0]], axis=1)
                rows1 = jnp.concatenate([jnp.zeros((SUB, SUB), BF), mt[1, 1]], axis=1)
                back = back + mm(jnp.concatenate([rows0, rows1], axis=0), dm)
            dxs.append(back)
        st, st_low = parts(st_ref[0, :, sl], 2)
        dcs, dcs_low = parts(dy[HALF:] * e1x, 2)
        accb_ref[0] += mm_nt(dcs, st) + (mm_nt(dcs_low, st) + mm_nt(dcs, st_low))
        dst, dst_low = parts(mm(c1t_ref[...], dcs) + mm(c1t_ref[...], dcs_low), 2)
        dxw = mm(b0_ref[...], dst)
        xw, xw_low = parts(x[:HALF] * twx, 2)
        accb_ref[1] += mm_nt(xw, dst) + (mm_nt(xw_low, dst) + mm_nt(xw, dst_low))
        dx0 = dxs[0] + dxw * ewx
        dxt = jnp.concatenate([dx0, dxs[1]], axis=0)
        wide = mm(jnp.concatenate(parts(x * dxt, 2), axis=0), et)
        acc_ref[2] += wide[:SEQ] + wide[SEQ:]
        dx = dtx * dxt + taps[5:6] * dy
        du = dx * (sg * (1.0 + u * (1.0 - sg)))
        g, sums = conv_back(du, xr, taps, pair_masks)
        gx_ref[:, sl] = g.astype(BF)
        gtx_ref[0:5, sl] += jnp.concatenate(sums, axis=0)
        return carried

    lax.fori_loop(0, 6 // PAIRS, lambda i, x: [one_pair(i * PAIRS + j, x) for j in range(PAIRS)][0], 0)
    sum_y, sum_x, sum_d = acc_ref[0], acc_ref[1], acc_ref[2]
    d_c1, d_b0 = accb_ref[0], accb_ref[1]
    d_b, d_c = [], []
    for k in (0, 1):
        bk, ck = blk(bb, k), blk(cb, k)
        m = {}
        for i, j in ((0, 0), (1, 0), (1, 1)):
            t = rows((SUB, SUB)) + (k * HALF + i * SUB)
            r = cols((SUB, SUB)) + (k * HALF + j * SUB)
            m[i, j] = jnp.where((t >= r) & same_doc(t, r, cut), ds_ref[k, i + j], 0.0).astype(BF)
        lowr = jnp.concatenate([m[1, 0], m[1, 1]], axis=1)
        d_c += [mm(m[0, 0], bk[:SUB]), mm(lowr, bk)]
        d_b += [mm_tn(m[0, 0], ck[:SUB]) + mm_tn(m[1, 0], ck[SUB:]), mm_tn(m[1, 1], ck[SUB:])]
    d_b = jnp.concatenate([jnp.concatenate(d_b[:2], axis=0) + d_b0] + d_b[2:], axis=0)
    d_c = jnp.concatenate(d_c[:2] + [jnp.concatenate(d_c[2:], axis=0) + d_c1], axis=0)
    for i, d in ((0, d_b), (1, d_c)):
        sl = slice(i * SUB, i * SUB + SUB)
        v = bcr_ref[:, sl]
        u = conv(v, tbc_ref[:, sl], masks)
        sg = sigmoid(u)
        g, sums = conv_back(d * (sg * (1.0 + u * (1.0 - sg))), v, tbc_ref[:, sl], masks)

        @pl.when(place_ref[3] == i)
        def _():
            keep_ref[...] = g
            for r, s in enumerate(sums):
                keepc_ref[r : r + 1] += s

        @pl.when(place_ref[3] != i)
        def _():
            send_ref[...] = g
            for r, s in enumerate(sums):
                sendc_ref[r : r + 1] += s

    hd = hd_ref[...]
    w = (sum_y - hd[2:3] * sum_x) - dt * sum_d
    tri = jnp.where((cols((SEQ, SEQ)) >= rows((SEQ, SEQ))) & same_doc(rows((SEQ, SEQ)), cols((SEQ, SEQ)), cut), 1.0, 0.0).astype(BF)
    run = split_right(tri, w)
    d_dt = sum_d + hd[1:2] * run
    gd = d_dt * sigmoid(dtr_ref[...] + hd[0:1])
    gdt_ref[...] = gd.astype(BF)
    ghd_ref[0:1] += jnp.sum(gd, axis=0, keepdims=True)
    ghd_ref[2:3] += skip_ref[0:1]
    ghd_ref[1:2] += jnp.sum(dt * run, axis=0, keepdims=True) * hd[1:2]


def ssd_backward(cut, place, x_raw, bc_raw, dt_raw, dy, y, st, taps_x, taps_bc, heads, spread, spread_t):
    return pl.pallas_call(
        bwd_kernel,
        grid=(2,),
        in_specs=[SMEM, SMEM, seq_spec(768), seq_spec(256), seq_spec(128), seq_spec(768), seq_spec(768),
                  pl.BlockSpec((1, 128, 768), lambda i: (i, 0, 0)), whole((8, 768)), whole((8, 256)), whole((8, 128)), whole((128, 768)), whole((768, 128))],
        out_specs=[seq_spec(768), seq_spec(128), seq_spec(128), seq_spec(128), whole((8, 768)), whole((8, 128)), whole((8, 128)), whole((8, 128))],
        out_shape=[jax.ShapeDtypeStruct((1024, 768), BF), jax.ShapeDtypeStruct((1024, 128), F32), jax.ShapeDtypeStruct((1024, 128), F32), jax.ShapeDtypeStruct((1024, 128), BF),
                   jax.ShapeDtypeStruct((8, 768), F32), jax.ShapeDtypeStruct((8, 128), F32), jax.ShapeDtypeStruct((8, 128), F32), jax.ShapeDtypeStruct((8, 128), F32)],
        scratch_shapes=[
            pltpu.VMEM((2, 3, SUB, SUB), F32),
            pltpu.VMEM((3, SEQ, SUB), F32),
            pltpu.VMEM((5 * SEQ, SUB), BF),
            pltpu.VMEM((2, 3, SUB, SUB), F32),
            pltpu.VMEM((2, 12, HALF, SUB), F32),
            pltpu.VMEM((2, SUB, HALF), F32),
            pltpu.VMEM((SUB, HALF), BF),
            pltpu.VMEM((HALF, SUB), BF),
            pltpu.VMEM((3, SEQ, SUB), F32),
            pltpu.VMEM((2, HALF, SUB), F32),
            pltpu.VMEM((8, SUB), F32),
        ],
        compiler_params=pltpu.CompilerParams(vmem_limit_bytes=VMEM_LIMIT),
        cost_estimate=pl.CostEstimate(flops=12_000_000_000, bytes_accessed=14_000_000, transcendentals=4_000_000),
    )(cut, place, x_raw, bc_raw, dt_raw, dy, y, st, taps_x, taps_bc, heads, spread, spread_t)


def place_blocks(pieces, w_ref, sem, row_of):
    for ref, k, first in pieces:
        for r in range(ref.shape[0]):
            for h in range(2):
                row = pl.multiple_of(row_of(k, first + r, h) * 48, 48)
                pltpu.make_async_copy(ref.at[r, h], w_ref.at[pl.ds(row, 48)], sem).start()


def ring_pieces(refs):
    return list(zip(refs, (0, 1, 3, 2, 2), (0, 0, 0, 0, 2)))


def start_halves(refs, which, buf, sems):
    for k in range(4):
        pltpu.make_async_copy(refs[k // 2].at[k % 2, which], buf.at[k], sems.at[k]).start()


def project_kernel(order_ref, place_ref, *refs):
    a_refs, t_refs = refs[0:5], refs[5:7]
    normed_ref, nt_ref, xr_ref, bc_ref, dt_ref, w_ref, wbc_ref, gain, tok, w_sem, t_sem = refs[7:]
    step = pl.program_id(0)

    @pl.when(step == 0)
    def _():
        z, xh, y = place_ref[0], place_ref[1], place_ref[2]
        start_halves(t_refs, 0, tok, t_sem)

        def row_of(k, r, h):
            return (lax.rem(z - k + 4, 4) * 2 + lax.rem(xh + h, 2)) * 4 + lax.rem(y - r + 4, 4)

        place_blocks(ring_pieces(a_refs), w_ref, w_sem, row_of)
        pltpu.make_async_copy(w_ref, w_ref, w_sem).wait()
        gain[...] = w_ref[:, 1024:1152].astype(F32).T[8:16]
        wbc_ref[...] = w_ref[:, 768:1024]

    pltpu.make_async_copy(t_refs[0].at[0, 0], tok.at[step], t_sem.at[step]).wait()
    wide = tok[step].astype(F32)
    inv = lax.rsqrt(jnp.mean(wide * wide, axis=-1, keepdims=True) + EPS)
    normed = (wide * inv * gain[4:5]).astype(BF)
    normed_ref[...] = normed
    nt_ref[...] = normed.T
    xr_ref[...] = mm(normed, w_ref[:, 0:768])
    bc_ref[...] = mm(normed, w_ref[:, 768:1024])
    dt_ref[...] = jnp.where(cols((HALF, SUB)) < 12, mm(normed, w_ref[:, 1024:1152]), 0.0)


ANY = pl.BlockSpec(memory_space=pl.ANY)


def by_order(width):
    return pl.BlockSpec((HALF, width), lambda i, order, place: (order[i], 0))


def turned():
    return pl.BlockSpec((1536, HALF), lambda i, order, place: (0, order[i]))


def fixed(shape):
    return pl.BlockSpec(shape, lambda i, *_: (0,) * len(shape))


def project(order, place, parts_in, tokens):
    sd = jax.ShapeDtypeStruct
    return pl.pallas_call(
        project_kernel,
        grid_spec=pltpu.PrefetchScalarGridSpec(
            num_scalar_prefetch=2,
            grid=(4,),
            in_specs=[ANY] * 7,
            out_specs=[by_order(1536), turned(), by_order(768), by_order(256), by_order(128), fixed((1536, 1152)), fixed((1536, 256)), fixed((8, 1536))],
            scratch_shapes=[pltpu.VMEM((4, HALF, 1536), BF), pltpu.SemaphoreType.DMA, pltpu.SemaphoreType.DMA((4,))],
        ),
        out_shape=[sd((1024, 1536), BF), sd((1536, 1024), BF), sd((1024, 768), F32), sd((1024, 256), F32), sd((1024, 128), F32), sd((1536, 1152), BF), sd((1536, 256), BF), sd((8, 1536), F32)],
        compiler_params=pltpu.CompilerParams(vmem_limit_bytes=VMEM_LIMIT),
        cost_estimate=pl.CostEstimate(flops=3_700_000_000, bytes_accessed=22_000_000, transcendentals=0),
    )(order, place, *parts_in, *tokens)


def gate_kernel(order_ref, place_ref, b0, b1, b2, b3, b4, c0, c1, normed_ref, y_ref, gg_ref, gate_ref, gs_ref, cot_ref, s_ref, w_ref, buf, w_sem, t_sem):
    step = pl.program_id(0)

    @pl.when(step == 0)
    def _():
        z, xh, y = place_ref[0], place_ref[1], place_ref[2]
        start_halves((c0, c1), 1, buf, t_sem)

        def row_of(k, r, h):
            return (lax.rem(z - r + 4, 4) * 2 + lax.rem(xh + h, 2)) * 4 + lax.rem(y - k + 4, 4)

        place_blocks(ring_pieces((b0, b1, b2, b3, b4)), w_ref, w_sem, row_of)
        pltpu.make_async_copy(w_ref, w_ref, w_sem).wait()

    pltpu.make_async_copy(c0.at[0, 1], buf.at[step], t_sem.at[step]).wait()
    cot = buf[step]
    cot_ref[...] = cot.T
    gate = mm(normed_ref[...], w_ref[:, 0:768])
    gs = mm(cot, w_ref[:, 768:1536])
    gate_ref[...] = gate
    gs_ref[...] = gs
    mixed = y_ref[...] * (gate * sigmoid(gate))
    sq = jnp.sum(mixed * mixed, axis=-1, keepdims=True)
    cr = jnp.sum((gs * gg_ref[0:1]) * mixed, axis=-1, keepdims=True)
    lane = cols((HALF, SUB))
    s_ref[...] = jnp.where(lane == 0, sq, jnp.where(lane == 1, cr, 0.0)).T[0:8]


def gate_side(order, place, parts_in, cots, normed, y, gg):
    sd = jax.ShapeDtypeStruct
    return pl.pallas_call(
        gate_kernel,
        grid_spec=pltpu.PrefetchScalarGridSpec(
            num_scalar_prefetch=2,
            grid=(4,),
            in_specs=[ANY] * 7 + [by_order(1536), by_order(768), fixed((8, 768))],
            out_specs=[by_order(768), by_order(768), turned(), pl.BlockSpec((8, HALF), lambda i, order, place: (0, order[i])), fixed((1536, 1536))],
            scratch_shapes=[pltpu.VMEM((4, HALF, 1536), BF), pltpu.SemaphoreType.DMA, pltpu.SemaphoreType.DMA((4,))],
        ),
        out_shape=[sd((1024, 768), F32), sd((1024, 768), F32), sd((1536, 1024), BF), sd((8, 1024), F32), sd((1536, 1536), BF)],
        compiler_params=pltpu.CompilerParams(vmem_limit_bytes=VMEM_LIMIT),
        cost_estimate=pl.CostEstimate(flops=4_900_000_000, bytes_accessed=30_000_000, transcendentals=800_000),
    )(order, place, *parts_in, *cots, normed, y, gg)


def mix_kernel(s0, s1, s2, s3, gate_ref, gs_ref, y_ref, gg_ref, scaled_ref, low_ref, dy_ref, gain_ref):
    sums = ((s0[...] + s1[...]) + (s2[...] + s3[...])).T
    inv = lax.rsqrt(sums[:, 0:1] / 3072 + EPS)
    corr = inv * inv * inv * (sums[:, 1:2] / 3072)
    gate, gs, y, gg = gate_ref[...], gs_ref[...], y_ref[...], gg_ref[0:1]
    sg = sigmoid(gate)
    act = gate * sg
    mixed = y * act
    normal = mixed * inv
    scaled_ref[...] = (normal * gg).astype(BF)
    gm = gs * gg * inv - mixed * corr
    low_ref[...] = (gm * y * (sg * (1.0 + gate * (1.0 - sg)))).astype(BF)
    dy_ref[...] = gm * act

    @pl.when(pl.program_id(0) == 0)
    def _():
        gain_ref[...] = jnp.zeros_like(gain_ref)

    gain_ref[0:1] += jnp.sum(gs * normal, axis=0, keepdims=True)


def mix(sums, gate, gs, y, gg):
    sd = jax.ShapeDtypeStruct
    block = pl.BlockSpec((HALF, 768), lambda i: (i, 0))
    return pl.pallas_call(
        mix_kernel,
        grid=(4,),
        in_specs=[pl.BlockSpec((8, HALF), lambda i: (0, i))] * 4 + [block] * 3 + [whole((8, 768))],
        out_specs=[block] * 3 + [whole((8, 768))],
        out_shape=[sd((1024, 768), BF), sd((1024, 768), BF), sd((1024, 768), F32), sd((8, 768), F32)],
        compiler_params=pltpu.CompilerParams(vmem_limit_bytes=VMEM_LIMIT),
        cost_estimate=pl.CostEstimate(flops=20_000_000, bytes_accessed=16_000_000, transcendentals=800_000),
    )(*sums, gate, gs, y, gg)


def outer_pair_kernel(n_ref, c_ref, g_ref, s_ref, o_ref):
    for at, a_ref, b_ref in ((0, n_ref, g_ref), (768, c_ref, s_ref)):
        r = mm(a_ref[...], b_ref[...]).astype(BF)
        for yi in range(4):
            for xi in range(2):
                row = (xi * 4 + yi) * 48
                o_ref[yi, xi * 48 : xi * 48 + 48, at : at + 768] = r[row : row + 48]


def outer_pair(normed_t, cot_t, gate_low, scaled):
    chunk = pl.BlockSpec((384, 1024), lambda i: (i, 0))
    return pl.pallas_call(
        outer_pair_kernel,
        grid=(4,),
        in_specs=[chunk, chunk, whole((1024, 768)), whole((1024, 768))],
        out_specs=pl.BlockSpec((4, 96, 1536), lambda i: (i, 0, 0)),
        out_shape=jax.ShapeDtypeStruct((16, 96, 1536), BF),
        compiler_params=pltpu.CompilerParams(vmem_limit_bytes=VMEM_LIMIT),
        cost_estimate=pl.CostEstimate(flops=4_900_000_000, bytes_accessed=14_000_000, transcendentals=0),
    )(normed_t, cot_t, gate_low, scaled)


def outer_z_kernel(place_ref, n_ref, g_ref, small_ref, *out):
    step = pl.program_id(0)
    y = place_ref[2]
    r = mm(n_ref[...], g_ref[...]).astype(BF)
    small = small_ref[...].astype(BF)
    for k in range(4):

        @pl.when(step == k)
        def _():
            for yi in range(4):
                to = lax.rem(yi - y + 4, 4)
                for xi in range(2):
                    at = (xi * 4 + yi) * 48
                    out[k][to, xi * 48 : xi * 48 + 48] = r[at : at + 48]
                out[k][to, 96:104] = small


def outer_side_kernel(place_ref, n_ref, g_ref, m_ref, d_ref, small_ref, maps_ref, *out):
    step = pl.program_id(0)
    y, xl = place_ref[2], place_ref[4]

    def columns(maps, steps):
        lane = cols(maps.shape)
        maps = jnp.where(xl == 0, maps, pltpu.roll(maps, 64, 1))
        return jnp.where(lane < 64, maps, pltpu.roll(steps, 64, 1)).astype(BF)

    n = n_ref[...]
    r = [mm(n, g_ref[...]).astype(BF), columns(mm(n, m_ref[...]), mm(n, d_ref[...]))]
    small = [small_ref[...].astype(BF), columns(maps_ref[:, 0:128], maps_ref[:, 128:256])]
    for k in range(4):

        @pl.when(step == k)
        def _():
            for part, lanes in ((0, slice(0, 256)), (1, slice(256, 384))):
                for yi in range(4):
                    to = lax.rem(yi - y + 4, 4)
                    for xi in range(2):
                        at = (xi * 4 + yi) * 48
                        out[k][to, xi * 48 : xi * 48 + 48, lanes] = r[part][at : at + 48]
                    out[k][to, 96:104, lanes] = small[part]


def outer_split(kernel, place, normed_t, grads, smalls, width):
    return pl.pallas_call(
        kernel,
        grid_spec=pltpu.PrefetchScalarGridSpec(
            num_scalar_prefetch=1,
            grid=(4,),
            in_specs=[pl.BlockSpec((384, 1024), lambda i, place: (lax.rem(place[0] + i, 4), 0))] + [spec for _, spec in grads] + [fixed(t.shape) for t in smalls],
            out_specs=[fixed((4, 104, width))] * 4,
        ),
        out_shape=[jax.ShapeDtypeStruct((4, 104, width), BF)] * 4,
        compiler_params=pltpu.CompilerParams(vmem_limit_bytes=VMEM_LIMIT),
        cost_estimate=pl.CostEstimate(flops=2 * 1024 * 1536 * width, bytes_accessed=5_000_000, transcendentals=0),
    )(place, normed_t, *[g for g, _ in grads], *smalls)


def fold_kernel(*refs):
    for parts4, lanes in ((refs[0:4], slice(0, 512)), (refs[4:8], slice(512, 896))):
        for k in range(4):
            near = parts4[1][k].astype(F32) + parts4[3][k].astype(F32)
            refs[8 + k][:, lanes] = ((parts4[0][k].astype(F32) + parts4[2][k].astype(F32)) + near).astype(BF)


def fold(a_parts, b_parts):
    vmem = pl.BlockSpec(memory_space=pltpu.VMEM)
    return pl.pallas_call(
        fold_kernel,
        in_specs=[vmem] * 8,
        out_specs=[vmem] * 4,
        out_shape=[jax.ShapeDtypeStruct((104, 896), BF)] * 4,
        compiler_params=pltpu.CompilerParams(vmem_limit_bytes=VMEM_LIMIT),
        cost_estimate=pl.CostEstimate(flops=1, bytes_accessed=1, transcendentals=0),
    )(*a_parts, *b_parts)


def rows_out(place_ref, total, out):
    for base in range(4):

        @pl.when(place_ref[3] * 2 + place_ref[4] == base)
        def _():
            for ref, at in zip(out, (base, base ^ 2, base ^ 1, base ^ 3)):
                ref[...] = total[at * HALF : at * HALF + HALF].astype(ref.dtype)


def out_kernel(place_ref, s_ref, w_ref, *out):
    rows_out(place_ref, mm_nt(s_ref[...], w_ref[...]), out)


def token_kernel(place_ref, g_ref, x_ref, d_ref, wz_ref, wx_ref, wd_ref, own_ref, mate_ref, send_ref):
    total = mm_nt(g_ref[...], wz_ref[...]) + mm_nt(x_ref[...], wx_ref[...]) + mm_nt(d_ref[...], wd_ref[...])
    rows_out(place_ref, total, [own_ref, send_ref.at[0:HALF], mate_ref, send_ref.at[HALF:SEQ]])


def by_rows(kernel, place, tokens, weights, places, outs, work=1):
    columns = lambda at: lambda i, place: (i, at(place))
    return pl.pallas_call(
        kernel,
        grid_spec=pltpu.PrefetchScalarGridSpec(
            num_scalar_prefetch=1,
            grid=(6,),
            in_specs=[fixed(t.shape) for t in tokens] + [pl.BlockSpec((256, t.shape[1]), columns(at)) for t, at in zip(tokens, places)],
            out_specs=[pl.BlockSpec((n, 256), lambda i, place: (0, i)) for n, _ in outs],
        ),
        out_shape=[jax.ShapeDtypeStruct((n, 1536), t) for n, t in outs],
        compiler_params=pltpu.CompilerParams(vmem_limit_bytes=VMEM_LIMIT),
        cost_estimate=pl.CostEstimate(flops=work, bytes_accessed=1, transcendentals=0),
    )(place, *tokens, *weights)


def sum_pieces_kernel(place_ref, p0, p1, p2, p3, zo_ref, keep_ref, send_ref):
    total = (p0[...].astype(F32) + p2[...].astype(F32)) + (p1[...].astype(F32) + p3[...].astype(F32))
    small = total[96:104].astype(BF)
    send_ref[48:56, 0:896] = small
    keep_ref[48:56, 0:896] = small.astype(F32)
    for xh in (0, 1):

        @pl.when(place_ref[1] == xh)
        def _():
            keep_ref[0:48, 0:896] = total[xh * 48 : xh * 48 + 48]
            send_ref[0:48, 0:896] = total[48 - xh * 48 : 96 - xh * 48].astype(BF)

    for xh in (0, 1):

        @pl.when(place_ref[1] == xh)
        def _():
            keep_ref[0:48, 896:2432] = zo_ref[xh * 48 : xh * 48 + 48].astype(F32)
            send_ref[0:48, 896:2432] = zo_ref[48 - xh * 48 : 96 - xh * 48]

    keep_ref[48:56, 896:2432] = jnp.zeros((8, 1536), F32)
    send_ref[48:56, 896:2432] = jnp.zeros((8, 1536), BF)


def sum_far_kernel(place_ref, own_ref, far_ref, keep_ref, send_ref):
    total = own_ref[...] + far_ref[...].astype(F32)
    keep_ref[24:32] = total[48:56]
    send_ref[24:32] = total[48:56]
    for core in (0, 1):

        @pl.when(place_ref[3] == core)
        def _():
            keep_ref[0:24] = total[core * 24 : core * 24 + 24]
            send_ref[0:24] = total[24 - core * 24 : 48 - core * 24]


def whole_call(kernel, place, arrays, shapes):
    vmem = pl.BlockSpec(memory_space=pltpu.VMEM)
    return pl.pallas_call(
        kernel,
        in_specs=[SMEM] + [vmem] * len(arrays),
        out_specs=[vmem] * len(shapes),
        out_shape=shapes,
        compiler_params=pltpu.CompilerParams(vmem_limit_bytes=VMEM_LIMIT),
        cost_estimate=pl.CostEstimate(flops=1, bytes_accessed=1, transcendentals=0),
    )(place, *arrays)


def sum_pieces(place, pieces, zo):
    shapes = [jax.ShapeDtypeStruct((56, 2432), F32), jax.ShapeDtypeStruct((56, 2432), BF)]
    return whole_call(sum_pieces_kernel, place, [*pieces, zo], shapes)


def sum_far(place, own, far):
    return whole_call(sum_far_kernel, place, [own, far], [jax.ShapeDtypeStruct((32, 2432), F32)] * 2)


def after_kernel(x_ref, *refs):
    pass


def after(x, *deps):
    return pl.pallas_call(
        after_kernel,
        in_specs=[ANY] * (1 + len(deps)),
        out_specs=ANY,
        out_shape=jax.ShapeDtypeStruct(x.shape, x.dtype),
        input_output_aliases={0: 0},
    )(x, *deps)


def swap(a, axis):
    return lax.ppermute(a, axis, [(0, 1), (1, 0)])


def turn(a, axis, k):
    return lax.ppermute(a, axis, [(i, (i + k) % 4) for i in range(4)])


def pair(own, other, axis):
    first = lax.axis_index(axis) == 0
    return jnp.stack([jnp.where(first, own, other), jnp.where(first, other, own)])


def mine(a, axis, dim, size):
    i = lax.axis_index(axis)
    return (
        lax.dynamic_slice_in_dim(a, i * size, size, dim),
        lax.dynamic_slice_in_dim(a, (1 - i) * size, size, dim),
    )


def turns(a, axis):
    return [a] + [turn(a, axis, k) for k in (1, 2, 3)]


def shards(resid, cotangent, segments, pre_gain, w_z, w_x, w_bc, w_dt, conv_x, conv_x_bias, conv_bc, conv_bc_bias, dt_bias, a_log, d_skip, gate_gain, w_out):
    core, xl = lax.axis_index("c"), lax.axis_index("xl")
    place = jnp.stack([lax.axis_index("z"), lax.axis_index("xh"), lax.axis_index("y"), core, xl])
    base = core * 2 + xl
    order = jnp.stack([core * 2, core * 2 + 1, 2 - core * 2, 3 - core * 2])

    own_bc = jnp.concatenate([w_bc, pre_gain[:, None], jnp.zeros((12, 127), BF)], axis=1)
    keep_x, send_x = mine(w_x, "c", 1, 768)
    keep_dt, send_dt = mine(w_dt, "c", 1, 12)
    bc_x, bc_c = swap(own_bc, "xl"), swap(own_bc, "c")
    bc_d = lax.ppermute(own_bc, ("c", "xl"), [(i, 3 - i) for i in range(4)])
    got = swap(jnp.concatenate([send_x, send_dt], axis=1), "c")
    bc48 = pair(pair(own_bc, bc_x, "xl"), pair(bc_c, bc_d, "xl"), "c").reshape(48, 384)
    xdt = pair(jnp.concatenate([keep_x, keep_dt], axis=1), got, "c").reshape(48, 780)
    first = jnp.concatenate([xdt[:, :768], bc48[:, :256], xdt[:, 768:], bc48[:, 256:372]], axis=1)
    first_far = swap(first, "xh")
    first = jnp.stack([first, first_far])

    keep_z, send_z = mine(w_z, "c", 1, 768)
    keep_o, send_o = mine(w_out.T, "c", 1, 768)
    got = swap(jnp.concatenate([send_z, send_o], axis=1), "c")
    second = pair(jnp.concatenate([keep_z, keep_o], axis=1), got, "c").reshape(48, 1536)
    second = jnp.stack([second, swap(second, "xh")])

    half = lax.all_gather(jnp.stack([resid, cotangent]), "xl", axis=0, tiled=False)
    near_x, near = turns(first, "y"), turns(second, "z")
    b_own = jnp.stack(near)
    b_ahead, b_back = turn(b_own, "y", 1), turn(b_own, "y", 3)
    a_own = after(jnp.stack(near_x), *near[1:])
    a_ahead, a_back = turn(a_own, "z", 1), turn(a_own, "z", 3)
    a_parts = [a_own, a_ahead, a_back, turn(after(a_ahead[:2], b_ahead, b_back), "z", 1), turn(after(a_back[2:], b_ahead, b_back), "z", 3)]

    def own(a, size):
        return mine(a, "c", a.ndim - 1, size)[0]

    cx, cxb, gg = own(conv_x, 768), own(conv_x_bias, 768), own(gate_gain, 768)
    dtb, al, dsk = own(dt_bias, 12), own(a_log, 12), own(d_skip, 12)
    taps_x = jnp.concatenate([cx, cxb[None], jnp.repeat(dsk, 64)[None], jnp.zeros((2, 768), F32)], axis=0)
    taps_bc = jnp.concatenate([conv_bc, conv_bc_bias[None], jnp.zeros((3, 256), F32)], axis=0)
    wide_heads = lambda v: jnp.pad(v, (0, 116))[None]
    heads = jnp.concatenate([wide_heads(dtb), wide_heads(-jnp.exp(al)), wide_heads(dsk), jnp.zeros((5, 128), F32)], axis=0)
    gains = jnp.broadcast_to(gg[None], (8, 768))
    spread_np = np.arange(768)[None, :] // 64 == np.arange(128)[:, None]
    spread, spread_t = spread_np.astype(BF), np.ascontiguousarray(spread_np.T).astype(BF)
    segments = after(segments, near[1])
    cut = jnp.sum((segments == segments[0]).astype(jnp.int32))[None]
    cuts = pair(cut, swap(cut, "c"), "c").reshape(2)

    half = after(half, a_parts[1], a_parts[2], b_ahead, b_back, taps_x, taps_bc, heads, gains, cuts, order, place)
    tokens = [half, swap(half, "c")]
    normed, normed_t, x_raw, bc_raw, dt_raw, w_1, w_maps, gain_rows = project(order, place, a_parts, tokens)

    b_ahead, b_back = after(b_ahead, dt_raw), after(b_back, dt_raw)
    b_parts = [b_own, b_ahead, b_back, turn(b_ahead[:2], "y", 1), turn(b_back[2:], "y", 3)]
    y, st = ssd_forward(cuts, x_raw, bc_raw, dt_raw, taps_x, taps_bc, heads, spread)

    gate, gs, cot_t, sums, w_2 = gate_side(order, place, b_parts, tokens, normed, y, gains)
    sums_c, sums_x = swap(sums, "c"), swap(sums, "xl")
    sums_d = lax.ppermute(sums, ("c", "xl"), [(i, 3 - i) for i in range(4)])
    scaled, gate_low, dy, g_gain = mix([sums, sums_c, sums_x, sums_d], gate, gs, y, gains)

    def exchange(rows):
        diagonal = lax.ppermute(rows[3], ("c", "xl"), [(i, 3 - i) for i in range(4)])
        return rows[0], swap(rows[1], "c"), swap(rows[2], "xl"), diagonal

    out_rows = by_rows(out_kernel, place, [scaled], [w_2], [lambda place: 1], [(HALF, F32)] + [(HALF, BF)] * 3)
    g_zo = outer_pair(normed_t, after(cot_t, out_rows[1]), gate_low, scaled)
    g_zo_z = lax.psum_scatter(g_zo.reshape(1536, 1536), "z", scatter_dimension=0, tiled=True)
    g_zo_y = lax.psum_scatter(g_zo_z, "y", scatter_dimension=0, tiled=True)
    out_rows = exchange(out_rows)
    wide = lambda a: a.astype(F32)
    layer_out = (wide(resid) + ((out_rows[0] + wide(out_rows[1])) + (wide(out_rows[2]) + wide(out_rows[3])))).astype(BF)

    dy = after(dy, g_zo)
    x_low, keep, send, gdt, g_tx, keep_c, send_c, g_hd = ssd_backward(cuts, place, x_raw, bc_raw, dt_raw, dy, y, st, taps_x, taps_bc, heads, spread, spread_t)

    keep, keep_c = keep + swap(after(send, *out_rows[1:]), "c"), keep_c + swap(send_c, "c")
    keep_h = keep_c.astype(BF)
    keep = jnp.concatenate([keep.astype(BF), keep_h, (keep_c - keep_h.astype(F32)).astype(BF)], axis=0)
    small_x = jnp.concatenate([g_tx[:5], g_gain[:1], jnp.zeros((2, 768), F32)], axis=0)
    left = pl.BlockSpec((1024, 512), lambda i, place: (0, 0))
    right = pl.BlockSpec((1024, 256), lambda i, place: (0, 2))
    a_grad = outer_split(outer_z_kernel, place, normed_t, [(x_low, left)], [small_x[:, :512]], 512)
    a_grad = [a_grad[0]] + [turn(a_grad[k], "z", k) for k in (1, 2, 3)]
    far = swap(keep, "xl")
    group = keep.astype(F32) + far.astype(F32)
    bc_low = after(group[:1024].astype(BF), g_zo_z)
    small_s = jnp.concatenate([group[1024:1032] + group[1032:], g_hd], axis=1)
    full = lambda t: (t, fixed(t.shape))
    b_grad = outer_split(outer_side_kernel, place, normed_t, [(x_low, right), full(bc_low), full(gdt)], [small_x[:, 512:], small_s], 384)
    b_first = b_grad[0]
    b_grad = [b_first] + [turn(b_grad[k], "z", k) for k in (1, 2, 3)]
    token_rows = by_rows(token_kernel, place, [after(gate_low, b_first), x_low, gdt], [w_2, w_1, w_1], [lambda place: 0, lambda place: 0, lambda place: 8], [(HALF, F32), (HALF, F32), (SEQ, BF)], 20_000_000_000)
    token_far = swap(after(token_rows[2], *a_grad[1:], *b_grad[1:]), "c")
    pieces = fold(a_grad, b_grad)
    token_far = after(token_far, pieces[1], g_zo_y)
    grad_own = token_rows[0] + wide(token_far[:HALF])
    grad_far = swap((token_rows[1] + wide(token_far[HALF:])).astype(BF), "xl")
    pieces = [pieces[0]] + [turn(pieces[k], "y", k) for k in (1, 2, 3)]

    rows_own, rows_send = mine(bc_low, "c", 0, SEQ)
    bc_own = pair(rows_own, swap(rows_send, "c"), "c")
    bc_own = jnp.concatenate([bc_own[0], bc_own[1]], axis=1)
    bc_own = lax.dynamic_slice_in_dim(bc_own, xl * 256, 256, 0)
    bc_part = lax.dot_general(bc_own, w_maps, (((1,), (1,)), ((), ())), preferred_element_type=F32)
    grad_normed = (grad_own + wide(grad_far)) + bc_part

    keep, send = sum_pieces(place, pieces, g_zo_y)
    keep, send = sum_far(place, after(keep, grad_far), swap(send, "xh"))
    far = swap(send, "c")

    gain_wide = gain_rows[4]
    rw = resid.astype(F32)
    inv = lax.rsqrt(jnp.mean(rw * rw, axis=-1, keepdims=True) + EPS)
    inner = jnp.sum(gain_wide[None, :] * grad_normed * rw, axis=-1, keepdims=True)
    grad_resid = cotangent.astype(F32) + gain_wide[None, :] * grad_normed * inv - rw * (inv * inv * inv) * inner / 1536

    got = pair(keep, far, "c")
    both = lambda rows, at, width: jnp.concatenate([got[0, rows, at : at + width], got[1, rows, at : at + width]], axis=1)
    main, rest = slice(0, 24), slice(24, 32)
    grad_w_x, grad_w_z, grad_w_out_t = both(main, 0, 768), both(main, 896, 768), both(main, 1664, 768)
    grad_w_dt = both(main, 832, 12)
    bc24, conv24 = both(main, 768, 64), both(rest, 768, 64)
    small_wide = both(rest, 0, 768)
    small_heads = both(rest, 832, 12)

    tall = lambda a, b: jnp.sum(a.astype(F32) * b, axis=1)
    pg = tall(w_z, grad_w_z) + tall(w_x, grad_w_x) + tall(w_dt, grad_w_dt)
    pg, pg_send = mine(pg, "xl", 0, 12)
    bc12, bc_send = mine(bc24, "xl", 0, 12)
    far = swap(jnp.concatenate([bc_send, conv24, jnp.pad(pg_send, (0, 116))[None]], axis=0), "xl")
    got = pair(jnp.concatenate([bc12, conv24], axis=0), far[:20], "xl")
    got = got.reshape(2, 20, 2, 64).transpose(1, 2, 0, 3).reshape(20, 256)
    grad_w_bc, grad_conv_bc = got[:12], got[12:]
    grad_pre_gain = (pg + far[20, :12] + tall(w_bc, grad_w_bc)) / pre_gain.astype(F32)
    return (
        layer_out,
        grad_resid,
        grad_pre_gain,
        grad_w_z,
        grad_w_x,
        grad_w_bc,
        grad_w_dt,
        small_wide[:4],
        small_wide[4],
        grad_conv_bc[:4],
        grad_conv_bc[4],
        small_heads[0],
        small_heads[1],
        small_heads[2],
        small_wide[5],
        grad_w_out_t.T,
    )


def solution(mesh):
    fine = Mesh(mesh.devices.reshape(4, 2, 4, 2, 2), ("z", "xh", "y", "c", "xl"))
    dp, tp, every = ("z", "xh", "y", "c"), "xl", ("z", "xh", "y", "c", "xl")
    return jax.shard_map(
        shards,
        mesh=fine,
        in_specs=(P(every, None), P(every, None), P(dp), P(every), P(dp, tp), P(dp, tp), P(every, None), P(dp, tp), P(None, tp), P(tp), P(), P(), P(tp), P(tp), P(tp), P(tp), P(tp, dp)),
        out_specs=(P(every, None), P(every, None), P(every), P(dp, tp), P(dp, tp), P(every, None), P(dp, tp), P(None, tp), P(tp), P(), P(), P(tp), P(tp), P(tp), P(tp), P(tp, dp)),
        check_vma=False,
    )
```

```python
import jax
import jax.numpy as jnp
import numpy as np
from jax import lax
from jax.experimental import pallas as pl
from jax.experimental.pallas import tpu as pltpu
from jax.sharding import Mesh, PartitionSpec as P

EPS = 1e-05
VMEM_LIMIT = 60 * 1024 * 1024
BF = jnp.bfloat16
F32 = jnp.float32
SEQ = 512
HALF = 256
SUB = 128
PAIRS = 2


def mm(a, b):
    return jnp.dot(a, b, preferred_element_type=F32)


def mm_nt(a, b):
    return lax.dot_general(a, b, (((1,), (1,)), ((), ())), preferred_element_type=F32)


def mm_tn(a, b):
    return lax.dot_general(a, b, (((0,), (0,)), ((), ())), preferred_element_type=F32)


def parts(v, count):
    out = []
    for _ in range(count):
        low = v.astype(BF)
        out.append(low)
        v = v - low.astype(F32)
    return out


def split_left(v, m, count=2):
    return sum(mm(p, m) for p in parts(v, count))


def split_right(m, v, count=3):
    return sum(mm(m, p) for p in parts(v, count))


def rows(shape):
    return lax.broadcasted_iota(jnp.int32, shape, 0)


def cols(shape):
    return lax.broadcasted_iota(jnp.int32, shape, 1)


def softplus(v):
    e = jnp.exp(-jnp.abs(v))
    tail = jnp.where(e < 1e-3, e * (1.0 - 0.5 * e), jnp.log(1.0 + e))
    return jnp.maximum(v, 0.0) + tail


def sigmoid(v):
    return 1.0 / (1.0 + jnp.exp(-v))


def same_doc(t, s, cut):
    return (t < cut) == (s < cut)


def conv_masks(cut):
    t = rows((SEQ, SUB))
    return [jnp.where((t >= j) & ((t < cut) | (t - j >= cut)), 1.0, 0.0) for j in (1, 2, 3)]


def conv(v, taps, masks):
    u = taps[4:5] + taps[3:4] * v
    for j in (1, 2, 3):
        u = u + taps[3 - j : 4 - j] * (pltpu.roll(v, j, 0) * masks[j - 1])
    return u


def time_steps(dt_raw, heads, cut):
    dt = softplus(dt_raw + heads[0:1])
    a = dt * heads[1:2]
    tri = jnp.where(rows((HALF, HALF)) >= cols((HALF, HALF)), 1.0, 0.0).astype(BF)
    c = [split_right(tri, a[:HALF]), split_right(tri, a[HALF:])]
    t = rows((HALF, SUB))
    ending = same_doc(t, HALF - 1, cut)
    alive = same_doc(t + HALF, HALF - 1, cut)
    ew = jnp.where(ending, jnp.exp(c[0][HALF - 1 : HALF] - c[0]), 0.0)
    e1 = jnp.where(alive, jnp.exp(c[1]), 0.0)
    return dt, c, ew, e1


def masked_scores(cb, bb, block, cut, lower=True):
    out = {}
    for i, j in ((0, 0), (1, 0), (1, 1)):
        ti, sj = slice(i * SUB, i * SUB + SUB), slice(j * SUB, j * SUB + SUB)
        if lower:
            s = mm_nt(cb[ti], bb[sj])
            t = rows((SUB, SUB)) + (block * HALF + i * SUB)
            r = cols((SUB, SUB)) + (block * HALF + j * SUB)
        else:
            s = mm_nt(bb[sj], cb[ti])
            r = rows((SUB, SUB)) + (block * HALF + j * SUB)
            t = cols((SUB, SUB)) + (block * HALF + i * SUB)
        out[i, j] = jnp.where((t >= r) & same_doc(t, r, cut), s, 0.0)
    return out


def head_lanes(k):
    lane = cols((HALF, SUB))
    return (lane < 64) if k == 0 else (lane >= 64)


def fill_columns(c, ccol_ref, ct_ref):
    for k in (0, 1):
        ct_ref[k] = c[k].T
        for head in range(12):
            ccol_ref[k, head] = jnp.broadcast_to(c[k][:, head : head + 1], (HALF, SUB))


def put_stack(ref, values):
    at = 0
    for v in values:
        for p in parts(v, 2):
            ref[at : at + v.shape[0]] = p
            at += v.shape[0]


def spread_stack(ref, e, heights):
    wide, out, at = mm(ref[...], e), [], 0
    for n in heights:
        out.append(wide[at : at + n] + wide[at + n : at + 2 * n])
        at += 2 * n
    return out


BLOCKS = ((0, 0), (1, 0), (1, 1))


def fwd_kernel(cut_ref, xr_ref, bcr_ref, dtr_ref, tx_ref, tbc_ref, hd_ref, e_ref, y_ref, st_ref):
    cut = cut_ref[pl.program_id(0)]
    masks = conv_masks(cut)
    act = []
    for i in range(2):
        sl = slice(i * SUB, i * SUB + SUB)
        u = conv(bcr_ref[:, sl], tbc_ref[:, sl], masks)
        act.append(parts(u * sigmoid(u), 2))
    (bb, bb_low), (cb, cb_low) = act
    cb3 = jnp.concatenate([cb, cb_low, cb], axis=1)
    bb3 = jnp.concatenate([bb, bb, bb_low], axis=1)
    dt, c, ew, e1 = time_steps(dtr_ref[...], hd_ref[...], cut)
    ct = [c[0].T, c[1].T]
    tw = ew * dt[:HALF]
    scores = [masked_scores(cb3[k * HALF : k * HALF + HALF], bb3[k * HALF : k * HALF + HALF], k, cut) for k in (0, 1)]
    b0t, b0t_low = bb[:HALF].T, bb_low[:HALF].T
    for p in range(6):
        sl = slice(p * SUB, p * SUB + SUB)
        e = e_ref[:, sl]
        u = conv(xr_ref[:, sl], tx_ref[:, sl], masks)
        x = u * sigmoid(u)
        xtf = x * split_left(dt, e)
        xh = xtf.astype(BF)
        xhf = xh.astype(F32)
        xl_turned = pltpu.roll(xtf - xhf, 64, 1).astype(BF)
        skip = tx_ref[5:6, sl] * x
        xw, xw_low = parts(x[:HALF] * split_left(tw, e), 2)
        st = mm(b0t, xw) + (mm(b0t, xw_low) + mm(b0t_low, xw))
        st_ref[0, :, sl] = st
        st, st_low = parts(st, 2)
        carry = (mm(cb[HALF:], st) + (mm(cb[HALF:], st_low) + mm(cb_low[HALF:], st))) * split_left(e1, e)
        for k in (0, 1):
            ys = [[], []]
            for h in (0, 1):
                head = 2 * p + h
                at = slice(k * HALF, k * HALF + HALF)
                xm = jnp.where(head_lanes(h), xh[at], xl_turned[at])
                col = c[k][:, head : head + 1]
                row = ct[k][head : head + 1, :]
                m = {}
                for i, j in ((0, 0), (1, 0), (1, 1)):
                    gap = col[i * SUB : i * SUB + SUB] - row[:, j * SUB : j * SUB + SUB]
                    full = jnp.exp(jnp.minimum(gap, 0.0)) * scores[k][i, j]
                    m[i, j] = parts(full, 2)
                ys[0].append(mm(jnp.concatenate(m[0, 0], axis=1), jnp.concatenate([xm[:SUB], xm[:SUB]], axis=0)))
                wide = [m[1, 0][0], m[1, 1][0], m[1, 0][1], m[1, 1][1]]
                ys[1].append(mm(jnp.concatenate(wide, axis=1), jnp.concatenate([xm, xm], axis=0)))
            for i in (0, 1):
                at = k * HALF + i * SUB
                first = cols((SUB, SUB)) < 64
                y0, y1 = ys[i]
                y = jnp.where(first, y0, y1) + pltpu.roll(jnp.where(first, y1, y0), 64, 1) + skip[at : at + SUB]
                if k == 1:
                    y = y + carry[i * SUB : i * SUB + SUB]
                y_ref[at : at + SUB, sl] = y


def seq_spec(width):
    return pl.BlockSpec((SEQ, width), lambda i: (i, 0))


def whole(shape):
    return pl.BlockSpec(shape, lambda i: (0,) * len(shape))


SMEM = pl.BlockSpec(memory_space=pltpu.SMEM)


def ssd_forward(cut, x_raw, bc_raw, dt_raw, taps_x, taps_bc, heads, spread):
    return pl.pallas_call(
        fwd_kernel,
        grid=(2,),
        in_specs=[SMEM, seq_spec(768), seq_spec(256), seq_spec(128), whole((8, 768)), whole((8, 256)), whole((8, 128)), whole((128, 768))],
        out_specs=[seq_spec(768), pl.BlockSpec((1, 128, 768), lambda i: (i, 0, 0))],
        out_shape=[jax.ShapeDtypeStruct((1024, 768), F32), jax.ShapeDtypeStruct((2, 128, 768), F32)],
        compiler_params=pltpu.CompilerParams(vmem_limit_bytes=VMEM_LIMIT),
        cost_estimate=pl.CostEstimate(flops=4_000_000_000, bytes_accessed=9_000_000, transcendentals=4_000_000),
    )(cut, x_raw, bc_raw, dt_raw, taps_x, taps_bc, heads, spread)


def bwd_kernel(cut_ref, place_ref, xr_ref, bcr_ref, dtr_ref, dy_ref, y_ref, st_ref, tx_ref, tbc_ref, hd_ref, e_ref, et_ref,
               gx_ref, keep_ref, send_ref, gdt_ref, gtx_ref, keepc_ref, sendc_ref, ghd_ref,
               ds_ref, masks_ref, steps_ref, up_ref, ccol_ref, ct_ref, c1t_ref, b0_ref, acc_ref, accb_ref, skip_ref):
    seq = pl.program_id(0)
    cut = cut_ref[seq]
    masks = conv_masks(cut)

    def conv_back(du, v, taps, masks):
        g = taps[3:4] * du
        sums = [jnp.sum(du * v, axis=0, keepdims=True)]
        for j in (1, 2, 3):
            dm = du * masks[j - 1]
            g = g + taps[3 - j : 4 - j] * pltpu.roll(dm, SEQ - j, 0)
            sums.append(jnp.sum(dm * pltpu.roll(v, j, 0), axis=0, keepdims=True))
        return g, [sums[3], sums[2], sums[1], sums[0], jnp.sum(du, axis=0, keepdims=True)]

    @pl.when(seq == 0)
    def _():
        gtx_ref[...] = jnp.zeros_like(gtx_ref)
        keepc_ref[...] = jnp.zeros_like(keepc_ref)
        sendc_ref[...] = jnp.zeros_like(sendc_ref)
        ghd_ref[...] = jnp.zeros_like(ghd_ref)

    act = []
    for i in range(2):
        sl = slice(i * SUB, i * SUB + SUB)
        u = conv(bcr_ref[:, sl], tbc_ref[:, sl], masks)
        act.append((u * sigmoid(u)).astype(BF))
    for j in range(3):
        masks_ref[j] = masks[j]
    bb, cb = act
    dt, c, ew, e1 = time_steps(dtr_ref[...], hd_ref[...], cut)
    fill_columns(c, ccol_ref, ct_ref)
    put_stack(steps_ref, [dt, ew * dt[:HALF], e1, ew])
    blk = lambda a, k: a[k * HALF : k * HALF + HALF]
    for k in (0, 1):
        up = masked_scores(blk(cb, k), blk(bb, k), k, cut, lower=False)
        for n, at in enumerate(BLOCKS):
            up_ref[k, n] = up[at]
    c1t_ref[...] = cb[HALF:].T
    b0_ref[...] = bb[:HALF]
    ds_ref[...] = jnp.zeros_like(ds_ref)
    acc_ref[...] = jnp.zeros_like(acc_ref)
    accb_ref[...] = jnp.zeros_like(accb_ref)
    skip_ref[...] = jnp.zeros_like(skip_ref)

    def one_pair(p, carried):
        sl = pl.ds(pl.multiple_of(p * SUB, SUB), SUB)
        e, et, taps = e_ref[:, sl], et_ref[sl, :], tx_ref[:, sl]
        xr = xr_ref[:, sl]
        pair_masks = [masks_ref[j] for j in range(3)]
        u = conv(xr, taps, pair_masks)
        sg = sigmoid(u)
        x = u * sg
        dtx, twx, e1x, ewx = spread_stack(steps_ref, e, (SEQ, HALF, HALF, HALF))
        xtf = x * dtx
        xt = xtf.astype(BF)
        dy = dy_ref[:, sl]
        dyb = dy.astype(BF)
        dyh = dyb.astype(F32)
        xh = xt.astype(F32)
        xl = (xtf - xh).astype(BF)
        dl_turned = pltpu.roll(dy - dyh, 64, 1).astype(BF)
        xh_turned = pltpu.roll(xh, 64, 1).astype(BF)
        skip = jnp.broadcast_to(jnp.sum(dy * x, axis=0, keepdims=True), (16, SUB))
        stack = parts(dyh * y_ref[:, sl], 2) + parts(dyh * x, 2) + parts(skip, 3)
        wide = mm(jnp.concatenate(stack, axis=0), et)
        acc_ref[0] += wide[0:SEQ] + wide[SEQ : 2 * SEQ]
        acc_ref[1] += wide[2 * SEQ : 3 * SEQ] + wide[3 * SEQ : 4 * SEQ]
        skip_ref[...] += wide[2048:2056] + wide[2064:2072] + wide[2080:2088]
        dxs = []
        for k in (0, 1):
            back = 0.0
            for h in (0, 1):
                head = 2 * p + h
                lanes, none = head_lanes(h), jnp.zeros((), BF)
                dm = jnp.where(lanes, blk(dyb, k), none)
                dm2 = jnp.concatenate([jnp.where(lanes, blk(dyb, k), blk(dl_turned, k)), dm], axis=1)
                xm2 = jnp.concatenate([jnp.where(lanes, blk(xt, k), blk(xh_turned, k)), jnp.where(lanes, blk(xl, k), none)], axis=1)
                row = ct_ref[k, pl.ds(head, 1), :]
                gfull = mm_nt(dm2, xm2)
                mt = {}
                for n, (i, j) in enumerate(BLOCKS):
                    ti, sj = slice(i * SUB, i * SUB + SUB), slice(j * SUB, j * SUB + SUB)
                    decay = jnp.exp(-jnp.abs(ccol_ref[k, head, ti, :] - row[:, sj]))
                    if i == j:
                        decay_t = decay
                    else:
                        decay_t = jnp.exp(-jnp.abs(ccol_ref[k, head, sj, :] - row[:, ti]))
                    ds_ref[k, i + j] += gfull[ti, sj] * decay
                    mt[i, j] = (decay_t * up_ref[k, n]).astype(BF)
                rows0 = jnp.concatenate([mt[0, 0], mt[1, 0]], axis=1)
                rows1 = jnp.concatenate([jnp.zeros((SUB, SUB), BF), mt[1, 1]], axis=1)
                back = back + mm(jnp.concatenate([rows0, rows1], axis=0), dm)
            dxs.append(back)
        st, st_low = parts(st_ref[0, :, sl], 2)
        dcs, dcs_low = parts(dy[HALF:] * e1x, 2)
        accb_ref[0] += mm_nt(dcs, st) + (mm_nt(dcs_low, st) + mm_nt(dcs, st_low))
        dst, dst_low = parts(mm(c1t_ref[...], dcs) + mm(c1t_ref[...], dcs_low), 2)
        dxw = mm(b0_ref[...], dst)
        xw, xw_low = parts(x[:HALF] * twx, 2)
        accb_ref[1] += mm_nt(xw, dst) + (mm_nt(xw_low, dst) + mm_nt(xw, dst_low))
        dx0 = dxs[0] + dxw * ewx
        dxt = jnp.concatenate([dx0, dxs[1]], axis=0)
        wide = mm(jnp.concatenate(parts(x * dxt, 2), axis=0), et)
        acc_ref[2] += wide[:SEQ] + wide[SEQ:]
        dx = dtx * dxt + taps[5:6] * dy
        du = dx * (sg * (1.0 + u * (1.0 - sg)))
        g, sums = conv_back(du, xr, taps, pair_masks)
        gx_ref[:, sl] = g.astype(BF)
        gtx_ref[0:5, sl] += jnp.concatenate(sums, axis=0)
        return carried

    lax.fori_loop(0, 6 // PAIRS, lambda i, x: [one_pair(i * PAIRS + j, x) for j in range(PAIRS)][0], 0)
    sum_y, sum_x, sum_d = acc_ref[0], acc_ref[1], acc_ref[2]
    d_c1, d_b0 = accb_ref[0], accb_ref[1]
    d_b, d_c = [], []
    for k in (0, 1):
        bk, ck = blk(bb, k), blk(cb, k)
        m = {}
        for i, j in ((0, 0), (1, 0), (1, 1)):
            t = rows((SUB, SUB)) + (k * HALF + i * SUB)
            r = cols((SUB, SUB)) + (k * HALF + j * SUB)
            m[i, j] = jnp.where((t >= r) & same_doc(t, r, cut), ds_ref[k, i + j], 0.0).astype(BF)
        lowr = jnp.concatenate([m[1, 0], m[1, 1]], axis=1)
        d_c += [mm(m[0, 0], bk[:SUB]), mm(lowr, bk)]
        d_b += [mm_tn(m[0, 0], ck[:SUB]) + mm_tn(m[1, 0], ck[SUB:]), mm_tn(m[1, 1], ck[SUB:])]
    d_b = jnp.concatenate([jnp.concatenate(d_b[:2], axis=0) + d_b0] + d_b[2:], axis=0)
    d_c = jnp.concatenate(d_c[:2] + [jnp.concatenate(d_c[2:], axis=0) + d_c1], axis=0)
    for i, d in ((0, d_b), (1, d_c)):
        sl = slice(i * SUB, i * SUB + SUB)
        v = bcr_ref[:, sl]
        u = conv(v, tbc_ref[:, sl], masks)
        sg = sigmoid(u)
        g, sums = conv_back(d * (sg * (1.0 + u * (1.0 - sg))), v, tbc_ref[:, sl], masks)

        @pl.when(place_ref[3] == i)
        def _():
            keep_ref[...] = g
            for r, s in enumerate(sums):
                keepc_ref[r : r + 1] += s

        @pl.when(place_ref[3] != i)
        def _():
            send_ref[...] = g
            for r, s in enumerate(sums):
                sendc_ref[r : r + 1] += s

    hd = hd_ref[...]
    w = (sum_y - hd[2:3] * sum_x) - dt * sum_d
    tri = jnp.where((cols((SEQ, SEQ)) >= rows((SEQ, SEQ))) & same_doc(rows((SEQ, SEQ)), cols((SEQ, SEQ)), cut), 1.0, 0.0).astype(BF)
    run = split_right(tri, w)
    d_dt = sum_d + hd[1:2] * run
    gd = d_dt * sigmoid(dtr_ref[...] + hd[0:1])
    gdt_ref[...] = gd.astype(BF)
    ghd_ref[0:1] += jnp.sum(gd, axis=0, keepdims=True)
    ghd_ref[2:3] += skip_ref[0:1]
    ghd_ref[1:2] += jnp.sum(dt * run, axis=0, keepdims=True) * hd[1:2]


def ssd_backward(cut, place, x_raw, bc_raw, dt_raw, dy, y, st, taps_x, taps_bc, heads, spread, spread_t):
    return pl.pallas_call(
        bwd_kernel,
        grid=(2,),
        in_specs=[SMEM, SMEM, seq_spec(768), seq_spec(256), seq_spec(128), seq_spec(768), seq_spec(768),
                  pl.BlockSpec((1, 128, 768), lambda i: (i, 0, 0)), whole((8, 768)), whole((8, 256)), whole((8, 128)), whole((128, 768)), whole((768, 128))],
        out_specs=[seq_spec(768), seq_spec(128), seq_spec(128), seq_spec(128), whole((8, 768)), whole((8, 128)), whole((8, 128)), whole((8, 128))],
        out_shape=[jax.ShapeDtypeStruct((1024, 768), BF), jax.ShapeDtypeStruct((1024, 128), F32), jax.ShapeDtypeStruct((1024, 128), F32), jax.ShapeDtypeStruct((1024, 128), BF),
                   jax.ShapeDtypeStruct((8, 768), F32), jax.ShapeDtypeStruct((8, 128), F32), jax.ShapeDtypeStruct((8, 128), F32), jax.ShapeDtypeStruct((8, 128), F32)],
        scratch_shapes=[
            pltpu.VMEM((2, 3, SUB, SUB), F32),
            pltpu.VMEM((3, SEQ, SUB), F32),
            pltpu.VMEM((5 * SEQ, SUB), BF),
            pltpu.VMEM((2, 3, SUB, SUB), F32),
            pltpu.VMEM((2, 12, HALF, SUB), F32),
            pltpu.VMEM((2, SUB, HALF), F32),
            pltpu.VMEM((SUB, HALF), BF),
            pltpu.VMEM((HALF, SUB), BF),
            pltpu.VMEM((3, SEQ, SUB), F32),
            pltpu.VMEM((2, HALF, SUB), F32),
            pltpu.VMEM((8, SUB), F32),
        ],
        compiler_params=pltpu.CompilerParams(vmem_limit_bytes=VMEM_LIMIT),
        cost_estimate=pl.CostEstimate(flops=12_000_000_000, bytes_accessed=14_000_000, transcendentals=4_000_000),
    )(cut, place, x_raw, bc_raw, dt_raw, dy, y, st, taps_x, taps_bc, heads, spread, spread_t)


def place_blocks(pieces, w_ref, sem, row_of):
    for ref, k, first in pieces:
        for r in range(ref.shape[0]):
            for h in range(2):
                row = pl.multiple_of(row_of(k, first + r, h) * 48, 48)
                pltpu.make_async_copy(ref.at[r, h], w_ref.at[pl.ds(row, 48)], sem).start()


def ring_pieces(refs):
    return list(zip(refs, (0, 1, 3, 2, 2), (0, 0, 0, 0, 2)))


def start_halves(refs, which, buf, sems):
    for k in range(4):
        pltpu.make_async_copy(refs[k // 2].at[k % 2, which], buf.at[k], sems.at[k]).start()


def project_kernel(order_ref, place_ref, *refs):
    a_refs, t_refs = refs[0:5], refs[5:7]
    normed_ref, nt_ref, xr_ref, bc_ref, dt_ref, w_ref, wbc_ref, gain, tok, w_sem, t_sem = refs[7:]
    step = pl.program_id(0)

    @pl.when(step == 0)
    def _():
        z, xh, y = place_ref[0], place_ref[1], place_ref[2]
        start_halves(t_refs, 0, tok, t_sem)

        def row_of(k, r, h):
            return (lax.rem(z - k + 4, 4) * 2 + lax.rem(xh + h, 2)) * 4 + lax.rem(y - r + 4, 4)

        place_blocks(ring_pieces(a_refs), w_ref, w_sem, row_of)
        pltpu.make_async_copy(w_ref, w_ref, w_sem).wait()
        gain[...] = w_ref[:, 1024:1152].astype(F32).T[8:16]
        wbc_ref[...] = w_ref[:, 768:1024]

    pltpu.make_async_copy(t_refs[0].at[0, 0], tok.at[step], t_sem.at[step]).wait()
    wide = tok[step].astype(F32)
    inv = lax.rsqrt(jnp.mean(wide * wide, axis=-1, keepdims=True) + EPS)
    normed = (wide * inv * gain[4:5]).astype(BF)
    normed_ref[...] = normed
    nt_ref[...] = normed.T
    xr_ref[...] = mm(normed, w_ref[:, 0:768])
    bc_ref[...] = mm(normed, w_ref[:, 768:1024])
    dt_ref[...] = jnp.where(cols((HALF, SUB)) < 12, mm(normed, w_ref[:, 1024:1152]), 0.0)


ANY = pl.BlockSpec(memory_space=pl.ANY)


def by_order(width):
    return pl.BlockSpec((HALF, width), lambda i, order, place: (order[i], 0))


def turned():
    return pl.BlockSpec((1536, HALF), lambda i, order, place: (0, order[i]))


def fixed(shape):
    return pl.BlockSpec(shape, lambda i, *_: (0,) * len(shape))


def project(order, place, parts_in, tokens):
    sd = jax.ShapeDtypeStruct
    return pl.pallas_call(
        project_kernel,
        grid_spec=pltpu.PrefetchScalarGridSpec(
            num_scalar_prefetch=2,
            grid=(4,),
            in_specs=[ANY] * 7,
            out_specs=[by_order(1536), turned(), by_order(768), by_order(256), by_order(128), fixed((1536, 1152)), fixed((1536, 256)), fixed((8, 1536))],
            scratch_shapes=[pltpu.VMEM((4, HALF, 1536), BF), pltpu.SemaphoreType.DMA, pltpu.SemaphoreType.DMA((4,))],
        ),
        out_shape=[sd((1024, 1536), BF), sd((1536, 1024), BF), sd((1024, 768), F32), sd((1024, 256), F32), sd((1024, 128), F32), sd((1536, 1152), BF), sd((1536, 256), BF), sd((8, 1536), F32)],
        compiler_params=pltpu.CompilerParams(vmem_limit_bytes=VMEM_LIMIT),
        cost_estimate=pl.CostEstimate(flops=3_700_000_000, bytes_accessed=22_000_000, transcendentals=0),
    )(order, place, *parts_in, *tokens)


def gate_kernel(order_ref, place_ref, b0, b1, b2, b3, b4, c0, c1, normed_ref, y_ref, gg_ref, gate_ref, gs_ref, cot_ref, s_ref, w_ref, buf, w_sem, t_sem):
    step = pl.program_id(0)

    @pl.when(step == 0)
    def _():
        z, xh, y = place_ref[0], place_ref[1], place_ref[2]
        start_halves((c0, c1), 1, buf, t_sem)

        def row_of(k, r, h):
            return (lax.rem(z - r + 4, 4) * 2 + lax.rem(xh + h, 2)) * 4 + lax.rem(y - k + 4, 4)

        place_blocks(ring_pieces((b0, b1, b2, b3, b4)), w_ref, w_sem, row_of)
        pltpu.make_async_copy(w_ref, w_ref, w_sem).wait()

    pltpu.make_async_copy(c0.at[0, 1], buf.at[step], t_sem.at[step]).wait()
    cot = buf[step]
    cot_ref[...] = cot.T
    gate = mm(normed_ref[...], w_ref[:, 0:768])
    gs = mm(cot, w_ref[:, 768:1536])
    gate_ref[...] = gate
    gs_ref[...] = gs
    mixed = y_ref[...] * (gate * sigmoid(gate))
    sq = jnp.sum(mixed * mixed, axis=-1, keepdims=True)
    cr = jnp.sum((gs * gg_ref[0:1]) * mixed, axis=-1, keepdims=True)
    lane = cols((HALF, SUB))
    s_ref[...] = jnp.where(lane == 0, sq, jnp.where(lane == 1, cr, 0.0)).T[0:8]


def gate_side(order, place, parts_in, cots, normed, y, gg):
    sd = jax.ShapeDtypeStruct
    return pl.pallas_call(
        gate_kernel,
        grid_spec=pltpu.PrefetchScalarGridSpec(
            num_scalar_prefetch=2,
            grid=(4,),
            in_specs=[ANY] * 7 + [by_order(1536), by_order(768), fixed((8, 768))],
            out_specs=[by_order(768), by_order(768), turned(), pl.BlockSpec((8, HALF), lambda i, order, place: (0, order[i])), fixed((1536, 1536))],
            scratch_shapes=[pltpu.VMEM((4, HALF, 1536), BF), pltpu.SemaphoreType.DMA, pltpu.SemaphoreType.DMA((4,))],
        ),
        out_shape=[sd((1024, 768), F32), sd((1024, 768), F32), sd((1536, 1024), BF), sd((8, 1024), F32), sd((1536, 1536), BF)],
        compiler_params=pltpu.CompilerParams(vmem_limit_bytes=VMEM_LIMIT),
        cost_estimate=pl.CostEstimate(flops=4_900_000_000, bytes_accessed=30_000_000, transcendentals=800_000),
    )(order, place, *parts_in, *cots, normed, y, gg)


MIX, OUT, OUTER = 4, 6, 4


def middle_kernel(place_ref, s0, s1, s2, s3, gate_ref, gs_ref, y_ref, gg_ref, w_ref, n_ref, c_ref,
                  low_ref, dy_ref, gain_ref, own_ref, core_ref, xl_ref, both_ref, grad_ref, scaled, gated):
    step = pl.program_id(0)

    @pl.when(step < MIX)
    def _():
        sums = ((s0[...] + s1[...]) + (s2[...] + s3[...])).T
        inv = lax.rsqrt(sums[:, 0:1] / 3072 + EPS)
        corr = inv * inv * inv * (sums[:, 1:2] / 3072)
        gate, gs, y, gg = gate_ref[...], gs_ref[...], y_ref[...], gg_ref[0:1]
        sg = sigmoid(gate)
        act = gate * sg
        mixed = y * act
        normal = mixed * inv
        at = pl.ds(pl.multiple_of(step * HALF, HALF), HALF)
        scaled[at] = (normal * gg).astype(BF)
        gm = gs * gg * inv - mixed * corr
        low = (gm * y * (sg * (1.0 + gate * (1.0 - sg)))).astype(BF)
        gated[at] = low
        low_ref[...] = low
        dy_ref[...] = gm * act

        @pl.when(step == 0)
        def _():
            gain_ref[...] = jnp.zeros_like(gain_ref)

        gain_ref[0:1] += jnp.sum(gs * normal, axis=0, keepdims=True)

    @pl.when((step >= MIX) & (step < MIX + OUT))
    def _():
        rows_out(place_ref, mm_nt(scaled[...], w_ref[...]), [own_ref, core_ref, xl_ref, both_ref])

    @pl.when(step >= MIX + OUT)
    def _():
        for at, a_ref, b_ref in ((0, n_ref, gated), (768, c_ref, scaled)):
            r = mm(a_ref[...], b_ref[...]).astype(BF)
            for yi in range(4):
                for xi in range(2):
                    row = (xi * 4 + yi) * 48
                    grad_ref[yi, xi * 48 : xi * 48 + 48, at : at + 768] = r[row : row + 48]


def middle(place, sums, gate, gs, y, gg, w_2, normed_t, cot_t):
    sd = jax.ShapeDtypeStruct
    mix_at = lambda i: jnp.minimum(i, MIX - 1)
    out_at = lambda i: jnp.clip(i - MIX, 0, OUT - 1)
    outer_at = lambda i: jnp.maximum(i - MIX - OUT, 0)
    tokens = pl.BlockSpec((HALF, 768), lambda i, place: (mix_at(i), 0))
    chunk = pl.BlockSpec((384, 1024), lambda i, place: (outer_at(i), 0))
    rows_spec = pl.BlockSpec((HALF, 256), lambda i, place: (0, out_at(i)))
    return pl.pallas_call(
        middle_kernel,
        grid_spec=pltpu.PrefetchScalarGridSpec(
            num_scalar_prefetch=1,
            grid=(MIX + OUT + OUTER,),
            in_specs=[pl.BlockSpec((8, HALF), lambda i, place: (0, mix_at(i)))] * 4
            + [tokens] * 3
            + [fixed((8, 768)), pl.BlockSpec((256, 768), lambda i, place: (out_at(i), 1)), chunk, chunk],
            out_specs=[tokens, tokens, fixed((8, 768))] + [rows_spec] * 4 + [pl.BlockSpec((4, 96, 1536), lambda i, place: (outer_at(i), 0, 0))],
            scratch_shapes=[pltpu.VMEM((1024, 768), BF), pltpu.VMEM((1024, 768), BF)],
        ),
        out_shape=[sd((1024, 768), BF), sd((1024, 768), F32), sd((8, 768), F32), sd((HALF, 1536), F32)]
        + [sd((HALF, 1536), BF)] * 3
        + [sd((16, 96, 1536), BF)],
        compiler_params=pltpu.CompilerParams(vmem_limit_bytes=VMEM_LIMIT),
        cost_estimate=pl.CostEstimate(flops=7_300_000_000, bytes_accessed=30_000_000, transcendentals=800_000),
    )(place, *sums, gate, gs, y, gg, w_2, normed_t, cot_t)


def outer_z_kernel(place_ref, n_ref, g_ref, small_ref, *out):
    step = pl.program_id(0)
    y = place_ref[2]
    r = mm(n_ref[...], g_ref[...]).astype(BF)
    small = small_ref[...].astype(BF)
    for k in range(4):

        @pl.when(step == k)
        def _():
            for yi in range(4):
                to = lax.rem(yi - y + 4, 4)
                for xi in range(2):
                    at = (xi * 4 + yi) * 48
                    out[k][to, xi * 48 : xi * 48 + 48] = r[at : at + 48]
                out[k][to, 96:104] = small


def outer_side_kernel(place_ref, n_ref, g_ref, m_ref, d_ref, small_ref, maps_ref, *out):
    step = pl.program_id(0)
    y, xl = place_ref[2], place_ref[4]

    def columns(maps, steps):
        lane = cols(maps.shape)
        maps = jnp.where(xl == 0, maps, pltpu.roll(maps, 64, 1))
        return jnp.where(lane < 64, maps, pltpu.roll(steps, 64, 1)).astype(BF)

    n = n_ref[...]
    r = [mm(n, g_ref[...]).astype(BF), columns(mm(n, m_ref[...]), mm(n, d_ref[...]))]
    small = [small_ref[...].astype(BF), columns(maps_ref[:, 0:128], maps_ref[:, 128:256])]
    for k in range(4):

        @pl.when(step == k)
        def _():
            for part, lanes in ((0, slice(0, 256)), (1, slice(256, 384))):
                for yi in range(4):
                    to = lax.rem(yi - y + 4, 4)
                    for xi in range(2):
                        at = (xi * 4 + yi) * 48
                        out[k][to, xi * 48 : xi * 48 + 48, lanes] = r[part][at : at + 48]
                    out[k][to, 96:104, lanes] = small[part]


def outer_split(kernel, place, normed_t, grads, smalls, width):
    return pl.pallas_call(
        kernel,
        grid_spec=pltpu.PrefetchScalarGridSpec(
            num_scalar_prefetch=1,
            grid=(4,),
            in_specs=[pl.BlockSpec((384, 1024), lambda i, place: (lax.rem(place[0] + i, 4), 0))] + [spec for _, spec in grads] + [fixed(t.shape) for t in smalls],
            out_specs=[fixed((4, 104, width))] * 4,
        ),
        out_shape=[jax.ShapeDtypeStruct((4, 104, width), BF)] * 4,
        compiler_params=pltpu.CompilerParams(vmem_limit_bytes=VMEM_LIMIT),
        cost_estimate=pl.CostEstimate(flops=2 * 1024 * 1536 * width, bytes_accessed=5_000_000, transcendentals=0),
    )(place, normed_t, *[g for g, _ in grads], *smalls)


def fold_kernel(*refs):
    for parts4, lanes in ((refs[0:4], slice(0, 512)), (refs[4:8], slice(512, 896))):
        for k in range(4):
            near = parts4[1][k].astype(F32) + parts4[3][k].astype(F32)
            refs[8 + k][:, lanes] = ((parts4[0][k].astype(F32) + parts4[2][k].astype(F32)) + near).astype(BF)


def fold(a_parts, b_parts):
    vmem = pl.BlockSpec(memory_space=pltpu.VMEM)
    return pl.pallas_call(
        fold_kernel,
        in_specs=[vmem] * 8,
        out_specs=[vmem] * 4,
        out_shape=[jax.ShapeDtypeStruct((104, 896), BF)] * 4,
        compiler_params=pltpu.CompilerParams(vmem_limit_bytes=VMEM_LIMIT),
        cost_estimate=pl.CostEstimate(flops=1, bytes_accessed=1, transcendentals=0),
    )(*a_parts, *b_parts)


def rows_out(place_ref, total, out):
    for base in range(4):

        @pl.when(place_ref[3] * 2 + place_ref[4] == base)
        def _():
            for ref, at in zip(out, (base, base ^ 2, base ^ 1, base ^ 3)):
                ref[...] = total[at * HALF : at * HALF + HALF].astype(ref.dtype)


def token_kernel(place_ref, g_ref, x_ref, d_ref, wz_ref, wx_ref, wd_ref, own_ref, mate_ref, send_ref):
    total = mm_nt(g_ref[...], wz_ref[...]) + mm_nt(x_ref[...], wx_ref[...]) + mm_nt(d_ref[...], wd_ref[...])
    rows_out(place_ref, total, [own_ref, send_ref.at[0:HALF], mate_ref, send_ref.at[HALF:SEQ]])


def by_rows(kernel, place, tokens, weights, places, outs, work=1):
    columns = lambda at: lambda i, place: (i, at(place))
    return pl.pallas_call(
        kernel,
        grid_spec=pltpu.PrefetchScalarGridSpec(
            num_scalar_prefetch=1,
            grid=(6,),
            in_specs=[fixed(t.shape) for t in tokens] + [pl.BlockSpec((256, t.shape[1]), columns(at)) for t, at in zip(tokens, places)],
            out_specs=[pl.BlockSpec((n, 256), lambda i, place: (0, i)) for n, _ in outs],
        ),
        out_shape=[jax.ShapeDtypeStruct((n, 1536), t) for n, t in outs],
        compiler_params=pltpu.CompilerParams(vmem_limit_bytes=VMEM_LIMIT),
        cost_estimate=pl.CostEstimate(flops=work, bytes_accessed=1, transcendentals=0),
    )(place, *tokens, *weights)


def sum_pieces_kernel(place_ref, p0, p1, p2, p3, zo_ref, keep_ref, send_ref):
    total = (p0[...].astype(F32) + p2[...].astype(F32)) + (p1[...].astype(F32) + p3[...].astype(F32))
    small = total[96:104].astype(BF)
    send_ref[48:56, 0:896] = small
    keep_ref[48:56, 0:896] = small.astype(F32)
    for xh in (0, 1):

        @pl.when(place_ref[1] == xh)
        def _():
            keep_ref[0:48, 0:896] = total[xh * 48 : xh * 48 + 48]
            send_ref[0:48, 0:896] = total[48 - xh * 48 : 96 - xh * 48].astype(BF)

    for xh in (0, 1):

        @pl.when(place_ref[1] == xh)
        def _():
            keep_ref[0:48, 896:2432] = zo_ref[xh * 48 : xh * 48 + 48].astype(F32)
            send_ref[0:48, 896:2432] = zo_ref[48 - xh * 48 : 96 - xh * 48]

    keep_ref[48:56, 896:2432] = jnp.zeros((8, 1536), F32)
    send_ref[48:56, 896:2432] = jnp.zeros((8, 1536), BF)


def sum_far_kernel(place_ref, own_ref, far_ref, keep_ref, send_ref):
    total = own_ref[...] + far_ref[...].astype(F32)
    keep_ref[24:32] = total[48:56]
    send_ref[24:32] = total[48:56]
    for core in (0, 1):

        @pl.when(place_ref[3] == core)
        def _():
            keep_ref[0:24] = total[core * 24 : core * 24 + 24]
            send_ref[0:24] = total[24 - core * 24 : 48 - core * 24]


def whole_call(kernel, place, arrays, shapes):
    vmem = pl.BlockSpec(memory_space=pltpu.VMEM)
    return pl.pallas_call(
        kernel,
        in_specs=[SMEM] + [vmem] * len(arrays),
        out_specs=[vmem] * len(shapes),
        out_shape=shapes,
        compiler_params=pltpu.CompilerParams(vmem_limit_bytes=VMEM_LIMIT),
        cost_estimate=pl.CostEstimate(flops=1, bytes_accessed=1, transcendentals=0),
    )(place, *arrays)


def sum_pieces(place, pieces, zo):
    shapes = [jax.ShapeDtypeStruct((56, 2432), F32), jax.ShapeDtypeStruct((56, 2432), BF)]
    return whole_call(sum_pieces_kernel, place, [*pieces, zo], shapes)


def sum_far(place, own, far):
    return whole_call(sum_far_kernel, place, [own, far], [jax.ShapeDtypeStruct((32, 2432), F32)] * 2)


def after_kernel(x_ref, *refs):
    pass


def after(x, *deps):
    return pl.pallas_call(
        after_kernel,
        in_specs=[ANY] * (1 + len(deps)),
        out_specs=ANY,
        out_shape=jax.ShapeDtypeStruct(x.shape, x.dtype),
        input_output_aliases={0: 0},
    )(x, *deps)


def swap(a, axis):
    return lax.ppermute(a, axis, [(0, 1), (1, 0)])


def turn(a, axis, k):
    return lax.ppermute(a, axis, [(i, (i + k) % 4) for i in range(4)])


def pair(own, other, axis):
    first = lax.axis_index(axis) == 0
    return jnp.stack([jnp.where(first, own, other), jnp.where(first, other, own)])


def mine(a, axis, dim, size):
    i = lax.axis_index(axis)
    return (
        lax.dynamic_slice_in_dim(a, i * size, size, dim),
        lax.dynamic_slice_in_dim(a, (1 - i) * size, size, dim),
    )


def turns(a, axis):
    return [a] + [turn(a, axis, k) for k in (1, 2, 3)]


def shards(resid, cotangent, segments, pre_gain, w_z, w_x, w_bc, w_dt, conv_x, conv_x_bias, conv_bc, conv_bc_bias, dt_bias, a_log, d_skip, gate_gain, w_out):
    core, xl = lax.axis_index("c"), lax.axis_index("xl")
    place = jnp.stack([lax.axis_index("z"), lax.axis_index("xh"), lax.axis_index("y"), core, xl])
    base = core * 2 + xl
    order = jnp.stack([core * 2, core * 2 + 1, 2 - core * 2, 3 - core * 2])

    own_bc = jnp.concatenate([w_bc, pre_gain[:, None], jnp.zeros((12, 127), BF)], axis=1)
    keep_x, send_x = mine(w_x, "c", 1, 768)
    keep_dt, send_dt = mine(w_dt, "c", 1, 12)
    bc_x, bc_c = swap(own_bc, "xl"), swap(own_bc, "c")
    bc_d = lax.ppermute(own_bc, ("c", "xl"), [(i, 3 - i) for i in range(4)])
    got = swap(jnp.concatenate([send_x, send_dt], axis=1), "c")
    bc48 = pair(pair(own_bc, bc_x, "xl"), pair(bc_c, bc_d, "xl"), "c").reshape(48, 384)
    xdt = pair(jnp.concatenate([keep_x, keep_dt], axis=1), got, "c").reshape(48, 780)
    first = jnp.concatenate([xdt[:, :768], bc48[:, :256], xdt[:, 768:], bc48[:, 256:372]], axis=1)
    first_far = swap(first, "xh")
    first = jnp.stack([first, first_far])

    keep_z, send_z = mine(w_z, "c", 1, 768)
    keep_o, send_o = mine(w_out.T, "c", 1, 768)
    got = swap(jnp.concatenate([send_z, send_o], axis=1), "c")
    second = pair(jnp.concatenate([keep_z, keep_o], axis=1), got, "c").reshape(48, 1536)
    second = jnp.stack([second, swap(second, "xh")])

    half = lax.all_gather(jnp.stack([resid, cotangent]), "xl", axis=0, tiled=False)
    near_x, near = turns(first, "y"), turns(second, "z")
    b_own = jnp.stack(near)
    b_ahead, b_back = turn(b_own, "y", 1), turn(b_own, "y", 3)
    a_own = after(jnp.stack(near_x), *near[1:])
    a_ahead, a_back = turn(a_own, "z", 1), turn(a_own, "z", 3)
    a_parts = [a_own, a_ahead, a_back, turn(after(a_ahead[:2], b_ahead, b_back), "z", 1), turn(after(a_back[2:], b_ahead, b_back), "z", 3)]

    def own(a, size):
        return mine(a, "c", a.ndim - 1, size)[0]

    cx, cxb, gg = own(conv_x, 768), own(conv_x_bias, 768), own(gate_gain, 768)
    dtb, al, dsk = own(dt_bias, 12), own(a_log, 12), own(d_skip, 12)
    taps_x = jnp.concatenate([cx, cxb[None], jnp.repeat(dsk, 64)[None], jnp.zeros((2, 768), F32)], axis=0)
    taps_bc = jnp.concatenate([conv_bc, conv_bc_bias[None], jnp.zeros((3, 256), F32)], axis=0)
    wide_heads = lambda v: jnp.pad(v, (0, 116))[None]
    heads = jnp.concatenate([wide_heads(dtb), wide_heads(-jnp.exp(al)), wide_heads(dsk), jnp.zeros((5, 128), F32)], axis=0)
    gains = jnp.broadcast_to(gg[None], (8, 768))
    spread_np = np.arange(768)[None, :] // 64 == np.arange(128)[:, None]
    spread, spread_t = spread_np.astype(BF), np.ascontiguousarray(spread_np.T).astype(BF)
    segments = after(segments, near[1])
    cut = jnp.sum((segments == segments[0]).astype(jnp.int32))[None]
    cuts = pair(cut, swap(cut, "c"), "c").reshape(2)

    half = after(half, a_parts[1], a_parts[2], b_ahead, b_back, taps_x, taps_bc, heads, gains, cuts, order, place)
    tokens = [half, swap(half, "c")]
    normed, normed_t, x_raw, bc_raw, dt_raw, w_1, w_maps, gain_rows = project(order, place, a_parts, tokens)

    b_ahead, b_back = after(b_ahead, dt_raw), after(b_back, dt_raw)
    b_parts = [b_own, b_ahead, b_back, turn(b_ahead[:2], "y", 1), turn(b_back[2:], "y", 3)]
    y, st = ssd_forward(cuts, x_raw, bc_raw, dt_raw, taps_x, taps_bc, heads, spread)

    gate, gs, cot_t, sums, w_2 = gate_side(order, place, b_parts, tokens, normed, y, gains)
    sums_c, sums_x = swap(sums, "c"), swap(sums, "xl")
    sums_d = lax.ppermute(sums, ("c", "xl"), [(i, 3 - i) for i in range(4)])
    gate_low, dy, g_gain, *out_rows, g_zo = middle(place, [sums, sums_c, sums_x, sums_d], gate, gs, y, gains, w_2, normed_t, cot_t)

    def exchange(rows):
        diagonal = lax.ppermute(rows[3], ("c", "xl"), [(i, 3 - i) for i in range(4)])
        return rows[0], swap(rows[1], "c"), swap(rows[2], "xl"), diagonal

    g_zo_z = lax.psum_scatter(g_zo.reshape(1536, 1536), "z", scatter_dimension=0, tiled=True)
    g_zo_y = lax.psum_scatter(g_zo_z, "y", scatter_dimension=0, tiled=True)
    out_rows = exchange(out_rows)
    wide = lambda a: a.astype(F32)
    layer_out = (wide(resid) + ((out_rows[0] + wide(out_rows[1])) + (wide(out_rows[2]) + wide(out_rows[3])))).astype(BF)

    x_low, keep, send, gdt, g_tx, keep_c, send_c, g_hd = ssd_backward(cuts, place, x_raw, bc_raw, dt_raw, dy, y, st, taps_x, taps_bc, heads, spread, spread_t)

    keep, keep_c = keep + swap(after(send, *out_rows[1:]), "c"), keep_c + swap(send_c, "c")
    keep_h = keep_c.astype(BF)
    keep = jnp.concatenate([keep.astype(BF), keep_h, (keep_c - keep_h.astype(F32)).astype(BF)], axis=0)
    small_x = jnp.concatenate([g_tx[:5], g_gain[:1], jnp.zeros((2, 768), F32)], axis=0)
    left = pl.BlockSpec((1024, 512), lambda i, place: (0, 0))
    right = pl.BlockSpec((1024, 256), lambda i, place: (0, 2))
    a_grad = outer_split(outer_z_kernel, place, normed_t, [(x_low, left)], [small_x[:, :512]], 512)
    a_grad = [a_grad[0]] + [turn(a_grad[k], "z", k) for k in (1, 2, 3)]
    far = swap(keep, "xl")
    group = keep.astype(F32) + far.astype(F32)
    bc_low = after(group[:1024].astype(BF), g_zo_z)
    small_s = jnp.concatenate([group[1024:1032] + group[1032:], g_hd], axis=1)
    full = lambda t: (t, fixed(t.shape))
    b_grad = outer_split(outer_side_kernel, place, normed_t, [(x_low, right), full(bc_low), full(gdt)], [small_x[:, 512:], small_s], 384)
    b_first = b_grad[0]
    b_grad = [b_first] + [turn(b_grad[k], "z", k) for k in (1, 2, 3)]
    token_rows = by_rows(token_kernel, place, [after(gate_low, b_first), x_low, gdt], [w_2, w_1, w_1], [lambda place: 0, lambda place: 0, lambda place: 8], [(HALF, F32), (HALF, F32), (SEQ, BF)], 20_000_000_000)
    token_far = swap(after(token_rows[2], *a_grad[1:], *b_grad[1:]), "c")
    pieces = fold(a_grad, b_grad)
    token_far = after(token_far, pieces[1], g_zo_y)
    grad_own = token_rows[0] + wide(token_far[:HALF])
    grad_far = swap((token_rows[1] + wide(token_far[HALF:])).astype(BF), "xl")
    pieces = [pieces[0]] + [turn(pieces[k], "y", k) for k in (1, 2, 3)]

    rows_own, rows_send = mine(bc_low, "c", 0, SEQ)
    bc_own = pair(rows_own, swap(rows_send, "c"), "c")
    bc_own = jnp.concatenate([bc_own[0], bc_own[1]], axis=1)
    bc_own = lax.dynamic_slice_in_dim(bc_own, xl * 256, 256, 0)
    bc_part = lax.dot_general(bc_own, w_maps, (((1,), (1,)), ((), ())), preferred_element_type=F32)
    grad_normed = (grad_own + wide(grad_far)) + bc_part

    keep, send = sum_pieces(place, pieces, g_zo_y)
    keep, send = sum_far(place, after(keep, grad_far), swap(send, "xh"))
    far = swap(send, "c")

    gain_wide = gain_rows[4]
    rw = resid.astype(F32)
    inv = lax.rsqrt(jnp.mean(rw * rw, axis=-1, keepdims=True) + EPS)
    inner = jnp.sum(gain_wide[None, :] * grad_normed * rw, axis=-1, keepdims=True)
    grad_resid = cotangent.astype(F32) + gain_wide[None, :] * grad_normed * inv - rw * (inv * inv * inv) * inner / 1536

    got = pair(keep, far, "c")
    both = lambda rows, at, width: jnp.concatenate([got[0, rows, at : at + width], got[1, rows, at : at + width]], axis=1)
    main, rest = slice(0, 24), slice(24, 32)
    grad_w_x, grad_w_z, grad_w_out_t = both(main, 0, 768), both(main, 896, 768), both(main, 1664, 768)
    grad_w_dt = both(main, 832, 12)
    bc24, conv24 = both(main, 768, 64), both(rest, 768, 64)
    small_wide = both(rest, 0, 768)
    small_heads = both(rest, 832, 12)

    tall = lambda a, b: jnp.sum(a.astype(F32) * b, axis=1)
    pg = tall(w_z, grad_w_z) + tall(w_x, grad_w_x) + tall(w_dt, grad_w_dt)
    pg, pg_send = mine(pg, "xl", 0, 12)
    bc12, bc_send = mine(bc24, "xl", 0, 12)
    far = swap(jnp.concatenate([bc_send, conv24, jnp.pad(pg_send, (0, 116))[None]], axis=0), "xl")
    got = pair(jnp.concatenate([bc12, conv24], axis=0), far[:20], "xl")
    got = got.reshape(2, 20, 2, 64).transpose(1, 2, 0, 3).reshape(20, 256)
    grad_w_bc, grad_conv_bc = got[:12], got[12:]
    grad_pre_gain = (pg + far[20, :12] + tall(w_bc, grad_w_bc)) / pre_gain.astype(F32)
    return (
        layer_out,
        grad_resid,
        grad_pre_gain,
        grad_w_z,
        grad_w_x,
        grad_w_bc,
        grad_w_dt,
        small_wide[:4],
        small_wide[4],
        grad_conv_bc[:4],
        grad_conv_bc[4],
        small_heads[0],
        small_heads[1],
        small_heads[2],
        small_wide[5],
        grad_w_out_t.T,
    )


def solution(mesh):
    fine = Mesh(mesh.devices.reshape(4, 2, 4, 2, 2), ("z", "xh", "y", "c", "xl"))
    dp, tp, every = ("z", "xh", "y", "c"), "xl", ("z", "xh", "y", "c", "xl")
    return jax.shard_map(
        shards,
        mesh=fine,
        in_specs=(P(every, None), P(every, None), P(dp), P(every), P(dp, tp), P(dp, tp), P(every, None), P(dp, tp), P(None, tp), P(tp), P(), P(), P(tp), P(tp), P(tp), P(tp), P(tp, dp)),
        out_specs=(P(every, None), P(every, None), P(every), P(dp, tp), P(dp, tp), P(every, None), P(dp, tp), P(None, tp), P(tp), P(), P(), P(tp), P(tp), P(tp), P(tp), P(tp, dp)),
        check_vma=False,
    )
```

```python
import jax
import jax.numpy as jnp
import numpy as np
from jax import lax
from jax.experimental import pallas as pl
from jax.experimental.pallas import tpu as pltpu
from jax.sharding import Mesh, PartitionSpec as P

EPS = 1e-05
VMEM_LIMIT = 60 * 1024 * 1024
BF = jnp.bfloat16
F32 = jnp.float32
SEQ = 512
HALF = 256
SUB = 128
PAIRS = 2


def mm(a, b):
    return jnp.dot(a, b, preferred_element_type=F32)


def mm_nt(a, b):
    return lax.dot_general(a, b, (((1,), (1,)), ((), ())), preferred_element_type=F32)


def mm_tn(a, b):
    return lax.dot_general(a, b, (((0,), (0,)), ((), ())), preferred_element_type=F32)


def parts(v, count):
    out = []
    for _ in range(count):
        low = v.astype(BF)
        out.append(low)
        v = v - low.astype(F32)
    return out


def split_left(v, m, count=2):
    return sum(mm(p, m) for p in parts(v, count))


def split_right(m, v, count=3):
    return sum(mm(m, p) for p in parts(v, count))


def rows(shape):
    return lax.broadcasted_iota(jnp.int32, shape, 0)


def cols(shape):
    return lax.broadcasted_iota(jnp.int32, shape, 1)


def softplus(v):
    e = jnp.exp(-jnp.abs(v))
    tail = jnp.where(e < 1e-3, e * (1.0 - 0.5 * e), jnp.log(1.0 + e))
    return jnp.maximum(v, 0.0) + tail


def sigmoid(v):
    return 1.0 / (1.0 + jnp.exp(-v))


def same_doc(t, s, cut):
    return (t < cut) == (s < cut)


def conv_masks(cut):
    t = rows((SEQ, SUB))
    return [jnp.where((t >= j) & ((t < cut) | (t - j >= cut)), 1.0, 0.0) for j in (1, 2, 3)]


def conv(v, taps, masks):
    u = taps[4:5] + taps[3:4] * v
    for j in (1, 2, 3):
        u = u + taps[3 - j : 4 - j] * (pltpu.roll(v, j, 0) * masks[j - 1])
    return u


def time_steps(dt_raw, heads, cut):
    dt = softplus(dt_raw + heads[0:1])
    a = dt * heads[1:2]
    tri = jnp.where(rows((HALF, HALF)) >= cols((HALF, HALF)), 1.0, 0.0).astype(BF)
    c = [split_right(tri, a[:HALF]), split_right(tri, a[HALF:])]
    t = rows((HALF, SUB))
    ending = same_doc(t, HALF - 1, cut)
    alive = same_doc(t + HALF, HALF - 1, cut)
    ew = jnp.where(ending, jnp.exp(c[0][HALF - 1 : HALF] - c[0]), 0.0)
    e1 = jnp.where(alive, jnp.exp(c[1]), 0.0)
    return dt, c, ew, e1


def masked_scores(cb, bb, block, cut, lower=True):
    out = {}
    for i, j in ((0, 0), (1, 0), (1, 1)):
        ti, sj = slice(i * SUB, i * SUB + SUB), slice(j * SUB, j * SUB + SUB)
        if lower:
            s = mm_nt(cb[ti], bb[sj])
            t = rows((SUB, SUB)) + (block * HALF + i * SUB)
            r = cols((SUB, SUB)) + (block * HALF + j * SUB)
        else:
            s = mm_nt(bb[sj], cb[ti])
            r = rows((SUB, SUB)) + (block * HALF + j * SUB)
            t = cols((SUB, SUB)) + (block * HALF + i * SUB)
        out[i, j] = jnp.where((t >= r) & same_doc(t, r, cut), s, 0.0)
    return out


def head_lanes(k):
    lane = cols((HALF, SUB))
    return (lane < 64) if k == 0 else (lane >= 64)


def fill_columns(c, ccol_ref, ct_ref):
    for k in (0, 1):
        ct_ref[k] = c[k].T
        for head in range(12):
            ccol_ref[k, head] = jnp.broadcast_to(c[k][:, head : head + 1], (HALF, SUB))


def put_stack(ref, values):
    at = 0
    for v in values:
        for p in parts(v, 2):
            ref[at : at + v.shape[0]] = p
            at += v.shape[0]


def spread_stack(ref, e, heights):
    wide, out, at = mm(ref[...], e), [], 0
    for n in heights:
        out.append(wide[at : at + n] + wide[at + n : at + 2 * n])
        at += 2 * n
    return out


BLOCKS = ((0, 0), (1, 0), (1, 1))


def fwd_kernel(cut_ref, xr_ref, bcr_ref, dtr_ref, tx_ref, tbc_ref, hd_ref, e_ref, y_ref, st_ref):
    cut = cut_ref[pl.program_id(0)]
    masks = conv_masks(cut)
    act = []
    for i in range(2):
        sl = slice(i * SUB, i * SUB + SUB)
        u = conv(bcr_ref[:, sl], tbc_ref[:, sl], masks)
        act.append(parts(u * sigmoid(u), 2))
    (bb, bb_low), (cb, cb_low) = act
    cb3 = jnp.concatenate([cb, cb_low, cb], axis=1)
    bb3 = jnp.concatenate([bb, bb, bb_low], axis=1)
    dt, c, ew, e1 = time_steps(dtr_ref[...], hd_ref[...], cut)
    ct = [c[0].T, c[1].T]
    tw = ew * dt[:HALF]
    scores = [masked_scores(cb3[k * HALF : k * HALF + HALF], bb3[k * HALF : k * HALF + HALF], k, cut) for k in (0, 1)]
    b0t, b0t_low = bb[:HALF].T, bb_low[:HALF].T
    for p in range(6):
        sl = slice(p * SUB, p * SUB + SUB)
        e = e_ref[:, sl]
        u = conv(xr_ref[:, sl], tx_ref[:, sl], masks)
        x = u * sigmoid(u)
        xtf = x * split_left(dt, e)
        xh = xtf.astype(BF)
        xhf = xh.astype(F32)
        xl_turned = pltpu.roll(xtf - xhf, 64, 1).astype(BF)
        skip = tx_ref[5:6, sl] * x
        xw, xw_low = parts(x[:HALF] * split_left(tw, e), 2)
        st = mm(b0t, xw) + (mm(b0t, xw_low) + mm(b0t_low, xw))
        st_ref[0, :, sl] = st
        st, st_low = parts(st, 2)
        carry = (mm(cb[HALF:], st) + (mm(cb[HALF:], st_low) + mm(cb_low[HALF:], st))) * split_left(e1, e)
        for k in (0, 1):
            ys = [[], []]
            for h in (0, 1):
                head = 2 * p + h
                at = slice(k * HALF, k * HALF + HALF)
                xm = jnp.where(head_lanes(h), xh[at], xl_turned[at])
                col = c[k][:, head : head + 1]
                row = ct[k][head : head + 1, :]
                m = {}
                for i, j in ((0, 0), (1, 0), (1, 1)):
                    gap = col[i * SUB : i * SUB + SUB] - row[:, j * SUB : j * SUB + SUB]
                    full = jnp.exp(jnp.minimum(gap, 0.0)) * scores[k][i, j]
                    m[i, j] = parts(full, 2)
                ys[0].append(mm(jnp.concatenate(m[0, 0], axis=1), jnp.concatenate([xm[:SUB], xm[:SUB]], axis=0)))
                wide = [m[1, 0][0], m[1, 1][0], m[1, 0][1], m[1, 1][1]]
                ys[1].append(mm(jnp.concatenate(wide, axis=1), jnp.concatenate([xm, xm], axis=0)))
            for i in (0, 1):
                at = k * HALF + i * SUB
                first = cols((SUB, SUB)) < 64
                y0, y1 = ys[i]
                y = jnp.where(first, y0, y1) + pltpu.roll(jnp.where(first, y1, y0), 64, 1) + skip[at : at + SUB]
                if k == 1:
                    y = y + carry[i * SUB : i * SUB + SUB]
                y_ref[at : at + SUB, sl] = y


def seq_spec(width):
    return pl.BlockSpec((SEQ, width), lambda i: (i, 0))


def whole(shape):
    return pl.BlockSpec(shape, lambda i: (0,) * len(shape))


SMEM = pl.BlockSpec(memory_space=pltpu.SMEM)


def ssd_forward(cut, x_raw, bc_raw, dt_raw, taps_x, taps_bc, heads, spread):
    return pl.pallas_call(
        fwd_kernel,
        grid=(2,),
        in_specs=[SMEM, seq_spec(768), seq_spec(256), seq_spec(128), whole((8, 768)), whole((8, 256)), whole((8, 128)), whole((128, 768))],
        out_specs=[seq_spec(768), pl.BlockSpec((1, 128, 768), lambda i: (i, 0, 0))],
        out_shape=[jax.ShapeDtypeStruct((1024, 768), F32), jax.ShapeDtypeStruct((2, 128, 768), F32)],
        compiler_params=pltpu.CompilerParams(vmem_limit_bytes=VMEM_LIMIT),
        cost_estimate=pl.CostEstimate(flops=4_000_000_000, bytes_accessed=9_000_000, transcendentals=4_000_000),
    )(cut, x_raw, bc_raw, dt_raw, taps_x, taps_bc, heads, spread)


def bwd_kernel(cut_ref, place_ref, xr_ref, bcr_ref, dtr_ref, dy_ref, y_ref, st_ref, tx_ref, tbc_ref, hd_ref, e_ref, et_ref,
               gx_ref, keep_ref, send_ref, gdt_ref, gtx_ref, keepc_ref, sendc_ref, ghd_ref,
               ds_ref, masks_ref, steps_ref, up_ref, ccol_ref, ct_ref, c1t_ref, b0_ref, acc_ref, accb_ref, skip_ref):
    seq = pl.program_id(0)
    cut = cut_ref[seq]
    masks = conv_masks(cut)

    def conv_back(du, v, taps, masks):
        g = taps[3:4] * du
        sums = [jnp.sum(du * v, axis=0, keepdims=True)]
        for j in (1, 2, 3):
            dm = du * masks[j - 1]
            g = g + taps[3 - j : 4 - j] * pltpu.roll(dm, SEQ - j, 0)
            sums.append(jnp.sum(dm * pltpu.roll(v, j, 0), axis=0, keepdims=True))
        return g, [sums[3], sums[2], sums[1], sums[0], jnp.sum(du, axis=0, keepdims=True)]

    @pl.when(seq == 0)
    def _():
        gtx_ref[...] = jnp.zeros_like(gtx_ref)
        keepc_ref[...] = jnp.zeros_like(keepc_ref)
        sendc_ref[...] = jnp.zeros_like(sendc_ref)
        ghd_ref[...] = jnp.zeros_like(ghd_ref)

    act = []
    for i in range(2):
        sl = slice(i * SUB, i * SUB + SUB)
        u = conv(bcr_ref[:, sl], tbc_ref[:, sl], masks)
        act.append((u * sigmoid(u)).astype(BF))
    for j in range(3):
        masks_ref[j] = masks[j]
    bb, cb = act
    dt, c, ew, e1 = time_steps(dtr_ref[...], hd_ref[...], cut)
    fill_columns(c, ccol_ref, ct_ref)
    put_stack(steps_ref, [dt, ew * dt[:HALF], e1, ew])
    blk = lambda a, k: a[k * HALF : k * HALF + HALF]
    for k in (0, 1):
        up = masked_scores(blk(cb, k), blk(bb, k), k, cut, lower=False)
        for n, at in enumerate(BLOCKS):
            up_ref[k, n] = up[at]
    c1t_ref[...] = cb[HALF:].T
    b0_ref[...] = bb[:HALF]
    ds_ref[...] = jnp.zeros_like(ds_ref)
    acc_ref[...] = jnp.zeros_like(acc_ref)
    accb_ref[...] = jnp.zeros_like(accb_ref)
    skip_ref[...] = jnp.zeros_like(skip_ref)

    def one_pair(p, carried):
        sl = pl.ds(pl.multiple_of(p * SUB, SUB), SUB)
        e, et, taps = e_ref[:, sl], et_ref[sl, :], tx_ref[:, sl]
        xr = xr_ref[:, sl]
        pair_masks = [masks_ref[j] for j in range(3)]
        u = conv(xr, taps, pair_masks)
        sg = sigmoid(u)
        x = u * sg
        dtx, twx, e1x, ewx = spread_stack(steps_ref, e, (SEQ, HALF, HALF, HALF))
        xtf = x * dtx
        xt = xtf.astype(BF)
        dy = dy_ref[:, sl]
        dyb = dy.astype(BF)
        dyh = dyb.astype(F32)
        xh = xt.astype(F32)
        xl = (xtf - xh).astype(BF)
        dl_turned = pltpu.roll(dy - dyh, 64, 1).astype(BF)
        xh_turned = pltpu.roll(xh, 64, 1).astype(BF)
        skip = jnp.broadcast_to(jnp.sum(dy * x, axis=0, keepdims=True), (16, SUB))
        stack = parts(dyh * y_ref[:, sl], 2) + parts(dyh * x, 2) + parts(skip, 3)
        wide = mm(jnp.concatenate(stack, axis=0), et)
        acc_ref[0] += wide[0:SEQ] + wide[SEQ : 2 * SEQ]
        acc_ref[1] += wide[2 * SEQ : 3 * SEQ] + wide[3 * SEQ : 4 * SEQ]
        skip_ref[...] += wide[2048:2056] + wide[2064:2072] + wide[2080:2088]
        dxs = []
        for k in (0, 1):
            back = 0.0
            for h in (0, 1):
                head = 2 * p + h
                lanes, none = head_lanes(h), jnp.zeros((), BF)
                dm = jnp.where(lanes, blk(dyb, k), none)
                dm2 = jnp.concatenate([jnp.where(lanes, blk(dyb, k), blk(dl_turned, k)), dm], axis=1)
                xm2 = jnp.concatenate([jnp.where(lanes, blk(xt, k), blk(xh_turned, k)), jnp.where(lanes, blk(xl, k), none)], axis=1)
                row = ct_ref[k, pl.ds(head, 1), :]
                gfull = mm_nt(dm2, xm2)
                mt = {}
                for n, (i, j) in enumerate(BLOCKS):
                    ti, sj = slice(i * SUB, i * SUB + SUB), slice(j * SUB, j * SUB + SUB)
                    decay = jnp.exp(-jnp.abs(ccol_ref[k, head, ti, :] - row[:, sj]))
                    if i == j:
                        decay_t = decay
                    else:
                        decay_t = jnp.exp(-jnp.abs(ccol_ref[k, head, sj, :] - row[:, ti]))
                    ds_ref[k, i + j] += gfull[ti, sj] * decay
                    mt[i, j] = (decay_t * up_ref[k, n]).astype(BF)
                rows0 = jnp.concatenate([mt[0, 0], mt[1, 0]], axis=1)
                rows1 = jnp.concatenate([jnp.zeros((SUB, SUB), BF), mt[1, 1]], axis=1)
                back = back + mm(jnp.concatenate([rows0, rows1], axis=0), dm)
            dxs.append(back)
        st, st_low = parts(st_ref[0, :, sl], 2)
        dcs, dcs_low = parts(dy[HALF:] * e1x, 2)
        accb_ref[0] += mm_nt(dcs, st) + (mm_nt(dcs_low, st) + mm_nt(dcs, st_low))
        dst, dst_low = parts(mm(c1t_ref[...], dcs) + mm(c1t_ref[...], dcs_low), 2)
        dxw = mm(b0_ref[...], dst)
        xw, xw_low = parts(x[:HALF] * twx, 2)
        accb_ref[1] += mm_nt(xw, dst) + (mm_nt(xw_low, dst) + mm_nt(xw, dst_low))
        dx0 = dxs[0] + dxw * ewx
        dxt = jnp.concatenate([dx0, dxs[1]], axis=0)
        wide = mm(jnp.concatenate(parts(x * dxt, 2), axis=0), et)
        acc_ref[2] += wide[:SEQ] + wide[SEQ:]
        dx = dtx * dxt + taps[5:6] * dy
        du = dx * (sg * (1.0 + u * (1.0 - sg)))
        g, sums = conv_back(du, xr, taps, pair_masks)
        gx_ref[:, sl] = g.astype(BF)
        gtx_ref[0:5, sl] += jnp.concatenate(sums, axis=0)
        return carried

    lax.fori_loop(0, 6 // PAIRS, lambda i, x: [one_pair(i * PAIRS + j, x) for j in range(PAIRS)][0], 0)
    sum_y, sum_x, sum_d = acc_ref[0], acc_ref[1], acc_ref[2]
    d_c1, d_b0 = accb_ref[0], accb_ref[1]
    d_b, d_c = [], []
    for k in (0, 1):
        bk, ck = blk(bb, k), blk(cb, k)
        m = {}
        for i, j in ((0, 0), (1, 0), (1, 1)):
            t = rows((SUB, SUB)) + (k * HALF + i * SUB)
            r = cols((SUB, SUB)) + (k * HALF + j * SUB)
            m[i, j] = jnp.where((t >= r) & same_doc(t, r, cut), ds_ref[k, i + j], 0.0).astype(BF)
        lowr = jnp.concatenate([m[1, 0], m[1, 1]], axis=1)
        d_c += [mm(m[0, 0], bk[:SUB]), mm(lowr, bk)]
        d_b += [mm_tn(m[0, 0], ck[:SUB]) + mm_tn(m[1, 0], ck[SUB:]), mm_tn(m[1, 1], ck[SUB:])]
    d_b = jnp.concatenate([jnp.concatenate(d_b[:2], axis=0) + d_b0] + d_b[2:], axis=0)
    d_c = jnp.concatenate(d_c[:2] + [jnp.concatenate(d_c[2:], axis=0) + d_c1], axis=0)
    for i, d in ((0, d_b), (1, d_c)):
        sl = slice(i * SUB, i * SUB + SUB)
        v = bcr_ref[:, sl]
        u = conv(v, tbc_ref[:, sl], masks)
        sg = sigmoid(u)
        g, sums = conv_back(d * (sg * (1.0 + u * (1.0 - sg))), v, tbc_ref[:, sl], masks)

        @pl.when(place_ref[3] == i)
        def _():
            keep_ref[...] = g
            for r, s in enumerate(sums):
                keepc_ref[r : r + 1] += s

        @pl.when(place_ref[3] != i)
        def _():
            send_ref[...] = g
            for r, s in enumerate(sums):
                sendc_ref[r : r + 1] += s

    hd = hd_ref[...]
    w = (sum_y - hd[2:3] * sum_x) - dt * sum_d
    tri = jnp.where((cols((SEQ, SEQ)) >= rows((SEQ, SEQ))) & same_doc(rows((SEQ, SEQ)), cols((SEQ, SEQ)), cut), 1.0, 0.0).astype(BF)
    run = split_right(tri, w)
    d_dt = sum_d + hd[1:2] * run
    gd = d_dt * sigmoid(dtr_ref[...] + hd[0:1])
    gdt_ref[...] = gd.astype(BF)
    ghd_ref[0:1] += jnp.sum(gd, axis=0, keepdims=True)
    ghd_ref[2:3] += skip_ref[0:1]
    ghd_ref[1:2] += jnp.sum(dt * run, axis=0, keepdims=True) * hd[1:2]


def ssd_backward(cut, place, x_raw, bc_raw, dt_raw, dy, y, st, taps_x, taps_bc, heads, spread, spread_t):
    return pl.pallas_call(
        bwd_kernel,
        grid=(2,),
        in_specs=[SMEM, SMEM, seq_spec(768), seq_spec(256), seq_spec(128), seq_spec(768), seq_spec(768),
                  pl.BlockSpec((1, 128, 768), lambda i: (i, 0, 0)), whole((8, 768)), whole((8, 256)), whole((8, 128)), whole((128, 768)), whole((768, 128))],
        out_specs=[seq_spec(768), seq_spec(128), seq_spec(128), seq_spec(128), whole((8, 768)), whole((8, 128)), whole((8, 128)), whole((8, 128))],
        out_shape=[jax.ShapeDtypeStruct((1024, 768), BF), jax.ShapeDtypeStruct((1024, 128), F32), jax.ShapeDtypeStruct((1024, 128), F32), jax.ShapeDtypeStruct((1024, 128), BF),
                   jax.ShapeDtypeStruct((8, 768), F32), jax.ShapeDtypeStruct((8, 128), F32), jax.ShapeDtypeStruct((8, 128), F32), jax.ShapeDtypeStruct((8, 128), F32)],
        scratch_shapes=[
            pltpu.VMEM((2, 3, SUB, SUB), F32),
            pltpu.VMEM((3, SEQ, SUB), F32),
            pltpu.VMEM((5 * SEQ, SUB), BF),
            pltpu.VMEM((2, 3, SUB, SUB), F32),
            pltpu.VMEM((2, 12, HALF, SUB), F32),
            pltpu.VMEM((2, SUB, HALF), F32),
            pltpu.VMEM((SUB, HALF), BF),
            pltpu.VMEM((HALF, SUB), BF),
            pltpu.VMEM((3, SEQ, SUB), F32),
            pltpu.VMEM((2, HALF, SUB), F32),
            pltpu.VMEM((8, SUB), F32),
        ],
        compiler_params=pltpu.CompilerParams(vmem_limit_bytes=VMEM_LIMIT),
        cost_estimate=pl.CostEstimate(flops=12_000_000_000, bytes_accessed=14_000_000, transcendentals=4_000_000),
    )(cut, place, x_raw, bc_raw, dt_raw, dy, y, st, taps_x, taps_bc, heads, spread, spread_t)


def place_blocks(pieces, w_ref, sem, row_of):
    for ref, k, first in pieces:
        for r in range(ref.shape[0]):
            for h in range(2):
                row = pl.multiple_of(row_of(k, first + r, h) * 48, 48)
                pltpu.make_async_copy(ref.at[r, h], w_ref.at[pl.ds(row, 48)], sem).start()


def ring_pieces(refs):
    return list(zip(refs, (0, 1, 3, 2, 2), (0, 0, 0, 0, 2)))


def start_halves(refs, which, buf, sems):
    for k in range(4):
        pltpu.make_async_copy(refs[k // 2].at[k % 2, which], buf.at[k], sems.at[k]).start()


def project_kernel(order_ref, place_ref, *refs):
    a_refs, t_refs = refs[0:5], refs[5:7]
    normed_ref, nt_ref, xr_ref, bc_ref, dt_ref, w_ref, wbc_ref, gain, tok, w_sem, t_sem = refs[7:]
    step = pl.program_id(0)

    @pl.when(step == 0)
    def _():
        z, xh, y = place_ref[0], place_ref[1], place_ref[2]
        start_halves(t_refs, 0, tok, t_sem)

        def row_of(k, r, h):
            return (lax.rem(z - k + 4, 4) * 2 + lax.rem(xh + h, 2)) * 4 + lax.rem(y - r + 4, 4)

        place_blocks(ring_pieces(a_refs), w_ref, w_sem, row_of)
        pltpu.make_async_copy(w_ref, w_ref, w_sem).wait()
        gain[...] = w_ref[:, 1024:1152].astype(F32).T[8:16]
        wbc_ref[...] = w_ref[:, 768:1024]

    pltpu.make_async_copy(t_refs[0].at[0, 0], tok.at[step], t_sem.at[step]).wait()
    wide = tok[step].astype(F32)
    inv = lax.rsqrt(jnp.mean(wide * wide, axis=-1, keepdims=True) + EPS)
    normed = (wide * inv * gain[4:5]).astype(BF)
    normed_ref[...] = normed
    nt_ref[...] = normed.T
    xr_ref[...] = mm(normed, w_ref[:, 0:768])
    bc_ref[...] = mm(normed, w_ref[:, 768:1024])
    dt_ref[...] = jnp.where(cols((HALF, SUB)) < 12, mm(normed, w_ref[:, 1024:1152]), 0.0)


ANY = pl.BlockSpec(memory_space=pl.ANY)


def by_order(width):
    return pl.BlockSpec((HALF, width), lambda i, order, place: (order[i], 0))


def turned():
    return pl.BlockSpec((1536, HALF), lambda i, order, place: (0, order[i]))


def fixed(shape):
    return pl.BlockSpec(shape, lambda i, *_: (0,) * len(shape))


def project(order, place, parts_in, tokens):
    sd = jax.ShapeDtypeStruct
    return pl.pallas_call(
        project_kernel,
        grid_spec=pltpu.PrefetchScalarGridSpec(
            num_scalar_prefetch=2,
            grid=(4,),
            in_specs=[ANY] * 7,
            out_specs=[by_order(1536), turned(), by_order(768), by_order(256), by_order(128), fixed((1536, 1152)), fixed((1536, 256)), fixed((8, 1536))],
            scratch_shapes=[pltpu.VMEM((4, HALF, 1536), BF), pltpu.SemaphoreType.DMA, pltpu.SemaphoreType.DMA((4,))],
        ),
        out_shape=[sd((1024, 1536), BF), sd((1536, 1024), BF), sd((1024, 768), F32), sd((1024, 256), F32), sd((1024, 128), F32), sd((1536, 1152), BF), sd((1536, 256), BF), sd((8, 1536), F32)],
        compiler_params=pltpu.CompilerParams(vmem_limit_bytes=VMEM_LIMIT),
        cost_estimate=pl.CostEstimate(flops=3_700_000_000, bytes_accessed=22_000_000, transcendentals=0),
    )(order, place, *parts_in, *tokens)


def gate_kernel(order_ref, place_ref, b0, b1, b2, b3, b4, c0, c1, normed_ref, y_ref, gg_ref, gate_ref, gs_ref, cot_ref, s_ref, w_ref, buf, w_sem, t_sem):
    step = pl.program_id(0)

    @pl.when(step == 0)
    def _():
        z, xh, y = place_ref[0], place_ref[1], place_ref[2]
        start_halves((c0, c1), 1, buf, t_sem)

        def row_of(k, r, h):
            return (lax.rem(z - r + 4, 4) * 2 + lax.rem(xh + h, 2)) * 4 + lax.rem(y - k + 4, 4)

        place_blocks(ring_pieces((b0, b1, b2, b3, b4)), w_ref, w_sem, row_of)
        pltpu.make_async_copy(w_ref, w_ref, w_sem).wait()

    pltpu.make_async_copy(c0.at[0, 1], buf.at[step], t_sem.at[step]).wait()
    cot = buf[step]
    cot_ref[...] = cot.T
    gate = mm(normed_ref[...], w_ref[:, 0:768])
    gs = mm(cot, w_ref[:, 768:1536])
    gate_ref[...] = gate
    gs_ref[...] = gs
    mixed = y_ref[...] * (gate * sigmoid(gate))
    sq = jnp.sum(mixed * mixed, axis=-1, keepdims=True)
    cr = jnp.sum((gs * gg_ref[0:1]) * mixed, axis=-1, keepdims=True)
    lane = cols((HALF, SUB))
    s_ref[...] = jnp.where(lane == 0, sq, jnp.where(lane == 1, cr, 0.0)).T[0:8]


def gate_side(order, place, parts_in, cots, normed, y, gg):
    sd = jax.ShapeDtypeStruct
    return pl.pallas_call(
        gate_kernel,
        grid_spec=pltpu.PrefetchScalarGridSpec(
            num_scalar_prefetch=2,
            grid=(4,),
            in_specs=[ANY] * 7 + [by_order(1536), by_order(768), fixed((8, 768))],
            out_specs=[by_order(768), by_order(768), turned(), pl.BlockSpec((8, HALF), lambda i, order, place: (0, order[i])), fixed((1536, 1536))],
            scratch_shapes=[pltpu.VMEM((4, HALF, 1536), BF), pltpu.SemaphoreType.DMA, pltpu.SemaphoreType.DMA((4,))],
        ),
        out_shape=[sd((1024, 768), F32), sd((1024, 768), F32), sd((1536, 1024), BF), sd((8, 1024), F32), sd((1536, 1536), BF)],
        compiler_params=pltpu.CompilerParams(vmem_limit_bytes=VMEM_LIMIT),
        cost_estimate=pl.CostEstimate(flops=4_900_000_000, bytes_accessed=30_000_000, transcendentals=800_000),
    )(order, place, *parts_in, *cots, normed, y, gg)


MIX, OUT, OUTER = 4, 6, 4


def middle_kernel(place_ref, s0, s1, s2, s3, gate_ref, gs_ref, y_ref, gg_ref, w_ref, n_ref, c_ref,
                  low_ref, dy_ref, gain_ref, own_ref, core_ref, xl_ref, both_ref, grad_ref, scaled, gated):
    step = pl.program_id(0)

    @pl.when(step < MIX)
    def _():
        sums = ((s0[...] + s1[...]) + (s2[...] + s3[...])).T
        inv = lax.rsqrt(sums[:, 0:1] / 3072 + EPS)
        corr = inv * inv * inv * (sums[:, 1:2] / 3072)
        gate, gs, y, gg = gate_ref[...], gs_ref[...], y_ref[...], gg_ref[0:1]
        sg = sigmoid(gate)
        act = gate * sg
        mixed = y * act
        normal = mixed * inv
        at = pl.ds(pl.multiple_of(step * HALF, HALF), HALF)
        scaled[at] = (normal * gg).astype(BF)
        gm = gs * gg * inv - mixed * corr
        low = (gm * y * (sg * (1.0 + gate * (1.0 - sg)))).astype(BF)
        gated[at] = low
        low_ref[...] = low
        dy_ref[...] = gm * act

        @pl.when(step == 0)
        def _():
            gain_ref[...] = jnp.zeros_like(gain_ref)

        gain_ref[0:1] += jnp.sum(gs * normal, axis=0, keepdims=True)

    @pl.when((step >= MIX) & (step < MIX + OUT))
    def _():
        rows_out(place_ref, mm_nt(scaled[...], w_ref[...]), [own_ref, core_ref, xl_ref, both_ref])

    @pl.when(step >= MIX + OUT)
    def _():
        for at, a_ref, b_ref in ((0, n_ref, gated), (768, c_ref, scaled)):
            r = mm(a_ref[...], b_ref[...]).astype(BF)
            for yi in range(4):
                for xi in range(2):
                    row = (xi * 4 + yi) * 48
                    grad_ref[yi, xi * 48 : xi * 48 + 48, at : at + 768] = r[row : row + 48]


def middle(place, sums, gate, gs, y, gg, w_2, normed_t, cot_t):
    sd = jax.ShapeDtypeStruct
    mix_at = lambda i: jnp.minimum(i, MIX - 1)
    out_at = lambda i: jnp.clip(i - MIX, 0, OUT - 1)
    outer_at = lambda i: jnp.maximum(i - MIX - OUT, 0)
    tokens = pl.BlockSpec((HALF, 768), lambda i, place: (mix_at(i), 0))
    chunk = pl.BlockSpec((384, 1024), lambda i, place: (outer_at(i), 0))
    rows_spec = pl.BlockSpec((HALF, 256), lambda i, place: (0, out_at(i)))
    return pl.pallas_call(
        middle_kernel,
        grid_spec=pltpu.PrefetchScalarGridSpec(
            num_scalar_prefetch=1,
            grid=(MIX + OUT + OUTER,),
            in_specs=[pl.BlockSpec((8, HALF), lambda i, place: (0, mix_at(i)))] * 4
            + [tokens] * 3
            + [fixed((8, 768)), pl.BlockSpec((256, 768), lambda i, place: (out_at(i), 1)), chunk, chunk],
            out_specs=[tokens, tokens, fixed((8, 768))] + [rows_spec] * 4 + [pl.BlockSpec((4, 96, 1536), lambda i, place: (outer_at(i), 0, 0))],
            scratch_shapes=[pltpu.VMEM((1024, 768), BF), pltpu.VMEM((1024, 768), BF)],
        ),
        out_shape=[sd((1024, 768), BF), sd((1024, 768), F32), sd((8, 768), F32), sd((HALF, 1536), F32)]
        + [sd((HALF, 1536), BF)] * 3
        + [sd((16, 96, 1536), BF)],
        compiler_params=pltpu.CompilerParams(vmem_limit_bytes=VMEM_LIMIT),
        cost_estimate=pl.CostEstimate(flops=7_300_000_000, bytes_accessed=30_000_000, transcendentals=800_000),
    )(place, *sums, gate, gs, y, gg, w_2, normed_t, cot_t)


def outer_z_kernel(place_ref, n_ref, g_ref, small_ref, *out):
    step = pl.program_id(0)
    y = place_ref[2]
    r = mm(n_ref[...], g_ref[...]).astype(BF)
    small = small_ref[...].astype(BF)
    for k in range(4):

        @pl.when(step == k)
        def _():
            for yi in range(4):
                to = lax.rem(yi - y + 4, 4)
                for xi in range(2):
                    at = (xi * 4 + yi) * 48
                    out[k][to, xi * 48 : xi * 48 + 48] = r[at : at + 48]
                out[k][to, 96:104] = small


def outer_side_kernel(place_ref, n_ref, g_ref, m_ref, d_ref, small_ref, maps_ref, *out):
    step = pl.program_id(0)
    y, xl = place_ref[2], place_ref[4]

    def columns(maps, steps):
        lane = cols(maps.shape)
        maps = jnp.where(xl == 0, maps, pltpu.roll(maps, 64, 1))
        return jnp.where(lane < 64, maps, pltpu.roll(steps, 64, 1)).astype(BF)

    n = n_ref[...]
    r = [mm(n, g_ref[...]).astype(BF), columns(mm(n, m_ref[...]), mm(n, d_ref[...]))]
    small = [small_ref[...].astype(BF), columns(maps_ref[:, 0:128], maps_ref[:, 128:256])]
    for k in range(4):

        @pl.when(step == k)
        def _():
            for part, lanes in ((0, slice(0, 256)), (1, slice(256, 384))):
                for yi in range(4):
                    to = lax.rem(yi - y + 4, 4)
                    for xi in range(2):
                        at = (xi * 4 + yi) * 48
                        out[k][to, xi * 48 : xi * 48 + 48, lanes] = r[part][at : at + 48]
                    out[k][to, 96:104, lanes] = small[part]


def outer_split(kernel, place, normed_t, grads, smalls, width):
    return pl.pallas_call(
        kernel,
        grid_spec=pltpu.PrefetchScalarGridSpec(
            num_scalar_prefetch=1,
            grid=(4,),
            in_specs=[pl.BlockSpec((384, 1024), lambda i, place: (lax.rem(place[0] + i, 4), 0))] + [spec for _, spec in grads] + [fixed(t.shape) for t in smalls],
            out_specs=[fixed((4, 104, width))] * 4,
        ),
        out_shape=[jax.ShapeDtypeStruct((4, 104, width), BF)] * 4,
        compiler_params=pltpu.CompilerParams(vmem_limit_bytes=VMEM_LIMIT),
        cost_estimate=pl.CostEstimate(flops=1, bytes_accessed=1, transcendentals=0),
    )(place, normed_t, *[g for g, _ in grads], *smalls)


def fold_kernel(*refs):
    for parts4, lanes in ((refs[0:4], slice(0, 512)), (refs[4:8], slice(512, 896))):
        for k in range(4):
            near = parts4[1][k].astype(F32) + parts4[3][k].astype(F32)
            refs[8 + k][:, lanes] = ((parts4[0][k].astype(F32) + parts4[2][k].astype(F32)) + near).astype(BF)


def fold(a_parts, b_parts):
    vmem = pl.BlockSpec(memory_space=pltpu.VMEM)
    return pl.pallas_call(
        fold_kernel,
        in_specs=[vmem] * 8,
        out_specs=[vmem] * 4,
        out_shape=[jax.ShapeDtypeStruct((104, 896), BF)] * 4,
        compiler_params=pltpu.CompilerParams(vmem_limit_bytes=VMEM_LIMIT),
        cost_estimate=pl.CostEstimate(flops=1, bytes_accessed=1, transcendentals=0),
    )(*a_parts, *b_parts)


def rows_out(place_ref, total, out):
    for base in range(4):

        @pl.when(place_ref[3] * 2 + place_ref[4] == base)
        def _():
            for ref, at in zip(out, (base, base ^ 2, base ^ 1, base ^ 3)):
                ref[...] = total[at * HALF : at * HALF + HALF].astype(ref.dtype)


def token_kernel(place_ref, g_ref, x_ref, d_ref, wz_ref, wx_ref, wd_ref, own_ref, mate_ref, send_ref):
    total = mm_nt(g_ref[...], wz_ref[...]) + mm_nt(x_ref[...], wx_ref[...]) + mm_nt(d_ref[...], wd_ref[...])
    rows_out(place_ref, total, [own_ref, send_ref.at[0:HALF], mate_ref, send_ref.at[HALF:SEQ]])


def by_rows(kernel, place, tokens, weights, places, outs, work=1):
    columns = lambda at: lambda i, place: (i, at(place))
    return pl.pallas_call(
        kernel,
        grid_spec=pltpu.PrefetchScalarGridSpec(
            num_scalar_prefetch=1,
            grid=(6,),
            in_specs=[fixed(t.shape) for t in tokens] + [pl.BlockSpec((256, t.shape[1]), columns(at)) for t, at in zip(tokens, places)],
            out_specs=[pl.BlockSpec((n, 256), lambda i, place: (0, i)) for n, _ in outs],
        ),
        out_shape=[jax.ShapeDtypeStruct((n, 1536), t) for n, t in outs],
        compiler_params=pltpu.CompilerParams(vmem_limit_bytes=VMEM_LIMIT),
        cost_estimate=pl.CostEstimate(flops=work, bytes_accessed=1, transcendentals=0),
    )(place, *tokens, *weights)


def sum_pieces_kernel(place_ref, p0, p1, p2, p3, zo_ref, keep_ref, send_ref):
    total = (p0[...].astype(F32) + p2[...].astype(F32)) + (p1[...].astype(F32) + p3[...].astype(F32))
    small = total[96:104].astype(BF)
    send_ref[48:56, 0:896] = small
    keep_ref[48:56, 0:896] = small.astype(F32)
    for xh in (0, 1):

        @pl.when(place_ref[1] == xh)
        def _():
            keep_ref[0:48, 0:896] = total[xh * 48 : xh * 48 + 48]
            send_ref[0:48, 0:896] = total[48 - xh * 48 : 96 - xh * 48].astype(BF)

    for xh in (0, 1):

        @pl.when(place_ref[1] == xh)
        def _():
            keep_ref[0:48, 896:2432] = zo_ref[xh * 48 : xh * 48 + 48].astype(F32)
            send_ref[0:48, 896:2432] = zo_ref[48 - xh * 48 : 96 - xh * 48]

    keep_ref[48:56, 896:2432] = jnp.zeros((8, 1536), F32)
    send_ref[48:56, 896:2432] = jnp.zeros((8, 1536), BF)


def sum_far_kernel(place_ref, own_ref, far_ref, keep_ref, send_ref):
    total = own_ref[...] + far_ref[...].astype(F32)
    keep_ref[24:32] = total[48:56]
    send_ref[24:32] = total[48:56]
    for core in (0, 1):

        @pl.when(place_ref[3] == core)
        def _():
            keep_ref[0:24] = total[core * 24 : core * 24 + 24]
            send_ref[0:24] = total[24 - core * 24 : 48 - core * 24]


def whole_call(kernel, place, arrays, shapes):
    vmem = pl.BlockSpec(memory_space=pltpu.VMEM)
    return pl.pallas_call(
        kernel,
        in_specs=[SMEM] + [vmem] * len(arrays),
        out_specs=[vmem] * len(shapes),
        out_shape=shapes,
        compiler_params=pltpu.CompilerParams(vmem_limit_bytes=VMEM_LIMIT),
        cost_estimate=pl.CostEstimate(flops=1, bytes_accessed=1, transcendentals=0),
    )(place, *arrays)


def sum_pieces(place, pieces, zo):
    shapes = [jax.ShapeDtypeStruct((56, 2432), F32), jax.ShapeDtypeStruct((56, 2432), BF)]
    return whole_call(sum_pieces_kernel, place, [*pieces, zo], shapes)


def sum_far(place, own, far):
    return whole_call(sum_far_kernel, place, [own, far], [jax.ShapeDtypeStruct((32, 2432), F32)] * 2)


def after_kernel(x_ref, *refs):
    pass


def after(x, *deps):
    return pl.pallas_call(
        after_kernel,
        in_specs=[ANY] * (1 + len(deps)),
        out_specs=ANY,
        out_shape=jax.ShapeDtypeStruct(x.shape, x.dtype),
        input_output_aliases={0: 0},
    )(x, *deps)


def swap(a, axis):
    return lax.ppermute(a, axis, [(0, 1), (1, 0)])


def turn(a, axis, k):
    return lax.ppermute(a, axis, [(i, (i + k) % 4) for i in range(4)])


def pair(own, other, axis):
    first = lax.axis_index(axis) == 0
    return jnp.stack([jnp.where(first, own, other), jnp.where(first, other, own)])


def mine(a, axis, dim, size):
    i = lax.axis_index(axis)
    return (
        lax.dynamic_slice_in_dim(a, i * size, size, dim),
        lax.dynamic_slice_in_dim(a, (1 - i) * size, size, dim),
    )


def turns(a, axis):
    return [a] + [turn(a, axis, k) for k in (1, 2, 3)]


def shards(resid, cotangent, segments, pre_gain, w_z, w_x, w_bc, w_dt, conv_x, conv_x_bias, conv_bc, conv_bc_bias, dt_bias, a_log, d_skip, gate_gain, w_out):
    core, xl = lax.axis_index("c"), lax.axis_index("xl")
    place = jnp.stack([lax.axis_index("z"), lax.axis_index("xh"), lax.axis_index("y"), core, xl])
    base = core * 2 + xl
    order = jnp.stack([core * 2, core * 2 + 1, 2 - core * 2, 3 - core * 2])

    own_bc = jnp.concatenate([w_bc, pre_gain[:, None], jnp.zeros((12, 127), BF)], axis=1)
    keep_x, send_x = mine(w_x, "c", 1, 768)
    keep_dt, send_dt = mine(w_dt, "c", 1, 12)
    bc_x, bc_c = swap(own_bc, "xl"), swap(own_bc, "c")
    bc_d = lax.ppermute(own_bc, ("c", "xl"), [(i, 3 - i) for i in range(4)])
    got = swap(jnp.concatenate([send_x, send_dt], axis=1), "c")
    bc48 = pair(pair(own_bc, bc_x, "xl"), pair(bc_c, bc_d, "xl"), "c").reshape(48, 384)
    xdt = pair(jnp.concatenate([keep_x, keep_dt], axis=1), got, "c").reshape(48, 780)
    first = jnp.concatenate([xdt[:, :768], bc48[:, :256], xdt[:, 768:], bc48[:, 256:372]], axis=1)
    first_far = swap(first, "xh")
    first = jnp.stack([first, first_far])

    keep_z, send_z = mine(w_z, "c", 1, 768)
    keep_o, send_o = mine(w_out.T, "c", 1, 768)
    got = swap(jnp.concatenate([send_z, send_o], axis=1), "c")
    second = pair(jnp.concatenate([keep_z, keep_o], axis=1), got, "c").reshape(48, 1536)
    second = jnp.stack([second, swap(second, "xh")])

    half = lax.all_gather(jnp.stack([resid, cotangent]), "xl", axis=0, tiled=False)
    near_x, near = turns(first, "y"), turns(second, "z")
    b_own = jnp.stack(near)
    b_ahead, b_back = turn(b_own, "y", 1), turn(b_own, "y", 3)
    a_own = after(jnp.stack(near_x), *near[1:])
    a_ahead, a_back = turn(a_own, "z", 1), turn(a_own, "z", 3)
    a_parts = [a_own, a_ahead, a_back, turn(after(a_ahead[:2], b_ahead, b_back), "z", 1), turn(after(a_back[2:], b_ahead, b_back), "z", 3)]

    def own(a, size):
        return mine(a, "c", a.ndim - 1, size)[0]

    cx, cxb, gg = own(conv_x, 768), own(conv_x_bias, 768), own(gate_gain, 768)
    dtb, al, dsk = own(dt_bias, 12), own(a_log, 12), own(d_skip, 12)
    taps_x = jnp.concatenate([cx, cxb[None], jnp.repeat(dsk, 64)[None], jnp.zeros((2, 768), F32)], axis=0)
    taps_bc = jnp.concatenate([conv_bc, conv_bc_bias[None], jnp.zeros((3, 256), F32)], axis=0)
    wide_heads = lambda v: jnp.pad(v, (0, 116))[None]
    heads = jnp.concatenate([wide_heads(dtb), wide_heads(-jnp.exp(al)), wide_heads(dsk), jnp.zeros((5, 128), F32)], axis=0)
    gains = jnp.broadcast_to(gg[None], (8, 768))
    spread_np = np.arange(768)[None, :] // 64 == np.arange(128)[:, None]
    spread, spread_t = spread_np.astype(BF), np.ascontiguousarray(spread_np.T).astype(BF)
    segments = after(segments, near[1])
    cut = jnp.sum((segments == segments[0]).astype(jnp.int32))[None]
    cuts = pair(cut, swap(cut, "c"), "c").reshape(2)

    half = after(half, a_parts[1], a_parts[2], b_ahead, b_back, taps_x, taps_bc, heads, gains, cuts, order, place)
    tokens = [half, swap(half, "c")]
    normed, normed_t, x_raw, bc_raw, dt_raw, w_1, w_maps, gain_rows = project(order, place, a_parts, tokens)

    b_ahead, b_back = after(b_ahead, dt_raw), after(b_back, dt_raw)
    b_parts = [b_own, b_ahead, b_back, turn(b_ahead[:2], "y", 1), turn(b_back[2:], "y", 3)]
    y, st = ssd_forward(cuts, x_raw, bc_raw, dt_raw, taps_x, taps_bc, heads, spread)

    gate, gs, cot_t, sums, w_2 = gate_side(order, place, b_parts, tokens, normed, y, gains)
    sums_c, sums_x = swap(sums, "c"), swap(sums, "xl")
    sums_d = lax.ppermute(sums, ("c", "xl"), [(i, 3 - i) for i in range(4)])
    gate_low, dy, g_gain, *out_rows, g_zo = middle(place, [sums, sums_c, sums_x, sums_d], gate, gs, y, gains, w_2, normed_t, cot_t)

    def exchange(rows):
        diagonal = lax.ppermute(rows[3], ("c", "xl"), [(i, 3 - i) for i in range(4)])
        return rows[0], swap(rows[1], "c"), swap(rows[2], "xl"), diagonal

    g_zo_z = lax.psum_scatter(g_zo.reshape(1536, 1536), "z", scatter_dimension=0, tiled=True)
    g_zo_y = lax.psum_scatter(g_zo_z, "y", scatter_dimension=0, tiled=True)
    out_rows = exchange(out_rows)
    wide = lambda a: a.astype(F32)
    layer_out = (wide(resid) + ((out_rows[0] + wide(out_rows[1])) + (wide(out_rows[2]) + wide(out_rows[3])))).astype(BF)

    x_low, keep, send, gdt, g_tx, keep_c, send_c, g_hd = ssd_backward(cuts, place, x_raw, bc_raw, dt_raw, dy, y, st, taps_x, taps_bc, heads, spread, spread_t)

    small_x = jnp.concatenate([g_tx[:5], g_gain[:1], jnp.zeros((2, 768), F32)], axis=0)
    left = pl.BlockSpec((1024, 512), lambda i, place: (0, 0))
    right = pl.BlockSpec((1024, 256), lambda i, place: (0, 2))
    a_grad = outer_split(outer_z_kernel, place, normed_t, [(x_low, left)], [small_x[:, :512]], 512)
    a_grad = [a_grad[0]] + [turn(a_grad[k], "z", k) for k in (1, 2, 3)]
    keep, keep_c = keep + swap(after(send, a_grad[0], *out_rows[1:]), "c"), keep_c + swap(send_c, "c")
    keep_h = keep_c.astype(BF)
    keep = jnp.concatenate([keep.astype(BF), keep_h, (keep_c - keep_h.astype(F32)).astype(BF)], axis=0)
    far = swap(keep, "xl")
    group = keep.astype(F32) + far.astype(F32)
    bc_low = after(group[:1024].astype(BF), g_zo_z)
    small_s = jnp.concatenate([group[1024:1032] + group[1032:], g_hd], axis=1)
    full = lambda t: (t, fixed(t.shape))
    b_grad = outer_split(outer_side_kernel, place, normed_t, [(x_low, right), full(bc_low), full(gdt)], [small_x[:, 512:], small_s], 384)
    b_first = b_grad[0]
    b_grad = [b_first] + [turn(b_grad[k], "z", k) for k in (1, 2, 3)]
    rows_own, rows_send = mine(bc_low, "c", 0, SEQ)
    rows_far = swap(rows_send, "c")
    bc_own = pair(rows_own, rows_far, "c")
    bc_own = jnp.concatenate([bc_own[0], bc_own[1]], axis=1)
    bc_own = lax.dynamic_slice_in_dim(bc_own, xl * 256, 256, 0)
    token_rows = by_rows(token_kernel, place, [after(gate_low, b_first, bc_own), x_low, gdt], [w_2, w_1, w_1], [lambda place: 0, lambda place: 0, lambda place: 8], [(HALF, F32), (HALF, F32), (SEQ, BF)], 20_000_000_000)
    token_far = swap(after(token_rows[2], *a_grad[1:], *b_grad[1:]), "c")
    pieces = fold(a_grad, b_grad)
    token_far = after(token_far, pieces[1], g_zo_y)
    grad_own = token_rows[0] + wide(token_far[:HALF])
    grad_far = swap((token_rows[1] + wide(token_far[HALF:])).astype(BF), "xl")
    pieces = [pieces[0]] + [turn(pieces[k], "y", k) for k in (1, 2, 3)]

    bc_part = lax.dot_general(bc_own, w_maps, (((1,), (1,)), ((), ())), preferred_element_type=F32)
    grad_normed = (grad_own + wide(grad_far)) + bc_part

    keep, send = sum_pieces(place, pieces, g_zo_y)
    keep, send = sum_far(place, after(keep, grad_far), swap(send, "xh"))
    far = swap(send, "c")

    gain_wide = gain_rows[4]
    rw = resid.astype(F32)
    inv = lax.rsqrt(jnp.mean(rw * rw, axis=-1, keepdims=True) + EPS)
    inner = jnp.sum(gain_wide[None, :] * grad_normed * rw, axis=-1, keepdims=True)
    grad_resid = cotangent.astype(F32) + gain_wide[None, :] * grad_normed * inv - rw * (inv * inv * inv) * inner / 1536

    got = pair(keep, far, "c")
    both = lambda rows, at, width: jnp.concatenate([got[0, rows, at : at + width], got[1, rows, at : at + width]], axis=1)
    main, rest = slice(0, 24), slice(24, 32)
    grad_w_x, grad_w_z, grad_w_out_t = both(main, 0, 768), both(main, 896, 768), both(main, 1664, 768)
    grad_w_dt = both(main, 832, 12)
    bc24, conv24 = both(main, 768, 64), both(rest, 768, 64)
    small_wide = both(rest, 0, 768)
    small_heads = both(rest, 832, 12)

    tall = lambda a, b: jnp.sum(a.astype(F32) * b, axis=1)
    pg = tall(w_z, grad_w_z) + tall(w_x, grad_w_x) + tall(w_dt, grad_w_dt)
    pg, pg_send = mine(pg, "xl", 0, 12)
    bc12, bc_send = mine(bc24, "xl", 0, 12)
    far = swap(jnp.concatenate([bc_send, conv24, jnp.pad(pg_send, (0, 116))[None]], axis=0), "xl")
    got = pair(jnp.concatenate([bc12, conv24], axis=0), far[:20], "xl")
    got = got.reshape(2, 20, 2, 64).transpose(1, 2, 0, 3).reshape(20, 256)
    grad_w_bc, grad_conv_bc = got[:12], got[12:]
    grad_pre_gain = (pg + far[20, :12] + tall(w_bc, grad_w_bc)) / pre_gain.astype(F32)
    return (
        layer_out,
        grad_resid,
        grad_pre_gain,
        grad_w_z,
        grad_w_x,
        grad_w_bc,
        grad_w_dt,
        small_wide[:4],
        small_wide[4],
        grad_conv_bc[:4],
        grad_conv_bc[4],
        small_heads[0],
        small_heads[1],
        small_heads[2],
        small_wide[5],
        grad_w_out_t.T,
    )


def solution(mesh):
    fine = Mesh(mesh.devices.reshape(4, 2, 4, 2, 2), ("z", "xh", "y", "c", "xl"))
    dp, tp, every = ("z", "xh", "y", "c"), "xl", ("z", "xh", "y", "c", "xl")
    return jax.shard_map(
        shards,
        mesh=fine,
        in_specs=(P(every, None), P(every, None), P(dp), P(every), P(dp, tp), P(dp, tp), P(every, None), P(dp, tp), P(None, tp), P(tp), P(), P(), P(tp), P(tp), P(tp), P(tp), P(tp, dp)),
        out_specs=(P(every, None), P(every, None), P(every), P(dp, tp), P(dp, tp), P(every, None), P(dp, tp), P(None, tp), P(tp), P(), P(), P(tp), P(tp), P(tp), P(tp), P(tp, dp)),
        check_vma=False,
    )
```

```python
import jax
import jax.numpy as jnp
import numpy as np
from jax import lax
from jax.experimental import pallas as pl
from jax.experimental.pallas import tpu as pltpu
from jax.sharding import Mesh, PartitionSpec as P

EPS = 1e-05
VMEM_LIMIT = 60 * 1024 * 1024
BF = jnp.bfloat16
F32 = jnp.float32
SEQ = 512
HALF = 256
SUB = 128
PAIRS = 2


def mm(a, b):
    return jnp.dot(a, b, preferred_element_type=F32)


def mm_nt(a, b):
    return lax.dot_general(a, b, (((1,), (1,)), ((), ())), preferred_element_type=F32)


def mm_tn(a, b):
    return lax.dot_general(a, b, (((0,), (0,)), ((), ())), preferred_element_type=F32)


def parts(v, count):
    out = []
    for _ in range(count):
        low = v.astype(BF)
        out.append(low)
        v = v - low.astype(F32)
    return out


def split_left(v, m, count=2):
    return sum(mm(p, m) for p in parts(v, count))


def split_right(m, v, count=3):
    return sum(mm(m, p) for p in parts(v, count))


def rows(shape):
    return lax.broadcasted_iota(jnp.int32, shape, 0)


def cols(shape):
    return lax.broadcasted_iota(jnp.int32, shape, 1)


def softplus(v):
    e = jnp.exp(-jnp.abs(v))
    tail = jnp.where(e < 1e-3, e * (1.0 - 0.5 * e), jnp.log(1.0 + e))
    return jnp.maximum(v, 0.0) + tail


def sigmoid(v):
    return 1.0 / (1.0 + jnp.exp(-v))


def same_doc(t, s, cut):
    return (t < cut) == (s < cut)


def conv_masks(cut):
    t = rows((SEQ, SUB))
    return [jnp.where((t >= j) & ((t < cut) | (t - j >= cut)), 1.0, 0.0) for j in (1, 2, 3)]


def conv(v, taps, masks):
    u = taps[4:5] + taps[3:4] * v
    for j in (1, 2, 3):
        u = u + taps[3 - j : 4 - j] * (pltpu.roll(v, j, 0) * masks[j - 1])
    return u


def time_steps(dt_raw, heads, cut):
    dt = softplus(dt_raw + heads[0:1])
    a = dt * heads[1:2]
    tri = jnp.where(rows((HALF, HALF)) >= cols((HALF, HALF)), 1.0, 0.0).astype(BF)
    c = [split_right(tri, a[:HALF]), split_right(tri, a[HALF:])]
    t = rows((HALF, SUB))
    ending = same_doc(t, HALF - 1, cut)
    alive = same_doc(t + HALF, HALF - 1, cut)
    ew = jnp.where(ending, jnp.exp(c[0][HALF - 1 : HALF] - c[0]), 0.0)
    e1 = jnp.where(alive, jnp.exp(c[1]), 0.0)
    return dt, c, ew, e1


def masked_scores(cb, bb, block, cut, lower=True):
    out = {}
    for i, j in ((0, 0), (1, 0), (1, 1)):
        ti, sj = slice(i * SUB, i * SUB + SUB), slice(j * SUB, j * SUB + SUB)
        if lower:
            s = mm_nt(cb[ti], bb[sj])
            t = rows((SUB, SUB)) + (block * HALF + i * SUB)
            r = cols((SUB, SUB)) + (block * HALF + j * SUB)
        else:
            s = mm_nt(bb[sj], cb[ti])
            r = rows((SUB, SUB)) + (block * HALF + j * SUB)
            t = cols((SUB, SUB)) + (block * HALF + i * SUB)
        out[i, j] = jnp.where((t >= r) & same_doc(t, r, cut), s, 0.0)
    return out


def head_lanes(k):
    lane = cols((HALF, SUB))
    return (lane < 64) if k == 0 else (lane >= 64)


def fill_columns(c, ccol_ref, ct_ref):
    for k in (0, 1):
        ct_ref[k] = c[k].T
        for head in range(12):
            ccol_ref[k, head] = jnp.broadcast_to(c[k][:, head : head + 1], (HALF, SUB))


def put_stack(ref, values):
    at = 0
    for v in values:
        for p in parts(v, 2):
            ref[at : at + v.shape[0]] = p
            at += v.shape[0]


def spread_stack(ref, e, heights):
    wide, out, at = mm(ref[...], e), [], 0
    for n in heights:
        out.append(wide[at : at + n] + wide[at + n : at + 2 * n])
        at += 2 * n
    return out


BLOCKS = ((0, 0), (1, 0), (1, 1))


def fwd_kernel(cut_ref, xr_ref, bcr_ref, dtr_ref, tx_ref, tbc_ref, hd_ref, e_ref, y_ref, st_ref):
    cut = cut_ref[pl.program_id(0)]
    masks = conv_masks(cut)
    act = []
    for i in range(2):
        sl = slice(i * SUB, i * SUB + SUB)
        u = conv(bcr_ref[:, sl], tbc_ref[:, sl], masks)
        act.append(parts(u * sigmoid(u), 2))
    (bb, bb_low), (cb, cb_low) = act
    cb3 = jnp.concatenate([cb, cb_low, cb], axis=1)
    bb3 = jnp.concatenate([bb, bb, bb_low], axis=1)
    dt, c, ew, e1 = time_steps(dtr_ref[...], hd_ref[...], cut)
    ct = [c[0].T, c[1].T]
    tw = ew * dt[:HALF]
    scores = [masked_scores(cb3[k * HALF : k * HALF + HALF], bb3[k * HALF : k * HALF + HALF], k, cut) for k in (0, 1)]
    b0t, b0t_low = bb[:HALF].T, bb_low[:HALF].T
    for p in range(6):
        sl = slice(p * SUB, p * SUB + SUB)
        e = e_ref[:, sl]
        u = conv(xr_ref[:, sl], tx_ref[:, sl], masks)
        x = u * sigmoid(u)
        xtf = x * split_left(dt, e)
        xh = xtf.astype(BF)
        xhf = xh.astype(F32)
        xl_turned = pltpu.roll(xtf - xhf, 64, 1).astype(BF)
        skip = tx_ref[5:6, sl] * x
        xw, xw_low = parts(x[:HALF] * split_left(tw, e), 2)
        st = mm(b0t, xw) + (mm(b0t, xw_low) + mm(b0t_low, xw))
        st_ref[0, :, sl] = st
        st, st_low = parts(st, 2)
        carry = (mm(cb[HALF:], st) + (mm(cb[HALF:], st_low) + mm(cb_low[HALF:], st))) * split_left(e1, e)
        for k in (0, 1):
            ys = [[], []]
            for h in (0, 1):
                head = 2 * p + h
                at = slice(k * HALF, k * HALF + HALF)
                xm = jnp.where(head_lanes(h), xh[at], xl_turned[at])
                col = c[k][:, head : head + 1]
                row = ct[k][head : head + 1, :]
                m = {}
                for i, j in ((0, 0), (1, 0), (1, 1)):
                    gap = col[i * SUB : i * SUB + SUB] - row[:, j * SUB : j * SUB + SUB]
                    full = jnp.exp(jnp.minimum(gap, 0.0)) * scores[k][i, j]
                    m[i, j] = parts(full, 2)
                ys[0].append(mm(jnp.concatenate(m[0, 0], axis=1), jnp.concatenate([xm[:SUB], xm[:SUB]], axis=0)))
                wide = [m[1, 0][0], m[1, 1][0], m[1, 0][1], m[1, 1][1]]
                ys[1].append(mm(jnp.concatenate(wide, axis=1), jnp.concatenate([xm, xm], axis=0)))
            for i in (0, 1):
                at = k * HALF + i * SUB
                first = cols((SUB, SUB)) < 64
                y0, y1 = ys[i]
                y = jnp.where(first, y0, y1) + pltpu.roll(jnp.where(first, y1, y0), 64, 1) + skip[at : at + SUB]
                if k == 1:
                    y = y + carry[i * SUB : i * SUB + SUB]
                y_ref[at : at + SUB, sl] = y


def seq_spec(width):
    return pl.BlockSpec((SEQ, width), lambda i: (i, 0))


def whole(shape):
    return pl.BlockSpec(shape, lambda i: (0,) * len(shape))


SMEM = pl.BlockSpec(memory_space=pltpu.SMEM)


def ssd_forward(cut, x_raw, bc_raw, dt_raw, taps_x, taps_bc, heads, spread):
    return pl.pallas_call(
        fwd_kernel,
        grid=(2,),
        in_specs=[SMEM, seq_spec(768), seq_spec(256), seq_spec(128), whole((8, 768)), whole((8, 256)), whole((8, 128)), whole((128, 768))],
        out_specs=[seq_spec(768), pl.BlockSpec((1, 128, 768), lambda i: (i, 0, 0))],
        out_shape=[jax.ShapeDtypeStruct((1024, 768), F32), jax.ShapeDtypeStruct((2, 128, 768), F32)],
        compiler_params=pltpu.CompilerParams(vmem_limit_bytes=VMEM_LIMIT),
        cost_estimate=pl.CostEstimate(flops=4_000_000_000, bytes_accessed=9_000_000, transcendentals=4_000_000),
    )(cut, x_raw, bc_raw, dt_raw, taps_x, taps_bc, heads, spread)


def bwd_kernel(cut_ref, place_ref, xr_ref, bcr_ref, dtr_ref, dy_ref, y_ref, st_ref, tx_ref, tbc_ref, hd_ref, e_ref, et_ref,
               gx_ref, keep_ref, send_ref, gdt_ref, gtx_ref, keepc_ref, sendc_ref, ghd_ref,
               ds_ref, masks_ref, steps_ref, up_ref, ccol_ref, ct_ref, c1t_ref, b0_ref, acc_ref, accb_ref, skip_ref):
    seq = pl.program_id(0)
    cut = cut_ref[seq]
    masks = conv_masks(cut)

    def conv_back(du, v, taps, masks):
        g = taps[3:4] * du
        sums = [jnp.sum(du * v, axis=0, keepdims=True)]
        for j in (1, 2, 3):
            dm = du * masks[j - 1]
            g = g + taps[3 - j : 4 - j] * pltpu.roll(dm, SEQ - j, 0)
            sums.append(jnp.sum(dm * pltpu.roll(v, j, 0), axis=0, keepdims=True))
        return g, [sums[3], sums[2], sums[1], sums[0], jnp.sum(du, axis=0, keepdims=True)]

    @pl.when(seq == 0)
    def _():
        gtx_ref[...] = jnp.zeros_like(gtx_ref)
        keepc_ref[...] = jnp.zeros_like(keepc_ref)
        sendc_ref[...] = jnp.zeros_like(sendc_ref)
        ghd_ref[...] = jnp.zeros_like(ghd_ref)

    act = []
    for i in range(2):
        sl = slice(i * SUB, i * SUB + SUB)
        u = conv(bcr_ref[:, sl], tbc_ref[:, sl], masks)
        act.append((u * sigmoid(u)).astype(BF))
    for j in range(3):
        masks_ref[j] = masks[j]
    bb, cb = act
    dt, c, ew, e1 = time_steps(dtr_ref[...], hd_ref[...], cut)
    fill_columns(c, ccol_ref, ct_ref)
    put_stack(steps_ref, [dt, ew * dt[:HALF], e1, ew])
    blk = lambda a, k: a[k * HALF : k * HALF + HALF]
    for k in (0, 1):
        up = masked_scores(blk(cb, k), blk(bb, k), k, cut, lower=False)
        for n, at in enumerate(BLOCKS):
            up_ref[k, n] = up[at]
    c1t_ref[...] = cb[HALF:].T
    b0_ref[...] = bb[:HALF]
    ds_ref[...] = jnp.zeros_like(ds_ref)
    acc_ref[...] = jnp.zeros_like(acc_ref)
    accb_ref[...] = jnp.zeros_like(accb_ref)
    skip_ref[...] = jnp.zeros_like(skip_ref)

    def one_pair(p, carried):
        sl = pl.ds(pl.multiple_of(p * SUB, SUB), SUB)
        e, et, taps = e_ref[:, sl], et_ref[sl, :], tx_ref[:, sl]
        xr = xr_ref[:, sl]
        pair_masks = [masks_ref[j] for j in range(3)]
        u = conv(xr, taps, pair_masks)
        sg = sigmoid(u)
        x = u * sg
        dtx, twx, e1x, ewx = spread_stack(steps_ref, e, (SEQ, HALF, HALF, HALF))
        xtf = x * dtx
        xt = xtf.astype(BF)
        dy = dy_ref[:, sl]
        dyb = dy.astype(BF)
        dyh = dyb.astype(F32)
        xh = xt.astype(F32)
        xl = (xtf - xh).astype(BF)
        dl_turned = pltpu.roll(dy - dyh, 64, 1).astype(BF)
        xh_turned = pltpu.roll(xh, 64, 1).astype(BF)
        skip = jnp.broadcast_to(jnp.sum(dy * x, axis=0, keepdims=True), (16, SUB))
        stack = parts(dyh * y_ref[:, sl], 2) + parts(dyh * x, 2) + parts(skip, 3)
        wide = mm(jnp.concatenate(stack, axis=0), et)
        acc_ref[0] += wide[0:SEQ] + wide[SEQ : 2 * SEQ]
        acc_ref[1] += wide[2 * SEQ : 3 * SEQ] + wide[3 * SEQ : 4 * SEQ]
        skip_ref[...] += wide[2048:2056] + wide[2064:2072] + wide[2080:2088]
        dxs = []
        for k in (0, 1):
            back = 0.0
            for h in (0, 1):
                head = 2 * p + h
                lanes, none = head_lanes(h), jnp.zeros((), BF)
                dm = jnp.where(lanes, blk(dyb, k), none)
                dm2 = jnp.concatenate([jnp.where(lanes, blk(dyb, k), blk(dl_turned, k)), dm], axis=1)
                xm2 = jnp.concatenate([jnp.where(lanes, blk(xt, k), blk(xh_turned, k)), jnp.where(lanes, blk(xl, k), none)], axis=1)
                row = ct_ref[k, pl.ds(head, 1), :]
                gfull = mm_nt(dm2, xm2)
                mt = {}
                for n, (i, j) in enumerate(BLOCKS):
                    ti, sj = slice(i * SUB, i * SUB + SUB), slice(j * SUB, j * SUB + SUB)
                    decay = jnp.exp(-jnp.abs(ccol_ref[k, head, ti, :] - row[:, sj]))
                    if i == j:
                        decay_t = decay
                    else:
                        decay_t = jnp.exp(-jnp.abs(ccol_ref[k, head, sj, :] - row[:, ti]))
                    ds_ref[k, i + j] += gfull[ti, sj] * decay
                    mt[i, j] = (decay_t * up_ref[k, n]).astype(BF)
                rows0 = jnp.concatenate([mt[0, 0], mt[1, 0]], axis=1)
                rows1 = jnp.concatenate([jnp.zeros((SUB, SUB), BF), mt[1, 1]], axis=1)
                back = back + mm(jnp.concatenate([rows0, rows1], axis=0), dm)
            dxs.append(back)
        st, st_low = parts(st_ref[0, :, sl], 2)
        dcs, dcs_low = parts(dy[HALF:] * e1x, 2)
        accb_ref[0] += mm_nt(dcs, st) + (mm_nt(dcs_low, st) + mm_nt(dcs, st_low))
        dst, dst_low = parts(mm(c1t_ref[...], dcs) + mm(c1t_ref[...], dcs_low), 2)
        dxw = mm(b0_ref[...], dst)
        xw, xw_low = parts(x[:HALF] * twx, 2)
        accb_ref[1] += mm_nt(xw, dst) + (mm_nt(xw_low, dst) + mm_nt(xw, dst_low))
        dx0 = dxs[0] + dxw * ewx
        dxt = jnp.concatenate([dx0, dxs[1]], axis=0)
        wide = mm(jnp.concatenate(parts(x * dxt, 2), axis=0), et)
        acc_ref[2] += wide[:SEQ] + wide[SEQ:]
        dx = dtx * dxt + taps[5:6] * dy
        du = dx * (sg * (1.0 + u * (1.0 - sg)))
        g, sums = conv_back(du, xr, taps, pair_masks)
        gx_ref[:, sl] = g.astype(BF)
        gtx_ref[0:5, sl] += jnp.concatenate(sums, axis=0)
        return carried

    lax.fori_loop(0, 6 // PAIRS, lambda i, x: [one_pair(i * PAIRS + j, x) for j in range(PAIRS)][0], 0)
    sum_y, sum_x, sum_d = acc_ref[0], acc_ref[1], acc_ref[2]
    d_c1, d_b0 = accb_ref[0], accb_ref[1]
    d_b, d_c = [], []
    for k in (0, 1):
        bk, ck = blk(bb, k), blk(cb, k)
        m = {}
        for i, j in ((0, 0), (1, 0), (1, 1)):
            t = rows((SUB, SUB)) + (k * HALF + i * SUB)
            r = cols((SUB, SUB)) + (k * HALF + j * SUB)
            m[i, j] = jnp.where((t >= r) & same_doc(t, r, cut), ds_ref[k, i + j], 0.0).astype(BF)
        lowr = jnp.concatenate([m[1, 0], m[1, 1]], axis=1)
        d_c += [mm(m[0, 0], bk[:SUB]), mm(lowr, bk)]
        d_b += [mm_tn(m[0, 0], ck[:SUB]) + mm_tn(m[1, 0], ck[SUB:]), mm_tn(m[1, 1], ck[SUB:])]
    d_b = jnp.concatenate([jnp.concatenate(d_b[:2], axis=0) + d_b0] + d_b[2:], axis=0)
    d_c = jnp.concatenate(d_c[:2] + [jnp.concatenate(d_c[2:], axis=0) + d_c1], axis=0)
    for i, d in ((0, d_b), (1, d_c)):
        sl = slice(i * SUB, i * SUB + SUB)
        v = bcr_ref[:, sl]
        u = conv(v, tbc_ref[:, sl], masks)
        sg = sigmoid(u)
        g, sums = conv_back(d * (sg * (1.0 + u * (1.0 - sg))), v, tbc_ref[:, sl], masks)

        @pl.when(place_ref[3] == i)
        def _():
            keep_ref[...] = g
            for r, s in enumerate(sums):
                keepc_ref[r : r + 1] += s

        @pl.when(place_ref[3] != i)
        def _():
            send_ref[...] = g
            for r, s in enumerate(sums):
                sendc_ref[r : r + 1] += s

    hd = hd_ref[...]
    w = (sum_y - hd[2:3] * sum_x) - dt * sum_d
    tri = jnp.where((cols((SEQ, SEQ)) >= rows((SEQ, SEQ))) & same_doc(rows((SEQ, SEQ)), cols((SEQ, SEQ)), cut), 1.0, 0.0).astype(BF)
    run = split_right(tri, w)
    d_dt = sum_d + hd[1:2] * run
    gd = d_dt * sigmoid(dtr_ref[...] + hd[0:1])
    gdt_ref[...] = gd.astype(BF)
    ghd_ref[0:1] += jnp.sum(gd, axis=0, keepdims=True)
    ghd_ref[2:3] += skip_ref[0:1]
    ghd_ref[1:2] += jnp.sum(dt * run, axis=0, keepdims=True) * hd[1:2]


def ssd_backward(cut, place, x_raw, bc_raw, dt_raw, dy, y, st, taps_x, taps_bc, heads, spread, spread_t):
    return pl.pallas_call(
        bwd_kernel,
        grid=(2,),
        in_specs=[SMEM, SMEM, seq_spec(768), seq_spec(256), seq_spec(128), seq_spec(768), seq_spec(768),
                  pl.BlockSpec((1, 128, 768), lambda i: (i, 0, 0)), whole((8, 768)), whole((8, 256)), whole((8, 128)), whole((128, 768)), whole((768, 128))],
        out_specs=[seq_spec(768), seq_spec(128), seq_spec(128), seq_spec(128), whole((8, 768)), whole((8, 128)), whole((8, 128)), whole((8, 128))],
        out_shape=[jax.ShapeDtypeStruct((1024, 768), BF), jax.ShapeDtypeStruct((1024, 128), F32), jax.ShapeDtypeStruct((1024, 128), F32), jax.ShapeDtypeStruct((1024, 128), BF),
                   jax.ShapeDtypeStruct((8, 768), F32), jax.ShapeDtypeStruct((8, 128), F32), jax.ShapeDtypeStruct((8, 128), F32), jax.ShapeDtypeStruct((8, 128), F32)],
        scratch_shapes=[
            pltpu.VMEM((2, 3, SUB, SUB), F32),
            pltpu.VMEM((3, SEQ, SUB), F32),
            pltpu.VMEM((5 * SEQ, SUB), BF),
            pltpu.VMEM((2, 3, SUB, SUB), F32),
            pltpu.VMEM((2, 12, HALF, SUB), F32),
            pltpu.VMEM((2, SUB, HALF), F32),
            pltpu.VMEM((SUB, HALF), BF),
            pltpu.VMEM((HALF, SUB), BF),
            pltpu.VMEM((3, SEQ, SUB), F32),
            pltpu.VMEM((2, HALF, SUB), F32),
            pltpu.VMEM((8, SUB), F32),
        ],
        compiler_params=pltpu.CompilerParams(vmem_limit_bytes=VMEM_LIMIT),
        cost_estimate=pl.CostEstimate(flops=12_000_000_000, bytes_accessed=14_000_000, transcendentals=4_000_000),
    )(cut, place, x_raw, bc_raw, dt_raw, dy, y, st, taps_x, taps_bc, heads, spread, spread_t)


def place_blocks(pieces, w_ref, sem, row_of, lanes=slice(None)):
    for ref, k, first in pieces:
        for r in range(ref.shape[0]):
            for h in range(2):
                row = pl.multiple_of(row_of(k, first + r, h) * 48, 48)
                pltpu.make_async_copy(ref.at[r, h, :, lanes], w_ref.at[pl.ds(row, 48), lanes], sem).start()


def ring_pieces(refs):
    return list(zip(refs, (0, 1, 3, 2, 2), (0, 0, 0, 0, 2)))


def start_halves(refs, which, buf, sems):
    for k in range(4):
        pltpu.make_async_copy(refs[k // 2].at[k % 2, which], buf.at[k], sems.at[k]).start()


def project_kernel(order_ref, place_ref, *refs):
    a_refs, t_refs = refs[0:5], refs[5:7]
    normed_ref, nt_ref, xr_ref, bc_ref, dt_ref, w_ref, wbc_ref, gain, tok, w_sem, t_sem = refs[7:]
    step = pl.program_id(0)

    @pl.when(step == 0)
    def _():
        z, xh, y = place_ref[0], place_ref[1], place_ref[2]
        start_halves(t_refs, 0, tok, t_sem)

        def row_of(k, r, h):
            return (lax.rem(z - k + 4, 4) * 2 + lax.rem(xh + h, 2)) * 4 + lax.rem(y - r + 4, 4)

        place_blocks(ring_pieces(a_refs), w_ref, w_sem, row_of)
        pltpu.make_async_copy(w_ref, w_ref, w_sem).wait()
        gain[...] = w_ref[:, 1024:1152].astype(F32).T[8:16]
        wbc_ref[...] = w_ref[:, 768:1024]

    pltpu.make_async_copy(t_refs[0].at[0, 0], tok.at[step], t_sem.at[step]).wait()
    wide = tok[step].astype(F32)
    inv = lax.rsqrt(jnp.mean(wide * wide, axis=-1, keepdims=True) + EPS)
    normed = (wide * inv * gain[4:5]).astype(BF)
    normed_ref[...] = normed
    nt_ref[...] = normed.T
    xr_ref[...] = mm(normed, w_ref[:, 0:768])
    bc_ref[...] = mm(normed, w_ref[:, 768:1024])
    dt_ref[...] = jnp.where(cols((HALF, SUB)) < 12, mm(normed, w_ref[:, 1024:1152]), 0.0)


ANY = pl.BlockSpec(memory_space=pl.ANY)


def by_order(width):
    return pl.BlockSpec((HALF, width), lambda i, order, place: (order[i], 0))


def turned():
    return pl.BlockSpec((1536, HALF), lambda i, order, place: (0, order[i]))


def fixed(shape):
    return pl.BlockSpec(shape, lambda i, *_: (0,) * len(shape))


def project(order, place, parts_in, tokens):
    sd = jax.ShapeDtypeStruct
    return pl.pallas_call(
        project_kernel,
        grid_spec=pltpu.PrefetchScalarGridSpec(
            num_scalar_prefetch=2,
            grid=(4,),
            in_specs=[ANY] * 7,
            out_specs=[by_order(1536), turned(), by_order(768), by_order(256), by_order(128), fixed((1536, 1152)), fixed((1536, 256)), fixed((8, 1536))],
            scratch_shapes=[pltpu.VMEM((4, HALF, 1536), BF), pltpu.SemaphoreType.DMA, pltpu.SemaphoreType.DMA((4,))],
        ),
        out_shape=[sd((1024, 1536), BF), sd((1536, 1024), BF), sd((1024, 768), F32), sd((1024, 256), F32), sd((1024, 128), F32), sd((1536, 1152), BF), sd((1536, 256), BF), sd((8, 1536), F32)],
        compiler_params=pltpu.CompilerParams(vmem_limit_bytes=VMEM_LIMIT),
        cost_estimate=pl.CostEstimate(flops=3_700_000_000, bytes_accessed=22_000_000, transcendentals=0),
    )(order, place, *parts_in, *tokens)


def gate_kernel(order_ref, place_ref, b0, b1, b2, b3, b4, c0, c1, normed_ref, y_ref, gg_ref, gate_ref, gs_ref, cot_ref, s_ref, w_ref, buf, w_sem, t_sem):
    step = pl.program_id(0)

    def arrived(n):
        half = w_ref.at[:, n * 768 : n * 768 + 768]
        pltpu.make_async_copy(half, half, w_sem.at[n]).wait()

    @pl.when(step == 0)
    def _():
        z, xh, y = place_ref[0], place_ref[1], place_ref[2]
        start_halves((c0, c1), 1, buf, t_sem)

        def row_of(k, r, h):
            return (lax.rem(z - r + 4, 4) * 2 + lax.rem(xh + h, 2)) * 4 + lax.rem(y - k + 4, 4)

        for n in (0, 1):
            place_blocks(ring_pieces((b0, b1, b2, b3, b4)), w_ref, w_sem.at[n], row_of, slice(n * 768, n * 768 + 768))
        arrived(0)

    pltpu.make_async_copy(c0.at[0, 1], buf.at[step], t_sem.at[step]).wait()
    cot = buf[step]
    cot_ref[...] = cot.T
    gate = mm(normed_ref[...], w_ref[:, 0:768])
    gate_ref[...] = gate

    @pl.when(step == 0)
    def _():
        arrived(1)

    gs = mm(cot, w_ref[:, 768:1536])
    gs_ref[...] = gs
    mixed = y_ref[...] * (gate * sigmoid(gate))
    sq = jnp.sum(mixed * mixed, axis=-1, keepdims=True)
    cr = jnp.sum((gs * gg_ref[0:1]) * mixed, axis=-1, keepdims=True)
    lane = cols((HALF, SUB))
    s_ref[...] = jnp.where(lane == 0, sq, jnp.where(lane == 1, cr, 0.0)).T[0:8]


def gate_side(order, place, parts_in, cots, normed, y, gg):
    sd = jax.ShapeDtypeStruct
    return pl.pallas_call(
        gate_kernel,
        grid_spec=pltpu.PrefetchScalarGridSpec(
            num_scalar_prefetch=2,
            grid=(4,),
            in_specs=[ANY] * 7 + [by_order(1536), by_order(768), fixed((8, 768))],
            out_specs=[by_order(768), by_order(768), turned(), pl.BlockSpec((8, HALF), lambda i, order, place: (0, order[i])), fixed((1536, 1536))],
            scratch_shapes=[pltpu.VMEM((4, HALF, 1536), BF), pltpu.SemaphoreType.DMA((2,)), pltpu.SemaphoreType.DMA((4,))],
        ),
        out_shape=[sd((1024, 768), F32), sd((1024, 768), F32), sd((1536, 1024), BF), sd((8, 1024), F32), sd((1536, 1536), BF)],
        compiler_params=pltpu.CompilerParams(vmem_limit_bytes=VMEM_LIMIT),
        cost_estimate=pl.CostEstimate(flops=4_900_000_000, bytes_accessed=30_000_000, transcendentals=800_000),
    )(order, place, *parts_in, *cots, normed, y, gg)


MIX, OUT, OUTER = 4, 6, 4


def middle_kernel(place_ref, s0, s1, s2, s3, gate_ref, gs_ref, y_ref, gg_ref, w_ref, n_ref, c_ref,
                  low_ref, dy_ref, gain_ref, own_ref, core_ref, xl_ref, both_ref, grad_ref, scaled, gated):
    step = pl.program_id(0)

    @pl.when(step < MIX)
    def _():
        sums = ((s0[...] + s1[...]) + (s2[...] + s3[...])).T
        inv = lax.rsqrt(sums[:, 0:1] / 3072 + EPS)
        corr = inv * inv * inv * (sums[:, 1:2] / 3072)
        gate, gs, y, gg = gate_ref[...], gs_ref[...], y_ref[...], gg_ref[0:1]
        sg = sigmoid(gate)
        act = gate * sg
        mixed = y * act
        normal = mixed * inv
        at = pl.ds(pl.multiple_of(step * HALF, HALF), HALF)
        scaled[at] = (normal * gg).astype(BF)
        gm = gs * gg * inv - mixed * corr
        low = (gm * y * (sg * (1.0 + gate * (1.0 - sg)))).astype(BF)
        gated[at] = low
        low_ref[...] = low
        dy_ref[...] = gm * act

        @pl.when(step == 0)
        def _():
            gain_ref[...] = jnp.zeros_like(gain_ref)

        gain_ref[0:1] += jnp.sum(gs * normal, axis=0, keepdims=True)

    @pl.when((step >= MIX) & (step < MIX + OUT))
    def _():
        rows_out(place_ref, mm_nt(scaled[...], w_ref[...]), [own_ref, core_ref, xl_ref, both_ref])

    @pl.when(step >= MIX + OUT)
    def _():
        for at, a_ref, b_ref in ((0, n_ref, gated), (768, c_ref, scaled)):
            r = mm(a_ref[...], b_ref[...]).astype(BF)
            for yi in range(4):
                for xi in range(2):
                    row = (xi * 4 + yi) * 48
                    grad_ref[yi, xi * 48 : xi * 48 + 48, at : at + 768] = r[row : row + 48]


def middle(place, sums, gate, gs, y, gg, w_2, normed_t, cot_t):
    sd = jax.ShapeDtypeStruct
    mix_at = lambda i: jnp.minimum(i, MIX - 1)
    out_at = lambda i: jnp.clip(i - MIX, 0, OUT - 1)
    outer_at = lambda i: jnp.maximum(i - MIX - OUT, 0)
    tokens = pl.BlockSpec((HALF, 768), lambda i, place: (mix_at(i), 0))
    chunk = pl.BlockSpec((384, 1024), lambda i, place: (outer_at(i), 0))
    rows_spec = pl.BlockSpec((HALF, 256), lambda i, place: (0, out_at(i)))
    return pl.pallas_call(
        middle_kernel,
        grid_spec=pltpu.PrefetchScalarGridSpec(
            num_scalar_prefetch=1,
            grid=(MIX + OUT + OUTER,),
            in_specs=[pl.BlockSpec((8, HALF), lambda i, place: (0, mix_at(i)))] * 4
            + [tokens] * 3
            + [fixed((8, 768)), pl.BlockSpec((256, 768), lambda i, place: (out_at(i), 1)), chunk, chunk],
            out_specs=[tokens, tokens, fixed((8, 768))] + [rows_spec] * 4 + [pl.BlockSpec((4, 96, 1536), lambda i, place: (outer_at(i), 0, 0))],
            scratch_shapes=[pltpu.VMEM((1024, 768), BF), pltpu.VMEM((1024, 768), BF)],
        ),
        out_shape=[sd((1024, 768), BF), sd((1024, 768), F32), sd((8, 768), F32), sd((HALF, 1536), F32)]
        + [sd((HALF, 1536), BF)] * 3
        + [sd((16, 96, 1536), BF)],
        compiler_params=pltpu.CompilerParams(vmem_limit_bytes=VMEM_LIMIT),
        cost_estimate=pl.CostEstimate(flops=7_300_000_000, bytes_accessed=30_000_000, transcendentals=800_000),
    )(place, *sums, gate, gs, y, gg, w_2, normed_t, cot_t)


def outer_z_kernel(place_ref, n_ref, g_ref, small_ref, *out):
    step = pl.program_id(0)
    y = place_ref[2]
    r = mm(n_ref[...], g_ref[...]).astype(BF)
    small = small_ref[...].astype(BF)
    for k in range(4):

        @pl.when(step == k)
        def _():
            for yi in range(4):
                to = lax.rem(yi - y + 4, 4)
                for xi in range(2):
                    at = (xi * 4 + yi) * 48
                    out[k][to, xi * 48 : xi * 48 + 48] = r[at : at + 48]
                out[k][to, 96:104] = small


def outer_side_kernel(place_ref, n_ref, g_ref, m_ref, d_ref, small_ref, maps_ref, *out):
    step = pl.program_id(0)
    y, xl = place_ref[2], place_ref[4]

    def columns(maps, steps):
        lane = cols(maps.shape)
        maps = jnp.where(xl == 0, maps, pltpu.roll(maps, 64, 1))
        return jnp.where(lane < 64, maps, pltpu.roll(steps, 64, 1)).astype(BF)

    n = n_ref[...]
    r = [mm(n, g_ref[...]).astype(BF), columns(mm(n, m_ref[...]), mm(n, d_ref[...]))]
    small = [small_ref[...].astype(BF), columns(maps_ref[:, 0:128], maps_ref[:, 128:256])]
    for k in range(4):

        @pl.when(step == k)
        def _():
            for part, lanes in ((0, slice(0, 256)), (1, slice(256, 384))):
                for yi in range(4):
                    to = lax.rem(yi - y + 4, 4)
                    for xi in range(2):
                        at = (xi * 4 + yi) * 48
                        out[k][to, xi * 48 : xi * 48 + 48, lanes] = r[part][at : at + 48]
                    out[k][to, 96:104, lanes] = small[part]


def outer_split(kernel, place, normed_t, grads, smalls, width):
    return pl.pallas_call(
        kernel,
        grid_spec=pltpu.PrefetchScalarGridSpec(
            num_scalar_prefetch=1,
            grid=(4,),
            in_specs=[pl.BlockSpec((384, 1024), lambda i, place: (lax.rem(place[0] + i, 4), 0))] + [spec for _, spec in grads] + [fixed(t.shape) for t in smalls],
            out_specs=[fixed((4, 104, width))] * 4,
        ),
        out_shape=[jax.ShapeDtypeStruct((4, 104, width), BF)] * 4,
        compiler_params=pltpu.CompilerParams(vmem_limit_bytes=VMEM_LIMIT),
        cost_estimate=pl.CostEstimate(flops=1, bytes_accessed=1, transcendentals=0),
    )(place, normed_t, *[g for g, _ in grads], *smalls)


def fold_kernel(*refs):
    for parts4, lanes in ((refs[0:4], slice(0, 512)), (refs[4:8], slice(512, 896))):
        for k in range(4):
            near = parts4[1][k].astype(F32) + parts4[3][k].astype(F32)
            refs[8 + k][:, lanes] = ((parts4[0][k].astype(F32) + parts4[2][k].astype(F32)) + near).astype(BF)


def fold(a_parts, b_parts):
    vmem = pl.BlockSpec(memory_space=pltpu.VMEM)
    return pl.pallas_call(
        fold_kernel,
        in_specs=[vmem] * 8,
        out_specs=[vmem] * 4,
        out_shape=[jax.ShapeDtypeStruct((104, 896), BF)] * 4,
        compiler_params=pltpu.CompilerParams(vmem_limit_bytes=VMEM_LIMIT),
        cost_estimate=pl.CostEstimate(flops=1, bytes_accessed=1, transcendentals=0),
    )(*a_parts, *b_parts)


def rows_out(place_ref, total, out):
    for base in range(4):

        @pl.when(place_ref[3] * 2 + place_ref[4] == base)
        def _():
            for ref, at in zip(out, (base, base ^ 2, base ^ 1, base ^ 3)):
                ref[...] = total[at * HALF : at * HALF + HALF].astype(ref.dtype)


def token_kernel(place_ref, g_ref, x_ref, d_ref, wz_ref, wx_ref, wd_ref, own_ref, mate_ref, send_ref):
    total = mm_nt(g_ref[...], wz_ref[...]) + mm_nt(x_ref[...], wx_ref[...]) + mm_nt(d_ref[...], wd_ref[...])
    rows_out(place_ref, total, [own_ref, send_ref.at[0:HALF], mate_ref, send_ref.at[HALF:SEQ]])


def by_rows(kernel, place, tokens, weights, places, outs, work=1):
    columns = lambda at: lambda i, place: (i, at(place))
    return pl.pallas_call(
        kernel,
        grid_spec=pltpu.PrefetchScalarGridSpec(
            num_scalar_prefetch=1,
            grid=(6,),
            in_specs=[fixed(t.shape) for t in tokens] + [pl.BlockSpec((256, t.shape[1]), columns(at)) for t, at in zip(tokens, places)],
            out_specs=[pl.BlockSpec((n, 256), lambda i, place: (0, i)) for n, _ in outs],
        ),
        out_shape=[jax.ShapeDtypeStruct((n, 1536), t) for n, t in outs],
        compiler_params=pltpu.CompilerParams(vmem_limit_bytes=VMEM_LIMIT),
        cost_estimate=pl.CostEstimate(flops=work, bytes_accessed=1, transcendentals=0),
    )(place, *tokens, *weights)


def sum_pieces_kernel(place_ref, p0, p1, p2, p3, zo_ref, keep_ref, send_ref):
    total = (p0[...].astype(F32) + p2[...].astype(F32)) + (p1[...].astype(F32) + p3[...].astype(F32))
    small = total[96:104].astype(BF)
    send_ref[48:56, 0:896] = small
    keep_ref[48:56, 0:896] = small.astype(F32)
    for xh in (0, 1):

        @pl.when(place_ref[1] == xh)
        def _():
            keep_ref[0:48, 0:896] = total[xh * 48 : xh * 48 + 48]
            send_ref[0:48, 0:896] = total[48 - xh * 48 : 96 - xh * 48].astype(BF)

    for xh in (0, 1):

        @pl.when(place_ref[1] == xh)
        def _():
            keep_ref[0:48, 896:2432] = zo_ref[xh * 48 : xh * 48 + 48].astype(F32)
            send_ref[0:48, 896:2432] = zo_ref[48 - xh * 48 : 96 - xh * 48]

    keep_ref[48:56, 896:2432] = jnp.zeros((8, 1536), F32)
    send_ref[48:56, 896:2432] = jnp.zeros((8, 1536), BF)


def sum_far_kernel(place_ref, own_ref, far_ref, keep_ref, send_ref):
    total = own_ref[...] + far_ref[...].astype(F32)
    keep_ref[24:32] = total[48:56]
    send_ref[24:32] = total[48:56]
    for core in (0, 1):

        @pl.when(place_ref[3] == core)
        def _():
            keep_ref[0:24] = total[core * 24 : core * 24 + 24]
            send_ref[0:24] = total[24 - core * 24 : 48 - core * 24]


def whole_call(kernel, place, arrays, shapes):
    vmem = pl.BlockSpec(memory_space=pltpu.VMEM)
    return pl.pallas_call(
        kernel,
        in_specs=[SMEM] + [vmem] * len(arrays),
        out_specs=[vmem] * len(shapes),
        out_shape=shapes,
        compiler_params=pltpu.CompilerParams(vmem_limit_bytes=VMEM_LIMIT),
        cost_estimate=pl.CostEstimate(flops=1, bytes_accessed=1, transcendentals=0),
    )(place, *arrays)


def sum_pieces(place, pieces, zo):
    shapes = [jax.ShapeDtypeStruct((56, 2432), F32), jax.ShapeDtypeStruct((56, 2432), BF)]
    return whole_call(sum_pieces_kernel, place, [*pieces, zo], shapes)


def sum_far(place, own, far):
    return whole_call(sum_far_kernel, place, [own, far], [jax.ShapeDtypeStruct((32, 2432), F32)] * 2)


def after_kernel(x_ref, *refs):
    pass


def after(x, *deps):
    return pl.pallas_call(
        after_kernel,
        in_specs=[ANY] * (1 + len(deps)),
        out_specs=ANY,
        out_shape=jax.ShapeDtypeStruct(x.shape, x.dtype),
        input_output_aliases={0: 0},
    )(x, *deps)


def swap(a, axis):
    return lax.ppermute(a, axis, [(0, 1), (1, 0)])


def turn(a, axis, k):
    return lax.ppermute(a, axis, [(i, (i + k) % 4) for i in range(4)])


def pair(own, other, axis):
    first = lax.axis_index(axis) == 0
    return jnp.stack([jnp.where(first, own, other), jnp.where(first, other, own)])


def mine(a, axis, dim, size):
    i = lax.axis_index(axis)
    return (
        lax.dynamic_slice_in_dim(a, i * size, size, dim),
        lax.dynamic_slice_in_dim(a, (1 - i) * size, size, dim),
    )


def turns(a, axis):
    return [a] + [turn(a, axis, k) for k in (1, 2, 3)]


def shards(resid, cotangent, segments, pre_gain, w_z, w_x, w_bc, w_dt, conv_x, conv_x_bias, conv_bc, conv_bc_bias, dt_bias, a_log, d_skip, gate_gain, w_out):
    core, xl = lax.axis_index("c"), lax.axis_index("xl")
    place = jnp.stack([lax.axis_index("z"), lax.axis_index("xh"), lax.axis_index("y"), core, xl])
    base = core * 2 + xl
    order = jnp.stack([core * 2, core * 2 + 1, 2 - core * 2, 3 - core * 2])

    own_bc = jnp.concatenate([w_bc, pre_gain[:, None], jnp.zeros((12, 127), BF)], axis=1)
    keep_x, send_x = mine(w_x, "c", 1, 768)
    keep_dt, send_dt = mine(w_dt, "c", 1, 12)
    bc_x, bc_c = swap(own_bc, "xl"), swap(own_bc, "c")
    bc_d = lax.ppermute(own_bc, ("c", "xl"), [(i, 3 - i) for i in range(4)])
    got = swap(jnp.concatenate([send_x, send_dt], axis=1), "c")
    bc48 = pair(pair(own_bc, bc_x, "xl"), pair(bc_c, bc_d, "xl"), "c").reshape(48, 384)
    xdt = pair(jnp.concatenate([keep_x, keep_dt], axis=1), got, "c").reshape(48, 780)
    first = jnp.concatenate([xdt[:, :768], bc48[:, :256], xdt[:, 768:], bc48[:, 256:372]], axis=1)
    first_far = swap(first, "xh")
    first = jnp.stack([first, first_far])

    keep_z, send_z = mine(w_z, "c", 1, 768)
    keep_o, send_o = mine(w_out.T, "c", 1, 768)
    got = swap(jnp.concatenate([send_z, send_o], axis=1), "c")
    second = pair(jnp.concatenate([keep_z, keep_o], axis=1), got, "c").reshape(48, 1536)
    second = jnp.stack([second, swap(second, "xh")])

    half = lax.all_gather(jnp.stack([resid, cotangent]), "xl", axis=0, tiled=False)
    near_x, near = turns(first, "y"), turns(second, "z")
    b_own = jnp.stack(near)
    b_ahead, b_back = turn(b_own, "y", 1), turn(b_own, "y", 3)
    a_own = after(jnp.stack(near_x), *near[1:])
    a_ahead, a_back = turn(a_own, "z", 1), turn(a_own, "z", 3)
    a_parts = [a_own, a_ahead, a_back, turn(after(a_ahead[:2], b_ahead, b_back), "z", 1), turn(after(a_back[2:], b_ahead, b_back), "z", 3)]

    def own(a, size):
        return mine(a, "c", a.ndim - 1, size)[0]

    cx, cxb, gg = own(conv_x, 768), own(conv_x_bias, 768), own(gate_gain, 768)
    dtb, al, dsk = own(dt_bias, 12), own(a_log, 12), own(d_skip, 12)
    taps_x = jnp.concatenate([cx, cxb[None], jnp.repeat(dsk, 64)[None], jnp.zeros((2, 768), F32)], axis=0)
    taps_bc = jnp.concatenate([conv_bc, conv_bc_bias[None], jnp.zeros((3, 256), F32)], axis=0)
    wide_heads = lambda v: jnp.pad(v, (0, 116))[None]
    heads = jnp.concatenate([wide_heads(dtb), wide_heads(-jnp.exp(al)), wide_heads(dsk), jnp.zeros((5, 128), F32)], axis=0)
    gains = jnp.broadcast_to(gg[None], (8, 768))
    spread_np = np.arange(768)[None, :] // 64 == np.arange(128)[:, None]
    spread, spread_t = spread_np.astype(BF), np.ascontiguousarray(spread_np.T).astype(BF)
    cut = jnp.sum((segments == after(segments[:1], near[1])).astype(jnp.int32))[None]
    cuts = pair(cut, swap(cut, "c"), "c").reshape(2)

    half = after(half, a_parts[1], a_parts[2], b_ahead, b_back, taps_x, taps_bc, heads, gains, cuts, order, place)
    tokens = [half, swap(half, "c")]
    normed, normed_t, x_raw, bc_raw, dt_raw, w_1, w_maps, gain_rows = project(order, place, a_parts, tokens)

    b_ahead, b_back = after(b_ahead, dt_raw), after(b_back, dt_raw)
    b_parts = [b_own, b_ahead, b_back, turn(b_ahead[:2], "y", 1), turn(b_back[2:], "y", 3)]
    y, st = ssd_forward(cuts, x_raw, bc_raw, dt_raw, taps_x, taps_bc, heads, spread)

    gate, gs, cot_t, sums, w_2 = gate_side(order, place, b_parts, tokens, normed, y, gains)
    sums_c, sums_x = swap(sums, "c"), swap(sums, "xl")
    sums_d = lax.ppermute(sums, ("c", "xl"), [(i, 3 - i) for i in range(4)])
    gate_low, dy, g_gain, *out_rows, g_zo = middle(place, [sums, sums_c, sums_x, sums_d], gate, gs, y, gains, w_2, normed_t, cot_t)

    def exchange(rows):
        diagonal = lax.ppermute(rows[3], ("c", "xl"), [(i, 3 - i) for i in range(4)])
        return rows[0], swap(rows[1], "c"), swap(rows[2], "xl"), diagonal

    g_zo_z = lax.psum_scatter(g_zo.reshape(1536, 1536), "z", scatter_dimension=0, tiled=True)
    g_zo_y = lax.psum_scatter(g_zo_z, "y", scatter_dimension=0, tiled=True)
    out_rows = exchange(out_rows)
    wide = lambda a: a.astype(F32)
    layer_out = (wide(resid) + ((out_rows[0] + wide(out_rows[1])) + (wide(out_rows[2]) + wide(out_rows[3])))).astype(BF)

    x_low, keep, send, gdt, g_tx, keep_c, send_c, g_hd = ssd_backward(cuts, place, x_raw, bc_raw, dt_raw, dy, y, st, taps_x, taps_bc, heads, spread, spread_t)

    small_x = jnp.concatenate([g_tx[:5], g_gain[:1], jnp.zeros((2, 768), F32)], axis=0)
    left = pl.BlockSpec((1024, 512), lambda i, place: (0, 0))
    right = pl.BlockSpec((1024, 256), lambda i, place: (0, 2))
    a_grad = outer_split(outer_z_kernel, place, normed_t, [(x_low, left)], [small_x[:, :512]], 512)
    a_grad = [a_grad[0]] + [turn(a_grad[k], "z", k) for k in (1, 2, 3)]
    keep, keep_c = keep + swap(after(send, a_grad[0], *out_rows[1:]), "c"), keep_c + swap(send_c, "c")
    keep_h = keep_c.astype(BF)
    keep = jnp.concatenate([keep.astype(BF), keep_h, (keep_c - keep_h.astype(F32)).astype(BF)], axis=0)
    far = swap(keep, "xl")
    group = keep.astype(F32) + far.astype(F32)
    bc_low = after(group[:1024].astype(BF), g_zo_z)
    small_s = jnp.concatenate([group[1024:1032] + group[1032:], g_hd], axis=1)
    full = lambda t: (t, fixed(t.shape))
    b_grad = outer_split(outer_side_kernel, place, normed_t, [(x_low, right), full(bc_low), full(gdt)], [small_x[:, 512:], small_s], 384)
    b_first = b_grad[0]
    b_grad = [b_first] + [turn(b_grad[k], "z", k) for k in (1, 2, 3)]
    rows_own, rows_send = mine(bc_low, "c", 0, SEQ)
    rows_far = swap(rows_send, "c")
    bc_own = pair(rows_own, rows_far, "c")
    bc_own = jnp.concatenate([bc_own[0], bc_own[1]], axis=1)
    bc_own = lax.dynamic_slice_in_dim(bc_own, xl * 256, 256, 0)
    token_rows = by_rows(token_kernel, place, [after(gate_low, b_first, bc_own), x_low, gdt], [w_2, w_1, w_1], [lambda place: 0, lambda place: 0, lambda place: 8], [(HALF, F32), (HALF, F32), (SEQ, BF)], 20_000_000_000)
    token_far = swap(after(token_rows[2], *a_grad[1:], *b_grad[1:]), "c")
    pieces = fold(a_grad, b_grad)
    token_far = after(token_far, pieces[1], g_zo_y)
    grad_own = token_rows[0] + wide(token_far[:HALF])
    grad_far = swap((token_rows[1] + wide(token_far[HALF:])).astype(BF), "xl")
    pieces = [pieces[0]] + [turn(pieces[k], "y", k) for k in (1, 2, 3)]

    bc_part = lax.dot_general(bc_own, w_maps, (((1,), (1,)), ((), ())), preferred_element_type=F32)
    grad_normed = (grad_own + wide(grad_far)) + bc_part

    keep, send = sum_pieces(place, pieces, g_zo_y)
    keep, send = sum_far(place, after(keep, grad_far), swap(send, "xh"))
    far = swap(send, "c")

    gain_wide = gain_rows[4]
    rw = resid.astype(F32)
    inv = lax.rsqrt(jnp.mean(rw * rw, axis=-1, keepdims=True) + EPS)
    inner = jnp.sum(gain_wide[None, :] * grad_normed * rw, axis=-1, keepdims=True)
    grad_resid = cotangent.astype(F32) + gain_wide[None, :] * grad_normed * inv - rw * (inv * inv * inv) * inner / 1536

    got = pair(keep, far, "c")
    both = lambda rows, at, width: jnp.concatenate([got[0, rows, at : at + width], got[1, rows, at : at + width]], axis=1)
    main, rest = slice(0, 24), slice(24, 32)
    grad_w_x, grad_w_z, grad_w_out_t = both(main, 0, 768), both(main, 896, 768), both(main, 1664, 768)
    grad_w_dt = both(main, 832, 12)
    bc24, conv24 = both(main, 768, 64), both(rest, 768, 64)
    small_wide = both(rest, 0, 768)
    small_heads = both(rest, 832, 12)

    tall = lambda a, b: jnp.sum(a.astype(F32) * b, axis=1)
    pg = tall(w_z, grad_w_z) + tall(w_x, grad_w_x) + tall(w_dt, grad_w_dt)
    pg, pg_send = mine(pg, "xl", 0, 12)
    bc12, bc_send = mine(bc24, "xl", 0, 12)
    far = swap(jnp.concatenate([bc_send, conv24, jnp.pad(pg_send, (0, 116))[None]], axis=0), "xl")
    got = pair(jnp.concatenate([bc12, conv24], axis=0), far[:20], "xl")
    got = got.reshape(2, 20, 2, 64).transpose(1, 2, 0, 3).reshape(20, 256)
    grad_w_bc, grad_conv_bc = got[:12], got[12:]
    grad_pre_gain = (pg + far[20, :12] + tall(w_bc, grad_w_bc)) / pre_gain.astype(F32)
    return (
        layer_out,
        grad_resid,
        grad_pre_gain,
        grad_w_z,
        grad_w_x,
        grad_w_bc,
        grad_w_dt,
        small_wide[:4],
        small_wide[4],
        grad_conv_bc[:4],
        grad_conv_bc[4],
        small_heads[0],
        small_heads[1],
        small_heads[2],
        small_wide[5],
        grad_w_out_t.T,
    )


def solution(mesh):
    fine = Mesh(mesh.devices.reshape(4, 2, 4, 2, 2), ("z", "xh", "y", "c", "xl"))
    dp, tp, every = ("z", "xh", "y", "c"), "xl", ("z", "xh", "y", "c", "xl")
    return jax.shard_map(
        shards,
        mesh=fine,
        in_specs=(P(every, None), P(every, None), P(dp), P(every), P(dp, tp), P(dp, tp), P(every, None), P(dp, tp), P(None, tp), P(tp), P(), P(), P(tp), P(tp), P(tp), P(tp), P(tp, dp)),
        out_specs=(P(every, None), P(every, None), P(every), P(dp, tp), P(dp, tp), P(every, None), P(dp, tp), P(None, tp), P(tp), P(), P(), P(tp), P(tp), P(tp), P(tp), P(tp, dp)),
        check_vma=False,
    )
```
